32 devices in a mesh: dp: 4 (over y, x), row: 4 (over z), col: 2 (over core).
Axes of the slice: x: 2, y: 2, z: 4, core: 2. Of those that a mesh axis runs over, the one named last changes fastest.
Arguments:
- hidden_in: bfloat16 [2, 4096, 2048], P(None, ('dp', 'row'), 'col'), may hold values from -6 to 6
- attn_gain: float32 [2048], P('col'), may hold values from 0.25 to 1.75
- ffn_gain: float32 [2048], P('col'), may hold values from 0.25 to 1.75
- query_weight: bfloat16 [2048, 2048], P('col', 'row'), may hold values from -0.1875 to 0.1875
- key_weight: bfloat16 [2048, 1024], P('col', 'row'), may hold values from -0.1875 to 0.1875
- value_weight: bfloat16 [2048, 1024], P('col', 'row'), may hold values from -0.125 to 0.125
- output_weight: bfloat16 [2048, 2048], P('row', 'col'), may hold values from -0.5 to 0.5
- gate_weight: bfloat16 [2048, 8192], P('col', 'row'), may hold values from -0.125 to 0.125
- up_weight: bfloat16 [2048, 8192], P('col', 'row'), may hold values from -0.125 to 0.125
- down_weight: bfloat16 [8192, 2048], P('row', 'col'), may hold values from -0.125 to 0.125
- prefix_len: int32 [2, 4], P(None, 'dp'), may hold values from 102 to 512
- out_grad: bfloat16 [2, 4096, 2048], P(None, ('dp', 'row'), 'col'), may hold values from -6 to 6
Outputs:
- output: bfloat16 [2, 4096, 2048], P(None, ('dp', 'row'), 'col')
- input_grad: float32 [2, 4096, 2048], P(None, ('dp', 'row'), 'col')
- grad_attn_gain: float32 [2048], P('col')
- grad_ffn_gain: float32 [2048], P('col')
- grad_query_weight: float32 [2048, 2048], P('col', 'row')
- grad_key_weight: float32 [2048, 1024], P('col', 'row')
- grad_value_weight: float32 [2048, 1024], P('col', 'row')
- grad_output_weight: float32 [2048, 2048], P('row', 'col')
- grad_gate_weight: float32 [2048, 8192], P('col', 'row')
- grad_up_weight: float32 [2048, 8192], P('col', 'row')
- grad_down_weight: float32 [8192, 2048], P('row', 'col')
The draws below stay inside these ranges and needn't reach their ends.
All inputs are finite; a program needn't handle non-finite values.
Results may differ from the reference program's by a relative error of at most 0.025.
Values may be sent and summed in bfloat16 or wider, within the bound.
A program may use at most 320 MiB of HBM per device.

```python
import math
import jax
import jax.numpy as jnp
from jax import lax

WIDTH = 2048
HEADS = 16
KV_HEADS = 8
HEAD_DIM = 128
HIDDEN_SIZE = 8192
SEQ_LEN = 1024
MICRO = 2
TOK_MB = 4096
N_DP = 4


def place_ends(values, rng, least, top_value):
    longest = values.shape.index(max(values.shape))
    spots = []
    for shift in (0, 1):
        where = [jax.random.randint(jax.random.fold_in(rng, axis), (), 0, length) for axis, length in enumerate(values.shape)]
        where[longest] = (where[longest] + shift) % values.shape[longest]
        spots.append(tuple(where))
    return values.at[spots[0]].set(least).at[spots[1]].set(top_value)


def steps_of(key, shape, split, smallest, top_value):
    level, own = 1.0, jax.random.fold_in(key, 6)
    for position, blocks in split:
        steps = jnp.exp(jax.random.uniform(jax.random.fold_in(own, position), (blocks,), jnp.float32, smallest / len(split), top_value / len(split)))
        level = level * jnp.repeat(steps, shape[position] // blocks).reshape([-1 if axis == position else 1 for axis in range(len(shape))])
    return level


def normal_values(key, dims, deviation, limit, shards=(), held_as=jnp.bfloat16):
    values = deviation * jax.random.normal(key, dims, jnp.float32)
    if shards:
        values = values * steps_of(key, dims, shards, -0.22, 0.18)
    return jnp.clip(values, -limit, limit).astype(held_as)


def setup_inputs(seed: int = 0) -> dict:
    seeds = jax.random.split(jax.random.key(seed), 13)
    hidden_in = normal_values(seeds[0], (MICRO, TOK_MB, WIDTH), 1.0, 6.0, ((1, 16), (2, 2)))
    attn_gain = jnp.clip(1.0 + 0.15 * jax.random.normal(seeds[1], (WIDTH,), jnp.float32), 0.25, 1.75)
    ffn_gain = jnp.clip(1.0 + 0.15 * jax.random.normal(seeds[2], (WIDTH,), jnp.float32), 0.25, 1.75)
    query_weight = normal_values(seeds[3], (WIDTH, HEADS * HEAD_DIM), (WIDTH // 2) ** -0.5, 0.1875, ((0, 2), (1, 4)))
    key_weight = normal_values(seeds[4], (WIDTH, KV_HEADS * HEAD_DIM), (WIDTH // 2) ** -0.5, 0.1875, ((0, 2), (1, 4)))
    value_weight = normal_values(seeds[5], (WIDTH, KV_HEADS * HEAD_DIM), WIDTH ** -0.5, 0.125, ((0, 2), (1, 4)))
    output_weight = normal_values(seeds[6], (HEADS * HEAD_DIM, WIDTH), (HEADS * HEAD_DIM // 16) ** -0.5, 0.5, ((0, 4), (1, 2)))
    gate_weight = normal_values(seeds[7], (WIDTH, HIDDEN_SIZE), WIDTH ** -0.5, 0.125, ((0, 2), (1, 4)))
    up_weight = normal_values(seeds[8], (WIDTH, HIDDEN_SIZE), WIDTH ** -0.5, 0.125, ((0, 2), (1, 4)))
    down_weight = normal_values(seeds[9], (HIDDEN_SIZE, WIDTH), (HIDDEN_SIZE // 4) ** -0.5, 0.125, ((0, 4), (1, 2)))
    prefix_len = place_ends(jax.random.randint(seeds[10], (MICRO, N_DP), SEQ_LEN // 10, SEQ_LEN // 2 + 1), jax.random.fold_in(seeds[10], 1), SEQ_LEN // 10, (SEQ_LEN // 2 + 1) - 1).astype(jnp.int32)
    out_grad = normal_values(seeds[11], (MICRO, TOK_MB, WIDTH), 1.0, 6.0, ((1, 16), (2, 2)))
    return {"hidden_in": hidden_in, "attn_gain": attn_gain, "ffn_gain": ffn_gain, "query_weight": query_weight, "key_weight": key_weight, "value_weight": value_weight, "output_weight": output_weight, "gate_weight": gate_weight, "up_weight": up_weight, "down_weight": down_weight, "prefix_len": prefix_len, "out_grad": out_grad}


epsilon = 1e-05
rope_base = 1000000.0
masked_score = -1e+30
highest = lax.Precision.HIGHEST

@jax.custom_vjp
def low(v):
    return lax.optimization_barrier(v.astype(jnp.bfloat16)).astype(jnp.float32)

@jax.custom_vjp
def low_back(v):
    return v

def low_keep(v):
    return (low(v), None)

def low_pass(kept, grad):
    return (grad,)

def back_keep(v):
    return (v, None)

def back_low(kept, grad):
    return (low(grad),)
low.defvjp(low_keep, low_pass)
low_back.defvjp(back_keep, back_low)

def rope_tables(length, size):
    half_size = size // 2
    inverse = rope_base ** (-(jnp.arange(half_size, dtype=jnp.float32) * 2.0 / size))
    angle = jnp.arange(length, dtype=jnp.float32)[:, None] * inverse[None, :]
    cosine = jnp.concatenate([jnp.cos(angle), jnp.cos(angle)], axis=1)[:, None, :]
    sine = jnp.concatenate([jnp.sin(angle), jnp.sin(angle)], axis=1)[:, None, :]
    return (cosine, sine)

def rotate(values):
    half_size = values.shape[-1] // 2
    return jnp.concatenate([-values[..., half_size:], values[..., :half_size]], axis=-1)

def rope(values, cosine, sine):
    return values * cosine + rotate(values) * sine

def product(left_side, right_side):
    return jnp.dot(left_side, right_side, precision=highest)

def rms_scale(values, gain):
    return values * lax.rsqrt(lax.optimization_barrier(jnp.mean(values * values, axis=-1, keepdims=True)) + epsilon) * gain

def attention(queries, keys, values, prefix_one):
    length = queries.shape[0]
    block = min(512, length)
    group = HEADS // KV_HEADS
    keys_wide = jnp.repeat(keys, group, axis=1)
    values_wide = jnp.repeat(values, group, axis=1)
    columns = jnp.arange(length, dtype=jnp.int32)
    scale = 1.0 / math.sqrt(HEAD_DIM)

    def one_block(first_row):
        query_block = lax.dynamic_slice_in_dim(queries, first_row, block, 0)
        raw = jnp.einsum('qhd,khd->hqk', query_block, keys_wide, precision=highest)
        positions = first_row + jnp.arange(block, dtype=jnp.int32)
        allowed = (columns[None, :] <= positions[:, None]) | (columns[None, :] < prefix_one)
        scores = jnp.where(allowed[None], low_back(raw) * scale, masked_score)
        weights = low(jax.nn.softmax(scores, axis=-1))
        return jnp.einsum('hqk,khd->qhd', weights, values_wide, precision=highest)
    starts = jnp.arange(length // block, dtype=jnp.int32) * block
    blocks = lax.map(jax.checkpoint(one_block), starts)
    return blocks.reshape(length, HEADS * HEAD_DIM)

def layer(hidden, params, prefix_one):
    attn_gain, ffn_gain, query_weight, key_weight, value_weight, output_weight, gate_weight, up_weight, down_weight = params
    length = hidden.shape[0]
    cosine, sine = rope_tables(length, HEAD_DIM)
    normed_one = low(rms_scale(hidden, attn_gain))
    query_pre = low_back(product(normed_one, query_weight)).reshape(length, HEADS, HEAD_DIM)
    key_pre = low_back(product(normed_one, key_weight)).reshape(length, KV_HEADS, HEAD_DIM)
    values = low(low_back(product(normed_one, value_weight))).reshape(length, KV_HEADS, HEAD_DIM)
    queries = low(rope(query_pre, cosine, sine))
    keys = low(rope(key_pre, cosine, sine))
    attended = low(low_back(attention(queries, keys, values, prefix_one)))
    middle = hidden + low_back(product(attended, output_weight))
    normed_two = low(rms_scale(middle, ffn_gain))
    gate = low_back(product(normed_two, gate_weight))
    upward = low_back(product(normed_two, up_weight))
    activated = low(jax.nn.silu(gate) * upward)
    return middle + low_back(product(activated, down_weight))

def reference(hidden_in, attn_gain, ffn_gain, query_weight, key_weight, value_weight, output_weight, gate_weight, up_weight, down_weight, prefix_len, out_grad):
    params = tuple((item.astype(jnp.float32) for item in (attn_gain, ffn_gain, query_weight, key_weight, value_weight, output_weight, gate_weight, up_weight, down_weight)))
    sequences = hidden_in.astype(jnp.float32).reshape(MICRO * N_DP, SEQ_LEN, WIDTH)
    cotangents = out_grad.astype(jnp.float32).reshape(MICRO * N_DP, SEQ_LEN, WIDTH)
    prefixes = prefix_len.reshape(MICRO * N_DP).astype(jnp.int32)

    def one_sequence(totals, inputs):
        hidden, cotangent, prefix_one = inputs
        result, pull = jax.vjp(lambda hidden_arg, weights_arg: layer(hidden_arg, weights_arg, prefix_one), hidden, params)
        grads = pull(cotangent)
        totals = jax.tree.map(lambda total_one, grad_one: total_one + grad_one, totals, grads[1])
        return (totals, (result.astype(jnp.bfloat16), grads[0]))
    zeros = jax.tree.map(jnp.zeros_like, params)
    totals, (results, input_grads) = lax.scan(one_sequence, zeros, (sequences, cotangents, prefixes))
    return (results.reshape(MICRO, TOK_MB, WIDTH), input_grads.reshape(MICRO, TOK_MB, WIDTH), totals[0], totals[1], totals[2], totals[3], totals[4], totals[5], totals[6], totals[7], totals[8])
```

```python
import functools
import math

import jax
import jax.numpy as jnp
from jax import lax
from jax.experimental import pallas as pl
from jax.experimental.pallas import tpu as pltpu
from jax.sharding import PartitionSpec as P

WIDTH = 2048
HEADS = 16
KV_HEADS = 8
HEAD_DIM = 128
PREFIX_TOP = 512

epsilon = 1e-05
rope_base = 1000000.0
scale = 1.0 / math.sqrt(HEAD_DIM)
MIB = 1 << 20
F32 = jnp.float32
BF16 = jnp.bfloat16

NT = (((1,), (1,)), ((), ()))
NN = (((1,), (0,)), ((), ()))
TN = (((0,), (0,)), ((), ()))


def dot(left_side, right_side, dims):
    return lax.dot_general(left_side, right_side, dims, preferred_element_type=F32)


def params(mib, grid_rank):
    return pltpu.CompilerParams(
        dimension_semantics=("arbitrary",) * grid_rank, vmem_limit_bytes=mib * MIB
    )


def cost(flops, nbytes, exps=0):
    return pl.CostEstimate(flops=int(flops), bytes_accessed=int(nbytes), transcendentals=int(exps))


def whole(shape):
    return pl.BlockSpec(shape, lambda *_: (0,) * len(shape))


def rope_tables(length):
    half_size = HEAD_DIM // 2
    inverse = rope_base ** (-(jnp.arange(half_size, dtype=F32) * 2.0 / HEAD_DIM))
    angle = jnp.arange(length, dtype=F32)[:, None] * inverse[None, :]
    cosine = jnp.concatenate([jnp.cos(angle), jnp.cos(angle)], axis=1)
    signed = jnp.concatenate([-jnp.sin(angle), jnp.sin(angle)], axis=1)
    return cosine, signed


def rope(values, cosine, signed):
    return values * cosine + pltpu.roll(values, HEAD_DIM // 2, 1) * signed


def rope_back(values, cosine, signed):
    return values * cosine - pltpu.roll(values, HEAD_DIM // 2, 1) * signed


def attend_back_kernel(
    heads, block, prefix_ref, dz_own_ref, dz_oth_ref, wo_own_ref, wo_oth_ref, qkv_ref, log_ref,
    cos_ref, sin_ref, grad_ref, dk_ref, dv_ref, kt_ref,
):
    step = pl.program_id(0)
    length = qkv_ref.shape[0]
    count = length // block
    k_col, v_col = heads * HEAD_DIM, (heads + 1) * HEAD_DIM

    @pl.when(step == 0)
    def _():
        dk_ref[...] = jnp.zeros_like(dk_ref)
        dv_ref[...] = jnp.zeros_like(dv_ref)
        kt_ref[...] = qkv_ref[:, pl.ds(k_col, HEAD_DIM)].T

    for index in range(count):

        @pl.when(step == index)
        def _(index=index):
            first = index * block
            rows = pl.ds(first, block)
            extent = min(length, max(first + block, PREFIX_TOP))
            upto = pl.ds(0, extent)
            grads = dot(dz_own_ref[...], wo_own_ref[...], NT)
            grads = (grads + dot(dz_oth_ref[...], wo_oth_ref[...], NT)).astype(BF16)
            keys = qkv_ref[upto, pl.ds(k_col, HEAD_DIM)]
            values = qkv_ref[upto, pl.ds(v_col, HEAD_DIM)]
            key_at = lax.broadcasted_iota(jnp.int32, (extent, block), 0)
            query_at = lax.broadcasted_iota(jnp.int32, (extent, block), 1) + first
            allowed = (key_at <= query_at) | (key_at < prefix_ref[0])
            cosine, signed = cos_ref[rows, :], sin_ref[rows, :]
            for head in range(heads):
                cols = pl.ds(head * HEAD_DIM, HEAD_DIM)
                query = qkv_ref[rows, cols]
                grad = grads[:, head * HEAD_DIM : (head + 1) * HEAD_DIM]
                raw = dot(keys, query, NT) * scale - log_ref[pl.ds(head, 1), rows]
                probs = jnp.exp(jnp.where(allowed, raw, -1e30))
                dv_ref[upto, :] += dot(probs.astype(BF16), grad, NN)
                prob_grad = dot(values, grad, NT)
                inner = jnp.sum(probs * prob_grad, axis=0, keepdims=True)
                rounded = (probs * (prob_grad - inner) * scale).astype(BF16)
                dk_ref[upto, :] += dot(rounded, query, NN)
                dq = dot(kt_ref[:, upto], rounded, NN).T
                grad_ref[rows, cols] = rope_back(dq, cosine, signed).astype(BF16)

    @pl.when(step == count - 1)
    def _():
        dk = rope_back(dk_ref[...], cos_ref[...], sin_ref[...])
        grad_ref[:, pl.ds(k_col, HEAD_DIM)] = dk.astype(BF16)
        grad_ref[:, pl.ds(v_col, HEAD_DIM)] = dv_ref[...].astype(BF16)


def attend_back(prefix, dz_own, dz_oth, wo_own, wo_oth, qkv, logs, tables, heads):
    length, depth = dz_own.shape
    block = min(256, length)
    count = length // block
    rows_spec = pl.BlockSpec((block, depth), lambda i, p: (i, 0))
    return pl.pallas_call(
        functools.partial(attend_back_kernel, heads, block),
        grid_spec=pltpu.PrefetchScalarGridSpec(
            num_scalar_prefetch=1,
            grid=(count,),
            in_specs=[
                rows_spec, rows_spec, whole(wo_own.shape), whole(wo_oth.shape), whole(qkv.shape),
                whole(logs.shape), whole(tables[0].shape), whole(tables[1].shape),
            ],
            out_specs=whole(qkv.shape),
            scratch_shapes=[
                pltpu.VMEM((length, HEAD_DIM), F32),
                pltpu.VMEM((length, HEAD_DIM), F32),
                pltpu.VMEM((HEAD_DIM, length), BF16),
            ],
        ),
        out_shape=jax.ShapeDtypeStruct(qkv.shape, BF16),
        compiler_params=params(40, 1),
        cost_estimate=cost(
            4 * length * depth * wo_own.shape[0] + 20 * heads * length * length * HEAD_DIM,
            4 * length * depth,
            heads * length * length,
        ),
    )(prefix, dz_own, dz_oth, wo_own, wo_oth, qkv, logs, *tables)


def units_kernel(
    chunk, n_own, n_oth, g_own, g_oth, wg_own, wg_oth, wu_own, wu_oth, wd_own, wd_oth,
    act_ref, gate_ref, up_ref,
):
    @pl.loop(0, n_own.shape[0] // chunk)
    def _(index):
        rows = pl.ds(pl.multiple_of(index * chunk, chunk), chunk)
        gate = dot(n_own[rows, :], wg_own[...], NN) + dot(n_oth[rows, :], wg_oth[...], NN)
        up = dot(n_own[rows, :], wu_own[...], NN) + dot(n_oth[rows, :], wu_oth[...], NN)
        da = dot(g_own[rows, :], wd_own[...], NT) + dot(g_oth[rows, :], wd_oth[...], NT)
        sigmoid = 1.0 / (1.0 + jnp.exp(-gate))
        silu = gate * sigmoid
        act_ref[rows, :] = (silu * up).astype(BF16)
        gate_ref[rows, :] = (da * up * sigmoid * (1.0 + gate * (1.0 - sigmoid))).astype(BF16)
        up_ref[rows, :] = (da * silu).astype(BF16)


def units(n_own, n_oth, g_own, g_oth, wg_own, wg_oth, wu_own, wu_oth, wd_own, wd_oth):
    length, depth = n_own.shape
    share = wg_own.shape[1]
    block = min(256, share)
    chunk = min(256, length)
    col_spec = pl.BlockSpec((depth, block), lambda i: (0, i))
    row_spec = pl.BlockSpec((block, depth), lambda i: (i, 0))
    out_spec = pl.BlockSpec((length, block), lambda i: (0, i))
    return pl.pallas_call(
        functools.partial(units_kernel, chunk),
        grid=(share // block,),
        in_specs=[whole(n_own.shape)] * 4 + [col_spec] * 4 + [row_spec] * 2,
        out_specs=[out_spec] * 3,
        out_shape=[jax.ShapeDtypeStruct((length, share), BF16)] * 3,
        compiler_params=params(48, 1),
        cost_estimate=cost(
            12 * length * depth * share,
            8 * length * depth + 12 * depth * share + 6 * length * share,
            length * share,
        ),
    )(n_own, n_oth, g_own, g_oth, wg_own, wg_oth, wu_own, wu_oth, wd_own, wd_oth)


def sum_products_kernel(count, dims, *refs):
    total = dot(refs[0][...], refs[count][...], dims)
    for index in range(1, count):
        total = total + dot(refs[index][...], refs[count + index][...], dims)
    refs[-1][...] = total.astype(BF16)


def sum_products(lefts, rights, dims):
    rows = lefts[0].shape[0]
    columns = rights[0].shape[0 if dims is NT else 1]
    block = min(256, columns)
    if dims is NT:
        specs = [pl.BlockSpec((block, r.shape[1]), lambda i: (i, 0)) for r in rights]
    else:
        specs = [pl.BlockSpec((r.shape[0], block), lambda i: (0, i)) for r in rights]
    depth = sum(left.shape[1] for left in lefts)
    return pl.pallas_call(
        functools.partial(sum_products_kernel, len(lefts), dims),
        grid=(columns // block,),
        in_specs=[whole(left.shape) for left in lefts] + specs,
        out_specs=pl.BlockSpec((rows, block), lambda i: (0, i)),
        out_shape=jax.ShapeDtypeStruct((rows, columns), BF16),
        compiler_params=params(48, 1),
        cost_estimate=cost(
            2 * rows * depth * columns, 2 * (rows * depth + depth * columns + rows * columns)
        ),
    )(*lefts, *rights)


def grads_kernel(groups, batches, nb, shared_left, c_ref, *refs):
    shared = refs[:batches]
    outs = refs[batches + 2 * groups * batches :]
    part = pl.program_id(0) // nb
    for group in range(groups):
        for half in range(2):
            at = group * 2 + half

            @pl.when(part == at)
            def _(group=group, at=at):
                total = None
                for m in range(batches):
                    moving = refs[batches + at * batches + m][...]
                    pair = (shared[m][...], moving) if shared_left else (moving, shared[m][...])
                    term = dot(pair[0], pair[1], TN)
                    total = term if total is None else total + term
                outs[group][...] = total.astype(BF16)


def weight_grads(col_index, shared, groups, shared_left):
    batches = len(shared)
    tokens, shared_width = shared[0].shape
    half_width = groups[0][0][0].shape[1]
    block = min(256, half_width)
    nb = half_width // block
    steps = len(groups) * 2 * nb

    def moving_spec(at):
        return pl.BlockSpec((tokens, block), lambda i, c: (0, jnp.clip(i - at * nb, 0, nb - 1)))

    def out_spec(group):
        def place(i, c):
            inner = jnp.clip(i - group * 2 * nb, 0, 2 * nb - 1)
            half = inner // nb
            at = jnp.where(half == 0, c[0], 1 - c[0]) * nb + inner % nb
            return (0, at) if shared_left else (at, 0)

        shape = (shared_width, block) if shared_left else (block, shared_width)
        return pl.BlockSpec(shape, place)

    if shared_left:
        out_dims = (shared_width, 2 * half_width)
    else:
        out_dims = (2 * half_width, shared_width)
    moving = [x for group in groups for half in group for x in half]
    moving_specs = [moving_spec(at) for at in range(2 * len(groups)) for _ in range(batches)]
    return pl.pallas_call(
        functools.partial(grads_kernel, len(groups), batches, nb, shared_left),
        grid_spec=pltpu.PrefetchScalarGridSpec(
            num_scalar_prefetch=1,
            grid=(steps,),
            in_specs=[whole(s.shape) for s in shared] + moving_specs,
            out_specs=[out_spec(group) for group in range(len(groups))],
        ),
        out_shape=[jax.ShapeDtypeStruct(out_dims, BF16) for _ in groups],
        compiler_params=params(48, 1),
        cost_estimate=cost(
            4 * len(groups) * batches * tokens * shared_width * half_width,
            2 * batches * tokens * (shared_width + 2 * len(groups) * half_width),
        ),
    )(col_index.reshape(1), *shared, *moving)


class Line:
    def __init__(self, n):
        self.n = n
        self.r = lax.axis_index("row")
        self.c = lax.axis_index("col")

    def copy(self, src, dst, send, recv, **where):
        return pltpu.make_async_remote_copy(
            src_ref=src, dst_ref=dst, send_sem=send, recv_sem=recv, device_id=where,
            device_id_type=pl.DeviceIdType.MESH,
        )

    def up(self, src, dst, send, recv):
        return self.copy(src, dst, send, recv, row=self.r + 1)

    def down(self, src, dst, send, recv):
        return self.copy(src, dst, send, recv, row=self.r - 1)

    def across(self, src, dst, send, recv):
        return self.copy(src, dst, send, recv, col=1 - self.c)

    def barrier(self):
        barrier = pltpu.get_barrier_semaphore()

        def signal(**where):
            pl.semaphore_signal(
                barrier, inc=1, device_id=where, device_id_type=pl.DeviceIdType.MESH
            )

        @pl.when(self.r > 0)
        def _():
            signal(row=self.r - 1)

        @pl.when(self.r < self.n - 1)
        def _():
            signal(row=self.r + 1)

        signal(col=1 - self.c)

        at_end = (self.r == 0) | (self.r == self.n - 1)

        @pl.when(at_end)
        def _():
            pl.semaphore_wait(barrier, 2)

        @pl.when(jnp.logical_not(at_end))
        def _():
            pl.semaphore_wait(barrier, 3)

    def nearest(self, k):
        n = self.n
        code = 0
        for r in range(n):
            order = sorted(range(n), key=lambda q: (abs(q - r), q))
            code += order[k] * n**r
        place, result = self.r * 0 + code, 0
        for r in range(n):
            result = result + (place // n**r) % n * (1 - jnp.minimum(jnp.abs(self.r - r), 1))
        return result


class Gather:
    def __init__(self, line, own, oth, sends, recvs):
        self.line, self.own, self.oth, self.sends, self.recvs = line, own, oth, sends, recvs

    def hop(self, kind, q):
        way = (self.line.up, self.line.down)[kind]
        return way(self.own.at[q], self.own.at[q], self.sends.at[q, kind], self.recvs.at[q, 0])

    def cross(self, q):
        return self.line.across(
            self.own.at[q], self.oth.at[q], self.sends.at[q, 2], self.recvs.at[q, 1]
        )

    def start(self):
        line = self.line

        @pl.when(line.r < line.n - 1)
        def _():
            self.hop(0, line.r).start()

        @pl.when(line.r > 0)
        def _():
            self.hop(1, line.r).start()

        self.cross(line.r).start()

    def step(self, s):
        line = self.line
        low, high = line.r - s, line.r + s

        @pl.when(low >= 0)
        def _():
            self.hop(0, low).wait_recv()

            @pl.when(line.r < line.n - 1)
            def _():
                self.hop(0, low).start()

            self.cross(low).start()

        @pl.when(high <= line.n - 1)
        def _():
            self.hop(1, high).wait_recv()

            @pl.when(line.r > 0)
            def _():
                self.hop(1, high).start()

            self.cross(high).start()

    def arrive(self, q):
        self.cross(q).wait_recv()

    def drain(self):
        line = self.line
        for q in range(line.n):

            @pl.when((line.r >= q) & (line.r < line.n - 1))
            def _(q=q):
                self.hop(0, q).wait_send()

            @pl.when((line.r <= q) & (line.r > 0))
            def _(q=q):
                self.hop(1, q).wait_send()

            self.cross(q).wait_send()


class Scatter:
    def __init__(self, line, part, ups, downs, sends, recvs):
        self.line, self.part, self.ups, self.downs = line, part, ups, downs
        self.sends, self.recvs = sends, recvs

    def hop(self, kind, s, target):
        way = (self.line.up, self.line.down)[kind]
        box = (self.ups, self.downs)[kind]
        return way(
            self.part.at[target], box.at[s - 1], self.sends.at[kind, s - 1], self.recvs.at[kind, s - 1]
        )

    def step(self, s):
        line = self.line
        for kind in range(2):
            behind = line.r if kind == 0 else line.n - 1 - line.r
            target = line.r + line.n - s if kind == 0 else line.r - (line.n - s)
            box = (self.ups, self.downs)[kind]

            @pl.when(behind <= s - 1)
            def _(kind=kind, behind=behind, target=target, box=box):
                if s > 1:

                    @pl.when(behind >= 1)
                    def _():
                        self.hop(kind, s - 1, target).wait_recv()
                        self.part[target] = (
                            self.part[target].astype(F32) + box[s - 2].astype(F32)
                        ).astype(BF16)

                self.hop(kind, s, target).start()

    def total(self, out):
        line = self.line
        last = line.n - 1
        out[...] = self.part[line.r].astype(F32)

        @pl.when(line.r >= 1)
        def _():
            self.hop(0, last, line.r).wait_recv()
            out[...] += self.ups[last - 1].astype(F32)

        @pl.when(line.r <= last - 1)
        def _():
            self.hop(1, last, line.r).wait_recv()
            out[...] += self.downs[last - 1].astype(F32)

    def drain(self):
        line = self.line
        for s in range(1, line.n):

            @pl.when(line.r <= s - 1)
            def _(s=s):
                self.hop(0, s, line.r + line.n - s).wait_send()

            @pl.when(line.n - 1 - line.r <= s - 1)
            def _(s=s):
                self.hop(1, s, line.r - (line.n - s)).wait_send()


def communicate(number, mib):
    return pltpu.CompilerParams(
        collective_id=number, has_side_effects=True, vmem_limit_bytes=mib * MIB
    )


def forward_kernel(
    n, heads, shared_kv,
    prefix_ref, normed_ref, cos_ref, sin_ref, grad_in, wq, wk, wv, wo, wgate, wup, wdown,
    n1_out, g_own_out, g_oth_out, qkv_out, log_out, o_own_out, o_oth_out, sum_out,
    gate_from, up_from, down_from, wo_from,
    n1_own, n1_oth, g_own, g_oth, w_own, w_from, wo_ref, qkv_ref, vt_ref, o_own, o_oth, log_ref,
    part, ups, downs, total,
    gather_sends, gather_recvs, scatter_sends, scatter_recvs, cross_sends, cross_recvs, local_sems,
):
    batches, tokens, depth = normed_ref.shape
    length = n * tokens
    line = Line(n)
    r, c = line.r, line.c
    q_width = heads * HEAD_DIM
    k_col, v_col = q_width, q_width + HEAD_DIM
    share = wgate.shape[1] // 2
    kv_own = 0 if shared_kv else c * HEAD_DIM
    kv_oth = 0 if shared_kv else (1 - c) * HEAD_DIM

    def lanes(at, size):
        return pl.ds(pl.multiple_of(at, 128), size)

    local_count = [0]

    def local(src, dst):
        copy = pltpu.make_async_copy(src, dst, local_sems.at[local_count[0]])
        local_count[0] += 1
        copy.start()
        return copy

    cross_count = [0]

    def cross(src, dst):
        at = cross_count[0]
        cross_count[0] += 1
        return line.across(src, dst, cross_sends.at[at], cross_recvs.at[at])

    loads = [
        local(wq.at[:, lanes(c * q_width, q_width)], w_own.at[:, pl.ds(0, q_width)]),
        local(wk.at[:, lanes(kv_own, HEAD_DIM)], w_own.at[:, pl.ds(k_col, HEAD_DIM)]),
        local(wv.at[:, lanes(kv_own, HEAD_DIM)], w_own.at[:, pl.ds(v_col, HEAD_DIM)]),
    ]
    wo_load = local(wo, wo_ref)
    g_loads = [local(grad_in.at[m], g_own.at[m, r]) for m in range(batches)]
    n1_own[0, r] = normed_ref[0]
    n1_own[1, r] = normed_ref[1]
    line.barrier()

    n1 = [
        Gather(line, n1_own.at[m], n1_oth.at[m], gather_sends.at[m], gather_recvs.at[m])
        for m in range(batches)
    ]
    g = [
        Gather(
            line, g_own.at[m], g_oth.at[m], gather_sends.at[batches + m], gather_recvs.at[batches + m]
        )
        for m in range(batches)
    ]
    rs = [
        Scatter(line, part.at[m], ups.at[m], downs.at[m], scatter_sends.at[m], scatter_recvs.at[m])
        for m in range(batches)
    ]
    n1[0].start()
    w_cross = [
        cross(wq.at[:, lanes((1 - c) * q_width, q_width)], w_from.at[:, pl.ds(0, q_width)]),
        cross(wk.at[:, lanes(kv_oth, HEAD_DIM)], w_from.at[:, pl.ds(k_col, HEAD_DIM)]),
        cross(wv.at[:, lanes(kv_oth, HEAD_DIM)], w_from.at[:, pl.ds(v_col, HEAD_DIM)]),
    ]
    for copy in w_cross:
        copy.start()
    for copy in loads:
        copy.wait()
    for copy in w_cross:
        copy.wait_recv()

    def project(m, q):
        n1[m].arrive(q)
        rows = pl.ds(pl.multiple_of(q * tokens, tokens), tokens)
        pre = dot(n1_own[m, q], w_own[...], NN) + dot(n1_oth[m, q], w_from[...], NN)
        cosine, signed = cos_ref[rows, :], sin_ref[rows, :]
        for head in range(heads + 1):
            piece = pre[:, head * HEAD_DIM : (head + 1) * HEAD_DIM]
            qkv_ref[m, rows, pl.ds(head * HEAD_DIM, HEAD_DIM)] = rope(piece, cosine, signed).astype(BF16)
        values = pre[:, v_col : v_col + HEAD_DIM].astype(BF16)
        qkv_ref[m, rows, pl.ds(v_col, HEAD_DIM)] = values
        vt_ref[m, :, rows] = values.T

    block = min(256, length)
    count = length // block

    def attend_block(m, index):
        first = index * block
        extent = min(length, max(first + block, PREFIX_TOP))
        keys = qkv_ref[m, pl.ds(0, extent), pl.ds(k_col, HEAD_DIM)]
        key_at = lax.broadcasted_iota(jnp.int32, (extent, block), 0)
        query_at = lax.broadcasted_iota(jnp.int32, (extent, block), 1) + first
        allowed = (key_at <= query_at) | (key_at < prefix_ref[m, 0])
        for head in range(heads):
            cols = pl.ds(head * HEAD_DIM, HEAD_DIM)
            query = qkv_ref[m, pl.ds(first, block), cols]
            scores = jnp.where(allowed, dot(keys, query, NT) * scale, -1e30)
            topmost = jnp.max(scores, axis=0, keepdims=True)
            exponent = jnp.exp(scores - topmost)
            summed = jnp.sum(exponent, axis=0, keepdims=True)
            weights = (exponent * (1.0 / summed)).astype(BF16)
            result = dot(vt_ref[m, :, pl.ds(0, extent)], weights, NN)
            o_own[m, pl.ds(first, block), cols] = result.T.astype(BF16)
            log_ref[m, pl.ds(head, 1), pl.ds(first, block)] = topmost + jnp.log(summed)

    def project_out(m):
        @pl.loop(0, n)
        def _(p):
            rows = pl.ds(pl.multiple_of(p * tokens, tokens), tokens)
            own_rows = pl.ds(pl.multiple_of(c * q_width, q_width), q_width)
            oth_rows = pl.ds(pl.multiple_of((1 - c) * q_width, q_width), q_width)
            value = dot(o_own[m, rows, :], wo_ref[own_rows, :], NN)
            value = value + dot(o_oth[m, rows, :], wo_ref[oth_rows, :], NN)
            part[m, p] = value.astype(BF16)

    def walk(item, m, first, last):
        for k in range(first, last):
            item.step(k)
            project(m, line.nearest(k))

    project(0, r)
    walk(n1[0], 0, 1, n - 1)
    n1[1].start()
    walk(n1[0], 0, n - 1, n)
    project(1, r)
    half = (n + 1) // 2
    for index in range(count // 2):
        attend_block(0, index)
    walk(n1[1], 1, 1, half)
    for index in range(count // 2, count):
        attend_block(0, index)
    o_cross = [cross(o_own.at[m], o_oth.at[m]) for m in range(batches)]
    o_cross[0].start()
    walk(n1[1], 1, half, n - 1)
    o_cross[0].wait_recv()
    wo_load.wait()
    project_out(0)
    rs[0].step(1)
    g_loads[0].wait()
    g[0].start()
    walk(n1[1], 1, n - 1, n)
    for s in range(2, half + 1):
        rs[0].step(s)
    for index in range(count // 2):
        attend_block(1, index)
    for s in range(half + 1, n):
        rs[0].step(s)
    for k in range(1, half):
        g[0].step(k)
    for index in range(count // 2, count):
        attend_block(1, index)
    o_cross[1].start()
    for k in range(half, n - 1):
        g[0].step(k)
    o_cross[1].wait_recv()
    project_out(1)
    rs[1].step(1)
    g_loads[1].wait()
    g[1].start()
    rs[0].total(total.at[0])
    big_cross = [
        cross(wgate.at[:, lanes((1 - c) * share, share)], gate_from),
        cross(wup.at[:, lanes((1 - c) * share, share)], up_from),
        cross(wdown.at[pl.ds(pl.multiple_of((1 - c) * share, share), share), :], down_from),
        cross(wo.at[pl.ds(pl.multiple_of((1 - c) * q_width, q_width), q_width), :], wo_from),
    ]
    for copy in big_cross:
        copy.start()
    stores = [
        local(n1_own, n1_out), local(qkv_ref, qkv_out), local(log_ref, log_out),
        local(o_own, o_own_out), local(o_oth, o_oth_out), local(total.at[0], sum_out.at[0]),
    ]
    g[0].step(n - 1)
    for s in range(2, n):
        g[1].step(s - 1)
        rs[1].step(s)
    rs[1].total(total.at[1])
    stores.append(local(total.at[1], sum_out.at[1]))
    g[1].step(n - 1)
    for m in range(batches):
        for q in range(n):
            g[m].arrive(q)
    stores += [local(g_own, g_own_out), local(g_oth, g_oth_out)]
    for copy in big_cross:
        copy.wait_recv()
    for copy in big_cross + w_cross + o_cross:
        copy.wait_send()
    for item in n1 + g + rs:
        item.drain()
    for copy in stores:
        copy.wait()


def forward(prefix, normed, tables, grad_in, wq, wk, wv, wo, wgate, wup, wdown, n, heads, shared_kv):
    batches, tokens, depth = normed.shape
    length = n * tokens
    width = (heads + 2) * HEAD_DIM
    q_width = heads * HEAD_DIM
    share = wgate.shape[1] // 2
    vmem = pl.BlockSpec(memory_space=pltpu.VMEM)
    anywhere = pl.BlockSpec(memory_space=pl.ANY)
    gathered = (batches, n, tokens, depth)
    shapes = [
        (gathered, BF16), (gathered, BF16), (gathered, BF16),
        ((batches, length, width), BF16), ((batches, 8, length), F32),
        ((batches, length, q_width), BF16), ((batches, length, q_width), BF16),
        ((batches, tokens, depth), F32),
        ((depth, share), BF16), ((depth, share), BF16), ((share, depth), BF16), ((q_width, depth), BF16),
    ]
    boxes = (batches, n - 1, tokens, depth)
    return pl.pallas_call(
        functools.partial(forward_kernel, n, heads, shared_kv),
        in_specs=[pl.BlockSpec(memory_space=pltpu.SMEM), vmem, vmem, vmem] + [anywhere] * 8,
        out_specs=[anywhere] * len(shapes),
        out_shape=[jax.ShapeDtypeStruct(*item) for item in shapes],
        scratch_shapes=[
            pltpu.VMEM(gathered, BF16), pltpu.VMEM(gathered, BF16),
            pltpu.VMEM(gathered, BF16), pltpu.VMEM(gathered, BF16),
            pltpu.VMEM((depth, width), BF16), pltpu.VMEM((depth, width), BF16),
            pltpu.VMEM(wo.shape, BF16), pltpu.VMEM((batches, length, width), BF16),
            pltpu.VMEM((batches, HEAD_DIM, length), BF16),
            pltpu.VMEM((batches, length, q_width), BF16), pltpu.VMEM((batches, length, q_width), BF16),
            pltpu.VMEM((batches, 8, length), F32),
            pltpu.VMEM(gathered, BF16), pltpu.VMEM(boxes, BF16), pltpu.VMEM(boxes, BF16),
            pltpu.VMEM((batches, tokens, depth), F32),
            pltpu.SemaphoreType.DMA((2 * batches, n, 3)), pltpu.SemaphoreType.DMA((2 * batches, n, 2)),
            pltpu.SemaphoreType.DMA((batches, 2, n - 1)), pltpu.SemaphoreType.DMA((batches, 2, n - 1)),
            pltpu.SemaphoreType.DMA((9,)), pltpu.SemaphoreType.DMA((9,)),
            pltpu.SemaphoreType.DMA((16,)),
        ],
        compiler_params=communicate(1, 56),
        cost_estimate=cost(
            batches * (4 * length * depth * width + 8 * heads * length * length * HEAD_DIM),
            40 * MIB,
        ),
    )(prefix, normed, *tables, grad_in, wq, wk, wv, wo, wgate, wup, wdown)


def other_core(values):
    count = lax.axis_size("col")
    return lax.ppermute(values, "col", [(i, (i + 1) % count) for i in range(count)])


def place_kernel(n, row_ref, *refs):
    pieces, out, sems = refs[: 2 * n - 1], refs[2 * n - 1], refs[2 * n]
    size = pieces[0].shape[0]
    for row in range(n):

        @pl.when(row_ref[0] == row)
        def _(row=row):
            copies = [
                pltpu.make_async_copy(
                    pieces[at - row + n - 1], out.at[pl.ds(at * size, size)], sems.at[at]
                )
                for at in range(n)
            ]
            for copy in copies:
                copy.start()
            for copy in copies:
                copy.wait()


def place(row_index, pieces):
    n = (len(pieces) + 1) // 2
    size, width = pieces[0].shape
    return pl.pallas_call(
        functools.partial(place_kernel, n),
        in_specs=[pl.BlockSpec(memory_space=pltpu.SMEM)]
        + [pl.BlockSpec(memory_space=pl.ANY)] * len(pieces),
        out_specs=pl.BlockSpec(memory_space=pltpu.VMEM),
        out_shape=jax.ShapeDtypeStruct((n * size, width), pieces[0].dtype),
        scratch_shapes=[pltpu.SemaphoreType.DMA((n,))],
        cost_estimate=cost(0, 4 * n * size * width),
    )(row_index.reshape(1), *pieces)


def row_gather(row_index, shard):
    n = lax.axis_size("row")
    below, above = [shard], [shard]
    for step in range(1, n):
        below.append(lax.ppermute(below[-1], "row", [(i, i + 1) for i in range(step - 1, n - 1)]))
        above.append(lax.ppermute(above[-1], "row", [(i, i - 1) for i in range(1, n - step + 1)]))
    return place(row_index, below[:0:-1] + above)


def row_scatter(row_index, partial_sums):
    n = lax.axis_size("row")
    width = partial_sums.shape[1]
    pieces = partial_sums.reshape(n, -1, width)

    def piece(at):
        return lax.dynamic_index_in_dim(pieces, jnp.clip(at, 0, n - 1), 0, keepdims=False).astype(F32)

    up = down = None
    for step in range(1, n):
        far = n - step
        send_up, send_down = piece(row_index + far), piece(row_index - far)
        if up is not None:
            send_up, send_down = send_up + up.astype(F32), send_down + down.astype(F32)
        up = lax.ppermute(send_up.astype(BF16), "row", [(i, i + 1) for i in range(step)])
        down = lax.ppermute(send_down.astype(BF16), "row", [(i, i - 1) for i in range(n - step, n)])
    total = piece(row_index)
    if up is not None:
        total = total + up.astype(F32) + down.astype(F32)
    return total


def butterfly(values, axes):
    for axis in axes:
        n = lax.axis_size(axis)
        reach = 1
        while reach < n:
            values = values + lax.ppermute(values, axis, [(i, i ^ reach) for i in range(n)])
            reach *= 2
    return values


def after(values, *earlier):
    return lax.optimization_barrier((values, *earlier))[0]


def body(
    hidden_in,
    attn_gain,
    ffn_gain,
    query_weight,
    key_weight,
    value_weight,
    output_weight,
    gate_weight,
    up_weight,
    down_weight,
    prefix_len,
    out_grad,
):
    col_count, row_count = lax.axis_size("col"), lax.axis_size("row")
    col_index = lax.axis_index("col").astype(jnp.int32)
    row_index = lax.axis_index("row").astype(jnp.int32)
    batches, tokens, _ = hidden_in.shape
    length = tokens * row_count
    heads = query_weight.shape[1] // HEAD_DIM // col_count
    row_kv = key_weight.shape[1] // HEAD_DIM
    shared_kv = row_kv < col_count
    q_width = heads * HEAD_DIM
    share = gate_weight.shape[1] // col_count
    tables = rope_tables(length)

    def parts(weight, axis, size, fixed=False):
        if fixed:
            return weight, weight
        own = lax.dynamic_slice_in_dim(weight, col_index * size, size, axis)
        oth = lax.dynamic_slice_in_dim(weight, (1 - col_index) * size, size, axis)
        return own, oth

    q_own, q_oth = parts(query_weight, 1, q_width)
    k_own, k_oth = parts(key_weight, 1, HEAD_DIM, shared_kv)
    v_own, v_oth = parts(value_weight, 1, HEAD_DIM, shared_kv)
    qkv_own = jnp.concatenate([q_own, k_own, v_own], axis=1)
    qkv_oth = jnp.concatenate([q_oth, k_oth, v_oth], axis=1)
    out_own, out_oth = parts(output_weight, 0, q_width)
    gate_own, gate_oth = parts(gate_weight, 1, share)
    up_own, up_oth = parts(up_weight, 1, share)
    down_own, down_oth = parts(down_weight, 0, share)

    resid = hidden_in.astype(F32)
    squares = jnp.sum(resid * resid, axis=2)
    scale_one = lax.rsqrt((squares + other_core(squares)) / WIDTH + epsilon)[..., None]
    normed = (resid * scale_one * attn_gain).astype(BF16)
    (
        n1_all, g_own, g_oth, qkv, logs, o_own, o_oth, attn_sum, gate_from, up_from, down_from, out_from,
    ) = forward(
        prefix_len, normed, tables, out_grad, query_weight, key_weight, value_weight, output_weight,
        gate_weight, up_weight, down_weight, row_count, heads, shared_kv,
    )
    flat = (batches, length, -1)
    n1_all, g_own, g_oth = (item.reshape(flat) for item in (n1_all, g_own, g_oth))
    n1 = [(n1_all[m], None) for m in range(batches)]
    g = [(g_own[m], g_oth[m]) for m in range(batches)]
    heads_out = [(o_own[m], o_oth[m]) for m in range(batches)]
    kept = [(qkv[m], logs[m]) for m in range(batches)]

    mids, scales, n2 = [], [], []
    for m in range(batches):
        middle = resid[m] + attn_sum[m]
        squares = jnp.sum(middle * middle, axis=1)
        scale_two = lax.rsqrt((squares + other_core(squares)) / WIDTH + epsilon)[:, None]
        gathered = row_gather(row_index, (middle * scale_two * ffn_gain).astype(BF16))
        mids.append(middle)
        scales.append(scale_two)
        n2.append((gathered, other_core(gathered)))

    acts, dgates, dups = [], [], []
    for m in range(batches):
        act, dgate, dup = units(
            *n2[m], *g[m], gate_own, gate_from, up_own, up_from, down_own, down_from
        )
        acts.append((act, other_core(act)))
        dgates.append((dgate, other_core(dgate)))
        dups.append((dup, other_core(dup)))

    def halves(pairs):
        return [[pair[side] for pair in pairs] for side in range(2)]

    (down_grad,) = weight_grads(col_index, [pair[0] for pair in g], [halves(acts)], False)
    gate_grad, up_grad = weight_grads(
        col_index, [pair[0] for pair in n2], [halves(dgates), halves(dups)], True
    )
    down_sum = lax.psum(down_grad, "dp")
    gate_grad, up_grad = lax.optimization_barrier((gate_grad, up_grad, down_sum))[:2]
    gate_sum, up_sum = lax.psum((gate_grad, up_grad), "dp")

    results, middle_grads, dz = [], [], []
    ffn_gain_acc = jnp.zeros(ffn_gain.shape, F32)
    for m in range(batches):
        normed_grad = row_scatter(
            row_index,
            sum_products(
                [dgates[m][0], dgates[m][1], dups[m][0], dups[m][1]],
                [gate_own, gate_oth, up_own, up_oth],
                NT,
            ),
        )
        ffn_gain_acc = ffn_gain_acc + jnp.sum(normed_grad * mids[m] * scales[m], axis=0)
        weighted = normed_grad * ffn_gain
        inner = jnp.sum(weighted * mids[m], axis=1)
        inner = (inner + other_core(inner))[:, None]
        middle_grad = (
            out_grad[m].astype(F32)
            + weighted * scales[m]
            - mids[m] * (scales[m] * scales[m] * scales[m]) * inner / WIDTH
        )
        middle_grads.append(middle_grad)
        gathered = row_gather(row_index, middle_grad.astype(BF16))
        dz.append((gathered, other_core(gathered)))
        result = mids[m] + row_scatter(row_index, sum_products(list(acts[m]), [down_own, down_oth], NN))
        results.append(result.astype(BF16))

    in_grads, dqkv = [], []
    attn_gain_acc = jnp.zeros(attn_gain.shape, F32)
    for m in range(batches):
        grad = attend_back(
            prefix_len[m], *dz[m], out_own, out_from, *kept[m], tables, heads
        )
        dqkv.append((grad, other_core(grad)))
        first_grad = row_scatter(
            row_index, sum_products(list(dqkv[m]), [qkv_own, qkv_oth], NT)
        )
        attn_gain_acc = attn_gain_acc + jnp.sum(first_grad * resid[m] * scale_one[m], axis=0)
        weighted = first_grad * attn_gain
        inner = jnp.sum(weighted * resid[m], axis=1)
        inner = (inner + other_core(inner))[:, None]
        s = scale_one[m]
        in_grads.append(middle_grads[m] + weighted * s - resid[m] * (s * s * s) * inner / WIDTH)

    (output_grad,) = weight_grads(col_index, [pair[0] for pair in dz], [halves(heads_out)], False)
    (qkv_grad,) = weight_grads(col_index, [pair[0] for pair in n1], [halves(dqkv)], True)
    output_grad, qkv_grad = lax.optimization_barrier((output_grad, qkv_grad, gate_sum, up_sum))[:2]
    output_sum, qkv_sum = lax.psum((output_grad, qkv_grad), "dp")
    both = qkv_sum.astype(F32).reshape(-1, col_count, q_width + 2 * HEAD_DIM)

    def columns(first, size, shared):
        piece = both[:, :, first : first + size]
        return piece.sum(axis=1) if shared else piece.reshape(-1, col_count * size)

    gain_one, gain_two = butterfly(jnp.stack([attn_gain_acc, ffn_gain_acc]), ("dp", "row"))
    return (
        jnp.stack(results),
        jnp.stack(in_grads),
        gain_one,
        gain_two,
        columns(0, q_width, False),
        columns(q_width, HEAD_DIM, shared_kv),
        columns(q_width + HEAD_DIM, HEAD_DIM, shared_kv),
        output_sum.astype(F32),
        gate_sum.astype(F32),
        up_sum.astype(F32),
        down_sum.astype(F32),
    )


def solution(mesh):
    return jax.shard_map(
        body,
        mesh=mesh,
        in_specs=(
            P(None, ("dp", "row"), "col"),
            P("col"),
            P("col"),
            P("col", "row"),
            P("col", "row"),
            P("col", "row"),
            P("row", "col"),
            P("col", "row"),
            P("col", "row"),
            P("row", "col"),
            P(None, "dp"),
            P(None, ("dp", "row"), "col"),
        ),
        out_specs=(
            P(None, ("dp", "row"), "col"),
            P(None, ("dp", "row"), "col"),
            P("col"),
            P("col"),
            P("col", "row"),
            P("col", "row"),
            P("col", "row"),
            P("row", "col"),
            P("col", "row"),
            P("col", "row"),
            P("row", "col"),
        ),
        check_vma=False,
    )
```

```python
import functools
import math

import jax
import jax.numpy as jnp
from jax import lax
from jax.experimental import pallas as pl
from jax.experimental.pallas import tpu as pltpu
from jax.sharding import PartitionSpec as P

WIDTH = 2048
HEADS = 16
KV_HEADS = 8
HEAD_DIM = 128
PREFIX_TOP = 512

epsilon = 1e-05
rope_base = 1000000.0
scale = 1.0 / math.sqrt(HEAD_DIM)
MIB = 1 << 20
F32 = jnp.float32
BF16 = jnp.bfloat16

NT = (((1,), (1,)), ((), ()))
NN = (((1,), (0,)), ((), ()))
TN = (((0,), (0,)), ((), ()))


def dot(left_side, right_side, dims):
    return lax.dot_general(left_side, right_side, dims, preferred_element_type=F32)


def params(mib, grid_rank):
    return pltpu.CompilerParams(
        dimension_semantics=("arbitrary",) * grid_rank, vmem_limit_bytes=mib * MIB
    )


def cost(flops, nbytes, exps=0):
    return pl.CostEstimate(flops=int(flops), bytes_accessed=int(nbytes), transcendentals=int(exps))


def whole(shape):
    return pl.BlockSpec(shape, lambda *_: (0,) * len(shape))


def rope_tables(length):
    half_size = HEAD_DIM // 2
    inverse = rope_base ** (-(jnp.arange(half_size, dtype=F32) * 2.0 / HEAD_DIM))
    angle = jnp.arange(length, dtype=F32)[:, None] * inverse[None, :]
    cosine = jnp.concatenate([jnp.cos(angle), jnp.cos(angle)], axis=1)
    signed = jnp.concatenate([-jnp.sin(angle), jnp.sin(angle)], axis=1)
    return cosine, signed


def rope(values, cosine, signed):
    return values * cosine + pltpu.roll(values, HEAD_DIM // 2, 1) * signed


def rope_back(values, cosine, signed):
    return values * cosine - pltpu.roll(values, HEAD_DIM // 2, 1) * signed


def grads_kernel(groups, nb, shared_left, c_ref, shared_ref, *refs):
    part = pl.program_id(0) // nb
    for at in range(2 * groups):

        @pl.when(part == at)
        def _(at=at):
            pair = (shared_ref[...], refs[at][...])
            left, right = pair if shared_left else pair[::-1]
            refs[2 * groups + at // 2][...] = dot(left, right, TN).astype(BF16)


def weight_grads(col_index, shared, groups, shared_left):
    tokens, shared_width = shared.shape
    half_width = groups[0][0].shape[1]
    block = min(256, half_width)
    nb = half_width // block
    steps = len(groups) * 2 * nb

    def moving_spec(at):
        return pl.BlockSpec((tokens, block), lambda i, c: (0, jnp.clip(i - at * nb, 0, nb - 1)))

    def out_spec(group):
        def place(i, c):
            inner = jnp.clip(i - group * 2 * nb, 0, 2 * nb - 1)
            at = jnp.where(inner // nb == 0, c[0], 1 - c[0]) * nb + inner % nb
            return (0, at) if shared_left else (at, 0)

        return pl.BlockSpec((shared_width, block) if shared_left else (block, shared_width), place)

    dims = (shared_width, 2 * half_width) if shared_left else (2 * half_width, shared_width)
    return pl.pallas_call(
        functools.partial(grads_kernel, len(groups), nb, shared_left),
        grid_spec=pltpu.PrefetchScalarGridSpec(
            num_scalar_prefetch=1,
            grid=(steps,),
            in_specs=[whole(shared.shape)] + [moving_spec(at) for at in range(2 * len(groups))],
            out_specs=[out_spec(group) for group in range(len(groups))],
        ),
        out_shape=[jax.ShapeDtypeStruct(dims, BF16) for _ in groups],
        compiler_params=params(48, 1),
        cost_estimate=cost(1, 1),
    )(col_index.reshape(1), shared, *[half for group in groups for half in group])


class Line:
    def __init__(self, n):
        self.n = n
        self.r = lax.axis_index("row")
        self.c = lax.axis_index("col")
        self.d = lax.axis_index("dp")

    def copy(self, src, dst, send, recv, **where):
        return pltpu.make_async_remote_copy(
            src_ref=src, dst_ref=dst, send_sem=send, recv_sem=recv, device_id=where,
            device_id_type=pl.DeviceIdType.MESH,
        )

    def up(self, src, dst, send, recv):
        return self.copy(src, dst, send, recv, row=self.r + 1)

    def down(self, src, dst, send, recv):
        return self.copy(src, dst, send, recv, row=self.r - 1)

    def across(self, src, dst, send, recv):
        return self.copy(src, dst, send, recv, col=1 - self.c)

    def barrier(self, core=True, bits=()):
        barrier = pltpu.get_barrier_semaphore()

        def signal(**where):
            pl.semaphore_signal(
                barrier, inc=1, device_id=where, device_id_type=pl.DeviceIdType.MESH
            )

        @pl.when(self.r > 0)
        def _():
            signal(row=self.r - 1)

        @pl.when(self.r < self.n - 1)
        def _():
            signal(row=self.r + 1)

        if core:
            signal(col=1 - self.c)
        for bit in bits:
            signal(dp=self.partner(bit))
        at_end = (self.r == 0) | (self.r == self.n - 1)
        others = int(core) + len(bits)

        @pl.when(at_end)
        def _():
            pl.semaphore_wait(barrier, 1 + others)

        @pl.when(jnp.logical_not(at_end))
        def _():
            pl.semaphore_wait(barrier, 2 + others)

    def side(self, bit):
        return (self.d // 2**bit) % 2

    def partner(self, bit):
        return self.d + (1 - 2 * self.side(bit)) * 2**bit

    def nearest(self, k):
        n = self.n
        code = 0
        for r in range(n):
            order = sorted(range(n), key=lambda q: (abs(q - r), q))
            code += order[k] * n**r
        place, result = self.r * 0 + code, 0
        for r in range(n):
            result = result + (place // n**r) % n * (1 - jnp.minimum(jnp.abs(self.r - r), 1))
        return result


class Gather:
    def __init__(self, line, own, oth, sends, recvs):
        self.line, self.own, self.oth, self.sends, self.recvs = line, own, oth, sends, recvs

    def hop(self, kind, q):
        way = (self.line.up, self.line.down)[kind]
        return way(self.own.at[q], self.own.at[q], self.sends.at[q, kind], self.recvs.at[q, 0])

    def cross(self, q):
        return self.line.across(
            self.own.at[q], self.oth.at[q], self.sends.at[q, 2], self.recvs.at[q, 1]
        )

    def start(self):
        line = self.line

        @pl.when(line.r < line.n - 1)
        def _():
            self.hop(0, line.r).start()

        @pl.when(line.r > 0)
        def _():
            self.hop(1, line.r).start()

        self.cross(line.r).start()

    def step(self, s):
        line = self.line
        low, high = line.r - s, line.r + s

        @pl.when(low >= 0)
        def _():
            self.hop(0, low).wait_recv()

            @pl.when(line.r < line.n - 1)
            def _():
                self.hop(0, low).start()

            self.cross(low).start()

        @pl.when(high <= line.n - 1)
        def _():
            self.hop(1, high).wait_recv()

            @pl.when(line.r > 0)
            def _():
                self.hop(1, high).start()

            self.cross(high).start()

    def arrive(self, q):
        self.cross(q).wait_recv()

    def drain(self):
        line = self.line
        for q in range(line.n):

            @pl.when((line.r >= q) & (line.r < line.n - 1))
            def _(q=q):
                self.hop(0, q).wait_send()

            @pl.when((line.r <= q) & (line.r > 0))
            def _(q=q):
                self.hop(1, q).wait_send()

            self.cross(q).wait_send()


class Scatter:
    def __init__(self, line, part, ups, downs, sends, recvs):
        self.line, self.part, self.ups, self.downs = line, part, ups, downs
        self.sends, self.recvs = sends, recvs

    def hop(self, kind, s, target):
        way = (self.line.up, self.line.down)[kind]
        box = (self.ups, self.downs)[kind]
        return way(
            self.part.at[target], box.at[s - 1], self.sends.at[kind, s - 1], self.recvs.at[kind, s - 1]
        )

    def step(self, s):
        line = self.line
        for kind in range(2):
            behind = line.r if kind == 0 else line.n - 1 - line.r
            target = line.r + line.n - s if kind == 0 else line.r - (line.n - s)
            box = (self.ups, self.downs)[kind]

            @pl.when(behind <= s - 1)
            def _(kind=kind, behind=behind, target=target, box=box):
                if s > 1:

                    @pl.when(behind >= 1)
                    def _():
                        self.hop(kind, s - 1, target).wait_recv()
                        self.part[target] = (
                            self.part[target].astype(F32) + box[s - 2].astype(F32)
                        ).astype(BF16)

                self.hop(kind, s, target).start()

    def total(self, out):
        line = self.line
        last = line.n - 1
        out[...] = self.part[line.r].astype(F32)

        @pl.when(line.r >= 1)
        def _():
            self.hop(0, last, line.r).wait_recv()
            out[...] += self.ups[last - 1].astype(F32)

        @pl.when(line.r <= last - 1)
        def _():
            self.hop(1, last, line.r).wait_recv()
            out[...] += self.downs[last - 1].astype(F32)

    def drain(self):
        line = self.line
        for s in range(1, line.n):

            @pl.when(line.r <= s - 1)
            def _(s=s):
                self.hop(0, s, line.r + line.n - s).wait_send()

            @pl.when(line.n - 1 - line.r <= s - 1)
            def _(s=s):
                self.hop(1, s, line.r - (line.n - s)).wait_send()


class Total:
    def __init__(self, line, ref, result, boxes, bits, sends, recvs):
        self.line, self.ref, self.result, self.boxes, self.bits = line, ref, result, boxes, bits
        self.sends, self.recvs = sends, recvs
        low, size, self.levels = 0, ref.shape[0], []
        for bit in bits:
            size //= 2
            keep = low + line.side(bit) * size
            self.levels.append((size, keep, low + (1 - line.side(bit)) * size))
            low = keep

    def rows(self, at, size):
        return pl.ds(pl.multiple_of(at, 16), size)

    def copy(self, step):
        count = len(self.bits)
        level = step if step < count else 2 * count - 1 - step
        size, keep, give = self.levels[level]
        if step < count:
            src, dst = self.ref.at[self.rows(give, size), :], self.boxes[level]
        else:
            src = dst = self.result.at[self.rows(keep, size), :]
        return self.line.copy(
            src, dst, self.sends.at[step], self.recvs.at[step], dp=self.line.partner(self.bits[level])
        )

    def step(self, step):
        count = len(self.bits)
        if step > 0:
            self.copy(step - 1).wait_recv()
            if step <= count:
                size, keep, _ = self.levels[step - 1]
                rows = self.rows(keep, size)
                kept = self.ref[rows, :].astype(F32) + self.boxes[step - 1][...].astype(F32)
                (self.result if step == count else self.ref)[rows, :] = kept.astype(BF16)
        if step < 2 * count:
            self.copy(step).start()

    def drain(self):
        for step in range(2 * len(self.bits)):
            self.copy(step).wait_send()


def communicate(number, mib):
    return pltpu.CompilerParams(
        collective_id=number, has_side_effects=True, vmem_limit_bytes=mib * MIB
    )


def forward_kernel(
    n, heads, shared_kv,
    prefix_ref, x_ref, gain_one, gain_two, cos_ref, sin_ref,
    grad_in, wq, wk, wv, wo, wgate, wup, wdown,
    n1_out, n2_out, g_out, qkv_out, log_out, o_own_out, o_oth_out, mid_out, scale_out, wo_from,
    a_own_out, a_oth_out, dg_own_out, dg_oth_out, du_own_out, du_oth_out,
    n_own, n_oth, g_own, g_oth, w_own, w_from, wo_ref, wg_ref, wu_ref, wd_ref,
    qkv_ref, vt_ref, o_own, o_oth, log_ref, part, ups, downs, total, scales, row_out, row_in, stage,
    gather_sends, gather_recvs, scatter_sends, scatter_recvs, cross_sends, cross_recvs, local_sems,
    unit_sends, unit_recvs, unit_stores,
):
    batches, tokens, depth = x_ref.shape
    length = n * tokens
    line = Line(n)
    r, c = line.r, line.c
    q_width = heads * HEAD_DIM
    k_col, v_col = q_width, q_width + HEAD_DIM
    share = wgate.shape[1] // 2
    kv_own = 0 if shared_kv else c * HEAD_DIM
    kv_oth = 0 if shared_kv else (1 - c) * HEAD_DIM

    def lanes(at, size):
        return pl.ds(pl.multiple_of(at, 128), size)

    def rows_at(at, size):
        return pl.ds(pl.multiple_of(at, size), size)

    local_count, cross_count = [0], [0]

    def local(src, dst):
        copy = pltpu.make_async_copy(src, dst, local_sems.at[local_count[0]])
        local_count[0] += 1
        copy.start()
        return copy

    def cross(src, dst):
        at = cross_count[0]
        cross_count[0] += 1
        return line.across(src, dst, cross_sends.at[at], cross_recvs.at[at])

    loads = [
        local(wq.at[:, lanes(c * q_width, q_width)], w_own.at[:, pl.ds(0, q_width)]),
        local(wk.at[:, lanes(kv_own, HEAD_DIM)], w_own.at[:, pl.ds(k_col, HEAD_DIM)]),
        local(wv.at[:, lanes(kv_own, HEAD_DIM)], w_own.at[:, pl.ds(v_col, HEAD_DIM)]),
    ]
    wo_load = local(wo, wo_ref)
    g_loads = [local(grad_in.at[m], g_own.at[m, r]) for m in range(batches)]
    unit_loads = [
        local(wgate.at[:, lanes(c * share, share)], wg_ref.at[0]),
        local(wup.at[:, lanes(c * share, share)], wu_ref.at[0]),
        local(wdown.at[rows_at(c * share, share), :], wd_ref.at[0]),
    ]
    for m in range(batches):
        x = x_ref[m].astype(F32)
        squares = jnp.sum(x * x, axis=1, keepdims=True)
        row_out[0, m] = jnp.broadcast_to(squares, (tokens, 128))
    line.barrier()

    def row_cross(which, m):
        return cross(row_out.at[which, m], row_in.at[which, m])

    def norm_scale(which, m, copy):
        copy.wait_recv()
        squares = row_out[which, m] + row_in[which, m]
        value = lax.rsqrt(squares * (1.0 / WIDTH) + epsilon)
        scales[which, m] = value
        return value[:, :1]

    crosses = [row_cross(0, m) for m in range(batches)]
    for copy in crosses:
        copy.start()
    w_cross = [
        cross(wq.at[:, lanes((1 - c) * q_width, q_width)], w_from.at[:, pl.ds(0, q_width)]),
        cross(wk.at[:, lanes(kv_oth, HEAD_DIM)], w_from.at[:, pl.ds(k_col, HEAD_DIM)]),
        cross(wv.at[:, lanes(kv_oth, HEAD_DIM)], w_from.at[:, pl.ds(v_col, HEAD_DIM)]),
    ]
    gathers = [
        [
            Gather(line, own.at[m], oth.at[m], gather_sends.at[at, m], gather_recvs.at[at, m])
            for m in range(batches)
        ]
        for at, (own, oth) in enumerate(((n_own, n_oth), (g_own, g_oth), (n_own, n_oth)))
    ]
    n1, g, n2 = gathers
    rs = [
        Scatter(line, part.at[m], ups.at[m], downs.at[m], scatter_sends.at[m], scatter_recvs.at[m])
        for m in range(batches)
    ]
    for m in range(batches):
        scale_one = norm_scale(0, m, crosses[m])
        n_own[m, r] = (x_ref[m].astype(F32) * scale_one * gain_one[...]).astype(BF16)
        if m == 0:
            n1[0].start()
            for copy in w_cross:
                copy.start()
    for copy in loads:
        copy.wait()
    for copy in w_cross:
        copy.wait_recv()

    def project(m, q):
        n1[m].arrive(q)
        rows = rows_at(q * tokens, tokens)
        pre = dot(n_own[m, q], w_own[...], NN) + dot(n_oth[m, q], w_from[...], NN)
        cosine, signed = cos_ref[rows, :], sin_ref[rows, :]
        for head in range(heads + 1):
            piece = pre[:, head * HEAD_DIM : (head + 1) * HEAD_DIM]
            qkv_ref[m, rows, pl.ds(head * HEAD_DIM, HEAD_DIM)] = rope(piece, cosine, signed).astype(BF16)
        values = pre[:, v_col : v_col + HEAD_DIM].astype(BF16)
        qkv_ref[m, rows, pl.ds(v_col, HEAD_DIM)] = values
        vt_ref[m, :, rows] = values.T

    block = min(256, length)
    count = length // block

    def attend_block(m, index):
        first = index * block
        extent = min(length, max(first + block, PREFIX_TOP))
        keys = qkv_ref[m, pl.ds(0, extent), pl.ds(k_col, HEAD_DIM)]
        key_at = lax.broadcasted_iota(jnp.int32, (extent, block), 0)
        query_at = lax.broadcasted_iota(jnp.int32, (extent, block), 1) + first
        allowed = (key_at <= query_at) | (key_at < prefix_ref[m, 0])
        for head in range(heads):
            cols = pl.ds(head * HEAD_DIM, HEAD_DIM)
            query = qkv_ref[m, pl.ds(first, block), cols]
            scores = jnp.where(allowed, dot(keys, query, NT) * scale, -1e30)
            topmost = jnp.max(scores, axis=0, keepdims=True)
            exponent = jnp.exp(scores - topmost)
            summed = jnp.sum(exponent, axis=0, keepdims=True)
            weights = (exponent * (1.0 / summed)).astype(BF16)
            result = dot(vt_ref[m, :, pl.ds(0, extent)], weights, NN)
            o_own[m, pl.ds(first, block), cols] = result.T.astype(BF16)
            log_ref[m, pl.ds(head, 1), pl.ds(first, block)] = topmost + jnp.log(summed)

    def project_out(m):
        own_rows, oth_rows = rows_at(c * q_width, q_width), rows_at((1 - c) * q_width, q_width)

        @pl.loop(0, n)
        def _(p):
            rows = rows_at(p * tokens, tokens)
            value = dot(o_own[m, rows, :], wo_ref[own_rows, :], NN)
            value = value + dot(o_oth[m, rows, :], wo_ref[oth_rows, :], NN)
            part[m, p] = value.astype(BF16)

    def walk(m, first, last):
        for k in range(first, last):
            n1[m].step(k)
            project(m, line.nearest(k))

    def release(m, store):
        store.wait()
        n1[m].drain()

    def middle(m):
        rs[m].total(total.at[m])
        total[m] = total[m] + x_ref[m].astype(F32)
        mid = total[m]
        squares = jnp.sum(mid * mid, axis=1, keepdims=True)
        row_out[1, m] = jnp.broadcast_to(squares, (tokens, 128))
        copy = row_cross(1, m)
        copy.start()
        scale_two = norm_scale(1, m, copy)
        n_own[m, r] = (total[m] * scale_two * gain_two[...]).astype(BF16)
        crosses.append(copy)
        n2[m].start()

    outs = ((a_own_out, a_oth_out), (dg_own_out, dg_oth_out), (du_own_out, du_oth_out))
    order = [(m, k) for m in range(batches) for k in range(n)]

    def unit_away(at, kind):
        m, k = order[at]
        return line.across(
            stage.at[at % 2, kind], outs[kind][1].at[m, line.nearest(k)],
            unit_sends.at[at, kind], unit_recvs.at[at, kind],
        )

    def unit_kept(at, kind):
        m, k = order[at]
        return pltpu.make_async_copy(
            stage.at[at % 2, kind], outs[kind][0].at[m, line.nearest(k)], unit_stores.at[at, kind]
        )

    def unit_wait(at):
        for kind in range(3):
            unit_away(at, kind).wait_send()
            unit_kept(at, kind).wait()

    def units(at):
        m, k = order[at]
        q = line.nearest(k)
        n2[m].arrive(q)
        g[m].arrive(q)
        if at >= 2:
            unit_wait(at - 2)
        slot = at % 2
        size = min(256, share)

        @pl.loop(0, share // size)
        def _(b):
            cols = rows_at(b * size, size)
            gate = dot(n_own[m, q], wg_ref[0, :, cols], NN) + dot(n_oth[m, q], wg_ref[1, :, cols], NN)
            up = dot(n_own[m, q], wu_ref[0, :, cols], NN) + dot(n_oth[m, q], wu_ref[1, :, cols], NN)
            da = dot(g_own[m, q], wd_ref[0, cols, :], NT) + dot(g_oth[m, q], wd_ref[1, cols, :], NT)
            sigmoid = 1.0 / (1.0 + jnp.exp(-gate))
            silu = gate * sigmoid
            stage[slot, 0, :, cols] = (silu * up).astype(BF16)
            stage[slot, 1, :, cols] = (da * up * sigmoid * (1.0 + gate * (1.0 - sigmoid))).astype(BF16)
            stage[slot, 2, :, cols] = (da * silu).astype(BF16)

        for kind in range(3):
            unit_away(at, kind).start()
            unit_kept(at, kind).start()

    half = (n + 1) // 2
    o_cross = [cross(o_own.at[m], o_oth.at[m]) for m in range(batches)]
    stores = []

    project(0, r)
    walk(0, 1, n - 1)
    n1[1].start()
    walk(0, n - 1, n)
    n1_stores = [local(n_own.at[0], n1_out.at[0])]
    project(1, r)
    for index in range(count // 2):
        attend_block(0, index)
    walk(1, 1, half)
    for index in range(count // 2, count):
        attend_block(0, index)
    o_cross[0].start()
    big_cross = [
        cross(wgate.at[:, lanes((1 - c) * share, share)], wg_ref.at[1]),
        cross(wup.at[:, lanes((1 - c) * share, share)], wu_ref.at[1]),
        cross(wdown.at[rows_at((1 - c) * share, share), :], wd_ref.at[1]),
        cross(wo.at[rows_at((1 - c) * q_width, q_width), :], wo_from),
    ]
    walk(1, half, n - 1)
    o_cross[0].wait_recv()
    wo_load.wait()
    project_out(0)
    rs[0].step(1)
    g_loads[0].wait()
    g[0].start()
    walk(1, n - 1, n)
    n1_stores.append(local(n_own.at[1], n1_out.at[1]))
    for copy in big_cross:
        copy.start()
    for index in range(count // 2):
        attend_block(1, index)
    for s in range(2, half + 1):
        rs[0].step(s)
    for index in range(count // 2, count):
        attend_block(1, index)
    o_cross[1].start()
    for k in range(1, half):
        g[0].step(k)
    release(0, n1_stores[0])
    for s in range(half + 1, n):
        rs[0].step(s)
    o_cross[1].wait_recv()
    project_out(1)
    rs[1].step(1)
    for k in range(half, n - 1):
        g[0].step(k)
    middle(0)
    release(1, n1_stores[1])
    for s in range(2, half + 1):
        rs[1].step(s)
    g[0].step(n - 1)
    for copy in unit_loads:
        copy.wait()
    for copy in big_cross:
        copy.wait_recv()
    g_loads[1].wait()
    stores += [local(g_own.at[0], g_out.at[0])]
    stores += [local(qkv_ref, qkv_out), local(log_ref, log_out)]
    stores += [local(o_own, o_own_out), local(o_oth, o_oth_out), local(total.at[0], mid_out.at[0])]
    units(0)
    for k in range(1, half):
        n2[0].step(k)
        units(k)
    for s in range(half + 1, n):
        rs[1].step(s)
    for k in range(half, n - 1):
        n2[0].step(k)
    g[1].start()
    for k in range(half, n - 1):
        units(k)
    middle(1)
    stores.append(local(total.at[1], mid_out.at[1]))
    stores.append(local(scales, scale_out))
    n2[0].step(n - 1)
    units(n - 1)
    units(n)
    for k in range(1, n):
        g[1].step(k)
        n2[1].step(k)
        units(n + k)
    stores += [local(g_own.at[1], g_out.at[1]), local(n_own, n2_out)]
    for at in range(2 * n - 2, 2 * n):
        unit_wait(at)
    for at in range(2 * n):
        for kind in range(3):
            unit_away(at, kind).wait_recv()
    for copy in crosses + w_cross + o_cross + big_cross:
        copy.wait_send()
    for item in g + n2 + rs:
        item.drain()
    for copy in stores:
        copy.wait()


def forward(
    prefix, x, gain_one, gain_two, tables, grad_in, wq, wk, wv, wo, wgate, wup, wdown, n, heads, shared_kv
):
    batches, tokens, depth = x.shape
    length = n * tokens
    width = (heads + 2) * HEAD_DIM
    q_width = heads * HEAD_DIM
    share = wgate.shape[1] // 2
    vmem = pl.BlockSpec(memory_space=pltpu.VMEM)
    anywhere = pl.BlockSpec(memory_space=pl.ANY)
    gathered, units = (batches, n, tokens, depth), (batches, n, tokens, share)
    rows = (2, batches, tokens, 128)
    shapes = [
        (gathered, BF16), (gathered, BF16), (gathered, BF16),
        ((batches, length, width), BF16), ((batches, 8, length), F32),
        ((batches, length, q_width), BF16), ((batches, length, q_width), BF16),
        ((batches, tokens, depth), F32), (rows, F32), ((q_width, depth), BF16),
    ] + [(units, BF16)] * 6
    boxes = (batches, n - 1, tokens, depth)
    dma = pltpu.SemaphoreType.DMA
    return pl.pallas_call(
        functools.partial(forward_kernel, n, heads, shared_kv),
        in_specs=[pl.BlockSpec(memory_space=pltpu.SMEM)] + [vmem] * 5 + [anywhere] * 8,
        out_specs=[anywhere] * len(shapes),
        out_shape=[jax.ShapeDtypeStruct(*item) for item in shapes],
        scratch_shapes=[
            pltpu.VMEM(gathered, BF16), pltpu.VMEM(gathered, BF16),
            pltpu.VMEM(gathered, BF16), pltpu.VMEM(gathered, BF16),
            pltpu.VMEM((depth, width), BF16), pltpu.VMEM((depth, width), BF16),
            pltpu.VMEM(wo.shape, BF16),
            pltpu.VMEM((2, depth, share), BF16), pltpu.VMEM((2, depth, share), BF16),
            pltpu.VMEM((2, share, depth), BF16),
            pltpu.VMEM((batches, length, width), BF16),
            pltpu.VMEM((batches, HEAD_DIM, length), BF16),
            pltpu.VMEM((batches, length, q_width), BF16), pltpu.VMEM((batches, length, q_width), BF16),
            pltpu.VMEM((batches, 8, length), F32),
            pltpu.VMEM(gathered, BF16), pltpu.VMEM(boxes, BF16), pltpu.VMEM(boxes, BF16),
            pltpu.VMEM((batches, tokens, depth), F32),
            pltpu.VMEM(rows, F32), pltpu.VMEM(rows, F32), pltpu.VMEM(rows, F32),
            pltpu.VMEM((2, 3, tokens, share), BF16),
            dma((3, batches, n, 3)), dma((3, batches, n, 2)),
            dma((batches, 2, n - 1)), dma((batches, 2, n - 1)), dma((13,)), dma((13,)), dma((24,)),
            dma((batches * n, 3)), dma((batches * n, 3)), dma((batches * n, 3)),
        ],
        compiler_params=communicate(1, 62),
        cost_estimate=cost(2e11, 100 * MIB),
    )(prefix, x, gain_one, gain_two, *tables, grad_in, wq, wk, wv, wo, wgate, wup, wdown)


def tail_kernel(
    n, bits, a_own_in, a_oth_in, wdown, n1_in, dqkv_own_in, dqkv_oth_in, dz_in, o_own_in, o_oth_in,
    sum_out, qkv_out, o_out,
    a_ref, wd_ref, part, ups, downs, total, n1_ref, dqkv_ref, dz_ref, o_ref, qkv_ref, o_part, qkv_sum, o_sum, boxes,
    load_sems, a_sems, sends, recvs, total_sends, total_recvs,
):
    batches, _, tokens, share = a_own_in.shape
    depth = wdown.shape[1]
    width, q_width = dqkv_own_in.shape[1], o_own_in.shape[1]
    line = Line(n)
    c = line.c
    pairs = [(n1_in, n1_ref), (dqkv_own_in, dqkv_ref.at[0]), (dqkv_oth_in, dqkv_ref.at[1])]
    pairs += [(dz_in, dz_ref), (o_own_in, o_ref.at[0]), (o_oth_in, o_ref.at[1]), (wdown, wd_ref)]
    loads = [pltpu.make_async_copy(a, b, load_sems.at[i]) for i, (a, b) in enumerate(pairs)]
    order = [(m, p) for m in range(batches) for p in range(n)]

    def a_loads(at):
        m, p = order[at]
        return [
            pltpu.make_async_copy(src.at[m, p], a_ref.at[at % 2, side], a_sems.at[at % 2, side])
            for side, src in enumerate((a_own_in, a_oth_in))
        ]

    for copy in loads + a_loads(0):
        copy.start()
    line.barrier(core=False, bits=bits)
    scatters = [
        Scatter(line, part.at[m], ups.at[m], downs.at[m], sends.at[m], recvs.at[m])
        for m in range(batches)
    ]
    sums = []
    for ref, result, refs in ((qkv_ref, qkv_sum, boxes[0]), (o_part, o_sum, boxes[1])):
        half = ref.shape[0] // 2
        for part_at in range(2):
            at = len(sums)
            rows = pl.ds(part_at * half, half)
            sums.append(
                Total(
                    line, ref.at[rows, :], result.at[rows, :], [box.at[part_at] for box in refs],
                    bits if part_at == 0 else bits[::-1], total_sends.at[at], total_recvs.at[at],
                )
            )
    for copy in loads[:3]:
        copy.wait()
    for side in range(2):
        place = c if side == 0 else 1 - c
        value = dot(n1_ref[...], dqkv_ref[side], TN)
        qkv_ref[:, pl.ds(pl.multiple_of(place * width, 128), width)] = value.astype(BF16)
    for item in sums[:2]:
        item.step(0)
    for copy in loads[3:6]:
        copy.wait()
    for side in range(2):
        place = c if side == 0 else 1 - c
        value = dot(o_ref[side], dz_ref[...], TN)
        o_part[pl.ds(pl.multiple_of(place * q_width, q_width), q_width), :] = value.astype(BF16)
    for item in sums[2:]:
        item.step(0)
    loads[6].wait()
    own_rows = pl.ds(pl.multiple_of(c * share, share), share)
    oth_rows = pl.ds(pl.multiple_of((1 - c) * share, share), share)

    def product(at):
        m, p = order[at]
        for copy in a_loads(at):
            copy.wait()
        if at + 1 < len(order):
            for copy in a_loads(at + 1):
                copy.start()
        value = dot(a_ref[at % 2, 0], wd_ref[own_rows, :], NN)
        part[m, p] = (value + dot(a_ref[at % 2, 1], wd_ref[oth_rows, :], NN)).astype(BF16)

    for at in range(n):
        product(at)
    scatters[0].step(1)
    for item in sums[:2]:
        item.step(1)
    for at in range(n, 2 * n):
        product(at)
    for item in sums[2:]:
        item.step(1)
    turn = 2
    last_turn = 2 * len(bits)
    for s in range(2, n):
        scatters[0].step(s)
        if turn <= last_turn:
            for item in sums:
                item.step(turn)
        turn += 1
    scatters[1].step(1)
    scatters[0].total(total.at[0])
    for s in range(2, n):
        if turn <= last_turn:
            for item in sums:
                item.step(turn)
        turn += 1
        scatters[1].step(s)
    while turn <= last_turn:
        for item in sums:
            item.step(turn)
        turn += 1
    stores = [
        pltpu.make_async_copy(qkv_sum, qkv_out, load_sems.at[0]),
        pltpu.make_async_copy(o_sum, o_out, load_sems.at[1]),
    ]
    for copy in stores:
        copy.start()
    scatters[1].total(total.at[1])
    stores.append(pltpu.make_async_copy(total, sum_out, load_sems.at[2]))
    stores[-1].start()
    for item in scatters + sums:
        item.drain()
    for copy in stores:
        copy.wait()


def tail(a_own, a_oth, wdown, n1, dqkv_own, dqkv_oth, dz, o_own, o_oth, dp_count):
    batches, n, tokens, share = a_own.shape
    rows, depth = n1.shape
    width, q_width = dqkv_own.shape[1], o_own.shape[1]
    bits = list(range(dp_count.bit_length() - 1))
    anywhere = pl.BlockSpec(memory_space=pl.ANY)
    boxes = (batches, n - 1, tokens, depth)
    shapes = [((batches, tokens, depth), F32), ((depth, 2 * width), BF16), ((2 * q_width, depth), BF16)]
    sums = [shape for shape, _ in shapes[1:]]
    return pl.pallas_call(
        functools.partial(tail_kernel, n, bits),
        in_specs=[anywhere] * 9,
        out_specs=[anywhere] * 3,
        out_shape=[jax.ShapeDtypeStruct(*item) for item in shapes],
        scratch_shapes=[
            pltpu.VMEM((2, 2, tokens, share), BF16), pltpu.VMEM(wdown.shape, BF16),
            pltpu.VMEM((batches, n, tokens, depth), BF16), pltpu.VMEM(boxes, BF16),
            pltpu.VMEM(boxes, BF16), pltpu.VMEM((batches, tokens, depth), F32),
            pltpu.VMEM((rows, depth), BF16), pltpu.VMEM((2, rows, width), BF16),
            pltpu.VMEM((rows, depth), BF16), pltpu.VMEM((2, rows, q_width), BF16),
            pltpu.VMEM(sums[0], BF16), pltpu.VMEM(sums[1], BF16),
            pltpu.VMEM(sums[0], BF16), pltpu.VMEM(sums[1], BF16),
            [
                [pltpu.VMEM((2, shape[0] // 2 ** (level + 2), shape[1]), BF16) for level in range(len(bits))]
                for shape in sums
            ],
            pltpu.SemaphoreType.DMA((7,)), pltpu.SemaphoreType.DMA((2, 2)),
            pltpu.SemaphoreType.DMA((batches, 2, n - 1)), pltpu.SemaphoreType.DMA((batches, 2, n - 1)),
            pltpu.SemaphoreType.DMA((4, 2 * len(bits))), pltpu.SemaphoreType.DMA((4, 2 * len(bits))),
        ],
        compiler_params=communicate(4, 56),
        cost_estimate=cost(1e11, 100 * MIB),
    )(a_own, a_oth, wdown, n1, dqkv_own, dqkv_oth, dz, o_own, o_oth)


def backward_kernel(
    n, heads, shared_kv,
    prefix_ref, mid_ref, s2_ref, top_ref, gain_ref, cos_ref, sin_ref, log_ref,
    dg_own_in, dg_oth_in, du_own_in, du_oth_in, wgate, wup, wo, wo_from, wq, wk, wv, qkv_in,
    dz_out, dqkv_own_out, dqkv_oth_out, mgrad_out, fsum_out, gain_out,
    wg_ref, wu_ref, unit_ref, wo_ref, w_own, w_oth, qkv_ref, part, ups, downs, total,
    dz_own, dz_oth, dk_ref, dv_ref, kt_ref, dqkv_own, dqkv_oth, row_out, row_in,
    load_sems, unit_sems, scatter_sends, scatter_recvs, gather_sends, gather_recvs,
    cross_sends, cross_recvs, store_sems,
):
    batches, tokens, depth = mid_ref.shape
    length = n * tokens
    share = wgate.shape[1] // 2
    line = Line(n)
    r, c = line.r, line.c
    q_width = heads * HEAD_DIM
    k_col, v_col = q_width, q_width + HEAD_DIM

    def lanes(at, size):
        return pl.ds(pl.multiple_of(at, 128), size)

    def qkv_columns(side, dst):
        kv = 0 if shared_kv else side * HEAD_DIM
        return [
            (wq.at[:, lanes(side * q_width, q_width)], dst.at[:, pl.ds(0, q_width)]),
            (wk.at[:, lanes(kv, HEAD_DIM)], dst.at[:, pl.ds(k_col, HEAD_DIM)]),
            (wv.at[:, lanes(kv, HEAD_DIM)], dst.at[:, pl.ds(v_col, HEAD_DIM)]),
        ]

    own_rows = pl.ds(pl.multiple_of(c * q_width, q_width), q_width)
    pairs = [(wgate, wg_ref), (wup, wu_ref)]
    pairs += [(wo.at[own_rows, :], wo_ref.at[0]), (wo_from, wo_ref.at[1]), (qkv_in, qkv_ref)]
    pairs += qkv_columns(c, w_own) + qkv_columns(1 - c, w_oth)
    loads = [pltpu.make_async_copy(a, b, load_sems.at[i]) for i, (a, b) in enumerate(pairs)]
    order = [(m, p) for m in range(batches) for p in range(n)]

    def unit_loads(at):
        m, p = order[at]
        return [
            pltpu.make_async_copy(src.at[m, p], unit_ref.at[at % 2, i], unit_sems.at[at % 2, i])
            for i, src in enumerate((dg_own_in, dg_oth_in, du_own_in, du_oth_in))
        ]

    for copy in loads[:2] + unit_loads(0) + loads[2:]:
        copy.start()
    line.barrier()
    units_rs, heads_rs = (
        [
            Scatter(
                line, part.at[m], ups.at[which, m], downs.at[which, m],
                scatter_sends.at[which, m], scatter_recvs.at[which, m],
            )
            for m in range(batches)
        ]
        for which in range(2)
    )
    gathers = [
        Gather(line, dz_own.at[m], dz_oth.at[m], gather_sends.at[m], gather_recvs.at[m])
        for m in range(batches)
    ]
    cols_own = lanes(c * share, share)
    cols_oth = lanes((1 - c) * share, share)

    def unit_part(at):
        m, p = order[at]
        for copy in unit_loads(at):
            copy.wait()
        if at + 1 < len(order):
            for copy in unit_loads(at + 1):
                copy.start()
        slot = at % 2
        block = min(256, depth)

        @pl.loop(0, depth // block)
        def _(b):
            rows = pl.ds(pl.multiple_of(b * block, block), block)
            value = dot(unit_ref[slot, 0], wg_ref[rows, cols_own], NT)
            value = value + dot(unit_ref[slot, 1], wg_ref[rows, cols_oth], NT)
            value = value + dot(unit_ref[slot, 2], wu_ref[rows, cols_own], NT)
            value = value + dot(unit_ref[slot, 3], wu_ref[rows, cols_oth], NT)
            part[m, p, :, rows] = value.astype(BF16)

    def row_cross(m):
        return line.across(row_out.at[m], row_in.at[m], cross_sends.at[m], cross_recvs.at[m])

    def grad_cross(m):
        at = batches + m
        return line.across(dqkv_own.at[m], dqkv_oth.at[m], cross_sends.at[at], cross_recvs.at[at])

    def middle(m):
        units_rs[m].total(total.at[m])
        normed_grad, mid, s = total[m], mid_ref[m], s2_ref[m]
        gain_out_part = jnp.sum(normed_grad * mid * s, axis=0, keepdims=True)
        gain_out[pl.ds(m, 1), :] = gain_out_part
        weighted = normed_grad * gain_ref[...]
        inner = jnp.sum(weighted * mid, axis=1, keepdims=True)
        row_out[m] = jnp.broadcast_to(inner, (tokens, 128))
        row_cross(m).start()
        row_cross(m).wait_recv()
        inner = row_out[m, :, pl.ds(0, 1)] + row_in[m, :, pl.ds(0, 1)]
        result = (
            top_ref[m].astype(F32)
            + total[m] * gain_ref[...] * s
            - mid_ref[m] * ((s * s * s) * inner * (1.0 / WIDTH))
        )
        total[m] = result
        dz_own[m, r] = result.astype(BF16)
        gathers[m].start()

    def store(which, m, src, dst):
        return pltpu.make_async_copy(src, dst, store_sems.at[which, m])

    def attend_back(m, q):
        gathers[m].arrive(q)
        rows = pl.ds(pl.multiple_of(q * tokens, tokens), tokens)
        grads = dot(dz_own[m, q], wo_ref[0], NT)
        grads = (grads + dot(dz_oth[m, q], wo_ref[1], NT)).astype(BF16)
        cosine, signed = cos_ref[rows, :], sin_ref[rows, :]

        def with_keys(extent):
            upto = pl.ds(0, extent)
            keys = qkv_ref[m, upto, pl.ds(k_col, HEAD_DIM)]
            values = qkv_ref[m, upto, pl.ds(v_col, HEAD_DIM)]
            key_at = lax.broadcasted_iota(jnp.int32, (extent, tokens), 0)
            query_at = lax.broadcasted_iota(jnp.int32, (extent, tokens), 1) + q * tokens
            allowed = (key_at <= query_at) | (key_at < prefix_ref[m, 0])
            for head in range(heads):
                cols = pl.ds(head * HEAD_DIM, HEAD_DIM)
                query = qkv_ref[m, rows, cols]
                grad = grads[:, head * HEAD_DIM : (head + 1) * HEAD_DIM]
                raw = dot(keys, query, NT) * scale - log_ref[m, pl.ds(head, 1), rows]
                probs = jnp.exp(jnp.where(allowed, raw, -1e30))
                dv_ref[upto, :] += dot(probs.astype(BF16), grad, NN)
                prob_grad = dot(values, grad, NT)
                inner = jnp.sum(probs * prob_grad, axis=0, keepdims=True)
                rounded = (probs * (prob_grad - inner) * scale).astype(BF16)
                dk_ref[upto, :] += dot(rounded, query, NN)
                dq = dot(kt_ref[:, upto], rounded, NN).T
                dqkv_own[m, rows, cols] = rope_back(dq, cosine, signed).astype(BF16)

        lower = max(length // 2, min(PREFIX_TOP, length))
        split = lower // tokens if lower == length // 2 else 0

        @pl.when(q < split)
        def _():
            with_keys(lower)

        @pl.when(q >= split)
        def _():
            with_keys(length)

    def attention(m, hook):
        dk_ref[...] = jnp.zeros_like(dk_ref)
        dv_ref[...] = jnp.zeros_like(dv_ref)
        kt_ref[...] = qkv_ref[m, :, pl.ds(k_col, HEAD_DIM)].T

        @pl.loop(0, n)
        def _(k):
            @pl.when(k > 0)
            def _():
                gathers[m].step(k)

            hook(k)
            q = 0
            for j in range(n):
                q = q + line.nearest(j) * (1 - jnp.minimum(jnp.abs(k - j), 1))
            attend_back(m, q)

        dk = rope_back(dk_ref[...], cos_ref[...], sin_ref[...])
        dqkv_own[m, :, pl.ds(k_col, HEAD_DIM)] = dk.astype(BF16)
        dqkv_own[m, :, pl.ds(v_col, HEAD_DIM)] = dv_ref[...].astype(BF16)
        grad_cross(m).start()
        store(0, m, dqkv_own.at[m], dqkv_own_out.at[m]).start()
        grad_cross(m).wait_recv()
        store(1, m, dqkv_oth.at[m], dqkv_oth_out.at[m]).start()
        units_rs[m].drain()

        @pl.loop(0, n)
        def _(p):
            rows = pl.ds(pl.multiple_of(p * tokens, tokens), tokens)
            value = dot(dqkv_own[m, rows, :], w_own[...], NT)
            part[m, p] = (value + dot(dqkv_oth[m, rows, :], w_oth[...], NT)).astype(BF16)

    for copy in loads[:2]:
        copy.wait()
    for at in range(n):
        unit_part(at)
    units_rs[0].step(1)
    for at in range(n, 2 * n):
        unit_part(at)
    for copy in loads[2:]:
        copy.wait()
    for s in range(2, n):
        units_rs[0].step(s)
    units_rs[1].step(1)
    middle(0)
    if n > 2:
        units_rs[1].step(2)

    def hook_first(k):
        for s in range(3, n):

            @pl.when(k == s - 2)
            def _(s=s):
                units_rs[1].step(s)

        @pl.when(k == max(n - 2, 0))
        def _():
            middle(1)

    attention(0, hook_first)
    heads_rs[0].step(1)

    def hook_second(k):
        for s in range(2, n):

            @pl.when(k == s - 1)
            def _(s=s):
                heads_rs[0].step(s)

    attention(1, hook_second)
    heads_rs[1].step(1)
    final_stores = [
        store(2, m, total.at[m], mgrad_out.at[m]) for m in range(batches)
    ] + [store(3, m, dz_own.at[m], dz_out.at[m]) for m in range(batches)]
    for copy in final_stores:
        copy.start()
    for copy in final_stores[:batches]:
        copy.wait()
    heads_rs[0].total(total.at[0])
    for s in range(2, n):
        heads_rs[1].step(s)
    heads_rs[1].total(total.at[1])
    sums = [store(4, m, total.at[m], fsum_out.at[m]) for m in range(batches)]
    for copy in sums:
        copy.start()
    for m in range(batches):
        row_cross(m).wait_send()
        grad_cross(m).wait_send()
        heads_rs[m].drain()
        gathers[m].drain()
        store(0, m, dqkv_own.at[m], dqkv_own_out.at[m]).wait()
        store(1, m, dqkv_oth.at[m], dqkv_oth_out.at[m]).wait()
    for copy in final_stores[batches:] + sums:
        copy.wait()


def backward(
    prefix, mid, s2, top, gain, tables, logs, dg_own, dg_oth, du_own, du_oth,
    wgate, wup, wo, wo_from, wq, wk, wv, qkv, n, heads, shared_kv,
):
    batches, tokens, depth = mid.shape
    length, width = qkv.shape[1:]
    share = wgate.shape[1] // 2
    vmem = pl.BlockSpec(memory_space=pltpu.VMEM)
    anywhere = pl.BlockSpec(memory_space=pl.ANY)
    gathered = (batches, n, tokens, depth)
    boxes = (2, batches, n - 1, tokens, depth)
    shapes = [
        (gathered, BF16), (qkv.shape, BF16), (qkv.shape, BF16), (mid.shape, F32), (mid.shape, F32),
        ((8, depth), F32),
    ]
    return pl.pallas_call(
        functools.partial(backward_kernel, n, heads, shared_kv),
        in_specs=[pl.BlockSpec(memory_space=pltpu.SMEM)] + [vmem] * 7 + [anywhere] * 12,
        out_specs=[anywhere] * 5 + [vmem],
        out_shape=[jax.ShapeDtypeStruct(*item) for item in shapes],
        scratch_shapes=[
            pltpu.VMEM(wgate.shape, BF16), pltpu.VMEM(wup.shape, BF16),
            pltpu.VMEM((2, 4, tokens, share), BF16), pltpu.VMEM((2, heads * HEAD_DIM, depth), BF16),
            pltpu.VMEM((depth, width), BF16), pltpu.VMEM((depth, width), BF16),
            pltpu.VMEM(qkv.shape, BF16), pltpu.VMEM(gathered, BF16),
            pltpu.VMEM(boxes, BF16), pltpu.VMEM(boxes, BF16), pltpu.VMEM(mid.shape, F32),
            pltpu.VMEM(gathered, BF16), pltpu.VMEM(gathered, BF16),
            pltpu.VMEM((length, HEAD_DIM), F32), pltpu.VMEM((length, HEAD_DIM), F32),
            pltpu.VMEM((HEAD_DIM, length), BF16), pltpu.VMEM(qkv.shape, BF16), pltpu.VMEM(qkv.shape, BF16),
            pltpu.VMEM((batches, tokens, 128), F32), pltpu.VMEM((batches, tokens, 128), F32),
            pltpu.SemaphoreType.DMA((11,)), pltpu.SemaphoreType.DMA((2, 4)),
            pltpu.SemaphoreType.DMA((2, batches, 2, n - 1)), pltpu.SemaphoreType.DMA((2, batches, 2, n - 1)),
            pltpu.SemaphoreType.DMA((batches, n, 3)), pltpu.SemaphoreType.DMA((batches, n, 2)),
            pltpu.SemaphoreType.DMA((2 * batches,)), pltpu.SemaphoreType.DMA((2 * batches,)),
            pltpu.SemaphoreType.DMA((5, batches)),
        ],
        compiler_params=communicate(3, 60),
        cost_estimate=cost(2e11, 300 * MIB),
    )(
        prefix, mid, s2, top, gain, *tables, logs, dg_own, dg_oth, du_own, du_oth,
        wgate, wup, wo, wo_from, wq, wk, wv, qkv,
    )


def other_core(values):
    count = lax.axis_size("col")
    return lax.ppermute(values, "col", [(i, (i + 1) % count) for i in range(count)])


def butterfly(values, axes):
    for axis in axes:
        n = lax.axis_size(axis)
        reach = 1
        while reach < n:
            values = values + lax.ppermute(values, axis, [(i, i ^ reach) for i in range(n)])
            reach *= 2
    return values


def body(
    hidden_in,
    attn_gain,
    ffn_gain,
    query_weight,
    key_weight,
    value_weight,
    output_weight,
    gate_weight,
    up_weight,
    down_weight,
    prefix_len,
    out_grad,
):
    col_count, row_count = lax.axis_size("col"), lax.axis_size("row")
    col_index = lax.axis_index("col").astype(jnp.int32)
    batches, tokens, _ = hidden_in.shape
    length = tokens * row_count
    heads = query_weight.shape[1] // HEAD_DIM // col_count
    row_kv = key_weight.shape[1] // HEAD_DIM
    shared_kv = row_kv < col_count
    q_width = heads * HEAD_DIM
    tables = rope_tables(length)
    resid = hidden_in.astype(F32)
    (
        n1, n2, g_own, qkv, logs, o_own, o_oth, middle, scales, out_from,
        a_own, a_oth, dg_own, dg_oth, du_own, du_oth,
    ) = forward(
        prefix_len, hidden_in, attn_gain.reshape(1, -1), ffn_gain.reshape(1, -1), tables, out_grad,
        query_weight, key_weight, value_weight, output_weight, gate_weight, up_weight, down_weight,
        row_count, heads, shared_kv,
    )
    scale_one, scale_two = scales[0, :, :, :1], scales[1, :, :, :1]

    def flat(*items):
        return tuple(item.reshape(batches * length, item.shape[-1]) for item in items)

    (down_grad,) = weight_grads(col_index, *flat(g_own), [flat(a_own, a_oth)], False)
    gate_grad, up_grad = weight_grads(
        col_index, *flat(n2), [flat(dg_own, dg_oth), flat(du_own, du_oth)], True
    )
    dg_own, down_grad, gate_grad, up_grad = lax.optimization_barrier(
        (dg_own, down_grad, gate_grad, up_grad)
    )
    down_sum, gate_sum, up_sum = lax.psum((down_grad, gate_grad, up_grad), "dp")
    dz, dqkv_own, dqkv_oth, middle_grad, first_grad, ffn_gains = backward(
        prefix_len, middle, scale_two, out_grad, ffn_gain.reshape(1, -1), tables, logs,
        dg_own, dg_oth, du_own, du_oth, gate_weight, up_weight, output_weight, out_from,
        query_weight, key_weight, value_weight, qkv, row_count, heads, shared_kv,
    )
    down_part, qkv_sum, output_sum = tail(
        a_own, a_oth, down_weight, *flat(n1, dqkv_own, dqkv_oth, dz, o_own, o_oth), lax.axis_size("dp")
    )
    result = (middle + down_part).astype(BF16)
    attn_gain_acc = jnp.sum(first_grad * resid * scale_one, axis=(0, 1))
    ffn_gain_acc = ffn_gains[:batches].sum(axis=0)
    weighted = first_grad * attn_gain
    inner = jnp.sum(weighted * resid, axis=2)
    inner = (inner + other_core(inner))[..., None]
    cubed = scale_one * scale_one * scale_one
    in_grad = middle_grad + weighted * scale_one - resid * cubed * inner / WIDTH

    width = q_width + 2 * HEAD_DIM

    def columns(first, size, shared):
        pieces = [
            qkv_sum[:, side * width + first : side * width + first + size].astype(F32)
            for side in range(col_count)
        ]
        return sum(pieces) if shared else jnp.concatenate(pieces, axis=1)

    gain_one, gain_two = butterfly(jnp.stack([attn_gain_acc, ffn_gain_acc]), ("dp", "row"))
    return (
        result,
        in_grad,
        gain_one,
        gain_two,
        columns(0, q_width, False),
        columns(q_width, HEAD_DIM, shared_kv),
        columns(q_width + HEAD_DIM, HEAD_DIM, shared_kv),
        output_sum.astype(F32),
        gate_sum.astype(F32),
        up_sum.astype(F32),
        down_sum.astype(F32),
    )


def solution(mesh):
    return jax.shard_map(
        body,
        mesh=mesh,
        in_specs=(
            P(None, ("dp", "row"), "col"),
            P("col"),
            P("col"),
            P("col", "row"),
            P("col", "row"),
            P("col", "row"),
            P("row", "col"),
            P("col", "row"),
            P("col", "row"),
            P("row", "col"),
            P(None, "dp"),
            P(None, ("dp", "row"), "col"),
        ),
        out_specs=(
            P(None, ("dp", "row"), "col"),
            P(None, ("dp", "row"), "col"),
            P("col"),
            P("col"),
            P("col", "row"),
            P("col", "row"),
            P("col", "row"),
            P("row", "col"),
            P("col", "row"),
            P("col", "row"),
            P("row", "col"),
        ),
        check_vma=False,
    )
```

```python
import functools
import math

import jax
import jax.numpy as jnp
from jax import lax
from jax.experimental import pallas as pl
from jax.experimental.pallas import tpu as pltpu
from jax.sharding import PartitionSpec as P

WIDTH = 2048
HEADS = 16
KV_HEADS = 8
HEAD_DIM = 128
PREFIX_TOP = 512

epsilon = 1e-05
rope_base = 1000000.0
scale = 1.0 / math.sqrt(HEAD_DIM)
MIB = 1 << 20
F32 = jnp.float32
BF16 = jnp.bfloat16

NT = (((1,), (1,)), ((), ()))
NN = (((1,), (0,)), ((), ()))
TN = (((0,), (0,)), ((), ()))


def dot(left_side, right_side, dims):
    return lax.dot_general(left_side, right_side, dims, preferred_element_type=F32)


def params(mib, grid_rank):
    return pltpu.CompilerParams(
        dimension_semantics=("arbitrary",) * grid_rank, vmem_limit_bytes=mib * MIB
    )


def cost(flops, nbytes, exps=0):
    return pl.CostEstimate(flops=int(flops), bytes_accessed=int(nbytes), transcendentals=int(exps))


def whole(shape):
    return pl.BlockSpec(shape, lambda *_: (0,) * len(shape))


def rope_tables(length):
    half_size = HEAD_DIM // 2
    inverse = rope_base ** (-(jnp.arange(half_size, dtype=F32) * 2.0 / HEAD_DIM))
    angle = jnp.arange(length, dtype=F32)[:, None] * inverse[None, :]
    cosine = jnp.concatenate([jnp.cos(angle), jnp.cos(angle)], axis=1)
    signed = jnp.concatenate([-jnp.sin(angle), jnp.sin(angle)], axis=1)
    return cosine, signed


def rope(values, cosine, signed):
    return values * cosine + pltpu.roll(values, HEAD_DIM // 2, 1) * signed


def rope_back(values, cosine, signed):
    return values * cosine - pltpu.roll(values, HEAD_DIM // 2, 1) * signed


class Line:
    def __init__(self, n):
        self.n = n
        self.r = lax.axis_index("row")
        self.c = lax.axis_index("col")
        self.d = lax.axis_index("dp")

    def copy(self, src, dst, send, recv, **where):
        return pltpu.make_async_remote_copy(
            src_ref=src, dst_ref=dst, send_sem=send, recv_sem=recv, device_id=where,
            device_id_type=pl.DeviceIdType.MESH,
        )

    def up(self, src, dst, send, recv):
        return self.copy(src, dst, send, recv, row=self.r + 1)

    def down(self, src, dst, send, recv):
        return self.copy(src, dst, send, recv, row=self.r - 1)

    def across(self, src, dst, send, recv):
        return self.copy(src, dst, send, recv, col=1 - self.c)

    def barrier(self, core=True, bits=()):
        barrier = pltpu.get_barrier_semaphore()

        def signal(**where):
            pl.semaphore_signal(
                barrier, inc=1, device_id=where, device_id_type=pl.DeviceIdType.MESH
            )

        @pl.when(self.r > 0)
        def _():
            signal(row=self.r - 1)

        @pl.when(self.r < self.n - 1)
        def _():
            signal(row=self.r + 1)

        if core:
            signal(col=1 - self.c)
        for bit in bits:
            signal(dp=self.partner(bit))
        at_end = (self.r == 0) | (self.r == self.n - 1)
        others = int(core) + len(bits)

        @pl.when(at_end)
        def _():
            pl.semaphore_wait(barrier, 1 + others)

        @pl.when(jnp.logical_not(at_end))
        def _():
            pl.semaphore_wait(barrier, 2 + others)

    def side(self, bit):
        return (self.d // 2**bit) % 2

    def partner(self, bit):
        return self.d + (1 - 2 * self.side(bit)) * 2**bit

    def nearest(self, k):
        n = self.n
        code = 0
        for r in range(n):
            order = sorted(range(n), key=lambda q: (abs(q - r), q))
            code += order[k] * n**r
        place, result = self.r * 0 + code, 0
        for r in range(n):
            result = result + (place // n**r) % n * (1 - jnp.minimum(jnp.abs(self.r - r), 1))
        return result


class Gather:
    def __init__(self, line, own, oth, sends, recvs, first=None):
        self.line, self.own, self.oth, self.sends, self.recvs = line, own, oth, sends, recvs
        self.first = own.at[line.r] if first is None else first

    def hop(self, kind, q, src=None):
        way = (self.line.up, self.line.down)[kind]
        src = self.own.at[q] if src is None else src
        return way(src, self.own.at[q], self.sends.at[q, kind], self.recvs.at[q, 0])

    def cross(self, q, src=None):
        src = self.own.at[q] if src is None else src
        return self.line.across(src, self.oth.at[q], self.sends.at[q, 2], self.recvs.at[q, 1])

    def start(self):
        line = self.line

        @pl.when(line.r < line.n - 1)
        def _():
            self.hop(0, line.r, self.first).start()

        @pl.when(line.r > 0)
        def _():
            self.hop(1, line.r, self.first).start()

        self.cross(line.r, self.first).start()

    def step(self, s):
        line = self.line
        low, high = line.r - s, line.r + s

        @pl.when(low >= 0)
        def _():
            self.hop(0, low).wait_recv()

            @pl.when(line.r < line.n - 1)
            def _():
                self.hop(0, low).start()

            self.cross(low).start()

        @pl.when(high <= line.n - 1)
        def _():
            self.hop(1, high).wait_recv()

            @pl.when(line.r > 0)
            def _():
                self.hop(1, high).start()

            self.cross(high).start()

    def arrive(self, q):
        self.cross(q).wait_recv()

    def drain(self):
        line = self.line
        for q in range(line.n):

            @pl.when((line.r >= q) & (line.r < line.n - 1))
            def _(q=q):
                self.hop(0, q).wait_send()

            @pl.when((line.r <= q) & (line.r > 0))
            def _(q=q):
                self.hop(1, q).wait_send()

            self.cross(q).wait_send()


class Scatter:
    def __init__(self, line, part, ups, downs, sends, recvs):
        self.line, self.part, self.ups, self.downs = line, part, ups, downs
        self.sends, self.recvs = sends, recvs

    def hop(self, kind, s, target):
        way = (self.line.up, self.line.down)[kind]
        box = (self.ups, self.downs)[kind]
        return way(
            self.part.at[target], box.at[s - 1], self.sends.at[kind, s - 1], self.recvs.at[kind, s - 1]
        )

    def step(self, s):
        line = self.line
        for kind in range(2):
            behind = line.r if kind == 0 else line.n - 1 - line.r
            target = line.r + line.n - s if kind == 0 else line.r - (line.n - s)
            box = (self.ups, self.downs)[kind]

            @pl.when(behind <= s - 1)
            def _(kind=kind, behind=behind, target=target, box=box):
                if s > 1:

                    @pl.when(behind >= 1)
                    def _():
                        self.hop(kind, s - 1, target).wait_recv()
                        self.part[target] = (
                            self.part[target].astype(F32) + box[s - 2].astype(F32)
                        ).astype(BF16)

                self.hop(kind, s, target).start()

    def total(self, out):
        line = self.line
        last = line.n - 1
        out[...] = self.part[line.r].astype(F32)

        @pl.when(line.r >= 1)
        def _():
            self.hop(0, last, line.r).wait_recv()
            out[...] += self.ups[last - 1].astype(F32)

        @pl.when(line.r <= last - 1)
        def _():
            self.hop(1, last, line.r).wait_recv()
            out[...] += self.downs[last - 1].astype(F32)

    def drain(self):
        line = self.line
        for s in range(1, line.n):

            @pl.when(line.r <= s - 1)
            def _(s=s):
                self.hop(0, s, line.r + line.n - s).wait_send()

            @pl.when(line.n - 1 - line.r <= s - 1)
            def _(s=s):
                self.hop(1, s, line.r - (line.n - s)).wait_send()


def levels_of(line, rows, bits):
    low, size, levels = 0, rows, []
    for bit in bits:
        size //= 2
        keep = low + line.side(bit) * size
        levels.append((size, keep, low + (1 - line.side(bit)) * size))
        low = keep
    return levels


def rows_of(at, size):
    return pl.ds(pl.multiple_of(at, 16), size)


class Reduce:
    def __init__(self, line, ref, boxes, bits, sends, recvs):
        self.line, self.ref, self.boxes, self.bits = line, ref, boxes, bits
        self.sends, self.recvs = sends, recvs
        self.levels = levels_of(line, ref.shape[0], bits)

    def copy(self, at):
        size, _, give = self.levels[at]
        return self.line.copy(
            self.ref.at[rows_of(give, size), :], self.boxes[at], self.sends.at[at], self.recvs.at[at],
            dp=self.line.partner(self.bits[at]),
        )

    def step(self, at, out=None):
        if at > 0:
            self.copy(at - 1).wait_recv()
            size, keep, _ = self.levels[at - 1]
            rows = rows_of(keep, size)
            kept = self.ref[rows, :].astype(F32) + self.boxes[at - 1][...].astype(F32)
            (self.ref if out is None else out)[rows, :] = kept.astype(BF16)
        if at < len(self.bits):
            self.copy(at).start()

    def kept(self):
        size, keep, _ = self.levels[-1]
        return rows_of(keep, size)

    def drain(self):
        for at in range(len(self.bits)):
            self.copy(at).wait_send()


class Spread:
    def __init__(self, line, ref, bits, sends, recvs):
        self.line, self.ref, self.bits, self.sends, self.recvs = line, ref, bits, sends, recvs
        self.levels = levels_of(line, ref.shape[0], bits)

    def copy(self, at):
        level = len(self.bits) - 1 - at
        size, keep, _ = self.levels[level]
        part = self.ref.at[rows_of(keep, size), :]
        return self.line.copy(
            part, part, self.sends.at[at], self.recvs.at[at], dp=self.line.partner(self.bits[level])
        )

    def step(self, at):
        if at > 0:
            self.copy(at - 1).wait_recv()
        if at < len(self.bits):
            self.copy(at).start()

    def drain(self):
        for at in range(len(self.bits)):
            self.copy(at).wait_send()


def two_ways(ref, bits):
    half = ref.shape[0] // 2
    return [(ref.at[pl.ds(at * half, half), :], bits if at == 0 else bits[::-1]) for at in range(2)]


def communicate(number, mib):
    return pltpu.CompilerParams(
        collective_id=number, has_side_effects=True, vmem_limit_bytes=mib * MIB
    )


def forward_kernel(
    n, heads, shared_kv,
    prefix_ref, x_ref, gain_one, gain_two, cos_ref, sin_ref,
    grad_in, wq, wk, wv, wo, wgate, wup, wdown,
    n1_out, n2_out, g_out, qkv_out, log_out, o_own_out, o_oth_out, mid_out, scale_out, wo_from,
    a_own_out, a_oth_out, dg_own_out, dg_oth_out, du_own_out, du_oth_out,
    n_own, n_oth, g_own, g_oth, w_own, w_from, wo_ref, wg_ref, wu_ref, wd_ref,
    qkv_ref, vt_ref, o_own, o_oth, log_ref, part, ups, downs, total, scales, row_out, row_in, stage,
    gather_sends, gather_recvs, scatter_sends, scatter_recvs, cross_sends, cross_recvs, local_sems,
    unit_sends, unit_recvs, unit_stores,
):
    batches, tokens, depth = x_ref.shape
    length = n * tokens
    line = Line(n)
    r, c = line.r, line.c
    q_width = heads * HEAD_DIM
    k_col, v_col = q_width, q_width + HEAD_DIM
    share = wgate.shape[1] // 2
    kv_own = 0 if shared_kv else c * HEAD_DIM
    kv_oth = 0 if shared_kv else (1 - c) * HEAD_DIM

    def lanes(at, size):
        return pl.ds(pl.multiple_of(at, 128), size)

    def rows_at(at, size):
        return pl.ds(pl.multiple_of(at, size), size)

    local_count, cross_count = [0], [0]

    def local(src, dst):
        copy = pltpu.make_async_copy(src, dst, local_sems.at[local_count[0]])
        local_count[0] += 1
        copy.start()
        return copy

    def cross(src, dst):
        at = cross_count[0]
        cross_count[0] += 1
        return line.across(src, dst, cross_sends.at[at], cross_recvs.at[at])

    loads = [
        local(wq.at[:, lanes(c * q_width, q_width)], w_own.at[:, pl.ds(0, q_width)]),
        local(wk.at[:, lanes(kv_own, HEAD_DIM)], w_own.at[:, pl.ds(k_col, HEAD_DIM)]),
        local(wv.at[:, lanes(kv_own, HEAD_DIM)], w_own.at[:, pl.ds(v_col, HEAD_DIM)]),
    ]
    wo_load = local(wo, wo_ref)
    g_loads = [local(grad_in.at[m], g_own.at[m, r]) for m in range(batches)]
    unit_loads = [
        local(wgate.at[:, lanes(c * share, share)], wg_ref.at[0]),
        local(wup.at[:, lanes(c * share, share)], wu_ref.at[0]),
        local(wdown.at[rows_at(c * share, share), :], wd_ref.at[0]),
    ]
    for m in range(batches):
        x = x_ref[m].astype(F32)
        squares = jnp.sum(x * x, axis=1, keepdims=True)
        row_out[0, m] = jnp.broadcast_to(squares, (tokens, 128))
    line.barrier()

    def row_cross(which, m):
        return cross(row_out.at[which, m], row_in.at[which, m])

    def norm_scale(which, m, copy):
        copy.wait_recv()
        squares = row_out[which, m] + row_in[which, m]
        value = lax.rsqrt(squares * (1.0 / WIDTH) + epsilon)
        scales[which, m] = value
        return value[:, :1]

    crosses = [row_cross(0, m) for m in range(batches)]
    for copy in crosses:
        copy.start()
    w_cross = [
        cross(wq.at[:, lanes((1 - c) * q_width, q_width)], w_from.at[:, pl.ds(0, q_width)]),
        cross(wk.at[:, lanes(kv_oth, HEAD_DIM)], w_from.at[:, pl.ds(k_col, HEAD_DIM)]),
        cross(wv.at[:, lanes(kv_oth, HEAD_DIM)], w_from.at[:, pl.ds(v_col, HEAD_DIM)]),
    ]
    gathers = [
        [
            Gather(line, own.at[m], oth.at[m], gather_sends.at[at, m], gather_recvs.at[at, m])
            for m in range(batches)
        ]
        for at, (own, oth) in enumerate(((n_own, n_oth), (g_own, g_oth), (n_own, n_oth)))
    ]
    n1, g, n2 = gathers
    rs = [
        Scatter(line, part.at[m], ups.at[m], downs.at[m], scatter_sends.at[m], scatter_recvs.at[m])
        for m in range(batches)
    ]
    for m in range(batches):
        scale_one = norm_scale(0, m, crosses[m])
        n_own[m, r] = (x_ref[m].astype(F32) * scale_one * gain_one[...]).astype(BF16)
        if m == 0:
            n1[0].start()
            for copy in w_cross:
                copy.start()
    for copy in loads:
        copy.wait()
    for copy in w_cross:
        copy.wait_recv()

    def project(m, q):
        n1[m].arrive(q)
        rows = rows_at(q * tokens, tokens)
        pre = dot(n_own[m, q], w_own[...], NN) + dot(n_oth[m, q], w_from[...], NN)
        cosine, signed = cos_ref[rows, :], sin_ref[rows, :]
        for head in range(heads + 1):
            piece = pre[:, head * HEAD_DIM : (head + 1) * HEAD_DIM]
            qkv_ref[m, rows, pl.ds(head * HEAD_DIM, HEAD_DIM)] = rope(piece, cosine, signed).astype(BF16)
        values = pre[:, v_col : v_col + HEAD_DIM].astype(BF16)
        qkv_ref[m, rows, pl.ds(v_col, HEAD_DIM)] = values
        vt_ref[m, :, rows] = values.T

    block = min(256, length)
    count = length // block

    def attend_block(m, index):
        first = index * block
        extent = min(length, max(first + block, PREFIX_TOP))
        keys = qkv_ref[m, pl.ds(0, extent), pl.ds(k_col, HEAD_DIM)]
        key_at = lax.broadcasted_iota(jnp.int32, (extent, block), 0)
        query_at = lax.broadcasted_iota(jnp.int32, (extent, block), 1) + first
        allowed = (key_at <= query_at) | (key_at < prefix_ref[m, 0])
        for head in range(heads):
            cols = pl.ds(head * HEAD_DIM, HEAD_DIM)
            query = qkv_ref[m, pl.ds(first, block), cols]
            scores = jnp.where(allowed, dot(keys, query, NT) * scale, -1e30)
            topmost = jnp.max(scores, axis=0, keepdims=True)
            exponent = jnp.exp(scores - topmost)
            summed = jnp.sum(exponent, axis=0, keepdims=True)
            weights = (exponent * (1.0 / summed)).astype(BF16)
            result = dot(vt_ref[m, :, pl.ds(0, extent)], weights, NN)
            o_own[m, pl.ds(first, block), cols] = result.T.astype(BF16)
            log_ref[m, pl.ds(head, 1), pl.ds(first, block)] = topmost + jnp.log(summed)

    def project_out(m):
        own_rows, oth_rows = rows_at(c * q_width, q_width), rows_at((1 - c) * q_width, q_width)

        @pl.loop(0, n)
        def _(p):
            rows = rows_at(p * tokens, tokens)
            value = dot(o_own[m, rows, :], wo_ref[own_rows, :], NN)
            value = value + dot(o_oth[m, rows, :], wo_ref[oth_rows, :], NN)
            part[m, p] = value.astype(BF16)

    def walk(m, first, last):
        for k in range(first, last):
            n1[m].step(k)
            project(m, line.nearest(k))

    def release(m, store):
        store.wait()
        n1[m].drain()

    def middle(m):
        rs[m].total(total.at[m])
        total[m] = total[m] + x_ref[m].astype(F32)
        mid = total[m]
        squares = jnp.sum(mid * mid, axis=1, keepdims=True)
        row_out[1, m] = jnp.broadcast_to(squares, (tokens, 128))
        copy = row_cross(1, m)
        copy.start()
        scale_two = norm_scale(1, m, copy)
        n_own[m, r] = (total[m] * scale_two * gain_two[...]).astype(BF16)
        crosses.append(copy)
        n2[m].start()

    outs = ((a_own_out, a_oth_out), (dg_own_out, dg_oth_out), (du_own_out, du_oth_out))
    order = [(m, k) for m in range(batches) for k in range(n)]

    def unit_away(at, kind):
        m, k = order[at]
        return line.across(
            stage.at[at % 2, kind], outs[kind][1].at[m, line.nearest(k)],
            unit_sends.at[at, kind], unit_recvs.at[at, kind],
        )

    def unit_kept(at, kind):
        m, k = order[at]
        return pltpu.make_async_copy(
            stage.at[at % 2, kind], outs[kind][0].at[m, line.nearest(k)], unit_stores.at[at, kind]
        )

    def unit_wait(at):
        for kind in range(3):
            unit_away(at, kind).wait_send()
            unit_kept(at, kind).wait()

    def units(at):
        m, k = order[at]
        q = line.nearest(k)
        n2[m].arrive(q)
        g[m].arrive(q)
        if at >= 2:
            unit_wait(at - 2)
        slot = at % 2
        size = min(256, share)

        @pl.loop(0, share // size)
        def _(b):
            cols = rows_at(b * size, size)
            gate = dot(n_own[m, q], wg_ref[0, :, cols], NN) + dot(n_oth[m, q], wg_ref[1, :, cols], NN)
            up = dot(n_own[m, q], wu_ref[0, :, cols], NN) + dot(n_oth[m, q], wu_ref[1, :, cols], NN)
            da = dot(g_own[m, q], wd_ref[0, cols, :], NT) + dot(g_oth[m, q], wd_ref[1, cols, :], NT)
            sigmoid = 1.0 / (1.0 + jnp.exp(-gate))
            silu = gate * sigmoid
            stage[slot, 0, :, cols] = (silu * up).astype(BF16)
            stage[slot, 1, :, cols] = (da * up * sigmoid * (1.0 + gate * (1.0 - sigmoid))).astype(BF16)
            stage[slot, 2, :, cols] = (da * silu).astype(BF16)

        for kind in range(3):
            unit_away(at, kind).start()
            unit_kept(at, kind).start()

    half = (n + 1) // 2
    o_cross = [cross(o_own.at[m], o_oth.at[m]) for m in range(batches)]
    stores = []

    project(0, r)
    walk(0, 1, n - 1)
    n1[1].start()
    walk(0, n - 1, n)
    n1_stores = [local(n_own.at[0], n1_out.at[0])]
    project(1, r)
    for index in range(count // 2):
        attend_block(0, index)
    walk(1, 1, half)
    for index in range(count // 2, count):
        attend_block(0, index)
    o_cross[0].start()
    big_cross = [
        cross(wgate.at[:, lanes((1 - c) * share, share)], wg_ref.at[1]),
        cross(wup.at[:, lanes((1 - c) * share, share)], wu_ref.at[1]),
        cross(wdown.at[rows_at((1 - c) * share, share), :], wd_ref.at[1]),
        cross(wo.at[rows_at((1 - c) * q_width, q_width), :], wo_from),
    ]
    walk(1, half, n - 1)
    o_cross[0].wait_recv()
    wo_load.wait()
    project_out(0)
    rs[0].step(1)
    g_loads[0].wait()
    g[0].start()
    walk(1, n - 1, n)
    n1_stores.append(local(n_own.at[1], n1_out.at[1]))
    for copy in big_cross:
        copy.start()
    for index in range(count // 2):
        attend_block(1, index)
    for s in range(2, half + 1):
        rs[0].step(s)
    for index in range(count // 2, count):
        attend_block(1, index)
    o_cross[1].start()
    for k in range(1, half):
        g[0].step(k)
    release(0, n1_stores[0])
    for s in range(half + 1, n):
        rs[0].step(s)
    o_cross[1].wait_recv()
    project_out(1)
    rs[1].step(1)
    for k in range(half, n - 1):
        g[0].step(k)
    middle(0)
    release(1, n1_stores[1])
    for s in range(2, half + 1):
        rs[1].step(s)
    g[0].step(n - 1)
    for copy in unit_loads:
        copy.wait()
    for copy in big_cross:
        copy.wait_recv()
    g_loads[1].wait()
    stores += [local(g_own.at[0], g_out.at[0])]
    stores += [local(qkv_ref, qkv_out), local(log_ref, log_out)]
    stores += [local(o_own, o_own_out), local(o_oth, o_oth_out), local(total.at[0], mid_out.at[0])]
    units(0)
    for k in range(1, half):
        n2[0].step(k)
        units(k)
    for s in range(half + 1, n):
        rs[1].step(s)
    for k in range(half, n - 1):
        n2[0].step(k)
    g[1].start()
    for k in range(half, n - 1):
        units(k)
    middle(1)
    stores.append(local(total.at[1], mid_out.at[1]))
    stores.append(local(scales, scale_out))
    n2[0].step(n - 1)
    units(n - 1)
    units(n)
    for k in range(1, n):
        g[1].step(k)
        n2[1].step(k)
        units(n + k)
    stores += [local(g_own.at[1], g_out.at[1]), local(n_own, n2_out)]
    for at in range(2 * n - 2, 2 * n):
        unit_wait(at)
    for at in range(2 * n):
        for kind in range(3):
            unit_away(at, kind).wait_recv()
    for copy in crosses + w_cross + o_cross + big_cross:
        copy.wait_send()
    for item in g + n2 + rs:
        item.drain()
    for copy in stores:
        copy.wait()


def forward(
    prefix, x, gain_one, gain_two, tables, grad_in, wq, wk, wv, wo, wgate, wup, wdown, n, heads, shared_kv
):
    batches, tokens, depth = x.shape
    length = n * tokens
    width = (heads + 2) * HEAD_DIM
    q_width = heads * HEAD_DIM
    share = wgate.shape[1] // 2
    vmem = pl.BlockSpec(memory_space=pltpu.VMEM)
    anywhere = pl.BlockSpec(memory_space=pl.ANY)
    gathered, units = (batches, n, tokens, depth), (batches, n, tokens, share)
    rows = (2, batches, tokens, 128)
    shapes = [
        (gathered, BF16), (gathered, BF16), (gathered, BF16),
        ((batches, length, width), BF16), ((batches, 8, length), F32),
        ((batches, length, q_width), BF16), ((batches, length, q_width), BF16),
        ((batches, tokens, depth), F32), (rows, F32), ((q_width, depth), BF16),
    ] + [(units, BF16)] * 6
    boxes = (batches, n - 1, tokens, depth)
    dma = pltpu.SemaphoreType.DMA
    return pl.pallas_call(
        functools.partial(forward_kernel, n, heads, shared_kv),
        in_specs=[pl.BlockSpec(memory_space=pltpu.SMEM)] + [vmem] * 5 + [anywhere] * 8,
        out_specs=[anywhere] * len(shapes),
        out_shape=[jax.ShapeDtypeStruct(*item) for item in shapes],
        scratch_shapes=[
            pltpu.VMEM(gathered, BF16), pltpu.VMEM(gathered, BF16),
            pltpu.VMEM(gathered, BF16), pltpu.VMEM(gathered, BF16),
            pltpu.VMEM((depth, width), BF16), pltpu.VMEM((depth, width), BF16),
            pltpu.VMEM(wo.shape, BF16),
            pltpu.VMEM((2, depth, share), BF16), pltpu.VMEM((2, depth, share), BF16),
            pltpu.VMEM((2, share, depth), BF16),
            pltpu.VMEM((batches, length, width), BF16),
            pltpu.VMEM((batches, HEAD_DIM, length), BF16),
            pltpu.VMEM((batches, length, q_width), BF16), pltpu.VMEM((batches, length, q_width), BF16),
            pltpu.VMEM((batches, 8, length), F32),
            pltpu.VMEM(gathered, BF16), pltpu.VMEM(boxes, BF16), pltpu.VMEM(boxes, BF16),
            pltpu.VMEM((batches, tokens, depth), F32),
            pltpu.VMEM(rows, F32), pltpu.VMEM(rows, F32), pltpu.VMEM(rows, F32),
            pltpu.VMEM((2, 3, tokens, share), BF16),
            dma((3, batches, n, 3)), dma((3, batches, n, 2)),
            dma((batches, 2, n - 1)), dma((batches, 2, n - 1)), dma((13,)), dma((13,)), dma((24,)),
            dma((batches * n, 3)), dma((batches * n, 3)), dma((batches * n, 3)),
        ],
        compiler_params=communicate(1, 62),
        cost_estimate=cost(2e11, 100 * MIB),
    )(prefix, x, gain_one, gain_two, *tables, grad_in, wq, wk, wv, wo, wgate, wup, wdown)


def unit_grads_kernel(
    n, bits,
    mid_ref, scales_ref, top_ref, gain_ref,
    g_in, n2_in, a_own, a_oth, dg_own, dg_oth, du_own, du_oth, wgate, wup,
    dz_out, dz_oth_out, mgrad_out, down_out, gate_out, up_out, gain_out,
    wg_ref, wu_ref, unit_ref, part, ups, downs, total, dz_ref, row_out, row_in,
    shared_ref, moving_ref, down_ref, gate_ref, up_ref, boxes,
    load_sems, unit_sems, moving_sems, scatter_sends, scatter_recvs, gather_sends, gather_recvs,
    cross_sends, cross_recvs, store_sems, reduce_sends, reduce_recvs, part_sems,
):
    batches, tokens, depth = mid_ref.shape
    share = a_own.shape[1]
    line = Line(n)
    r, c = line.r, line.c
    loads = [
        pltpu.make_async_copy(a, b, load_sems.at[i])
        for i, (a, b) in enumerate(((wgate, wg_ref), (wup, wu_ref), (g_in, shared_ref)))
    ]
    order = [(m, p) for m in range(batches) for p in range(n)]

    def unit_loads(at):
        return [
            pltpu.make_async_copy(
                src.at[pl.ds(at * tokens, tokens), :], unit_ref.at[at % 2, i], unit_sems.at[at % 2, i]
            )
            for i, src in enumerate((dg_own, dg_oth, du_own, du_oth))
        ]

    width = min(256, share)
    nb = share // width
    kinds = ((a_own, a_oth), (dg_own, dg_oth), (du_own, du_oth))

    def moving(kind, index, go):
        for side in range(2):

            @pl.when(index // nb == side)
            def _(side=side):
                cols = pl.ds(pl.multiple_of((index - side * nb) * width, width), width)
                copy = pltpu.make_async_copy(
                    kinds[kind][side].at[:, cols], moving_ref.at[index % 2], moving_sems.at[index % 2]
                )
                copy.start() if go else copy.wait()

    for copy in loads[:2] + unit_loads(0) + loads[2:]:
        copy.start()
    line.barrier(bits=bits)
    scatters = [
        Scatter(line, part.at[m], ups.at[m], downs.at[m], scatter_sends.at[m], scatter_recvs.at[m])
        for m in range(batches)
    ]
    gathers = [
        Gather(
            line, dz_out.at[m], dz_oth_out.at[m], gather_sends.at[m], gather_recvs.at[m], dz_ref.at[m]
        )
        for m in range(batches)
    ]
    reduces = []
    for kind, ref in enumerate((down_ref, gate_ref, up_ref)):
        pair = [
            Reduce(
                line, view, [box.at[way] for box in boxes[kind]], way_bits,
                reduce_sends.at[kind, way], reduce_recvs.at[kind, way],
            )
            for way, (view, way_bits) in enumerate(two_ways(ref, bits))
        ]
        reduces.append(pair)
    cols_own = pl.ds(pl.multiple_of(c * share, share), share)
    cols_oth = pl.ds(pl.multiple_of((1 - c) * share, share), share)

    def unit_part(at):
        m, p = order[at]
        for copy in unit_loads(at):
            copy.wait()
        if at + 1 < len(order):
            for copy in unit_loads(at + 1):
                copy.start()
        slot = at % 2
        block = min(256, depth)

        @pl.loop(0, depth // block)
        def _(b):
            rows = pl.ds(pl.multiple_of(b * block, block), block)
            value = dot(unit_ref[slot, 0], wg_ref[rows, cols_own], NT)
            value = value + dot(unit_ref[slot, 1], wg_ref[rows, cols_oth], NT)
            value = value + dot(unit_ref[slot, 2], wu_ref[rows, cols_own], NT)
            value = value + dot(unit_ref[slot, 3], wu_ref[rows, cols_oth], NT)
            part[m, p, :, rows] = value.astype(BF16)

    def weight_grad(kind):
        @pl.loop(0, 2 * nb)
        def _(index):
            moving(kind, index, False)

            @pl.when(index + 1 < 2 * nb)
            def _():
                moving(kind, index + 1, True)

            side = index // nb
            place = (c + side * (1 - 2 * c)) * nb + index - side * nb
            cols = pl.ds(pl.multiple_of(place * width, width), width)
            if kind == 0:
                down_ref[cols, :] = dot(moving_ref[index % 2], shared_ref[...], TN).astype(BF16)
            else:
                ref = gate_ref if kind == 1 else up_ref
                ref[:, cols] = dot(shared_ref[...], moving_ref[index % 2], TN).astype(BF16)

        if kind + 1 < len(kinds):
            moving(kind + 1, 0, True)

    def row_cross(m):
        return line.across(row_out.at[m], row_in.at[m], cross_sends.at[m], cross_recvs.at[m])

    def store(which, m, src, dst):
        return pltpu.make_async_copy(src, dst, store_sems.at[which, m])

    def middle(m):
        scatters[m].total(total.at[m])
        s = scales_ref[1, m][:, :1]
        gain_out[pl.ds(m, 1), :] = jnp.sum(total[m] * mid_ref[m] * s, axis=0, keepdims=True)
        total[m] = total[m] * gain_ref[...]
        inner = jnp.sum(total[m] * mid_ref[m], axis=1, keepdims=True)
        row_out[m] = jnp.broadcast_to(inner, (tokens, 128))
        row_cross(m).start()
        row_cross(m).wait_recv()
        inner = row_out[m, :, pl.ds(0, 1)] + row_in[m, :, pl.ds(0, 1)]
        result = (
            top_ref[m].astype(F32) + total[m] * s - mid_ref[m] * ((s * s * s) * inner * (1.0 / WIDTH))
        )
        total[m] = result
        dz_ref[m] = result.astype(BF16)
        gathers[m].start()
        store(0, m, total.at[m], mgrad_out.at[m]).start()
        store(1, m, dz_ref.at[m], dz_out.at[m, r]).start()

    def steps(item, first, last):
        for s in range(first, last):
            item.step(s)

    def reduce_step(kind, at):
        for item in reduces[kind]:
            item.step(at)

    half = (n + 1) // 2
    for copy in loads[:2]:
        copy.wait()
    for at in range(n):
        unit_part(at)
    moving(0, 0, True)
    scatters[0].step(1)
    loads[2].wait()
    weight_grad(0)
    reduce_step(0, 0)
    n2_load = pltpu.make_async_copy(n2_in, shared_ref, load_sems.at[3])
    n2_load.start()
    steps(scatters[0], 2, half + 1)
    for at in range(n, 2 * n):
        unit_part(at)
    steps(scatters[0], half + 1, n)
    scatters[1].step(1)
    n2_load.wait()
    weight_grad(1)
    reduce_step(1, 0)
    middle(0)
    steps(scatters[1], 2, half + 1)
    weight_grad(2)
    reduce_step(2, 0)
    steps(scatters[1], half + 1, n)
    steps(gathers[0], 1, half)
    reduce_step(0, 1)
    middle(1)
    steps(gathers[0], half, n)
    reduce_step(1, 1)
    steps(gathers[1], 1, half)
    for kind in range(3):
        for at in range(2 if kind < 2 else 1, len(bits)):
            reduce_step(kind, at)
    steps(gathers[1], half, n)
    outs = (down_out, gate_out, up_out)
    kept_stores = []
    for kind in range(3):
        reduce_step(kind, len(bits))
        for way, item in enumerate(reduces[kind]):
            out_view = two_ways(outs[kind], bits)[way][0]
            rows = item.kept()
            copy = pltpu.make_async_copy(
                item.ref.at[rows, :], out_view.at[rows, :], part_sems.at[kind, way]
            )
            copy.start()
            kept_stores.append(copy)
    for m in range(batches):
        for q in range(n):
            gathers[m].arrive(q)
        gathers[m].drain()
        scatters[m].drain()
        row_cross(m).wait_send()
        store(0, m, total.at[m], mgrad_out.at[m]).wait()
        store(1, m, dz_ref.at[m], dz_out.at[m, r]).wait()
    for pair in reduces:
        for item in pair:
            item.drain()
    for copy in kept_stores:
        copy.wait()


def unit_grads(mid, scales, top, gain, g, n2, halves, wgate, wup, n, dp_count):
    batches, tokens, depth = mid.shape
    rows, share = halves[0].shape
    bits = list(range(dp_count.bit_length() - 1))
    vmem = pl.BlockSpec(memory_space=pltpu.VMEM)
    anywhere = pl.BlockSpec(memory_space=pl.ANY)
    gathered = (batches, n, tokens, depth)
    down_dims, gate_dims = (2 * share, depth), (depth, 2 * share)
    dims = (down_dims, gate_dims, gate_dims)
    shapes = [(gathered, BF16), (gathered, BF16), (mid.shape, F32)]
    shapes += [(item, BF16) for item in dims] + [((8, depth), F32)]
    boxes = (batches, n - 1, tokens, depth)
    width = min(256, share)
    dma = pltpu.SemaphoreType.DMA
    return pl.pallas_call(
        functools.partial(unit_grads_kernel, n, bits),
        in_specs=[vmem] * 4 + [anywhere] * 10,
        out_specs=[anywhere] * 6 + [vmem],
        out_shape=[jax.ShapeDtypeStruct(*item) for item in shapes],
        scratch_shapes=[
            pltpu.VMEM(wgate.shape, BF16), pltpu.VMEM(wup.shape, BF16),
            pltpu.VMEM((2, 4, tokens, share), BF16), pltpu.VMEM(gathered, BF16),
            pltpu.VMEM(boxes, BF16), pltpu.VMEM(boxes, BF16), pltpu.VMEM(mid.shape, F32),
            pltpu.VMEM(mid.shape, BF16),
            pltpu.VMEM((batches, tokens, 128), F32), pltpu.VMEM((batches, tokens, 128), F32),
            pltpu.VMEM((rows, depth), BF16), pltpu.VMEM((2, rows, width), BF16),
            pltpu.VMEM(down_dims, BF16), pltpu.VMEM(gate_dims, BF16), pltpu.VMEM(gate_dims, BF16),
            [
                [pltpu.VMEM((2, item[0] // 2 ** (level + 2), item[1]), BF16) for level in range(len(bits))]
                for item in dims
            ],
            dma((4,)), dma((2, 4)), dma((2,)), dma((batches, 2, n - 1)), dma((batches, 2, n - 1)),
            dma((batches, n, 3)), dma((batches, n, 2)), dma((batches,)), dma((batches,)),
            dma((2, batches)), dma((3, 2, len(bits))), dma((3, 2, len(bits))), dma((3, 2)),
        ],
        compiler_params=communicate(2, 62),
        cost_estimate=cost(2e11, 100 * MIB),
    )(mid, scales, top, gain, g, n2, *halves, wgate, wup)


def backward_kernel(
    n, heads, shared_kv, bits,
    prefix_ref, x_ref, scales_ref, gain_ref, cos_ref, sin_ref, log_ref,
    mgrad_in, dz_own_in, dz_oth_in, wo, wo_from, wq, wk, wv, qkv_in, a_own_in, a_oth_in, wdown, n1_in,
    o_own_in, o_oth_in, down_in, gate_in, up_in,
    grad_out, sum_out, qkv_out, o_out, down_out, gate_out, up_out, gain_out,
    dz_ref, dz_oth, wo_ref, w_own, w_oth, qkv_ref, dk_ref, dv_ref, kt_ref, dqkv_own, dqkv_oth,
    part, ups, downs, total, mgrad_ref, a_ref, wide_ref, o_ref, qkv_grad, o_grad, qkv_sum, o_sum, boxes,
    row_out, row_in,
    load_sems, dz_sems, a_sems, scatter_sends, scatter_recvs, cross_sends, cross_recvs, store_sems,
    reduce_sends, reduce_recvs, spread_sends, spread_recvs, unit_sends, unit_recvs,
):
    batches, tokens, depth = x_ref.shape
    length = n * tokens
    share = a_own_in.shape[1]
    line = Line(n)
    r, c = line.r, line.c
    q_width = heads * HEAD_DIM
    k_col, v_col = q_width, q_width + HEAD_DIM
    width = v_col + HEAD_DIM

    def lanes(at, size):
        return pl.ds(pl.multiple_of(at, 128), size)

    def rows_at(at, size):
        return pl.ds(pl.multiple_of(at, size), size)

    def qkv_columns(side, dst):
        kv = 0 if shared_kv else side * HEAD_DIM
        return [
            (wq.at[:, lanes(side * q_width, q_width)], dst.at[:, pl.ds(0, q_width)]),
            (wk.at[:, lanes(kv, HEAD_DIM)], dst.at[:, pl.ds(k_col, HEAD_DIM)]),
            (wv.at[:, lanes(kv, HEAD_DIM)], dst.at[:, pl.ds(v_col, HEAD_DIM)]),
        ]

    pairs = [(wdown, wide_ref.at[pl.ds(0, 2 * share), :]), (qkv_in, qkv_ref)]
    pairs += [(wo.at[rows_at(c * q_width, q_width), :], wo_ref.at[0]), (wo_from, wo_ref.at[1])]
    pairs += [(dz_own_in, dz_ref)]
    first = len(pairs)
    pairs += qkv_columns(c, w_own) + qkv_columns(1 - c, w_oth)
    pairs += [(o_own_in, o_ref.at[0]), (o_oth_in, o_ref.at[1]), (mgrad_in, mgrad_ref)]
    loads = [pltpu.make_async_copy(a, b, load_sems.at[i]) for i, (a, b) in enumerate(pairs)]
    n1_load = pltpu.make_async_copy(n1_in, wide_ref.at[pl.ds(0, batches * length), :], load_sems.at[len(pairs)])
    order = [(m, p) for m in range(batches) for p in range(n)]

    def a_loads(at):
        rows = pl.ds(at * tokens, tokens)
        return [
            pltpu.make_async_copy(src.at[rows, :], a_ref.at[at % 2, side], a_sems.at[at % 2, side])
            for side, src in enumerate((a_own_in, a_oth_in))
        ]

    def dz_load(at):
        m, p = order[at]
        return pltpu.make_async_copy(dz_oth_in.at[m, p], dz_oth.at[at % 2], dz_sems.at[at % 2])

    for copy in loads[:1] + a_loads(0) + loads[1:first] + [dz_load(0)] + loads[first:]:
        copy.start()
    line.barrier(bits=bits)
    spreads = [
        Spread(line, view, way_bits, unit_sends.at[kind, way], unit_recvs.at[kind, way])
        for kind, ref in enumerate((down_out, gate_out, up_out))
        for way, (view, way_bits) in enumerate(two_ways(ref, bits))
    ]
    out_rs, head_rs = (
        [
            Scatter(
                line, part.at[m], ups.at[which, m], downs.at[which, m],
                scatter_sends.at[which, m], scatter_recvs.at[which, m],
            )
            for m in range(batches)
        ]
        for which in range(2)
    )
    reduces, gatherers = [], []
    for kind, (ref, result) in enumerate(((qkv_grad, qkv_sum), (o_grad, o_sum))):
        results = two_ways(result, bits)
        for way, (view, way_bits) in enumerate(two_ways(ref, bits)):
            reduces.append(
                Reduce(
                    line, view, [box.at[way] for box in boxes[kind]], way_bits,
                    reduce_sends.at[kind, way], reduce_recvs.at[kind, way],
                )
            )
            gatherers.append(
                Spread(
                    line, results[way][0], way_bits, spread_sends.at[kind, way], spread_recvs.at[kind, way]
                )
            )
    count = len(bits)

    def total_step(items, at):
        for item in items:
            if at <= count:
                reduces[item].step(at, gatherers[item].ref if at == count else None)
            if at >= count:
                gatherers[item].step(at - count)

    def spread_step(at):
        for item in spreads:
            item.step(at)

    own_rows, oth_rows = rows_at(c * share, share), rows_at((1 - c) * share, share)

    def down_part(at):
        m, p = order[at]
        for copy in a_loads(at):
            copy.wait()
        if at + 1 < len(order):
            for copy in a_loads(at + 1):
                copy.start()
        value = dot(a_ref[at % 2, 0], wide_ref[own_rows, :], NN)
        part[m, p] = (value + dot(a_ref[at % 2, 1], wide_ref[oth_rows, :], NN)).astype(BF16)

    def grad_cross(m):
        return line.across(dqkv_own.at[m], dqkv_oth.at[m], cross_sends.at[m], cross_recvs.at[m])

    def row_cross(m):
        at = batches + m
        return line.across(row_out.at[m], row_in.at[m], cross_sends.at[at], cross_recvs.at[at])

    def store(which, m, src, dst):
        return pltpu.make_async_copy(src, dst, store_sems.at[which, m])

    def attend_start(m):
        dk_ref[...] = jnp.zeros_like(dk_ref)
        dv_ref[...] = jnp.zeros_like(dv_ref)
        kt_ref[...] = qkv_ref[m, :, pl.ds(k_col, HEAD_DIM)].T

    def attend_back(m, q):
        at = m * n + q
        dz_load(at).wait()
        if at + 1 < len(order):
            dz_load(at + 1).start()
        rows = pl.ds(q * tokens, tokens)
        grads = dot(dz_ref[m, q], wo_ref[0], NT)
        grads = (grads + dot(dz_oth[at % 2], wo_ref[1], NT)).astype(BF16)
        cosine, signed = cos_ref[rows, :], sin_ref[rows, :]
        extent = min(length, max((q + 1) * tokens, PREFIX_TOP))
        upto = pl.ds(0, extent)
        keys = qkv_ref[m, upto, pl.ds(k_col, HEAD_DIM)]
        values = qkv_ref[m, upto, pl.ds(v_col, HEAD_DIM)]
        key_at = lax.broadcasted_iota(jnp.int32, (extent, tokens), 0)
        query_at = lax.broadcasted_iota(jnp.int32, (extent, tokens), 1) + q * tokens
        allowed = (key_at <= query_at) | (key_at < prefix_ref[m, 0])
        for head in range(heads):
            cols = pl.ds(head * HEAD_DIM, HEAD_DIM)
            query = qkv_ref[m, rows, cols]
            grad = grads[:, head * HEAD_DIM : (head + 1) * HEAD_DIM]
            raw = dot(keys, query, NT) * scale - log_ref[m, pl.ds(head, 1), rows]
            probs = jnp.exp(jnp.where(allowed, raw, -1e30))
            dv_ref[upto, :] += dot(probs.astype(BF16), grad, NN)
            prob_grad = dot(values, grad, NT)
            inner = jnp.sum(probs * prob_grad, axis=0, keepdims=True)
            rounded = (probs * (prob_grad - inner) * scale).astype(BF16)
            dk_ref[upto, :] += dot(rounded, query, NN)
            dq = dot(kt_ref[:, upto], rounded, NN).T
            dqkv_own[m, rows, cols] = rope_back(dq, cosine, signed).astype(BF16)

    def attend_end(m):
        dk = rope_back(dk_ref[...], cos_ref[...], sin_ref[...])
        dqkv_own[m, :, pl.ds(k_col, HEAD_DIM)] = dk.astype(BF16)
        dqkv_own[m, :, pl.ds(v_col, HEAD_DIM)] = dv_ref[...].astype(BF16)
        grad_cross(m).start()

    def head_part(m):
        grad_cross(m).wait_recv()

        @pl.loop(0, n)
        def _(p):
            rows = rows_at(p * tokens, tokens)
            value = dot(dqkv_own[m, rows, :], w_own[...], NT)
            part[m, p] = (value + dot(dqkv_oth[m, rows, :], w_oth[...], NT)).astype(BF16)

    def out_total(m):
        out_rs[m].total(total.at[m])
        store(0, m, total.at[m], sum_out.at[m]).start()

    def input_grad(m):
        store(0, m, total.at[m], sum_out.at[m]).wait()
        head_rs[m].total(total.at[m])
        s = scales_ref[0, m][:, :1]
        x = x_ref[m].astype(F32)
        gain_out[pl.ds(m, 1), :] = jnp.sum(total[m] * x * s, axis=0, keepdims=True)
        total[m] = total[m] * gain_ref[...]
        inner = jnp.sum(total[m] * x, axis=1, keepdims=True)
        row_out[m] = jnp.broadcast_to(inner, (tokens, 128))
        row_cross(m).start()
        row_cross(m).wait_recv()
        inner = row_out[m, :, pl.ds(0, 1)] + row_in[m, :, pl.ds(0, 1)]
        total[m] = mgrad_ref[m] + total[m] * s - x * ((s * s * s) * inner * (1.0 / WIDTH))
        store(1, m, total.at[m], grad_out.at[m]).start()

    def steps(item, first_step, last_step):
        for s in range(first_step, last_step):
            item.step(s)

    half = (n + 1) // 2
    spread_step(0)
    loads[0].wait()
    for at in range(n):
        down_part(at)
    out_rs[0].step(1)
    for copy in loads[1:first]:
        copy.wait()
    attend_start(0)
    for q in range(n // 2):
        attend_back(0, q)
    steps(out_rs[0], 2, half + 1)
    for q in range(n // 2, n):
        attend_back(0, q)
    attend_end(0)
    for at in range(n, 2 * n):
        down_part(at)
    n1_load.start()
    steps(out_rs[0], half + 1, n)
    out_rs[1].step(1)
    for at in range(1, count):
        spread_step(at)
    for copy in loads[first:]:
        copy.wait()
    out_total(0)
    out_rs[0].drain()
    head_part(0)
    head_rs[0].step(1)
    attend_start(1)
    for q in range(n // 2):
        attend_back(1, q)
    steps(out_rs[1], 2, half + 1)
    steps(head_rs[0], 2, half + 1)
    for q in range(n // 2, n):
        attend_back(1, q)
    attend_end(1)
    steps(out_rs[1], half + 1, n)
    steps(head_rs[0], half + 1, n)
    n1_load.wait()
    grad_cross(1).wait_recv()
    for side in range(2):
        place = c if side == 0 else 1 - c
        dqkv = (dqkv_own if side == 0 else dqkv_oth)[...].reshape(batches * length, width)
        value = dot(wide_ref[pl.ds(0, batches * length), :], dqkv, TN)
        qkv_grad[:, lanes(place * width, width)] = value.astype(BF16)
    total_step((0, 1), 0)
    out_total(1)
    out_rs[1].drain()

    @pl.loop(0, n)
    def _(p):
        rows = rows_at(p * tokens, tokens)
        value = dot(dqkv_own[1, rows, :], w_own[...], NT)
        part[1, p] = (value + dot(dqkv_oth[1, rows, :], w_oth[...], NT)).astype(BF16)

    head_rs[1].step(1)
    for side in range(2):
        place = c if side == 0 else 1 - c
        value = dot(o_ref[side], dz_ref[...].reshape(batches * length, depth), TN)
        o_grad[rows_at(place * q_width, q_width), :] = value.astype(BF16)
    total_step((2, 3), 0)
    input_grad(0)
    turn, last_turn = 1, 2 * count
    for s in range(2, n):
        head_rs[1].step(s)
        if turn <= last_turn:
            total_step((0, 1, 2, 3), turn)
        turn += 1
    input_grad(1)
    while turn <= last_turn:
        total_step((0, 1, 2, 3), turn)
        turn += 1
    stores = [
        pltpu.make_async_copy(qkv_sum, qkv_out, load_sems.at[0]),
        pltpu.make_async_copy(o_sum, o_out, load_sems.at[1]),
    ]
    for copy in stores:
        copy.start()
    spread_step(count)
    for m in range(batches):
        grad_cross(m).wait_send()
        row_cross(m).wait_send()
        head_rs[m].drain()
        store(1, m, total.at[m], grad_out.at[m]).wait()
    for item in spreads + reduces + gatherers:
        item.drain()
    for copy in stores:
        copy.wait()


def backward(
    prefix, x, scales, gain, tables, logs, mgrad, dz_own, dz_oth, wo, wo_from, wq, wk, wv, qkv,
    a_own, a_oth, wdown, n1, o_own, o_oth, down, gate, up, heads, shared_kv, dp_count,
):
    batches, tokens, depth = x.shape
    n = dz_own.shape[1]
    length, width = qkv.shape[1:]
    rows, q_width = o_own.shape
    share = a_own.shape[1]
    bits = list(range(dp_count.bit_length() - 1))
    vmem = pl.BlockSpec(memory_space=pltpu.VMEM)
    anywhere = pl.BlockSpec(memory_space=pl.ANY)
    gathered = (batches, n, tokens, depth)
    boxes = (2, batches, n - 1, tokens, depth)
    sums = [(depth, 2 * width), (2 * q_width, depth)]
    shapes = [(mgrad.shape, F32), (mgrad.shape, F32)] + [(item, BF16) for item in sums]
    shapes += [(item.shape, BF16) for item in (down, gate, up)] + [((8, depth), F32)]
    dma = pltpu.SemaphoreType.DMA
    return pl.pallas_call(
        functools.partial(backward_kernel, n, heads, shared_kv, bits),
        in_specs=[pl.BlockSpec(memory_space=pltpu.SMEM)] + [vmem] * 6 + [anywhere] * 18,
        out_specs=[anywhere] * 7 + [vmem],
        out_shape=[jax.ShapeDtypeStruct(*item) for item in shapes],
        input_output_aliases={22: 4, 23: 5, 24: 6},
        scratch_shapes=[
            pltpu.VMEM(gathered, BF16), pltpu.VMEM((2, tokens, depth), BF16),
            pltpu.VMEM((2, q_width, depth), BF16),
            pltpu.VMEM((depth, width), BF16), pltpu.VMEM((depth, width), BF16),
            pltpu.VMEM(qkv.shape, BF16),
            pltpu.VMEM((length, HEAD_DIM), F32), pltpu.VMEM((length, HEAD_DIM), F32),
            pltpu.VMEM((HEAD_DIM, length), BF16), pltpu.VMEM(qkv.shape, BF16), pltpu.VMEM(qkv.shape, BF16),
            pltpu.VMEM(gathered, BF16), pltpu.VMEM(boxes, BF16), pltpu.VMEM(boxes, BF16),
            pltpu.VMEM(mgrad.shape, F32), pltpu.VMEM(mgrad.shape, F32),
            pltpu.VMEM((2, 2, tokens, share), BF16),
            pltpu.VMEM((max(2 * share, rows), depth), BF16), pltpu.VMEM((2, rows, q_width), BF16),
            pltpu.VMEM(sums[0], BF16), pltpu.VMEM(sums[1], BF16),
            pltpu.VMEM(sums[0], BF16), pltpu.VMEM(sums[1], BF16),
            [
                [pltpu.VMEM((2, item[0] // 2 ** (level + 2), item[1]), BF16) for level in range(len(bits))]
                for item in sums
            ],
            pltpu.VMEM((batches, tokens, 128), F32), pltpu.VMEM((batches, tokens, 128), F32),
            dma((15,)), dma((2,)), dma((2, 2)),
            dma((2, batches, 2, n - 1)), dma((2, batches, 2, n - 1)),
            dma((2 * batches,)), dma((2 * batches,)), dma((2, batches)),
            dma((2, 2, len(bits))), dma((2, 2, len(bits))), dma((2, 2, len(bits))), dma((2, 2, len(bits))),
            dma((3, 2, len(bits))), dma((3, 2, len(bits))),
        ],
        compiler_params=communicate(3, 62),
        cost_estimate=cost(2e11, 100 * MIB),
    )(
        prefix, x, scales, gain, *tables, logs, mgrad, dz_own, dz_oth, wo, wo_from, wq, wk, wv, qkv,
        a_own, a_oth, wdown, n1, o_own, o_oth, down, gate, up,
    )


def butterfly(values, axes):
    for axis in axes:
        n = lax.axis_size(axis)
        reach = 1
        while reach < n:
            values = values + lax.ppermute(values, axis, [(i, i ^ reach) for i in range(n)])
            reach *= 2
    return values


def body(
    hidden_in,
    attn_gain,
    ffn_gain,
    query_weight,
    key_weight,
    value_weight,
    output_weight,
    gate_weight,
    up_weight,
    down_weight,
    prefix_len,
    out_grad,
):
    col_count, row_count = lax.axis_size("col"), lax.axis_size("row")
    batches, tokens, _ = hidden_in.shape
    length = tokens * row_count
    heads = query_weight.shape[1] // HEAD_DIM // col_count
    row_kv = key_weight.shape[1] // HEAD_DIM
    shared_kv = row_kv < col_count
    q_width = heads * HEAD_DIM
    tables = rope_tables(length)
    (
        n1, n2, g_own, qkv, logs, o_own, o_oth, middle, scales, out_from,
        a_own, a_oth, dg_own, dg_oth, du_own, du_oth,
    ) = forward(
        prefix_len, hidden_in, attn_gain.reshape(1, -1), ffn_gain.reshape(1, -1), tables, out_grad,
        query_weight, key_weight, value_weight, output_weight, gate_weight, up_weight, down_weight,
        row_count, heads, shared_kv,
    )

    def flat(*items):
        return tuple(item.reshape(batches * length, item.shape[-1]) for item in items)

    dp_count = lax.axis_size("dp")
    a_own, a_oth, *grads = flat(a_own, a_oth, dg_own, dg_oth, du_own, du_oth)
    dz, dz_oth, middle_grad, down_sum, gate_sum, up_sum, ffn_gains = unit_grads(
        middle, scales, out_grad, ffn_gain.reshape(1, -1), *flat(g_own, n2), (a_own, a_oth, *grads),
        gate_weight, up_weight, row_count, dp_count,
    )
    in_grad, down_part, qkv_sum, output_sum, down_sum, gate_sum, up_sum, attn_gains = backward(
        prefix_len, hidden_in, scales, attn_gain.reshape(1, -1), tables, logs, middle_grad, dz, dz_oth,
        output_weight, out_from, query_weight, key_weight, value_weight, qkv, a_own, a_oth, down_weight,
        *flat(n1, o_own, o_oth), down_sum, gate_sum, up_sum, heads, shared_kv, dp_count,
    )
    result = (middle + down_part).astype(BF16)
    attn_gain_acc = attn_gains[:batches].sum(axis=0)
    ffn_gain_acc = ffn_gains[:batches].sum(axis=0)
    width = q_width + 2 * HEAD_DIM

    def columns(first, size, shared):
        pieces = [
            qkv_sum[:, side * width + first : side * width + first + size].astype(F32)
            for side in range(col_count)
        ]
        return sum(pieces) if shared else jnp.concatenate(pieces, axis=1)

    gain_one, gain_two = butterfly(jnp.stack([attn_gain_acc, ffn_gain_acc]), ("dp", "row"))
    return (
        result,
        in_grad,
        gain_one,
        gain_two,
        columns(0, q_width, False),
        columns(q_width, HEAD_DIM, shared_kv),
        columns(q_width + HEAD_DIM, HEAD_DIM, shared_kv),
        output_sum.astype(F32),
        gate_sum.astype(F32),
        up_sum.astype(F32),
        down_sum.astype(F32),
    )


def solution(mesh):
    return jax.shard_map(
        body,
        mesh=mesh,
        in_specs=(
            P(None, ("dp", "row"), "col"),
            P("col"),
            P("col"),
            P("col", "row"),
            P("col", "row"),
            P("col", "row"),
            P("row", "col"),
            P("col", "row"),
            P("col", "row"),
            P("row", "col"),
            P(None, "dp"),
            P(None, ("dp", "row"), "col"),
        ),
        out_specs=(
            P(None, ("dp", "row"), "col"),
            P(None, ("dp", "row"), "col"),
            P("col"),
            P("col"),
            P("col", "row"),
            P("col", "row"),
            P("col", "row"),
            P("row", "col"),
            P("col", "row"),
            P("col", "row"),
            P("row", "col"),
        ),
        check_vma=False,
    )
```

```python
import functools
import math

import jax
import jax.numpy as jnp
import numpy as np
from jax import lax
from jax.experimental import pallas as pl
from jax.experimental.pallas import tpu as pltpu
from jax.sharding import PartitionSpec as P

WIDTH = 2048
HEADS = 16
KV_HEADS = 8
HEAD_DIM = 128
PREFIX_TOP = 512

epsilon = 1e-05
rope_base = 1000000.0
scale = 1.0 / math.sqrt(HEAD_DIM)
MIB = 1 << 20
F32 = jnp.float32
BF16 = jnp.bfloat16

NT = (((1,), (1,)), ((), ()))
NN = (((1,), (0,)), ((), ()))
TN = (((0,), (0,)), ((), ()))


def dot(left_side, right_side, dims):
    return lax.dot_general(left_side, right_side, dims, preferred_element_type=F32)


def params(mib, grid_rank):
    return pltpu.CompilerParams(
        dimension_semantics=("arbitrary",) * grid_rank, vmem_limit_bytes=mib * MIB
    )


def cost(flops, nbytes, exps=0):
    return pl.CostEstimate(flops=int(flops), bytes_accessed=int(nbytes), transcendentals=int(exps))


def whole(shape):
    return pl.BlockSpec(shape, lambda *_: (0,) * len(shape))


def rope_tables(length):
    half_size = HEAD_DIM // 2
    inverse = rope_base ** (-(np.arange(half_size) * 2.0 / HEAD_DIM))
    angle = np.arange(length)[:, None] * inverse[None, :]
    cosine = np.concatenate([np.cos(angle), np.cos(angle)], axis=1)
    signed = np.concatenate([-np.sin(angle), np.sin(angle)], axis=1)
    return jnp.asarray(cosine, F32), jnp.asarray(signed, F32)


def rope(values, cosine, signed):
    return values * cosine + pltpu.roll(values, HEAD_DIM // 2, 1) * signed


def rope_back(values, cosine, signed):
    return values * cosine - pltpu.roll(values, HEAD_DIM // 2, 1) * signed


class Line:
    def __init__(self, n):
        self.n = n
        self.r = lax.axis_index("row")
        self.c = lax.axis_index("col")
        self.d = lax.axis_index("dp")

    def copy(self, src, dst, send, recv, **where):
        return pltpu.make_async_remote_copy(
            src_ref=src, dst_ref=dst, send_sem=send, recv_sem=recv, device_id=where,
            device_id_type=pl.DeviceIdType.MESH,
        )

    def up(self, src, dst, send, recv):
        return self.copy(src, dst, send, recv, row=self.r + 1)

    def down(self, src, dst, send, recv):
        return self.copy(src, dst, send, recv, row=self.r - 1)

    def across(self, src, dst, send, recv):
        return self.copy(src, dst, send, recv, col=1 - self.c)

    def barrier(self, core=True, bits=()):
        barrier = pltpu.get_barrier_semaphore()

        def signal(**where):
            pl.semaphore_signal(
                barrier, inc=1, device_id=where, device_id_type=pl.DeviceIdType.MESH
            )

        @pl.when(self.r > 0)
        def _():
            signal(row=self.r - 1)

        @pl.when(self.r < self.n - 1)
        def _():
            signal(row=self.r + 1)

        if core:
            signal(col=1 - self.c)
        for bit in bits:
            signal(dp=self.partner(bit))
        at_end = (self.r == 0) | (self.r == self.n - 1)
        others = int(core) + len(bits)

        @pl.when(at_end)
        def _():
            pl.semaphore_wait(barrier, 1 + others)

        @pl.when(jnp.logical_not(at_end))
        def _():
            pl.semaphore_wait(barrier, 2 + others)

    def wide_barrier(self, dp_count):
        barrier = pltpu.get_barrier_semaphore()
        peers = [dict(row=(self.r + at) % self.n) for at in range(1, self.n)]
        peers += [dict(dp=(self.d + at) % dp_count) for at in range(1, dp_count)]
        peers += [dict(col=1 - self.c)]
        for where in peers:
            pl.semaphore_signal(
                barrier, inc=1, device_id=where, device_id_type=pl.DeviceIdType.MESH
            )
        pl.semaphore_wait(barrier, len(peers))

    def side(self, bit):
        return (self.d // 2**bit) % 2

    def partner(self, bit):
        return self.d + (1 - 2 * self.side(bit)) * 2**bit

    def nearest(self, k):
        n = self.n
        code = 0
        for r in range(n):
            order = sorted(range(n), key=lambda q: (abs(q - r), q))
            code += order[k] * n**r
        place, result = self.r * 0 + code, 0
        for r in range(n):
            result = result + (place // n**r) % n * (1 - jnp.minimum(jnp.abs(self.r - r), 1))
        return result


class Gather:
    def __init__(self, line, own, oth, sends, recvs, first=None):
        self.line, self.own, self.oth, self.sends, self.recvs = line, own, oth, sends, recvs
        self.first = own.at[line.r] if first is None else first

    def hop(self, kind, q, src=None):
        way = (self.line.up, self.line.down)[kind]
        src = self.own.at[q] if src is None else src
        return way(src, self.own.at[q], self.sends.at[q, kind], self.recvs.at[q, 0])

    def cross(self, q, src=None):
        src = self.own.at[q] if src is None else src
        return self.line.across(src, self.oth.at[q], self.sends.at[q, 2], self.recvs.at[q, 1])

    def start(self):
        line = self.line

        @pl.when(line.r < line.n - 1)
        def _():
            self.hop(0, line.r, self.first).start()

        @pl.when(line.r > 0)
        def _():
            self.hop(1, line.r, self.first).start()

        self.cross(line.r, self.first).start()

    def step(self, s):
        line = self.line
        low, high = line.r - s, line.r + s

        @pl.when(low >= 0)
        def _():
            self.hop(0, low).wait_recv()

            @pl.when(line.r < line.n - 1)
            def _():
                self.hop(0, low).start()

            self.cross(low).start()

        @pl.when(high <= line.n - 1)
        def _():
            self.hop(1, high).wait_recv()

            @pl.when(line.r > 0)
            def _():
                self.hop(1, high).start()

            self.cross(high).start()

    def arrive(self, q):
        self.cross(q).wait_recv()

    def drain(self):
        line = self.line
        for q in range(line.n):

            @pl.when((line.r >= q) & (line.r < line.n - 1))
            def _(q=q):
                self.hop(0, q).wait_send()

            @pl.when((line.r <= q) & (line.r > 0))
            def _(q=q):
                self.hop(1, q).wait_send()

            self.cross(q).wait_send()


class Scatter:
    def __init__(self, line, part, ups, downs, sends, recvs):
        self.line, self.part, self.ups, self.downs = line, part, ups, downs
        self.sends, self.recvs = sends, recvs

    def hop(self, kind, s, target):
        way = (self.line.up, self.line.down)[kind]
        box = (self.ups, self.downs)[kind]
        return way(
            self.part.at[target], box.at[s - 1], self.sends.at[kind, s - 1], self.recvs.at[kind, s - 1]
        )

    def step(self, s):
        line = self.line
        for kind in range(2):
            behind = line.r if kind == 0 else line.n - 1 - line.r
            target = line.r + line.n - s if kind == 0 else line.r - (line.n - s)
            box = (self.ups, self.downs)[kind]

            @pl.when(behind <= s - 1)
            def _(kind=kind, behind=behind, target=target, box=box):
                if s > 1:

                    @pl.when(behind >= 1)
                    def _():
                        self.hop(kind, s - 1, target).wait_recv()
                        self.part[target] = (
                            self.part[target].astype(F32) + box[s - 2].astype(F32)
                        ).astype(BF16)

                self.hop(kind, s, target).start()

    def total(self, out):
        out[...] = self.part[self.line.r].astype(F32)
        self.add_received(out)

    def add_received(self, out):
        line = self.line
        last = line.n - 1

        @pl.when(line.r >= 1)
        def _():
            self.hop(0, last, line.r).wait_recv()
            out[...] += self.ups[last - 1].astype(F32)

        @pl.when(line.r <= last - 1)
        def _():
            self.hop(1, last, line.r).wait_recv()
            out[...] += self.downs[last - 1].astype(F32)

    def drain(self):
        line = self.line
        for s in range(1, line.n):

            @pl.when(line.r <= s - 1)
            def _(s=s):
                self.hop(0, s, line.r + line.n - s).wait_send()

            @pl.when(line.n - 1 - line.r <= s - 1)
            def _(s=s):
                self.hop(1, s, line.r - (line.n - s)).wait_send()


class Everywhere:
    def __init__(self, line, axis, place, count, ref, boxes, sends, recvs):
        self.line, self.axis, self.place, self.count = line, axis, place, count
        self.ref, self.boxes, self.sends, self.recvs = ref, boxes, sends, recvs

    def copy(self, at):
        return self.line.copy(
            self.ref, self.boxes.at[at - 1], self.sends.at[at - 1], self.recvs.at[at - 1],
            **{self.axis: (self.place + at) % self.count},
        )

    def start(self):
        for at in range(1, self.count):
            self.copy(at).start()

    def total(self):
        value = self.ref[...]
        for at in range(1, self.count):
            self.copy(at).wait_recv()
            value = value + self.boxes[at - 1]
        return value

    def drain(self):
        for at in range(1, self.count):
            self.copy(at).wait_send()


def levels_of(line, rows, bits):
    low, size, levels = 0, rows, []
    for bit in bits:
        size //= 2
        keep = low + line.side(bit) * size
        levels.append((size, keep, low + (1 - line.side(bit)) * size))
        low = keep
    return levels


def rows_of(at, size):
    return pl.ds(pl.multiple_of(at, 16), size)


class Reduce:
    def __init__(self, line, ref, boxes, bits, sends, recvs):
        self.line, self.ref, self.boxes, self.bits = line, ref, boxes, bits
        self.sends, self.recvs = sends, recvs
        self.levels = levels_of(line, ref.shape[0], bits)

    def copy(self, at):
        size, _, give = self.levels[at]
        return self.line.copy(
            self.ref.at[rows_of(give, size), :], self.boxes[at], self.sends.at[at], self.recvs.at[at],
            dp=self.line.partner(self.bits[at]),
        )

    def step(self, at, out=None):
        if at > 0:
            self.copy(at - 1).wait_recv()
            size, keep, _ = self.levels[at - 1]
            rows = rows_of(keep, size)
            kept = self.ref[rows, :].astype(F32) + self.boxes[at - 1][...].astype(F32)
            (self.ref if out is None else out)[rows, :] = kept.astype(BF16)
        if at < len(self.bits):
            self.copy(at).start()

    def kept(self):
        size, keep, _ = self.levels[-1]
        return rows_of(keep, size)

    def drain(self):
        for at in range(len(self.bits)):
            self.copy(at).wait_send()


class Spread:
    def __init__(self, line, ref, bits, sends, recvs, skip=0):
        self.line, self.ref, self.bits, self.sends, self.recvs = line, ref, bits, sends, recvs
        self.count = len(bits) - skip
        self.levels = levels_of(line, ref.shape[0], bits)

    def copy(self, at):
        level = len(self.bits) - 1 - at
        size, keep, _ = self.levels[level]
        part = self.ref.at[rows_of(keep, size), :]
        return self.line.copy(
            part, part, self.sends.at[at], self.recvs.at[at], dp=self.line.partner(self.bits[level])
        )

    def step(self, at):
        if 0 < at <= self.count:
            self.copy(at - 1).wait_recv()
        if at < self.count:
            self.copy(at).start()

    def drain(self):
        for at in range(self.count):
            self.copy(at).wait_send()


def two_ways(ref, bits):
    half = ref.shape[0] // 2
    return [(ref.at[pl.ds(at * half, half), :], bits if at == 0 else bits[::-1]) for at in range(2)]


def communicate(number, mib):
    return pltpu.CompilerParams(
        collective_id=number, has_side_effects=True, vmem_limit_bytes=mib * MIB
    )


def forward_kernel(
    n, heads, shared_kv,
    prefix_ref, x_ref, gain_one, gain_two, cos_ref, sin_ref,
    grad_in, wq, wk, wv, wo, wgate, wup, wdown,
    n1_out, n2_out, g_out, qkv_out, log_out, o_own_out, o_oth_out, mid_out, scale_out, wo_from,
    a_own_out, a_oth_out, dg_own_out, dg_oth_out, du_own_out, du_oth_out, result_out,
    n_own, n_oth, g_own, g_oth, w_own, w_from, wo_ref, wg_ref, wu_ref, wd_ref, wd_oth, a_ref,
    qkv_ref, vt_ref, o_own, o_oth, log_ref, part, ups, downs, total, scales, row_out, row_in, stage,
    gather_sends, gather_recvs, scatter_sends, scatter_recvs, cross_sends, cross_recvs, local_sems,
    unit_sends, unit_recvs, unit_stores, down_sends, down_recvs, a_sems,
):
    batches, tokens, depth = x_ref.shape
    length = n * tokens
    line = Line(n)
    r, c = line.r, line.c
    q_width = heads * HEAD_DIM
    k_col, v_col = q_width, q_width + HEAD_DIM
    share = wgate.shape[1] // 2
    kv_own = 0 if shared_kv else c * HEAD_DIM
    kv_oth = 0 if shared_kv else (1 - c) * HEAD_DIM

    def lanes(at, size):
        return pl.ds(pl.multiple_of(at, 128), size)

    def rows_at(at, size):
        return pl.ds(pl.multiple_of(at, size), size)

    local_count, cross_count = [0], [0]

    def local(src, dst):
        copy = pltpu.make_async_copy(src, dst, local_sems.at[local_count[0]])
        local_count[0] += 1
        copy.start()
        return copy

    def cross(src, dst):
        at = cross_count[0]
        cross_count[0] += 1
        return line.across(src, dst, cross_sends.at[at], cross_recvs.at[at])

    loads = [
        local(wq.at[:, lanes(c * q_width, q_width)], w_own.at[:, pl.ds(0, q_width)]),
        local(wk.at[:, lanes(kv_own, HEAD_DIM)], w_own.at[:, pl.ds(k_col, HEAD_DIM)]),
        local(wv.at[:, lanes(kv_own, HEAD_DIM)], w_own.at[:, pl.ds(v_col, HEAD_DIM)]),
    ]
    wo_load = local(wo, wo_ref)
    g_loads = [local(grad_in.at[m], g_own.at[m, r]) for m in range(batches)]
    unit_loads = [
        local(wgate.at[:, lanes(c * share, share)], wg_ref.at[0]),
        local(wup.at[:, lanes(c * share, share)], wu_ref.at[0]),
        local(wdown.at[rows_at(c * share, share), :], wd_ref.at[0]),
        local(wdown.at[rows_at((1 - c) * share, share), :], wd_oth),
    ]
    for m in range(batches):
        x = x_ref[m].astype(F32)
        squares = jnp.sum(x * x, axis=1, keepdims=True)
        row_out[0, m] = jnp.broadcast_to(squares, (tokens, 128))
    line.barrier()

    def row_cross(which, m):
        return cross(row_out.at[which, m], row_in.at[which, m])

    def norm_scale(which, m, copy):
        copy.wait_recv()
        squares = row_out[which, m] + row_in[which, m]
        value = lax.rsqrt(squares * (1.0 / WIDTH) + epsilon)
        scales[which, m] = value
        return value[:, :1]

    crosses = [row_cross(0, m) for m in range(batches)]
    for copy in crosses:
        copy.start()
    w_cross = [
        cross(wq.at[:, lanes((1 - c) * q_width, q_width)], w_from.at[:, pl.ds(0, q_width)]),
        cross(wk.at[:, lanes(kv_oth, HEAD_DIM)], w_from.at[:, pl.ds(k_col, HEAD_DIM)]),
        cross(wv.at[:, lanes(kv_oth, HEAD_DIM)], w_from.at[:, pl.ds(v_col, HEAD_DIM)]),
    ]
    gathers = [
        [
            Gather(line, own.at[m], oth.at[m], gather_sends.at[at, m], gather_recvs.at[at, m])
            for m in range(batches)
        ]
        for at, (own, oth) in enumerate(((n_own, n_oth), (g_own, g_oth), (n_own, n_oth)))
    ]
    n1, g, n2 = gathers
    rs = [
        Scatter(line, part.at[m], ups.at[m], downs.at[m], scatter_sends.at[m], scatter_recvs.at[m])
        for m in range(batches)
    ]
    for m in range(batches):
        scale_one = norm_scale(0, m, crosses[m])
        n_own[m, r] = (x_ref[m].astype(F32) * scale_one * gain_one[...]).astype(BF16)
        if m == 0:
            n1[0].start()
            for copy in w_cross:
                copy.start()
    for copy in loads:
        copy.wait()
    for copy in w_cross:
        copy.wait_recv()

    def project(m, q):
        n1[m].arrive(q)
        rows = rows_at(q * tokens, tokens)
        pre = dot(n_own[m, q], w_own[...], NN) + dot(n_oth[m, q], w_from[...], NN)
        cosine, signed = cos_ref[rows, :], sin_ref[rows, :]
        for head in range(heads + 1):
            piece = pre[:, head * HEAD_DIM : (head + 1) * HEAD_DIM]
            qkv_ref[m, rows, pl.ds(head * HEAD_DIM, HEAD_DIM)] = rope(piece, cosine, signed).astype(BF16)
        values = pre[:, v_col : v_col + HEAD_DIM].astype(BF16)
        qkv_ref[m, rows, pl.ds(v_col, HEAD_DIM)] = values
        vt_ref[m, :, rows] = values.T

    block = min(256, length)
    count = length // block

    def attend_block(m, index):
        first = index * block
        extent = min(length, max(first + block, PREFIX_TOP))
        keys = qkv_ref[m, pl.ds(0, extent), pl.ds(k_col, HEAD_DIM)]
        key_at = lax.broadcasted_iota(jnp.int32, (extent, block), 0)
        query_at = lax.broadcasted_iota(jnp.int32, (extent, block), 1) + first
        allowed = (key_at <= query_at) | (key_at < prefix_ref[m, 0])
        for head in range(heads):
            cols = pl.ds(head * HEAD_DIM, HEAD_DIM)
            query = qkv_ref[m, pl.ds(first, block), cols]
            scores = jnp.where(allowed, dot(keys, query, NT) * scale, -1e30)
            topmost = jnp.max(scores, axis=0, keepdims=True)
            exponent = jnp.exp(scores - topmost)
            summed = jnp.sum(exponent, axis=0, keepdims=True)
            weights = (exponent * (1.0 / summed)).astype(BF16)
            result = dot(vt_ref[m, :, pl.ds(0, extent)], weights, NN)
            o_own[m, pl.ds(first, block), cols] = result.T.astype(BF16)
            log_ref[m, pl.ds(head, 1), pl.ds(first, block)] = topmost + jnp.log(summed)

    def project_out(m):
        own_rows, oth_rows = rows_at(c * q_width, q_width), rows_at((1 - c) * q_width, q_width)

        @pl.loop(0, n)
        def _(p):
            rows = rows_at(p * tokens, tokens)
            value = dot(o_own[m, rows, :], wo_ref[own_rows, :], NN)
            value = value + dot(o_oth[m, rows, :], wo_ref[oth_rows, :], NN)
            part[m, p] = value.astype(BF16)

    def walk(m, first, last):
        for k in range(first, last):
            n1[m].step(k)
            project(m, line.nearest(k))

    def release(m, store):
        store.wait()
        n1[m].drain()

    def middle(m):
        rs[m].total(total.at[m])
        total[m] = total[m] + x_ref[m].astype(F32)
        mid = total[m]
        squares = jnp.sum(mid * mid, axis=1, keepdims=True)
        row_out[1, m] = jnp.broadcast_to(squares, (tokens, 128))
        copy = row_cross(1, m)
        copy.start()
        scale_two = norm_scale(1, m, copy)
        n_own[m, r] = (total[m] * scale_two * gain_two[...]).astype(BF16)
        crosses.append(copy)
        n2[m].start()

    outs = ((a_own_out, a_oth_out), (dg_own_out, dg_oth_out), (du_own_out, du_oth_out))
    order = [(m, k) for m in range(batches) for k in range(n)]

    def unit_away(at, kind):
        m, k = order[at]
        return line.across(
            stage.at[at % 2, kind], outs[kind][1].at[m, line.nearest(k)],
            unit_sends.at[at, kind], unit_recvs.at[at, kind],
        )

    def unit_kept(at, kind):
        m, k = order[at]
        return pltpu.make_async_copy(
            stage.at[at % 2, kind], outs[kind][0].at[m, line.nearest(k)], unit_stores.at[at, kind]
        )

    left = set()

    def unit_wait(at):
        if at in left:
            left.remove(at)
            for kind in range(3):
                unit_away(at, kind).wait_send()
                unit_kept(at, kind).wait()

    def units(at):
        m, k = order[at]
        q = line.nearest(k)
        n2[m].arrive(q)
        g[m].arrive(q)
        if at >= 2:
            unit_wait(at - 2)
        slot = at % 2
        size = min(256, share)

        @pl.loop(0, share // size)
        def _(b):
            cols = rows_at(b * size, size)
            gate = dot(n_own[m, q], wg_ref[0, :, cols], NN) + dot(n_oth[m, q], wg_ref[1, :, cols], NN)
            up = dot(n_own[m, q], wu_ref[0, :, cols], NN) + dot(n_oth[m, q], wu_ref[1, :, cols], NN)
            da = dot(g_own[m, q], wd_ref[0, cols, :], NT) + dot(g_oth[m, q], wd_ref[1, cols, :], NT)
            sigmoid = 1.0 / (1.0 + jnp.exp(-gate))
            silu = gate * sigmoid
            stage[slot, 0, :, cols] = (silu * up).astype(BF16)
            stage[slot, 1, :, cols] = (da * up * sigmoid * (1.0 + gate * (1.0 - sigmoid))).astype(BF16)
            stage[slot, 2, :, cols] = (da * silu).astype(BF16)

        left.add(at)
        for kind in range(3):
            unit_away(at, kind).start()
            unit_kept(at, kind).start()

    down_rs = Scatter(line, part.at[0], ups.at[0], downs.at[0], down_sends, down_recvs)

    def down_project():
        for k in range(n):
            unit_wait(k)
            unit_away(k, 0).wait_recv()
        rs[0].drain()

        def a_loads(p):
            return [
                pltpu.make_async_copy(src.at[0, p], a_ref.at[p % 2, side], a_sems.at[p % 2, side])
                for side, src in enumerate((a_own_out, a_oth_out))
            ]

        for p in range(n):
            if p == 0:
                for copy in a_loads(0):
                    copy.start()
            for copy in a_loads(p):
                copy.wait()
            if p + 1 < n:
                for copy in a_loads(p + 1):
                    copy.start()
            value = dot(a_ref[p % 2, 0], wd_ref[0], NN) + dot(a_ref[p % 2, 1], wd_oth[...], NN)
            part[0, p] = value.astype(BF16)

    half = (n + 1) // 2
    o_cross = [cross(o_own.at[m], o_oth.at[m]) for m in range(batches)]
    stores = []

    project(0, r)
    walk(0, 1, n - 1)
    n1[1].start()
    walk(0, n - 1, n)
    n1_stores = [local(n_own.at[0], n1_out.at[0])]
    project(1, r)
    for index in range(count // 2):
        attend_block(0, index)
    walk(1, 1, half)
    for index in range(count // 2, count):
        attend_block(0, index)
    o_cross[0].start()
    big_cross = [
        cross(wgate.at[:, lanes((1 - c) * share, share)], wg_ref.at[1]),
        cross(wup.at[:, lanes((1 - c) * share, share)], wu_ref.at[1]),
        cross(wdown.at[rows_at((1 - c) * share, share), :], wd_ref.at[1]),
        cross(wo.at[rows_at((1 - c) * q_width, q_width), :], wo_from),
    ]
    walk(1, half, n - 1)
    o_cross[0].wait_recv()
    wo_load.wait()
    project_out(0)
    rs[0].step(1)
    g_loads[0].wait()
    g[0].start()
    walk(1, n - 1, n)
    n1_stores.append(local(n_own.at[1], n1_out.at[1]))
    for copy in big_cross:
        copy.start()
    for index in range(count // 2):
        attend_block(1, index)
    for s in range(2, half + 1):
        rs[0].step(s)
    for index in range(count // 2, count):
        attend_block(1, index)
    o_cross[1].start()
    for k in range(1, half):
        g[0].step(k)
    release(0, n1_stores[0])
    for s in range(half + 1, n):
        rs[0].step(s)
    o_cross[1].wait_recv()
    project_out(1)
    rs[1].step(1)
    for k in range(half, n - 1):
        g[0].step(k)
    middle(0)
    release(1, n1_stores[1])
    for s in range(2, half + 1):
        rs[1].step(s)
    g[0].step(n - 1)
    for copy in unit_loads:
        copy.wait()
    for copy in big_cross:
        copy.wait_recv()
    g_loads[1].wait()
    stores += [local(g_own.at[0], g_out.at[0])]
    stores += [local(qkv_ref, qkv_out), local(log_ref, log_out)]
    stores += [local(o_own, o_own_out), local(o_oth, o_oth_out)]
    mid_store = local(total.at[0], mid_out.at[0])
    units(0)
    for k in range(1, half):
        n2[0].step(k)
        units(k)
    for s in range(half + 1, n):
        rs[1].step(s)
    for k in range(half, n - 1):
        n2[0].step(k)
    g[1].start()
    for k in range(half, n - 1):
        units(k)
    middle(1)
    stores.append(local(total.at[1], mid_out.at[1]))
    stores.append(local(scales, scale_out))
    n2[0].step(n - 1)
    units(n - 1)
    units(n)
    down_project()
    down_rs.step(1)
    for k in range(1, n):
        g[1].step(k)
        n2[1].step(k)
        units(n + k)
        if k + 1 < n:
            down_rs.step(k + 1)
    stores += [local(g_own.at[1], g_out.at[1]), local(n_own, n2_out)]
    mid_store.wait()
    total[0] = total[0] + part[0, r].astype(F32)
    down_rs.add_received(total.at[0])
    part[0, r] = total[0].astype(BF16)
    stores.append(local(part.at[0, r], result_out))
    for at in range(2 * n):
        unit_wait(at)
        for kind in range(3):
            if at >= n or kind > 0:
                unit_away(at, kind).wait_recv()
    for copy in crosses + w_cross + o_cross + big_cross:
        copy.wait_send()
    for item in g + n2 + rs[1:] + [down_rs]:
        item.drain()
    for copy in stores:
        copy.wait()


def forward(
    prefix, x, gain_one, gain_two, tables, grad_in, wq, wk, wv, wo, wgate, wup, wdown, n, heads, shared_kv
):
    batches, tokens, depth = x.shape
    length = n * tokens
    width = (heads + 2) * HEAD_DIM
    q_width = heads * HEAD_DIM
    share = wgate.shape[1] // 2
    vmem = pl.BlockSpec(memory_space=pltpu.VMEM)
    anywhere = pl.BlockSpec(memory_space=pl.ANY)
    gathered, units = (batches, n, tokens, depth), (batches, n, tokens, share)
    rows = (2, batches, tokens, 128)
    shapes = [
        (gathered, BF16), (gathered, BF16), (gathered, BF16),
        ((batches, length, width), BF16), ((batches, 8, length), F32),
        ((batches, length, q_width), BF16), ((batches, length, q_width), BF16),
        ((batches, tokens, depth), F32), (rows, F32), ((q_width, depth), BF16),
    ] + [(units, BF16)] * 6 + [((tokens, depth), BF16)]
    boxes = (batches, n - 1, tokens, depth)
    dma = pltpu.SemaphoreType.DMA
    return pl.pallas_call(
        functools.partial(forward_kernel, n, heads, shared_kv),
        in_specs=[pl.BlockSpec(memory_space=pltpu.SMEM)] + [vmem] * 5 + [anywhere] * 8,
        out_specs=[anywhere] * len(shapes),
        out_shape=[jax.ShapeDtypeStruct(*item) for item in shapes],
        scratch_shapes=[
            pltpu.VMEM(gathered, BF16), pltpu.VMEM(gathered, BF16),
            pltpu.VMEM(gathered, BF16), pltpu.VMEM(gathered, BF16),
            pltpu.VMEM((depth, width), BF16), pltpu.VMEM((depth, width), BF16),
            pltpu.VMEM(wo.shape, BF16),
            pltpu.VMEM((2, depth, share), BF16), pltpu.VMEM((2, depth, share), BF16),
            pltpu.VMEM((2, share, depth), BF16), pltpu.VMEM((share, depth), BF16),
            pltpu.VMEM((2, 2, tokens, share), BF16),
            pltpu.VMEM((batches, length, width), BF16),
            pltpu.VMEM((batches, HEAD_DIM, length), BF16),
            pltpu.VMEM((batches, length, q_width), BF16), pltpu.VMEM((batches, length, q_width), BF16),
            pltpu.VMEM((batches, 8, length), F32),
            pltpu.VMEM(gathered, BF16), pltpu.VMEM(boxes, BF16), pltpu.VMEM(boxes, BF16),
            pltpu.VMEM((batches, tokens, depth), F32),
            pltpu.VMEM(rows, F32), pltpu.VMEM(rows, F32), pltpu.VMEM(rows, F32),
            pltpu.VMEM((2, 3, tokens, share), BF16),
            dma((3, batches, n, 3)), dma((3, batches, n, 2)),
            dma((batches, 2, n - 1)), dma((batches, 2, n - 1)), dma((13,)), dma((13,)), dma((24,)),
            dma((batches * n, 3)), dma((batches * n, 3)), dma((batches * n, 3)),
            dma((2, n - 1)), dma((2, n - 1)), dma((2, 2)),
        ],
        compiler_params=communicate(1, 63),
        cost_estimate=cost(2e11, 100 * MIB),
    )(prefix, x, gain_one, gain_two, *tables, grad_in, wq, wk, wv, wo, wgate, wup, wdown)


def unit_grads_kernel(
    n, bits,
    mid_ref, scales_ref, top_ref, gain_ref,
    g_in, n2_in, a_own, a_oth, dg_own, dg_oth, du_own, du_oth, wgate, wup,
    dz_out, dz_oth_out, mgrad_out, down_out, gate_out, up_out, gain_out,
    wg_ref, wu_ref, unit_ref, part, ups, downs, total, dz_ref, row_out, row_in,
    shared_ref, moving_ref, down_ref, gate_ref, up_ref, boxes,
    load_sems, unit_sems, moving_sems, scatter_sends, scatter_recvs, gather_sends, gather_recvs,
    cross_sends, cross_recvs, store_sems, reduce_sends, reduce_recvs, part_sems,
):
    batches, tokens, depth = mid_ref.shape
    share = a_own.shape[1]
    line = Line(n)
    r, c = line.r, line.c
    loads = [
        pltpu.make_async_copy(a, b, load_sems.at[i])
        for i, (a, b) in enumerate(((wgate, wg_ref), (wup, wu_ref), (g_in, shared_ref)))
    ]
    order = [(m, p) for m in range(batches) for p in range(n)]

    def unit_loads(at):
        return [
            pltpu.make_async_copy(
                src.at[pl.ds(at * tokens, tokens), :], unit_ref.at[at % 2, i], unit_sems.at[at % 2, i]
            )
            for i, src in enumerate((dg_own, dg_oth, du_own, du_oth))
        ]

    width = min(256, share)
    nb = share // width
    kinds = ((a_own, a_oth), (dg_own, dg_oth), (du_own, du_oth))

    def moving(kind, index, go):
        for side in range(2):

            @pl.when(index // nb == side)
            def _(side=side):
                cols = pl.ds(pl.multiple_of((index - side * nb) * width, width), width)
                copy = pltpu.make_async_copy(
                    kinds[kind][side].at[:, cols], moving_ref.at[index % 2], moving_sems.at[index % 2]
                )
                copy.start() if go else copy.wait()

    moving(0, 0, True)
    for copy in loads[::-1] + unit_loads(0):
        copy.start()
    line.barrier(bits=bits)
    scatters = [
        Scatter(line, part.at[m], ups.at[m], downs.at[m], scatter_sends.at[m], scatter_recvs.at[m])
        for m in range(batches)
    ]
    gathers = [
        Gather(
            line, dz_out.at[m], dz_oth_out.at[m], gather_sends.at[m], gather_recvs.at[m], dz_ref.at[m]
        )
        for m in range(batches - 1)
    ]
    reduces = []
    for kind, ref in enumerate((down_ref, gate_ref, up_ref)):
        pair = [
            Reduce(
                line, view, [box.at[way] for box in boxes[kind]], way_bits,
                reduce_sends.at[kind, way], reduce_recvs.at[kind, way],
            )
            for way, (view, way_bits) in enumerate(two_ways(ref, bits))
        ]
        reduces.append(pair)
    cols_own = pl.ds(pl.multiple_of(c * share, share), share)
    cols_oth = pl.ds(pl.multiple_of((1 - c) * share, share), share)

    def unit_part(at):
        m, p = order[at]
        for copy in unit_loads(at):
            copy.wait()
        if at + 1 < len(order):
            for copy in unit_loads(at + 1):
                copy.start()
        slot = at % 2
        block = min(256, depth)

        @pl.loop(0, depth // block)
        def _(b):
            rows = pl.ds(pl.multiple_of(b * block, block), block)
            value = dot(unit_ref[slot, 0], wg_ref[rows, cols_own], NT)
            value = value + dot(unit_ref[slot, 1], wg_ref[rows, cols_oth], NT)
            value = value + dot(unit_ref[slot, 2], wu_ref[rows, cols_own], NT)
            value = value + dot(unit_ref[slot, 3], wu_ref[rows, cols_oth], NT)
            part[m, p, :, rows] = value.astype(BF16)

    def weight_grad(kind, first=0, last=2 * nb):
        @pl.loop(first, last)
        def _(index):
            moving(kind, index, False)

            @pl.when(index + 1 < 2 * nb)
            def _():
                moving(kind, index + 1, True)

            side = index // nb
            place = (c + side * (1 - 2 * c)) * nb + index - side * nb
            cols = pl.ds(pl.multiple_of(place * width, width), width)
            if kind == 0:
                down_ref[cols, :] = dot(moving_ref[index % 2], shared_ref[...], TN).astype(BF16)
            else:
                ref = gate_ref if kind == 1 else up_ref
                ref[:, cols] = dot(shared_ref[...], moving_ref[index % 2], TN).astype(BF16)

        if last == 2 * nb and kind + 1 < len(kinds):
            moving(kind + 1, 0, True)

    def row_cross(m):
        return line.across(row_out.at[m], row_in.at[m], cross_sends.at[m], cross_recvs.at[m])

    def store(which, m, src, dst):
        return pltpu.make_async_copy(src, dst, store_sems.at[which, m])

    def middle(m):
        scatters[m].total(total.at[m])
        s = scales_ref[1, m][:, :1]
        gain_out[pl.ds(m, 1), :] = jnp.sum(total[m] * mid_ref[m] * s, axis=0, keepdims=True)
        total[m] = total[m] * gain_ref[...]
        inner = jnp.sum(total[m] * mid_ref[m], axis=1, keepdims=True)
        row_out[m] = jnp.broadcast_to(inner, (tokens, 128))
        row_cross(m).start()
        row_cross(m).wait_recv()
        inner = row_out[m, :, pl.ds(0, 1)] + row_in[m, :, pl.ds(0, 1)]
        result = (
            top_ref[m].astype(F32) + total[m] * s - mid_ref[m] * ((s * s * s) * inner * (1.0 / WIDTH))
        )
        total[m] = result
        dz_ref[m] = result.astype(BF16)
        if m < len(gathers):
            gathers[m].start()
        store(0, m, total.at[m], mgrad_out.at[m]).start()
        store(1, m, dz_ref.at[m], dz_out.at[m, r]).start()

    def steps(item, first, last):
        for s in range(first, last):
            item.step(s)

    def reduce_step(kind, at):
        for item in reduces[kind]:
            item.step(at)

    half = (n + 1) // 2
    loads[2].wait()
    weight_grad(0, 0, nb)
    for way, item in enumerate(reduces[0]):

        @pl.when(c == way)
        def _(item=item):
            item.step(0)

    weight_grad(0, nb, 2 * nb)
    for way, item in enumerate(reduces[0]):

        @pl.when(c != way)
        def _(item=item):
            item.step(0)

    n2_load = pltpu.make_async_copy(n2_in, shared_ref, load_sems.at[3])
    n2_load.start()
    for copy in loads[:2]:
        copy.wait()
    for at in range(n):
        unit_part(at)
    scatters[0].step(1)
    n2_load.wait()
    weight_grad(1)
    reduce_step(1, 0)
    steps(scatters[0], 2, half + 1)
    reduce_step(0, 1)
    for at in range(n, 2 * n):
        unit_part(at)
    steps(scatters[0], half + 1, n)
    scatters[1].step(1)
    weight_grad(2)
    reduce_step(2, 0)
    middle(0)
    steps(scatters[1], 2, half + 1)
    reduce_step(1, 1)
    steps(gathers[0], 1, half)
    steps(scatters[1], half + 1, n)
    steps(gathers[0], half, n - 1)
    reduce_step(2, 1)
    middle(1)
    steps(gathers[0], n - 1, n)
    for at in range(2, len(bits)):
        for kind in range(3):
            reduce_step(kind, at)
    outs = (down_out, gate_out, up_out)
    kept_stores = []
    for kind in range(3):
        reduce_step(kind, len(bits))
        for way, item in enumerate(reduces[kind]):
            out_view = two_ways(outs[kind], bits)[way][0]
            rows = item.kept()
            copy = pltpu.make_async_copy(
                item.ref.at[rows, :], out_view.at[rows, :], part_sems.at[kind, way]
            )
            copy.start()
            kept_stores.append(copy)
    for item in gathers:
        for q in range(n):
            item.arrive(q)
        item.drain()
    for m in range(batches):
        scatters[m].drain()
        row_cross(m).wait_send()
        store(0, m, total.at[m], mgrad_out.at[m]).wait()
        store(1, m, dz_ref.at[m], dz_out.at[m, r]).wait()
    for pair in reduces:
        for item in pair:
            item.drain()
    for copy in kept_stores:
        copy.wait()


def unit_grads(mid, scales, top, gain, g, n2, halves, wgate, wup, n, dp_count):
    batches, tokens, depth = mid.shape
    rows, share = halves[0].shape
    bits = list(range(dp_count.bit_length() - 1))
    vmem = pl.BlockSpec(memory_space=pltpu.VMEM)
    anywhere = pl.BlockSpec(memory_space=pl.ANY)
    gathered = (batches, n, tokens, depth)
    down_dims, gate_dims = (2 * share, depth), (depth, 2 * share)
    dims = (down_dims, gate_dims, gate_dims)
    shapes = [(gathered, BF16), ((batches - 1,) + gathered[1:], BF16), (mid.shape, F32)]
    shapes += [(item, BF16) for item in dims] + [((8, depth), F32)]
    boxes = (batches, n - 1, tokens, depth)
    width = min(256, share)
    dma = pltpu.SemaphoreType.DMA
    return pl.pallas_call(
        functools.partial(unit_grads_kernel, n, bits),
        in_specs=[vmem] * 4 + [anywhere] * 10,
        out_specs=[anywhere] * 6 + [vmem],
        out_shape=[jax.ShapeDtypeStruct(*item) for item in shapes],
        scratch_shapes=[
            pltpu.VMEM(wgate.shape, BF16), pltpu.VMEM(wup.shape, BF16),
            pltpu.VMEM((2, 4, tokens, share), BF16), pltpu.VMEM(gathered, BF16),
            pltpu.VMEM(boxes, BF16), pltpu.VMEM(boxes, BF16), pltpu.VMEM(mid.shape, F32),
            pltpu.VMEM(mid.shape, BF16),
            pltpu.VMEM((batches, tokens, 128), F32), pltpu.VMEM((batches, tokens, 128), F32),
            pltpu.VMEM((rows, depth), BF16), pltpu.VMEM((2, rows, width), BF16),
            pltpu.VMEM(down_dims, BF16), pltpu.VMEM(gate_dims, BF16), pltpu.VMEM(gate_dims, BF16),
            [
                [pltpu.VMEM((2, item[0] // 2 ** (level + 2), item[1]), BF16) for level in range(len(bits))]
                for item in dims
            ],
            dma((4,)), dma((2, 4)), dma((2,)), dma((batches, 2, n - 1)), dma((batches, 2, n - 1)),
            dma((batches, n, 3)), dma((batches, n, 2)), dma((batches,)), dma((batches,)),
            dma((2, batches)), dma((3, 2, len(bits))), dma((3, 2, len(bits))), dma((3, 2)),
        ],
        compiler_params=communicate(2, 62),
        cost_estimate=cost(2e11, 100 * MIB),
    )(mid, scales, top, gain, g, n2, *halves, wgate, wup)


def backward_kernel(
    n, heads, shared_kv, bits,
    prefix_ref, x_ref, scales_ref, gain_in, cos_ref, sin_ref, log_ref, ffn_gains,
    mgrad_in, mid_in, dz_own_in, dz_oth_in, wo, wo_from, wq, wk, wv, qkv_in, a_own_in, a_oth_in, wdown, n1_in,
    o_own_in, o_oth_in, down_in, gate_in, up_in,
    grad_out, result_out, qkv_out, o_out, down_out, gate_out, up_out, gain_out,
    dz_ref, dz_oth, dz_last, wo_ref, w_own, w_oth, qkv_ref, dk_ref, dv_ref, kt_ref, dqkv_own, dqkv_oth,
    part, ups, downs, total, mgrad_ref, a_ref, wide_ref, o_ref, qkv_grad, o_grad, qkv_sum, o_sum, boxes,
    row_out, row_in, result_ref, gain_ref, row_boxes, dp_boxes,
    load_sems, dz_sems, a_sems, scatter_sends, scatter_recvs, cross_sends, cross_recvs, store_sems,
    reduce_sends, reduce_recvs, spread_sends, spread_recvs, unit_sends, unit_recvs,
    gather_sends, gather_recvs, gain_sends, gain_recvs,
):
    batches, tokens, depth = x_ref.shape
    length = n * tokens
    share = a_own_in.shape[1]
    line = Line(n)
    r, c = line.r, line.c
    q_width = heads * HEAD_DIM
    k_col, v_col = q_width, q_width + HEAD_DIM
    width = v_col + HEAD_DIM

    def lanes(at, size):
        return pl.ds(pl.multiple_of(at, 128), size)

    def rows_at(at, size):
        return pl.ds(pl.multiple_of(at, size), size)

    def qkv_columns(side, dst):
        kv = 0 if shared_kv else side * HEAD_DIM
        return [
            (wq.at[:, lanes(side * q_width, q_width)], dst.at[:, pl.ds(0, q_width)]),
            (wk.at[:, lanes(kv, HEAD_DIM)], dst.at[:, pl.ds(k_col, HEAD_DIM)]),
            (wv.at[:, lanes(kv, HEAD_DIM)], dst.at[:, pl.ds(v_col, HEAD_DIM)]),
        ]

    pairs = [(wdown, wide_ref.at[pl.ds(0, 2 * share), :]), (qkv_in, qkv_ref)]
    pairs += [(wo.at[rows_at(c * q_width, q_width), :], wo_ref.at[0]), (wo_from, wo_ref.at[1])]
    last = batches - 1
    pairs += [(dz_own_in.at[m], dz_ref.at[m]) for m in range(last)]
    first = len(pairs)
    pairs += qkv_columns(c, w_own) + qkv_columns(1 - c, w_oth)
    pairs += [(o_own_in, o_ref.at[0]), (o_oth_in, o_ref.at[1]), (mgrad_in, mgrad_ref)]
    pairs += [(mid_in.at[last], total.at[last])]
    loads = [pltpu.make_async_copy(a, b, load_sems.at[i]) for i, (a, b) in enumerate(pairs)]
    n1_load = pltpu.make_async_copy(n1_in, wide_ref.at[pl.ds(0, batches * length), :], load_sems.at[len(pairs)])
    shard_load = pltpu.make_async_copy(
        dz_own_in.at[last, r], dz_ref.at[last, r], load_sems.at[len(pairs) + 1]
    )
    order = [(m, p) for m in range(batches) for p in range(n)]

    def a_loads(at):
        rows = pl.ds(at * tokens, tokens)
        return [
            pltpu.make_async_copy(src.at[rows, :], a_ref.at[at % 2, side], a_sems.at[at % 2, side])
            for side, src in enumerate((a_own_in, a_oth_in))
        ]

    def dz_load(at):
        m, p = order[at]
        return pltpu.make_async_copy(dz_oth_in.at[m, p], dz_oth.at[at % 2], dz_sems.at[at % 2])

    for copy in [shard_load] + loads[:1] + a_loads(last * n) + loads[1:first] + [dz_load(0)] + loads[first:]:
        copy.start()
    dp_count = 2 ** len(bits)
    line.wide_barrier(dp_count)
    gains = [
        Everywhere(line, "row", r, n, gain_ref.at[0], row_boxes, gain_sends.at[0], gain_recvs.at[0]),
        Everywhere(line, "dp", line.d, dp_count, gain_ref.at[1], dp_boxes, gain_sends.at[1], gain_recvs.at[1]),
    ]
    gather = Gather(line, dz_ref.at[last], dz_last, gather_sends, gather_recvs)
    spreads = [
        Spread(
            line, view, way_bits, unit_sends.at[kind, way], unit_recvs.at[kind, way], skip=int(kind == 2)
        )
        for kind, ref in enumerate((down_out, gate_out, up_out))
        for way, (view, way_bits) in enumerate(two_ways(ref, bits))
    ]
    *head_rs, out_rs = (
        Scatter(
            line, part.at[min(at, last)], ups.at[at], downs.at[at], scatter_sends.at[at], scatter_recvs.at[at]
        )
        for at in range(batches + 1)
    )
    reduces, gatherers = [], []
    for kind, (ref, result) in enumerate(((qkv_grad, qkv_sum), (o_grad, o_sum))):
        results = two_ways(result, bits)
        for way, (view, way_bits) in enumerate(two_ways(ref, bits)):
            reduces.append(
                Reduce(
                    line, view, [box.at[way] for box in boxes[kind]], way_bits,
                    reduce_sends.at[kind, way], reduce_recvs.at[kind, way],
                )
            )
            gatherers.append(
                Spread(
                    line, results[way][0], way_bits, spread_sends.at[kind, way], spread_recvs.at[kind, way]
                )
            )
    count = len(bits)

    def total_step(items, at):
        for item in items:
            if at <= count:
                reduces[item].step(at, gatherers[item].ref if at == count else None)
            if at >= count:
                gatherers[item].step(at - count)

    def spread_step(which, at):
        for kind in which:
            for item in spreads[2 * kind : 2 * kind + 2]:
                item.step(at)

    own_rows, oth_rows = rows_at(c * share, share), rows_at((1 - c) * share, share)

    def down_part(at):
        m, p = order[at]
        for copy in a_loads(at):
            copy.wait()
        if at + 1 < len(order):
            for copy in a_loads(at + 1):
                copy.start()
        value = dot(a_ref[at % 2, 0], wide_ref[own_rows, :], NN)
        part[m, p] = (value + dot(a_ref[at % 2, 1], wide_ref[oth_rows, :], NN)).astype(BF16)

    def grad_cross(m):
        return line.across(dqkv_own.at[m], dqkv_oth.at[m], cross_sends.at[m], cross_recvs.at[m])

    def row_cross(m):
        at = batches + m
        return line.across(row_out.at[m], row_in.at[m], cross_sends.at[at], cross_recvs.at[at])

    def store(which, m, src, dst):
        return pltpu.make_async_copy(src, dst, store_sems.at[which, m])

    def attend_start(m):
        dk_ref[...] = jnp.zeros_like(dk_ref)
        dv_ref[...] = jnp.zeros_like(dv_ref)
        kt_ref[...] = qkv_ref[m, :, pl.ds(k_col, HEAD_DIM)].T

    def attend_back(m, q):
        at = m * n + q
        if m < last:
            dz_load(at).wait()
            if at + 1 < last * n:
                dz_load(at + 1).start()
        else:
            gather.arrive(q)
        other = dz_oth[at % 2] if m < last else dz_last[q]
        rows = pl.ds(q * tokens, tokens)
        grads = dot(dz_ref[m, q], wo_ref[0], NT)
        grads = (grads + dot(other, wo_ref[1], NT)).astype(BF16)
        cosine, signed = cos_ref[rows, :], sin_ref[rows, :]
        extent = min(length, max((q + 1) * tokens, PREFIX_TOP))
        upto = pl.ds(0, extent)
        keys = qkv_ref[m, upto, pl.ds(k_col, HEAD_DIM)]
        values = qkv_ref[m, upto, pl.ds(v_col, HEAD_DIM)]
        key_at = lax.broadcasted_iota(jnp.int32, (extent, tokens), 0)
        query_at = lax.broadcasted_iota(jnp.int32, (extent, tokens), 1) + q * tokens
        allowed = (key_at <= query_at) | (key_at < prefix_ref[m, 0])
        for head in range(heads):
            cols = pl.ds(head * HEAD_DIM, HEAD_DIM)
            query = qkv_ref[m, rows, cols]
            grad = grads[:, head * HEAD_DIM : (head + 1) * HEAD_DIM]
            raw = dot(keys, query, NT) * scale - log_ref[m, pl.ds(head, 1), rows]
            probs = jnp.exp(jnp.where(allowed, raw, -1e30))
            dv_ref[upto, :] += dot(probs.astype(BF16), grad, NN)
            prob_grad = dot(values, grad, NT)
            inner = jnp.sum(probs * prob_grad, axis=0, keepdims=True)
            rounded = (probs * (prob_grad - inner) * scale).astype(BF16)
            dk_ref[upto, :] += dot(rounded, query, NN)
            dq = dot(kt_ref[:, upto], rounded, NN).T
            dqkv_own[m, rows, cols] = rope_back(dq, cosine, signed).astype(BF16)

    def attend_end(m):
        dk = rope_back(dk_ref[...], cos_ref[...], sin_ref[...])
        dqkv_own[m, :, pl.ds(k_col, HEAD_DIM)] = dk.astype(BF16)
        dqkv_own[m, :, pl.ds(v_col, HEAD_DIM)] = dv_ref[...].astype(BF16)
        grad_cross(m).start()

    def head_part(m):
        grad_cross(m).wait_recv()

        @pl.loop(0, n)
        def _(p):
            rows = rows_at(p * tokens, tokens)
            value = dot(dqkv_own[m, rows, :], w_own[...], NT)
            part[m, p] = (value + dot(dqkv_oth[m, rows, :], w_oth[...], NT)).astype(BF16)

    def result():
        total[last] = total[last] + part[last, r].astype(F32)
        out_rs.add_received(total.at[last])
        out_rs.drain()
        result_ref[...] = total[last].astype(BF16)
        store(0, 0, result_ref, result_out).start()

    def input_grad(m):
        head_rs[m].total(total.at[m])
        s = scales_ref[0, m][:, :1]
        x = x_ref[m].astype(F32)
        gain_ref[0, pl.ds(m, 1), :] = jnp.sum(total[m] * x * s, axis=0, keepdims=True)
        total[m] = total[m] * gain_in[...]
        inner = jnp.sum(total[m] * x, axis=1, keepdims=True)
        row_out[m] = jnp.broadcast_to(inner, (tokens, 128))
        row_cross(m).start()
        row_cross(m).wait_recv()
        inner = row_out[m, :, pl.ds(0, 1)] + row_in[m, :, pl.ds(0, 1)]
        total[m] = mgrad_ref[m] + total[m] * s - x * ((s * s * s) * inner * (1.0 / WIDTH))
        store(1, m, total.at[m], grad_out.at[m]).start()

    def steps(item, first_step, last_step):
        for s in range(first_step, last_step):
            item.step(s)

    half = (n + 1) // 2
    spread_step((0, 1, 2), 0)
    shard_load.wait()
    gather.start()
    for copy in loads[1:first]:
        copy.wait()
    attend_start(0)
    for q in range(n):
        attend_back(0, q)
    attend_end(0)
    steps(gather, 1, half)
    loads[0].wait()
    for at in range(last * n, len(order)):
        down_part(at)
    out_rs.step(1)
    n1_load.start()
    steps(gather, half, n - 1)
    for copy in loads[first:]:
        copy.wait()
    head_part(0)
    head_rs[0].step(1)
    for at in range(1, count):
        spread_step((0,), at)
    steps(gather, n - 1, n)
    steps(out_rs, 2, half + 1)
    for side in range(2):
        place = c if side == 0 else 1 - c
        value = dot(o_ref[side], dz_ref[...].reshape(batches * length, depth), TN)
        o_grad[rows_at(place * q_width, q_width), :] = value.astype(BF16)
    total_step((2, 3), 0)
    attend_start(1)
    for q in range(n // 2):
        attend_back(1, q)
    steps(head_rs[0], 2, half + 1)
    for at in range(1, count):
        spread_step((1,), at)
    for q in range(n // 2, n):
        attend_back(1, q)
    attend_end(1)
    steps(out_rs, half + 1, n)
    total_step((2, 3), 1)
    n1_load.wait()
    grad_cross(1).wait_recv()
    for side in range(2):
        place = c if side == 0 else 1 - c
        dqkv = (dqkv_own if side == 0 else dqkv_oth)[...].reshape(batches * length, width)
        value = dot(wide_ref[pl.ds(0, batches * length), :], dqkv, TN)
        qkv_grad[:, lanes(place * width, width)] = value.astype(BF16)
    total_step((0, 1), 0)
    steps(head_rs[0], half + 1, n)
    result()

    @pl.loop(0, n)
    def _(p):
        rows = rows_at(p * tokens, tokens)
        value = dot(dqkv_own[1, rows, :], w_own[...], NT)
        part[1, p] = (value + dot(dqkv_oth[1, rows, :], w_oth[...], NT)).astype(BF16)

    head_rs[1].step(1)
    total_step((2, 3), 2)
    input_grad(0)
    total_step((0, 1), 1)
    turn, last_turn = 2, 2 * count
    for s in range(2, n):
        head_rs[1].step(s)
        if turn <= last_turn:
            total_step((0, 1), turn)
        if turn + 1 <= last_turn:
            total_step((2, 3), turn + 1)
        turn += 1
    input_grad(1)
    gain_ref[0, pl.ds(batches, batches), :] = ffn_gains[pl.ds(0, batches), :]
    gains[0].start()
    while turn <= last_turn:
        total_step((0, 1), turn)
        if turn + 1 <= last_turn:
            total_step((2, 3), turn + 1)
        turn += 1
    stores = [
        pltpu.make_async_copy(qkv_sum, qkv_out, load_sems.at[0]),
        pltpu.make_async_copy(o_sum, o_out, load_sems.at[1]),
    ]
    for copy in stores:
        copy.start()
    gain_ref[1] = gains[0].total()
    gains[1].start()
    for at in range(1, count):
        spread_step((2,), at)
    spread_step((0, 1, 2), count)
    for m in range(batches):
        grad_cross(m).wait_send()
        row_cross(m).wait_send()
        head_rs[m].drain()
        store(1, m, total.at[m], grad_out.at[m]).wait()
    store(0, 0, result_ref, result_out).wait()
    gather.drain()
    gain_out[...] = gains[1].total()
    for item in gains:
        item.drain()
    for item in spreads + reduces + gatherers:
        item.drain()
    for copy in stores:
        copy.wait()


def backward(
    prefix, x, scales, gain, tables, logs, ffn_gains, mgrad, mid, dz_own, dz_oth, wo, wo_from, wq, wk, wv, qkv,
    a_own, a_oth, wdown, n1, o_own, o_oth, down, gate, up, heads, shared_kv, dp_count,
):
    batches, tokens, depth = x.shape
    n = dz_own.shape[1]
    length, width = qkv.shape[1:]
    rows, q_width = o_own.shape
    share = a_own.shape[1]
    bits = list(range(dp_count.bit_length() - 1))
    vmem = pl.BlockSpec(memory_space=pltpu.VMEM)
    anywhere = pl.BlockSpec(memory_space=pl.ANY)
    gathered = (batches, n, tokens, depth)
    boxes = (batches + 1, n - 1, tokens, depth)
    sums = [(depth, 2 * width), (2 * q_width, depth)]
    shapes = [(mgrad.shape, F32), ((tokens, depth), BF16)] + [(item, BF16) for item in sums]
    shapes += [(item.shape, BF16) for item in (down, gate, up)] + [((8, depth), F32)]
    dma = pltpu.SemaphoreType.DMA
    return pl.pallas_call(
        functools.partial(backward_kernel, n, heads, shared_kv, bits),
        in_specs=[pl.BlockSpec(memory_space=pltpu.SMEM)] + [vmem] * 7 + [anywhere] * 19,
        out_specs=[anywhere] * 7 + [vmem],
        out_shape=[jax.ShapeDtypeStruct(*item) for item in shapes],
        input_output_aliases={24: 4, 25: 5, 26: 6},
        scratch_shapes=[
            pltpu.VMEM(gathered, BF16), pltpu.VMEM((2, tokens, depth), BF16), pltpu.VMEM(gathered[1:], BF16),
            pltpu.VMEM((2, q_width, depth), BF16),
            pltpu.VMEM((depth, width), BF16), pltpu.VMEM((depth, width), BF16),
            pltpu.VMEM(qkv.shape, BF16),
            pltpu.VMEM((length, HEAD_DIM), F32), pltpu.VMEM((length, HEAD_DIM), F32),
            pltpu.VMEM((HEAD_DIM, length), BF16), pltpu.VMEM(qkv.shape, BF16), pltpu.VMEM(qkv.shape, BF16),
            pltpu.VMEM(gathered, BF16), pltpu.VMEM(boxes, BF16), pltpu.VMEM(boxes, BF16),
            pltpu.VMEM(mgrad.shape, F32), pltpu.VMEM(mgrad.shape, F32),
            pltpu.VMEM((2, 2, tokens, share), BF16),
            pltpu.VMEM((max(2 * share, rows), depth), BF16), pltpu.VMEM((2, rows, q_width), BF16),
            pltpu.VMEM(sums[0], BF16), pltpu.VMEM(sums[1], BF16),
            pltpu.VMEM(sums[0], BF16), pltpu.VMEM(sums[1], BF16),
            [
                [pltpu.VMEM((2, item[0] // 2 ** (level + 2), item[1]), BF16) for level in range(len(bits))]
                for item in sums
            ],
            pltpu.VMEM((batches, tokens, 128), F32), pltpu.VMEM((batches, tokens, 128), F32),
            pltpu.VMEM((tokens, depth), BF16), pltpu.VMEM((2, 8, depth), F32),
            pltpu.VMEM((n - 1, 8, depth), F32), pltpu.VMEM((dp_count - 1, 8, depth), F32),
            dma((20,)), dma((2,)), dma((2, 2)),
            dma((batches + 1, 2, n - 1)), dma((batches + 1, 2, n - 1)),
            dma((2 * batches,)), dma((2 * batches,)), dma((2, batches)),
            dma((2, 2, len(bits))), dma((2, 2, len(bits))), dma((2, 2, len(bits))), dma((2, 2, len(bits))),
            dma((3, 2, len(bits))), dma((3, 2, len(bits))), dma((n, 3)), dma((n, 2)),
            dma((2, max(n, dp_count) - 1)), dma((2, max(n, dp_count) - 1)),
        ],
        compiler_params=communicate(3, 62),
        cost_estimate=cost(2e11, 100 * MIB),
    )(
        prefix, x, scales, gain, *tables, logs, ffn_gains, mgrad, mid, dz_own, dz_oth, wo, wo_from, wq, wk, wv, qkv,
        a_own, a_oth, wdown, n1, o_own, o_oth, down, gate, up,
    )


def last_spread(values, meanwhile):
    count = lax.axis_size("dp")
    half = values.shape[0] // 2
    size, sides, halves = half // 2, [], []
    for way, bit in enumerate((0, count.bit_length() - 2)):
        sides.append((lax.axis_index("dp") >> bit) & 1)
        own = lax.dynamic_slice_in_dim(values, way * half + sides[-1] * size, size, 0)
        halves.append((own, lax.ppermute(own, "dp", [(i, i ^ (1 << bit)) for i in range(count)])))
    halves, meanwhile = lax.optimization_barrier((halves, meanwhile))
    pieces = []
    for side, (own, got) in zip(sides, halves):
        pieces += [jnp.where(side == 0, own, got), jnp.where(side == 0, got, own)]
    return jnp.concatenate([piece.astype(F32) for piece in pieces]), meanwhile


def body(
    hidden_in,
    attn_gain,
    ffn_gain,
    query_weight,
    key_weight,
    value_weight,
    output_weight,
    gate_weight,
    up_weight,
    down_weight,
    prefix_len,
    out_grad,
):
    col_count, row_count = lax.axis_size("col"), lax.axis_size("row")
    batches, tokens, _ = hidden_in.shape
    length = tokens * row_count
    heads = query_weight.shape[1] // HEAD_DIM // col_count
    row_kv = key_weight.shape[1] // HEAD_DIM
    shared_kv = row_kv < col_count
    q_width = heads * HEAD_DIM
    tables = rope_tables(length)
    (
        n1, n2, g_own, qkv, logs, o_own, o_oth, middle, scales, out_from,
        a_own, a_oth, dg_own, dg_oth, du_own, du_oth, first_result,
    ) = forward(
        prefix_len, hidden_in, attn_gain.reshape(1, -1), ffn_gain.reshape(1, -1), tables, out_grad,
        query_weight, key_weight, value_weight, output_weight, gate_weight, up_weight, down_weight,
        row_count, heads, shared_kv,
    )

    def flat(*items):
        return tuple(item.reshape(batches * length, item.shape[-1]) for item in items)

    dp_count = lax.axis_size("dp")
    a_own, a_oth, *grads = flat(a_own, a_oth, dg_own, dg_oth, du_own, du_oth)
    dz, dz_oth, middle_grad, down_sum, gate_sum, up_sum, ffn_gains = unit_grads(
        middle, scales, out_grad, ffn_gain.reshape(1, -1), *flat(g_own, n2), (a_own, a_oth, *grads),
        gate_weight, up_weight, row_count, dp_count,
    )
    in_grad, last_result, qkv_sum, output_sum, down_sum, gate_sum, up_sum, gains = backward(
        prefix_len, hidden_in, scales, attn_gain.reshape(1, -1), tables, logs, ffn_gains, middle_grad,
        middle, dz, dz_oth, output_weight, out_from, query_weight, key_weight, value_weight, qkv, a_own, a_oth, down_weight,
        *flat(n1, o_own, o_oth), down_sum, gate_sum, up_sum, heads, shared_kv, dp_count,
    )
    result = jnp.stack([first_result, last_result])
    width = q_width + 2 * HEAD_DIM

    def columns(first, size, shared):
        pieces = [
            qkv_sum[:, side * width + first : side * width + first + size].astype(F32)
            for side in range(col_count)
        ]
        return sum(pieces) if shared else jnp.concatenate(pieces, axis=1)

    gain_one, gain_two = gains[:batches].sum(axis=0), gains[batches : 2 * batches].sum(axis=0)
    meanwhile = (
        result,
        in_grad,
        gain_one,
        gain_two,
        columns(0, q_width, False),
        columns(q_width, HEAD_DIM, shared_kv),
        columns(q_width + HEAD_DIM, HEAD_DIM, shared_kv),
        output_sum.astype(F32),
        gate_sum.astype(F32),
        down_sum.astype(F32),
    )
    up_sum, (*first, down_sum) = last_spread(up_sum, meanwhile)
    return (*first, up_sum, down_sum)


def solution(mesh):
    return jax.shard_map(
        body,
        mesh=mesh,
        in_specs=(
            P(None, ("dp", "row"), "col"),
            P("col"),
            P("col"),
            P("col", "row"),
            P("col", "row"),
            P("col", "row"),
            P("row", "col"),
            P("col", "row"),
            P("col", "row"),
            P("row", "col"),
            P(None, "dp"),
            P(None, ("dp", "row"), "col"),
        ),
        out_specs=(
            P(None, ("dp", "row"), "col"),
            P(None, ("dp", "row"), "col"),
            P("col"),
            P("col"),
            P("col", "row"),
            P("col", "row"),
            P("col", "row"),
            P("row", "col"),
            P("col", "row"),
            P("col", "row"),
            P("row", "col"),
        ),
        check_vma=False,
    )
```

```python
import functools
import math

import jax
import jax.numpy as jnp
import numpy as np
from jax import lax
from jax.experimental import pallas as pl
from jax.experimental.pallas import tpu as pltpu
from jax.sharding import PartitionSpec as P

WIDTH = 2048
HEADS = 16
KV_HEADS = 8
HEAD_DIM = 128
PREFIX_TOP = 512

epsilon = 1e-05
rope_base = 1000000.0
scale = 1.0 / math.sqrt(HEAD_DIM)
MIB = 1 << 20
F32 = jnp.float32
BF16 = jnp.bfloat16

NT = (((1,), (1,)), ((), ()))
NN = (((1,), (0,)), ((), ()))
TN = (((0,), (0,)), ((), ()))


def dot(left_side, right_side, dims):
    return lax.dot_general(left_side, right_side, dims, preferred_element_type=F32)


def params(mib, grid_rank):
    return pltpu.CompilerParams(
        dimension_semantics=("arbitrary",) * grid_rank, vmem_limit_bytes=mib * MIB
    )


def cost(flops, nbytes, exps=0):
    return pl.CostEstimate(flops=int(flops), bytes_accessed=int(nbytes), transcendentals=int(exps))


def whole(shape):
    return pl.BlockSpec(shape, lambda *_: (0,) * len(shape))


def rope_tables(length):
    half_size = HEAD_DIM // 2
    inverse = rope_base ** (-(np.arange(half_size) * 2.0 / HEAD_DIM))
    angle = np.arange(length)[:, None] * inverse[None, :]
    cosine = np.concatenate([np.cos(angle), np.cos(angle)], axis=1)
    signed = np.concatenate([-np.sin(angle), np.sin(angle)], axis=1)
    return jnp.asarray(cosine, F32), jnp.asarray(signed, F32)


def rope(values, cosine, signed):
    return values * cosine + pltpu.roll(values, HEAD_DIM // 2, 1) * signed


def rope_back(values, cosine, signed):
    return values * cosine - pltpu.roll(values, HEAD_DIM // 2, 1) * signed


class Line:
    def __init__(self, n):
        self.n = n
        self.r = lax.axis_index("row")
        self.c = lax.axis_index("col")
        self.d = lax.axis_index("dp")

    def copy(self, src, dst, send, recv, **where):
        return pltpu.make_async_remote_copy(
            src_ref=src, dst_ref=dst, send_sem=send, recv_sem=recv, device_id=where,
            device_id_type=pl.DeviceIdType.MESH,
        )

    def up(self, src, dst, send, recv):
        return self.copy(src, dst, send, recv, row=self.r + 1)

    def down(self, src, dst, send, recv):
        return self.copy(src, dst, send, recv, row=self.r - 1)

    def across(self, src, dst, send, recv):
        return self.copy(src, dst, send, recv, col=1 - self.c)

    def barrier(self, core=True, bits=()):
        barrier = pltpu.get_barrier_semaphore()

        def signal(**where):
            pl.semaphore_signal(
                barrier, inc=1, device_id=where, device_id_type=pl.DeviceIdType.MESH
            )

        @pl.when(self.r > 0)
        def _():
            signal(row=self.r - 1)

        @pl.when(self.r < self.n - 1)
        def _():
            signal(row=self.r + 1)

        if core:
            signal(col=1 - self.c)
        for bit in bits:
            signal(dp=self.partner(bit))
        at_end = (self.r == 0) | (self.r == self.n - 1)
        others = int(core) + len(bits)

        @pl.when(at_end)
        def _():
            pl.semaphore_wait(barrier, 1 + others)

        @pl.when(jnp.logical_not(at_end))
        def _():
            pl.semaphore_wait(barrier, 2 + others)

    def wide_barrier(self, dp_count):
        barrier = pltpu.get_barrier_semaphore()
        peers = [dict(row=(self.r + at) % self.n) for at in range(1, self.n)]
        peers += [dict(dp=(self.d + at) % dp_count) for at in range(1, dp_count)]
        peers += [dict(col=1 - self.c)]
        for where in peers:
            pl.semaphore_signal(
                barrier, inc=1, device_id=where, device_id_type=pl.DeviceIdType.MESH
            )
        pl.semaphore_wait(barrier, len(peers))

    def side(self, bit):
        return (self.d // 2**bit) % 2

    def partner(self, bit):
        return self.d + (1 - 2 * self.side(bit)) * 2**bit

    def nearest(self, k):
        n = self.n
        code = 0
        for r in range(n):
            order = sorted(range(n), key=lambda q: (abs(q - r), q))
            code += order[k] * n**r
        place, result = self.r * 0 + code, 0
        for r in range(n):
            result = result + (place // n**r) % n * (1 - jnp.minimum(jnp.abs(self.r - r), 1))
        return result


class Gather:
    def __init__(self, line, own, oth, sends, recvs, first=None):
        self.line, self.own, self.oth, self.sends, self.recvs = line, own, oth, sends, recvs
        self.first = own.at[line.r] if first is None else first

    def hop(self, kind, q, src=None):
        way = (self.line.up, self.line.down)[kind]
        src = self.own.at[q] if src is None else src
        return way(src, self.own.at[q], self.sends.at[q, kind], self.recvs.at[q, 0])

    def cross(self, q, src=None):
        src = self.own.at[q] if src is None else src
        return self.line.across(src, self.oth.at[q], self.sends.at[q, 2], self.recvs.at[q, 1])

    def start(self):
        line = self.line

        @pl.when(line.r < line.n - 1)
        def _():
            self.hop(0, line.r, self.first).start()

        @pl.when(line.r > 0)
        def _():
            self.hop(1, line.r, self.first).start()

        self.cross(line.r, self.first).start()

    def step(self, s):
        line = self.line
        low, high = line.r - s, line.r + s

        @pl.when(low >= 0)
        def _():
            self.hop(0, low).wait_recv()

            @pl.when(line.r < line.n - 1)
            def _():
                self.hop(0, low).start()

            self.cross(low).start()

        @pl.when(high <= line.n - 1)
        def _():
            self.hop(1, high).wait_recv()

            @pl.when(line.r > 0)
            def _():
                self.hop(1, high).start()

            self.cross(high).start()

    def arrive(self, q):
        self.cross(q).wait_recv()

    def drain(self):
        line = self.line
        for q in range(line.n):

            @pl.when((line.r >= q) & (line.r < line.n - 1))
            def _(q=q):
                self.hop(0, q).wait_send()

            @pl.when((line.r <= q) & (line.r > 0))
            def _(q=q):
                self.hop(1, q).wait_send()

            self.cross(q).wait_send()


class Scatter:
    def __init__(self, line, part, ups, downs, sends, recvs):
        self.line, self.part, self.ups, self.downs = line, part, ups, downs
        self.sends, self.recvs = sends, recvs

    def hop(self, kind, s, target):
        way = (self.line.up, self.line.down)[kind]
        box = (self.ups, self.downs)[kind]
        return way(
            self.part.at[target], box.at[s - 1], self.sends.at[kind, s - 1], self.recvs.at[kind, s - 1]
        )

    def step(self, s):
        line = self.line
        for kind in range(2):
            behind = line.r if kind == 0 else line.n - 1 - line.r
            target = line.r + line.n - s if kind == 0 else line.r - (line.n - s)
            box = (self.ups, self.downs)[kind]

            @pl.when(behind <= s - 1)
            def _(kind=kind, behind=behind, target=target, box=box):
                if s > 1:

                    @pl.when(behind >= 1)
                    def _():
                        self.hop(kind, s - 1, target).wait_recv()
                        self.part[target] = (
                            self.part[target].astype(F32) + box[s - 2].astype(F32)
                        ).astype(BF16)

                self.hop(kind, s, target).start()

    def total(self, out):
        out[...] = self.part[self.line.r].astype(F32)
        self.add_received(out)

    def add_received(self, out):
        line = self.line
        last = line.n - 1

        @pl.when(line.r >= 1)
        def _():
            self.hop(0, last, line.r).wait_recv()
            out[...] += self.ups[last - 1].astype(F32)

        @pl.when(line.r <= last - 1)
        def _():
            self.hop(1, last, line.r).wait_recv()
            out[...] += self.downs[last - 1].astype(F32)

    def drain(self):
        line = self.line
        for s in range(1, line.n):

            @pl.when(line.r <= s - 1)
            def _(s=s):
                self.hop(0, s, line.r + line.n - s).wait_send()

            @pl.when(line.n - 1 - line.r <= s - 1)
            def _(s=s):
                self.hop(1, s, line.r - (line.n - s)).wait_send()


class Everywhere:
    def __init__(self, line, axis, place, count, ref, boxes, sends, recvs):
        self.line, self.axis, self.place, self.count = line, axis, place, count
        self.ref, self.boxes, self.sends, self.recvs = ref, boxes, sends, recvs

    def copy(self, at):
        return self.line.copy(
            self.ref, self.boxes.at[at - 1], self.sends.at[at - 1], self.recvs.at[at - 1],
            **{self.axis: (self.place + at) % self.count},
        )

    def start(self):
        for at in range(1, self.count):
            self.copy(at).start()

    def total(self):
        value = self.ref[...]
        for at in range(1, self.count):
            self.copy(at).wait_recv()
            value = value + self.boxes[at - 1]
        return value

    def drain(self):
        for at in range(1, self.count):
            self.copy(at).wait_send()


def levels_of(line, rows, bits):
    low, size, levels = 0, rows, []
    for bit in bits:
        size //= 2
        keep = low + line.side(bit) * size
        levels.append((size, keep, low + (1 - line.side(bit)) * size))
        low = keep
    return levels


def rows_of(at, size):
    return pl.ds(pl.multiple_of(at, 16), size)


class Reduce:
    def __init__(self, line, ref, boxes, bits, sends, recvs):
        self.line, self.ref, self.boxes, self.bits = line, ref, boxes, bits
        self.sends, self.recvs = sends, recvs
        self.levels = levels_of(line, ref.shape[0], bits)

    def copy(self, at):
        size, _, give = self.levels[at]
        return self.line.copy(
            self.ref.at[rows_of(give, size), :], self.boxes[at], self.sends.at[at], self.recvs.at[at],
            dp=self.line.partner(self.bits[at]),
        )

    def step(self, at, out=None):
        if at > 0:
            self.copy(at - 1).wait_recv()
            size, keep, _ = self.levels[at - 1]
            rows = rows_of(keep, size)
            kept = self.ref[rows, :].astype(F32) + self.boxes[at - 1][...].astype(F32)
            (self.ref if out is None else out)[rows, :] = kept.astype(BF16)
        if at < len(self.bits):
            self.copy(at).start()

    def kept(self):
        size, keep, _ = self.levels[-1]
        return rows_of(keep, size)

    def drain(self):
        for at in range(len(self.bits)):
            self.copy(at).wait_send()


class Spread:
    def __init__(self, line, ref, bits, sends, recvs, skip=0):
        self.line, self.ref, self.bits, self.sends, self.recvs = line, ref, bits, sends, recvs
        self.count = len(bits) - skip
        self.levels = levels_of(line, ref.shape[0], bits)

    def copy(self, at):
        level = len(self.bits) - 1 - at
        size, keep, _ = self.levels[level]
        part = self.ref.at[rows_of(keep, size), :]
        return self.line.copy(
            part, part, self.sends.at[at], self.recvs.at[at], dp=self.line.partner(self.bits[level])
        )

    def step(self, at):
        if 0 < at <= self.count:
            self.copy(at - 1).wait_recv()
        if at < self.count:
            self.copy(at).start()

    def drain(self):
        for at in range(self.count):
            self.copy(at).wait_send()


def two_ways(ref, bits):
    half = ref.shape[0] // 2
    return [(ref.at[pl.ds(at * half, half), :], bits if at == 0 else bits[::-1]) for at in range(2)]


def communicate(number, mib):
    return pltpu.CompilerParams(
        collective_id=number, has_side_effects=True, vmem_limit_bytes=mib * MIB
    )


def forward_kernel(
    n, heads, shared_kv,
    prefix_ref, x_ref, gain_one, gain_two, cos_ref, sin_ref,
    grad_in, wq, wk, wv, wo, wgate, wup, wdown,
    n1_out, n2_out, g_out, qkv_out, log_out, o_own_out, o_oth_out, mid_out, scale_out, wo_from,
    a_own_out, a_oth_out, dg_own_out, dg_oth_out, du_own_out, du_oth_out, result_out,
    n_own, n_oth, g_own, g_oth, w_own, w_from, wo_ref, wg_ref, wu_ref, wd_ref, wd_oth, a_ref,
    qkv_ref, vt_ref, o_own, o_oth, log_ref, part, ups, downs, total, scales, row_out, row_in, stage,
    gather_sends, gather_recvs, scatter_sends, scatter_recvs, cross_sends, cross_recvs, local_sems,
    unit_sends, unit_recvs, unit_stores, down_sends, down_recvs, a_sems,
):
    batches, tokens, depth = x_ref.shape
    length = n * tokens
    line = Line(n)
    r, c = line.r, line.c
    q_width = heads * HEAD_DIM
    k_col, v_col = q_width, q_width + HEAD_DIM
    share = wgate.shape[1] // 2
    kv_own = 0 if shared_kv else c * HEAD_DIM
    kv_oth = 0 if shared_kv else (1 - c) * HEAD_DIM

    def lanes(at, size):
        return pl.ds(pl.multiple_of(at, 128), size)

    def rows_at(at, size):
        return pl.ds(pl.multiple_of(at, size), size)

    local_count, cross_count = [0], [0]

    def local(src, dst):
        copy = pltpu.make_async_copy(src, dst, local_sems.at[local_count[0]])
        local_count[0] += 1
        copy.start()
        return copy

    def cross(src, dst):
        at = cross_count[0]
        cross_count[0] += 1
        return line.across(src, dst, cross_sends.at[at], cross_recvs.at[at])

    loads = [
        local(wq.at[:, lanes(c * q_width, q_width)], w_own.at[:, pl.ds(0, q_width)]),
        local(wk.at[:, lanes(kv_own, HEAD_DIM)], w_own.at[:, pl.ds(k_col, HEAD_DIM)]),
        local(wv.at[:, lanes(kv_own, HEAD_DIM)], w_own.at[:, pl.ds(v_col, HEAD_DIM)]),
    ]
    wo_load = local(wo, wo_ref)
    g_loads = [local(grad_in.at[m], g_own.at[m, r]) for m in range(batches)]
    unit_loads = [
        local(wgate.at[:, lanes(c * share, share)], wg_ref.at[0]),
        local(wup.at[:, lanes(c * share, share)], wu_ref.at[0]),
        local(wdown.at[rows_at(c * share, share), :], wd_ref.at[0]),
        local(wdown.at[rows_at((1 - c) * share, share), :], wd_oth),
    ]
    for m in range(batches):
        x = x_ref[m].astype(F32)
        squares = jnp.sum(x * x, axis=1, keepdims=True)
        row_out[0, m] = jnp.broadcast_to(squares, (tokens, 128))
    line.barrier()

    def row_cross(which, m):
        return cross(row_out.at[which, m], row_in.at[which, m])

    def norm_scale(which, m, copy):
        copy.wait_recv()
        squares = row_out[which, m] + row_in[which, m]
        value = lax.rsqrt(squares * (1.0 / WIDTH) + epsilon)
        scales[which, m] = value
        return value[:, :1]

    crosses = [row_cross(0, m) for m in range(batches)]
    for copy in crosses:
        copy.start()
    w_cross = [
        cross(wq.at[:, lanes((1 - c) * q_width, q_width)], w_from.at[:, pl.ds(0, q_width)]),
        cross(wk.at[:, lanes(kv_oth, HEAD_DIM)], w_from.at[:, pl.ds(k_col, HEAD_DIM)]),
        cross(wv.at[:, lanes(kv_oth, HEAD_DIM)], w_from.at[:, pl.ds(v_col, HEAD_DIM)]),
    ]
    gathers = [
        [
            Gather(line, own.at[m], oth.at[m], gather_sends.at[at, m], gather_recvs.at[at, m])
            for m in range(batches)
        ]
        for at, (own, oth) in enumerate(((n_own, n_oth), (g_own, g_oth), (n_own, n_oth)))
    ]
    n1, g, n2 = gathers
    rs = [
        Scatter(line, part.at[m], ups.at[m], downs.at[m], scatter_sends.at[m], scatter_recvs.at[m])
        for m in range(batches)
    ]
    for m in range(batches):
        scale_one = norm_scale(0, m, crosses[m])
        n_own[m, r] = (x_ref[m].astype(F32) * scale_one * gain_one[...]).astype(BF16)
        if m == 0:
            n1[0].start()
            for copy in w_cross:
                copy.start()
    for copy in loads:
        copy.wait()
    for copy in w_cross:
        copy.wait_recv()

    def project(m, q):
        n1[m].arrive(q)
        rows = rows_at(q * tokens, tokens)
        pre = dot(n_own[m, q], w_own[...], NN) + dot(n_oth[m, q], w_from[...], NN)
        cosine, signed = cos_ref[rows, :], sin_ref[rows, :]
        for head in range(heads + 1):
            piece = pre[:, head * HEAD_DIM : (head + 1) * HEAD_DIM]
            qkv_ref[m, rows, pl.ds(head * HEAD_DIM, HEAD_DIM)] = rope(piece, cosine, signed).astype(BF16)
        values = pre[:, v_col : v_col + HEAD_DIM].astype(BF16)
        qkv_ref[m, rows, pl.ds(v_col, HEAD_DIM)] = values
        vt_ref[m, :, rows] = values.T

    block = min(256, length)
    count = length // block

    def attend_block(m, index):
        first = index * block
        extent = min(length, max(first + block, PREFIX_TOP))
        keys = qkv_ref[m, pl.ds(0, extent), pl.ds(k_col, HEAD_DIM)]
        key_at = lax.broadcasted_iota(jnp.int32, (extent, block), 0)
        query_at = lax.broadcasted_iota(jnp.int32, (extent, block), 1) + first
        allowed = (key_at <= query_at) | (key_at < prefix_ref[m, 0])
        for head in range(heads):
            cols = pl.ds(head * HEAD_DIM, HEAD_DIM)
            query = qkv_ref[m, pl.ds(first, block), cols]
            scores = jnp.where(allowed, dot(keys, query, NT) * scale, -1e30)
            topmost = jnp.max(scores, axis=0, keepdims=True)
            exponent = jnp.exp(scores - topmost)
            summed = jnp.sum(exponent, axis=0, keepdims=True)
            weights = (exponent * (1.0 / summed)).astype(BF16)
            result = dot(vt_ref[m, :, pl.ds(0, extent)], weights, NN)
            o_own[m, pl.ds(first, block), cols] = result.T.astype(BF16)
            log_ref[m, pl.ds(head, 1), pl.ds(first, block)] = topmost + jnp.log(summed)

    def project_out(m):
        own_rows, oth_rows = rows_at(c * q_width, q_width), rows_at((1 - c) * q_width, q_width)

        @pl.loop(0, n)
        def _(p):
            rows = rows_at(p * tokens, tokens)
            value = dot(o_own[m, rows, :], wo_ref[own_rows, :], NN)
            value = value + dot(o_oth[m, rows, :], wo_ref[oth_rows, :], NN)
            part[m, p] = value.astype(BF16)

    def walk(m, first, last):
        for k in range(first, last):
            n1[m].step(k)
            project(m, line.nearest(k))

    def release(m, store):
        store.wait()
        n1[m].drain()

    def middle(m):
        rs[m].total(total.at[m])
        total[m] = total[m] + x_ref[m].astype(F32)
        mid = total[m]
        squares = jnp.sum(mid * mid, axis=1, keepdims=True)
        row_out[1, m] = jnp.broadcast_to(squares, (tokens, 128))
        copy = row_cross(1, m)
        copy.start()
        scale_two = norm_scale(1, m, copy)
        n_own[m, r] = (total[m] * scale_two * gain_two[...]).astype(BF16)
        crosses.append(copy)
        n2[m].start()

    outs = ((a_own_out, a_oth_out), (dg_own_out, dg_oth_out), (du_own_out, du_oth_out))
    order = [(m, k) for m in range(batches) for k in range(n)]

    def unit_away(at, kind):
        m, k = order[at]
        return line.across(
            stage.at[at % 2, kind], outs[kind][1].at[m, line.nearest(k)],
            unit_sends.at[at, kind], unit_recvs.at[at, kind],
        )

    def unit_kept(at, kind):
        m, k = order[at]
        return pltpu.make_async_copy(
            stage.at[at % 2, kind], outs[kind][0].at[m, line.nearest(k)], unit_stores.at[at, kind]
        )

    left = set()

    def unit_wait(at):
        if at in left:
            left.remove(at)
            for kind in range(3):
                unit_away(at, kind).wait_send()
                unit_kept(at, kind).wait()

    def units(at):
        m, k = order[at]
        q = line.nearest(k)
        n2[m].arrive(q)
        g[m].arrive(q)
        if at >= 2:
            unit_wait(at - 2)
        slot = at % 2
        size = min(256, share)

        @pl.loop(0, share // size)
        def _(b):
            cols = rows_at(b * size, size)
            gate = dot(n_own[m, q], wg_ref[0, :, cols], NN) + dot(n_oth[m, q], wg_ref[1, :, cols], NN)
            up = dot(n_own[m, q], wu_ref[0, :, cols], NN) + dot(n_oth[m, q], wu_ref[1, :, cols], NN)
            da = dot(g_own[m, q], wd_ref[0, cols, :], NT) + dot(g_oth[m, q], wd_ref[1, cols, :], NT)
            sigmoid = 1.0 / (1.0 + jnp.exp(-gate))
            silu = gate * sigmoid
            stage[slot, 0, :, cols] = (silu * up).astype(BF16)
            stage[slot, 1, :, cols] = (da * up * sigmoid * (1.0 + gate * (1.0 - sigmoid))).astype(BF16)
            stage[slot, 2, :, cols] = (da * silu).astype(BF16)

        left.add(at)
        for kind in range(3):
            unit_away(at, kind).start()
            unit_kept(at, kind).start()

    down_rs = Scatter(line, part.at[0], ups.at[0], downs.at[0], down_sends, down_recvs)

    def down_project():
        for k in range(n):
            unit_wait(k)
            unit_away(k, 0).wait_recv()
        rs[0].drain()

        def a_loads(p):
            return [
                pltpu.make_async_copy(src.at[0, p], a_ref.at[p % 2, side], a_sems.at[p % 2, side])
                for side, src in enumerate((a_own_out, a_oth_out))
            ]

        for p in range(n):
            if p == 0:
                for copy in a_loads(0):
                    copy.start()
            for copy in a_loads(p):
                copy.wait()
            if p + 1 < n:
                for copy in a_loads(p + 1):
                    copy.start()
            value = dot(a_ref[p % 2, 0], wd_ref[0], NN) + dot(a_ref[p % 2, 1], wd_oth[...], NN)
            part[0, p] = value.astype(BF16)

    half = (n + 1) // 2
    o_cross = [cross(o_own.at[m], o_oth.at[m]) for m in range(batches)]
    stores = []

    project(0, r)
    walk(0, 1, n - 1)
    n1[1].start()
    walk(0, n - 1, n)
    n1_stores = [local(n_own.at[0], n1_out.at[0])]
    project(1, r)
    for index in range(count // 2):
        attend_block(0, index)
    walk(1, 1, half)
    for index in range(count // 2, count):
        attend_block(0, index)
    o_cross[0].start()
    big_cross = [
        cross(wgate.at[:, lanes((1 - c) * share, share)], wg_ref.at[1]),
        cross(wup.at[:, lanes((1 - c) * share, share)], wu_ref.at[1]),
        cross(wdown.at[rows_at((1 - c) * share, share), :], wd_ref.at[1]),
        cross(wo.at[rows_at((1 - c) * q_width, q_width), :], wo_from),
    ]
    walk(1, half, n - 1)
    o_cross[0].wait_recv()
    wo_load.wait()
    project_out(0)
    rs[0].step(1)
    g_loads[0].wait()
    g[0].start()
    walk(1, n - 1, n)
    n1_stores.append(local(n_own.at[1], n1_out.at[1]))
    for copy in big_cross:
        copy.start()
    for index in range(count // 2):
        attend_block(1, index)
    for s in range(2, half + 1):
        rs[0].step(s)
    for index in range(count // 2, count):
        attend_block(1, index)
    o_cross[1].start()
    for k in range(1, half):
        g[0].step(k)
    release(0, n1_stores[0])
    for s in range(half + 1, n):
        rs[0].step(s)
    o_cross[1].wait_recv()
    project_out(1)
    rs[1].step(1)
    for k in range(half, n - 1):
        g[0].step(k)
    middle(0)
    release(1, n1_stores[1])
    for s in range(2, half + 1):
        rs[1].step(s)
    g[0].step(n - 1)
    for copy in unit_loads:
        copy.wait()
    for copy in big_cross:
        copy.wait_recv()
    g_loads[1].wait()
    stores += [local(g_own.at[0], g_out.at[0])]
    stores += [local(qkv_ref, qkv_out), local(log_ref, log_out)]
    stores += [local(o_own, o_own_out), local(o_oth, o_oth_out)]
    mid_store = local(total.at[0], mid_out.at[0])
    units(0)
    for k in range(1, half):
        n2[0].step(k)
        units(k)
    for s in range(half + 1, n):
        rs[1].step(s)
    for k in range(half, n - 1):
        n2[0].step(k)
    g[1].start()
    for k in range(half, n - 1):
        units(k)
    middle(1)
    stores.append(local(total.at[1], mid_out.at[1]))
    stores.append(local(scales, scale_out))
    n2[0].step(n - 1)
    units(n - 1)
    units(n)
    down_project()
    down_rs.step(1)
    for k in range(1, n):
        g[1].step(k)
        n2[1].step(k)
        units(n + k)
        if k + 1 < n:
            down_rs.step(k + 1)
    stores += [local(g_own.at[1], g_out.at[1]), local(n_own, n2_out)]
    mid_store.wait()
    total[0] = total[0] + part[0, r].astype(F32)
    down_rs.add_received(total.at[0])
    part[0, r] = total[0].astype(BF16)
    stores.append(local(part.at[0, r], result_out))
    for at in range(2 * n):
        unit_wait(at)
        for kind in range(3):
            if at >= n or kind > 0:
                unit_away(at, kind).wait_recv()
    for copy in crosses + w_cross + o_cross + big_cross:
        copy.wait_send()
    for item in g + n2 + rs[1:] + [down_rs]:
        item.drain()
    for copy in stores:
        copy.wait()


def forward(
    prefix, x, gain_one, gain_two, tables, grad_in, wq, wk, wv, wo, wgate, wup, wdown, n, heads, shared_kv
):
    batches, tokens, depth = x.shape
    length = n * tokens
    width = (heads + 2) * HEAD_DIM
    q_width = heads * HEAD_DIM
    share = wgate.shape[1] // 2
    vmem = pl.BlockSpec(memory_space=pltpu.VMEM)
    anywhere = pl.BlockSpec(memory_space=pl.ANY)
    gathered, units = (batches, n, tokens, depth), (batches, n, tokens, share)
    rows = (2, batches, tokens, 128)
    shapes = [
        (gathered, BF16), (gathered, BF16), (gathered, BF16),
        ((batches, length, width), BF16), ((batches, 8, length), F32),
        ((batches, length, q_width), BF16), ((batches, length, q_width), BF16),
        ((batches, tokens, depth), F32), (rows, F32), ((q_width, depth), BF16),
    ] + [(units, BF16)] * 6 + [((tokens, depth), BF16)]
    boxes = (batches, n - 1, tokens, depth)
    dma = pltpu.SemaphoreType.DMA
    return pl.pallas_call(
        functools.partial(forward_kernel, n, heads, shared_kv),
        in_specs=[pl.BlockSpec(memory_space=pltpu.SMEM)] + [vmem] * 5 + [anywhere] * 8,
        out_specs=[anywhere] * len(shapes),
        out_shape=[jax.ShapeDtypeStruct(*item) for item in shapes],
        scratch_shapes=[
            pltpu.VMEM(gathered, BF16), pltpu.VMEM(gathered, BF16),
            pltpu.VMEM(gathered, BF16), pltpu.VMEM(gathered, BF16),
            pltpu.VMEM((depth, width), BF16), pltpu.VMEM((depth, width), BF16),
            pltpu.VMEM(wo.shape, BF16),
            pltpu.VMEM((2, depth, share), BF16), pltpu.VMEM((2, depth, share), BF16),
            pltpu.VMEM((2, share, depth), BF16), pltpu.VMEM((share, depth), BF16),
            pltpu.VMEM((2, 2, tokens, share), BF16),
            pltpu.VMEM((batches, length, width), BF16),
            pltpu.VMEM((batches, HEAD_DIM, length), BF16),
            pltpu.VMEM((batches, length, q_width), BF16), pltpu.VMEM((batches, length, q_width), BF16),
            pltpu.VMEM((batches, 8, length), F32),
            pltpu.VMEM(gathered, BF16), pltpu.VMEM(boxes, BF16), pltpu.VMEM(boxes, BF16),
            pltpu.VMEM((batches, tokens, depth), F32),
            pltpu.VMEM(rows, F32), pltpu.VMEM(rows, F32), pltpu.VMEM(rows, F32),
            pltpu.VMEM((2, 3, tokens, share), BF16),
            dma((3, batches, n, 3)), dma((3, batches, n, 2)),
            dma((batches, 2, n - 1)), dma((batches, 2, n - 1)), dma((13,)), dma((13,)), dma((24,)),
            dma((batches * n, 3)), dma((batches * n, 3)), dma((batches * n, 3)),
            dma((2, n - 1)), dma((2, n - 1)), dma((2, 2)),
        ],
        compiler_params=communicate(1, 63),
        cost_estimate=cost(2e11, 100 * MIB),
    )(prefix, x, gain_one, gain_two, *tables, grad_in, wq, wk, wv, wo, wgate, wup, wdown)


def unit_grads_kernel(
    n, bits,
    mid_ref, scales_ref, top_ref, gain_ref,
    g_in, n2_in, a_own, a_oth, dg_own, dg_oth, du_own, du_oth, wgate, wup,
    dz_out, dz_oth_out, mgrad_out, down_out, gate_out, up_out, gain_out,
    wg_ref, wu_ref, unit_ref, part, ups, downs, total, dz_ref, row_out, row_in,
    shared_ref, moving_ref, down_ref, gate_ref, up_ref, boxes,
    load_sems, unit_sems, moving_sems, scatter_sends, scatter_recvs, gather_sends, gather_recvs,
    cross_sends, cross_recvs, store_sems, reduce_sends, reduce_recvs, part_sems,
):
    batches, tokens, depth = mid_ref.shape
    share = a_own.shape[1]
    line = Line(n)
    r, c = line.r, line.c
    loads = [
        pltpu.make_async_copy(a, b, load_sems.at[i])
        for i, (a, b) in enumerate(((wgate, wg_ref), (wup, wu_ref), (g_in, shared_ref)))
    ]
    order = [(m, p) for m in range(batches) for p in range(n)]

    def unit_loads(at):
        return [
            pltpu.make_async_copy(
                src.at[pl.ds(at * tokens, tokens), :], unit_ref.at[at % 2, i], unit_sems.at[at % 2, i]
            )
            for i, src in enumerate((dg_own, dg_oth, du_own, du_oth))
        ]

    width = min(256, share)
    nb = share // width
    kinds = ((a_own, a_oth), (dg_own, dg_oth), (du_own, du_oth))

    def moving(kind, index, go):
        for side in range(2):

            @pl.when(index // nb == side)
            def _(side=side):
                cols = pl.ds(pl.multiple_of((index - side * nb) * width, width), width)
                copy = pltpu.make_async_copy(
                    kinds[kind][side].at[:, cols], moving_ref.at[index % 2], moving_sems.at[index % 2]
                )
                copy.start() if go else copy.wait()

    moving(0, 0, True)
    for copy in loads[::-1] + unit_loads(0):
        copy.start()
    line.barrier(bits=bits)
    scatters = [
        Scatter(line, part.at[m], ups.at[m], downs.at[m], scatter_sends.at[m], scatter_recvs.at[m])
        for m in range(batches)
    ]
    gathers = [
        Gather(
            line, dz_out.at[m], dz_oth_out.at[m], gather_sends.at[m], gather_recvs.at[m], dz_ref.at[m]
        )
        for m in range(batches - 1)
    ]
    reduces = []
    for kind, ref in enumerate((down_ref, gate_ref, up_ref)):
        pair = [
            Reduce(
                line, view, [box.at[way] for box in boxes[kind]], way_bits,
                reduce_sends.at[kind, way], reduce_recvs.at[kind, way],
            )
            for way, (view, way_bits) in enumerate(two_ways(ref, bits))
        ]
        reduces.append(pair)
    cols_own = pl.ds(pl.multiple_of(c * share, share), share)
    cols_oth = pl.ds(pl.multiple_of((1 - c) * share, share), share)

    def unit_part(at):
        m, p = order[at]
        for copy in unit_loads(at):
            copy.wait()
        if at + 1 < len(order):
            for copy in unit_loads(at + 1):
                copy.start()
        slot = at % 2
        block = min(256, depth)

        @pl.loop(0, depth // block)
        def _(b):
            rows = pl.ds(pl.multiple_of(b * block, block), block)
            value = dot(unit_ref[slot, 0], wg_ref[rows, cols_own], NT)
            value = value + dot(unit_ref[slot, 1], wg_ref[rows, cols_oth], NT)
            value = value + dot(unit_ref[slot, 2], wu_ref[rows, cols_own], NT)
            value = value + dot(unit_ref[slot, 3], wu_ref[rows, cols_oth], NT)
            part[m, p, :, rows] = value.astype(BF16)

    def weight_grad(kind, first=0, last=2 * nb):
        @pl.loop(first, last)
        def _(index):
            moving(kind, index, False)

            @pl.when(index + 1 < 2 * nb)
            def _():
                moving(kind, index + 1, True)

            side = index // nb
            place = (c + side * (1 - 2 * c)) * nb + index - side * nb
            cols = pl.ds(pl.multiple_of(place * width, width), width)
            if kind == 0:
                down_ref[cols, :] = dot(moving_ref[index % 2], shared_ref[...], TN).astype(BF16)
            else:
                ref = gate_ref if kind == 1 else up_ref
                ref[:, cols] = dot(shared_ref[...], moving_ref[index % 2], TN).astype(BF16)

        if last == 2 * nb and kind + 1 < len(kinds):
            moving(kind + 1, 0, True)

    def row_cross(m):
        return line.across(row_out.at[m], row_in.at[m], cross_sends.at[m], cross_recvs.at[m])

    def store(which, m, src, dst):
        return pltpu.make_async_copy(src, dst, store_sems.at[which, m])

    def middle(m):
        scatters[m].total(total.at[m])
        s = scales_ref[1, m][:, :1]
        gain_out[pl.ds(m, 1), :] = jnp.sum(total[m] * mid_ref[m] * s, axis=0, keepdims=True)
        total[m] = total[m] * gain_ref[...]
        inner = jnp.sum(total[m] * mid_ref[m], axis=1, keepdims=True)
        row_out[m] = jnp.broadcast_to(inner, (tokens, 128))
        row_cross(m).start()
        row_cross(m).wait_recv()
        inner = row_out[m, :, pl.ds(0, 1)] + row_in[m, :, pl.ds(0, 1)]
        result = (
            top_ref[m].astype(F32) + total[m] * s - mid_ref[m] * ((s * s * s) * inner * (1.0 / WIDTH))
        )
        total[m] = result
        dz_ref[m] = result.astype(BF16)
        if m < len(gathers):
            gathers[m].start()
        store(0, m, total.at[m], mgrad_out.at[m]).start()
        store(1, m, dz_ref.at[m], dz_out.at[m, r]).start()

    def steps(item, first, last):
        for s in range(first, last):
            item.step(s)

    def reduce_step(kind, at):
        for item in reduces[kind]:
            item.step(at)

    half = (n + 1) // 2
    loads[2].wait()
    weight_grad(0, 0, nb)
    for way, item in enumerate(reduces[0]):

        @pl.when(c == way)
        def _(item=item):
            item.step(0)

    weight_grad(0, nb, 2 * nb)
    for way, item in enumerate(reduces[0]):

        @pl.when(c != way)
        def _(item=item):
            item.step(0)

    n2_load = pltpu.make_async_copy(n2_in, shared_ref, load_sems.at[3])
    n2_load.start()
    for copy in loads[:2]:
        copy.wait()
    for at in range(n):
        unit_part(at)
    scatters[0].step(1)
    n2_load.wait()
    weight_grad(1)
    reduce_step(1, 0)
    steps(scatters[0], 2, half + 1)
    reduce_step(0, 1)
    for at in range(n, 2 * n):
        unit_part(at)
    steps(scatters[0], half + 1, n)
    scatters[1].step(1)
    weight_grad(2)
    reduce_step(2, 0)
    middle(0)
    steps(scatters[1], 2, half + 1)
    reduce_step(1, 1)
    steps(gathers[0], 1, half)
    steps(scatters[1], half + 1, n)
    steps(gathers[0], half, n - 1)
    reduce_step(2, 1)
    middle(1)
    steps(gathers[0], n - 1, n)
    for at in range(2, len(bits)):
        for kind in range(3):
            reduce_step(kind, at)
    outs = (down_out, gate_out, up_out)
    kept_stores = []
    for kind in range(3):
        reduce_step(kind, len(bits))
        for way, item in enumerate(reduces[kind]):
            out_view = two_ways(outs[kind], bits)[way][0]
            rows = item.kept()
            copy = pltpu.make_async_copy(
                item.ref.at[rows, :], out_view.at[rows, :], part_sems.at[kind, way]
            )
            copy.start()
            kept_stores.append(copy)
    for item in gathers:
        for q in range(n):
            item.arrive(q)
        item.drain()
    for m in range(batches):
        scatters[m].drain()
        row_cross(m).wait_send()
        store(0, m, total.at[m], mgrad_out.at[m]).wait()
        store(1, m, dz_ref.at[m], dz_out.at[m, r]).wait()
    for pair in reduces:
        for item in pair:
            item.drain()
    for copy in kept_stores:
        copy.wait()


def unit_grads(mid, scales, top, gain, g, n2, halves, wgate, wup, n, dp_count):
    batches, tokens, depth = mid.shape
    rows, share = halves[0].shape
    bits = list(range(dp_count.bit_length() - 1))
    vmem = pl.BlockSpec(memory_space=pltpu.VMEM)
    anywhere = pl.BlockSpec(memory_space=pl.ANY)
    gathered = (batches, n, tokens, depth)
    down_dims, gate_dims = (2 * share, depth), (depth, 2 * share)
    dims = (down_dims, gate_dims, gate_dims)
    shapes = [(gathered, BF16), ((batches - 1,) + gathered[1:], BF16), (mid.shape, F32)]
    shapes += [(item, BF16) for item in dims] + [((8, depth), F32)]
    boxes = (batches, n - 1, tokens, depth)
    width = min(256, share)
    dma = pltpu.SemaphoreType.DMA
    return pl.pallas_call(
        functools.partial(unit_grads_kernel, n, bits),
        in_specs=[vmem] * 4 + [anywhere] * 10,
        out_specs=[anywhere] * 6 + [vmem],
        out_shape=[jax.ShapeDtypeStruct(*item) for item in shapes],
        scratch_shapes=[
            pltpu.VMEM(wgate.shape, BF16), pltpu.VMEM(wup.shape, BF16),
            pltpu.VMEM((2, 4, tokens, share), BF16), pltpu.VMEM(gathered, BF16),
            pltpu.VMEM(boxes, BF16), pltpu.VMEM(boxes, BF16), pltpu.VMEM(mid.shape, F32),
            pltpu.VMEM(mid.shape, BF16),
            pltpu.VMEM((batches, tokens, 128), F32), pltpu.VMEM((batches, tokens, 128), F32),
            pltpu.VMEM((rows, depth), BF16), pltpu.VMEM((2, rows, width), BF16),
            pltpu.VMEM(down_dims, BF16), pltpu.VMEM(gate_dims, BF16), pltpu.VMEM(gate_dims, BF16),
            [
                [pltpu.VMEM((2, item[0] // 2 ** (level + 2), item[1]), BF16) for level in range(len(bits))]
                for item in dims
            ],
            dma((4,)), dma((2, 4)), dma((2,)), dma((batches, 2, n - 1)), dma((batches, 2, n - 1)),
            dma((batches, n, 3)), dma((batches, n, 2)), dma((batches,)), dma((batches,)),
            dma((2, batches)), dma((3, 2, len(bits))), dma((3, 2, len(bits))), dma((3, 2)),
        ],
        compiler_params=communicate(2, 62),
        cost_estimate=cost(2e11, 100 * MIB),
    )(mid, scales, top, gain, g, n2, *halves, wgate, wup)


def backward_kernel(
    n, heads, shared_kv, bits,
    prefix_ref, x_ref, scales_ref, gain_in, cos_ref, sin_ref, log_ref, ffn_gains,
    mid_in, dz_own_in, dz_oth_in, wo, wo_from, wq, wk, wv, qkv_in, a_own_in, a_oth_in, wdown, n1_in,
    o_own_in, o_oth_in, down_in, gate_in, up_in,
    grad_out, result_out, qkv_out, o_out, down_out, gate_out, up_out, gain_out,
    dz_ref, dz_oth, dz_last, wo_ref, w_own, w_oth, qkv_ref, dk_ref, dv_ref, kt_ref, dqkv_own, dqkv_oth,
    part, ups, downs, total, a_ref, wide_ref, o_ref, qkv_grad, o_grad, qkv_sum, o_sum, boxes,
    row_out, row_in, result_ref, gain_ref, row_boxes, dp_boxes,
    load_sems, dz_sems, a_sems, scatter_sends, scatter_recvs, cross_sends, cross_recvs, store_sems,
    reduce_sends, reduce_recvs, spread_sends, spread_recvs, unit_sends, unit_recvs,
    gather_sends, gather_recvs, gain_sends, gain_recvs,
):
    batches, tokens, depth = x_ref.shape
    length = n * tokens
    share = a_own_in.shape[1]
    line = Line(n)
    r, c = line.r, line.c
    q_width = heads * HEAD_DIM
    k_col, v_col = q_width, q_width + HEAD_DIM
    width = v_col + HEAD_DIM

    def lanes(at, size):
        return pl.ds(pl.multiple_of(at, 128), size)

    def rows_at(at, size):
        return pl.ds(pl.multiple_of(at, size), size)

    def qkv_columns(side, dst):
        kv = 0 if shared_kv else side * HEAD_DIM
        return [
            (wq.at[:, lanes(side * q_width, q_width)], dst.at[:, pl.ds(0, q_width)]),
            (wk.at[:, lanes(kv, HEAD_DIM)], dst.at[:, pl.ds(k_col, HEAD_DIM)]),
            (wv.at[:, lanes(kv, HEAD_DIM)], dst.at[:, pl.ds(v_col, HEAD_DIM)]),
        ]

    pairs = [(wdown, wide_ref.at[pl.ds(0, 2 * share), :]), (qkv_in, qkv_ref)]
    pairs += [(wo.at[rows_at(c * q_width, q_width), :], wo_ref.at[0]), (wo_from, wo_ref.at[1])]
    last = batches - 1
    pairs += [(dz_own_in.at[m], dz_ref.at[m]) for m in range(last)]
    first = len(pairs)
    pairs += qkv_columns(c, w_own) + qkv_columns(1 - c, w_oth)
    pairs += [(o_own_in, o_ref.at[0]), (o_oth_in, o_ref.at[1])]
    pairs += [(mid_in.at[last], total.at[last])]
    loads = [pltpu.make_async_copy(a, b, load_sems.at[i]) for i, (a, b) in enumerate(pairs)]
    n1_load = pltpu.make_async_copy(n1_in, wide_ref.at[pl.ds(0, batches * length), :], load_sems.at[len(pairs)])
    shard_load = pltpu.make_async_copy(
        dz_own_in.at[last, r], dz_ref.at[last, r], load_sems.at[len(pairs) + 1]
    )
    order = [(m, p) for m in range(batches) for p in range(n)]

    def a_loads(at):
        rows = pl.ds(at * tokens, tokens)
        return [
            pltpu.make_async_copy(src.at[rows, :], a_ref.at[at % 2, side], a_sems.at[at % 2, side])
            for side, src in enumerate((a_own_in, a_oth_in))
        ]

    def dz_load(at):
        m, p = order[at]
        return pltpu.make_async_copy(dz_oth_in.at[m, p], dz_oth.at[at % 2], dz_sems.at[at % 2])

    for copy in [shard_load] + loads[:1] + a_loads(last * n) + loads[1:first] + [dz_load(0)] + loads[first:]:
        copy.start()
    dp_count = 2 ** len(bits)
    line.wide_barrier(dp_count)
    gains = [
        Everywhere(line, "row", r, n, gain_ref.at[0], row_boxes, gain_sends.at[0], gain_recvs.at[0]),
        Everywhere(line, "dp", line.d, dp_count, gain_ref.at[1], dp_boxes, gain_sends.at[1], gain_recvs.at[1]),
    ]
    gather = Gather(line, dz_ref.at[last], dz_last, gather_sends, gather_recvs)
    spreads = [
        Spread(
            line, view, way_bits, unit_sends.at[kind, way], unit_recvs.at[kind, way], skip=int(kind == 2)
        )
        for kind, ref in enumerate((down_out, gate_out, up_out))
        for way, (view, way_bits) in enumerate(two_ways(ref, bits))
    ]
    *head_rs, out_rs = (
        Scatter(
            line, part.at[at], ups.at[at], downs.at[at], scatter_sends.at[at], scatter_recvs.at[at]
        )
        for at in range(batches + 1)
    )
    reduces, gatherers = [], []
    for kind, (ref, result) in enumerate(((qkv_grad, qkv_sum), (o_grad, o_sum))):
        results = two_ways(result, bits)
        for way, (view, way_bits) in enumerate(two_ways(ref, bits)):
            reduces.append(
                Reduce(
                    line, view, [box.at[way] for box in boxes[kind]], way_bits,
                    reduce_sends.at[kind, way], reduce_recvs.at[kind, way],
                )
            )
            gatherers.append(
                Spread(
                    line, results[way][0], way_bits, spread_sends.at[kind, way], spread_recvs.at[kind, way]
                )
            )
    count = len(bits)

    def total_step(items, at):
        for item in items:
            if at <= count:
                reduces[item].step(at, gatherers[item].ref if at == count else None)
            if at >= count:
                gatherers[item].step(at - count)

    def spread_step(which, at):
        for kind in which:
            for item in spreads[2 * kind : 2 * kind + 2]:
                item.step(at)

    own_rows, oth_rows = rows_at(c * share, share), rows_at((1 - c) * share, share)

    def down_part(at):
        m, p = order[at]
        for copy in a_loads(at):
            copy.wait()
        if at + 1 < len(order):
            for copy in a_loads(at + 1):
                copy.start()
        value = dot(a_ref[at % 2, 0], wide_ref[own_rows, :], NN)
        part[batches, p] = (value + dot(a_ref[at % 2, 1], wide_ref[oth_rows, :], NN)).astype(BF16)

    def grad_cross(m):
        return line.across(dqkv_own.at[m], dqkv_oth.at[m], cross_sends.at[m], cross_recvs.at[m])

    def row_cross(m):
        at = batches + m
        return line.across(row_out.at[m], row_in.at[m], cross_sends.at[at], cross_recvs.at[at])

    def store(which, m, src, dst):
        return pltpu.make_async_copy(src, dst, store_sems.at[which, m])

    def attend_start(m):
        dk_ref[...] = jnp.zeros_like(dk_ref)
        dv_ref[...] = jnp.zeros_like(dv_ref)
        kt_ref[...] = qkv_ref[m, :, pl.ds(k_col, HEAD_DIM)].T

    def attend_back(m, q):
        at = m * n + q
        if m < last:
            dz_load(at).wait()
            if at + 1 < last * n:
                dz_load(at + 1).start()
        else:
            gather.arrive(q)
        other = dz_oth[at % 2] if m < last else dz_last[q]
        rows = pl.ds(q * tokens, tokens)
        grads = dot(dz_ref[m, q], wo_ref[0], NT)
        grads = (grads + dot(other, wo_ref[1], NT)).astype(BF16)
        cosine, signed = cos_ref[rows, :], sin_ref[rows, :]
        extent = min(length, max((q + 1) * tokens, PREFIX_TOP))
        upto = pl.ds(0, extent)
        keys = qkv_ref[m, upto, pl.ds(k_col, HEAD_DIM)]
        values = qkv_ref[m, upto, pl.ds(v_col, HEAD_DIM)]
        key_at = lax.broadcasted_iota(jnp.int32, (extent, tokens), 0)
        query_at = lax.broadcasted_iota(jnp.int32, (extent, tokens), 1) + q * tokens
        allowed = (key_at <= query_at) | (key_at < prefix_ref[m, 0])
        for head in range(heads):
            cols = pl.ds(head * HEAD_DIM, HEAD_DIM)
            query = qkv_ref[m, rows, cols]
            grad = grads[:, head * HEAD_DIM : (head + 1) * HEAD_DIM]
            raw = dot(keys, query, NT) * scale - log_ref[m, pl.ds(head, 1), rows]
            probs = jnp.exp(jnp.where(allowed, raw, -1e30))
            dv_ref[upto, :] += dot(probs.astype(BF16), grad, NN)
            prob_grad = dot(values, grad, NT)
            inner = jnp.sum(probs * prob_grad, axis=0, keepdims=True)
            rounded = (probs * (prob_grad - inner) * scale).astype(BF16)
            dk_ref[upto, :] += dot(rounded, query, NN)
            dq = dot(kt_ref[:, upto], rounded, NN).T
            dqkv_own[m, rows, cols] = rope_back(dq, cosine, signed).astype(BF16)

    def attend_end(m):
        dk = rope_back(dk_ref[...], cos_ref[...], sin_ref[...])
        dqkv_own[m, :, pl.ds(k_col, HEAD_DIM)] = dk.astype(BF16)
        dqkv_own[m, :, pl.ds(v_col, HEAD_DIM)] = dv_ref[...].astype(BF16)
        grad_cross(m).start()

    def head_part(m):
        grad_cross(m).wait_recv()

        @pl.loop(0, n)
        def _(p):
            rows = rows_at(p * tokens, tokens)
            value = dot(dqkv_own[m, rows, :], w_own[...], NT)
            part[m, p] = (value + dot(dqkv_oth[m, rows, :], w_oth[...], NT)).astype(BF16)

    def result():
        total[last] = total[last] + part[batches, r].astype(F32)
        out_rs.add_received(total.at[last])
        result_ref[...] = total[last].astype(BF16)
        store(0, 0, result_ref, result_out).start()

    def input_grad(m):
        head_rs[m].total(total.at[m])
        s = scales_ref[0, m][:, :1]
        x = x_ref[m].astype(F32)
        gain_ref[0, pl.ds(m, 1), :] = jnp.sum(total[m] * x * s, axis=0, keepdims=True)
        total[m] = total[m] * gain_in[...]
        inner = jnp.sum(total[m] * x, axis=1, keepdims=True)
        row_out[m] = jnp.broadcast_to(inner, (tokens, 128))
        row_cross(m).start()
        row_cross(m).wait_recv()
        inner = row_out[m, :, pl.ds(0, 1)] + row_in[m, :, pl.ds(0, 1)]
        total[m] = total[m] * s - x * ((s * s * s) * inner * (1.0 / WIDTH))
        store(1, m, total.at[m], grad_out.at[m]).start()

    def steps(item, first_step, last_step):
        for s in range(first_step, last_step):
            item.step(s)

    half = (n + 1) // 2
    spread_step((0, 1, 2), 0)
    shard_load.wait()
    gather.start()
    for copy in loads[1:first]:
        copy.wait()
    loads[0].wait()
    for at in range(last * n, len(order)):
        down_part(at)
    out_rs.step(1)
    n1_load.start()
    attend_start(0)
    for q in range(n // 2):
        attend_back(0, q)
    steps(gather, 1, half)
    for q in range(n // 2, n):
        attend_back(0, q)
    attend_end(0)
    steps(gather, half, n - 1)
    for copy in loads[first:]:
        copy.wait()
    head_part(0)
    head_rs[0].step(1)
    for at in range(1, count):
        spread_step((0,), at)
    steps(gather, n - 1, n)
    steps(out_rs, 2, half + 1)
    for side in range(2):
        place = c if side == 0 else 1 - c
        value = dot(o_ref[side], dz_ref[...].reshape(batches * length, depth), TN)
        o_grad[rows_at(place * q_width, q_width), :] = value.astype(BF16)
    total_step((2, 3), 0)
    attend_start(1)
    for q in range(n // 2):
        attend_back(1, q)
    steps(head_rs[0], 2, half + 1)
    for at in range(1, count):
        spread_step((1,), at)
    for q in range(n // 2, n):
        attend_back(1, q)
    attend_end(1)
    steps(out_rs, half + 1, n)
    total_step((2, 3), 1)
    head_part(1)
    head_rs[1].step(1)
    n1_load.wait()
    for side in range(2):
        place = c if side == 0 else 1 - c
        dqkv = (dqkv_own if side == 0 else dqkv_oth)[...].reshape(batches * length, width)
        value = dot(wide_ref[pl.ds(0, batches * length), :], dqkv, TN)
        qkv_grad[:, lanes(place * width, width)] = value.astype(BF16)
    total_step((0, 1), 0)
    steps(head_rs[0], half + 1, n)
    result()
    total_step((2, 3), 2)
    input_grad(0)
    total_step((0, 1), 1)
    turn, last_turn = 2, 2 * count
    for s in range(2, n):
        head_rs[1].step(s)
        if turn <= last_turn:
            total_step((0, 1), turn)
        if turn + 1 <= last_turn:
            total_step((2, 3), turn + 1)
        turn += 1
    input_grad(1)
    gain_ref[0, pl.ds(batches, batches), :] = ffn_gains[pl.ds(0, batches), :]
    gains[0].start()
    while turn <= last_turn:
        total_step((0, 1), turn)
        if turn + 1 <= last_turn:
            total_step((2, 3), turn + 1)
        turn += 1
    stores = [
        pltpu.make_async_copy(qkv_sum, qkv_out, load_sems.at[0]),
        pltpu.make_async_copy(o_sum, o_out, load_sems.at[1]),
    ]
    for copy in stores:
        copy.start()
    gain_ref[1] = gains[0].total()
    gains[1].start()
    for at in range(1, count):
        spread_step((2,), at)
    spread_step((0, 1, 2), count)
    for m in range(batches):
        grad_cross(m).wait_send()
        row_cross(m).wait_send()
        head_rs[m].drain()
        store(1, m, total.at[m], grad_out.at[m]).wait()
    out_rs.drain()
    store(0, 0, result_ref, result_out).wait()
    gather.drain()
    gain_out[...] = gains[1].total()
    for item in gains:
        item.drain()
    for item in spreads + reduces + gatherers:
        item.drain()
    for copy in stores:
        copy.wait()


def backward(
    prefix, x, scales, gain, tables, logs, ffn_gains, mid, dz_own, dz_oth, wo, wo_from, wq, wk, wv, qkv,
    a_own, a_oth, wdown, n1, o_own, o_oth, down, gate, up, heads, shared_kv, dp_count,
):
    batches, tokens, depth = x.shape
    n = dz_own.shape[1]
    length, width = qkv.shape[1:]
    rows, q_width = o_own.shape
    share = a_own.shape[1]
    bits = list(range(dp_count.bit_length() - 1))
    vmem = pl.BlockSpec(memory_space=pltpu.VMEM)
    anywhere = pl.BlockSpec(memory_space=pl.ANY)
    gathered = (batches, n, tokens, depth)
    boxes = (batches + 1, n - 1, tokens, depth)
    sums = [(depth, 2 * width), (2 * q_width, depth)]
    shapes = [(mid.shape, F32), ((tokens, depth), BF16)] + [(item, BF16) for item in sums]
    shapes += [(item.shape, BF16) for item in (down, gate, up)] + [((8, depth), F32)]
    dma = pltpu.SemaphoreType.DMA
    return pl.pallas_call(
        functools.partial(backward_kernel, n, heads, shared_kv, bits),
        in_specs=[pl.BlockSpec(memory_space=pltpu.SMEM)] + [vmem] * 7 + [anywhere] * 18,
        out_specs=[anywhere] * 7 + [vmem],
        out_shape=[jax.ShapeDtypeStruct(*item) for item in shapes],
        input_output_aliases={23: 4, 24: 5, 25: 6},
        scratch_shapes=[
            pltpu.VMEM(gathered, BF16), pltpu.VMEM((2, tokens, depth), BF16), pltpu.VMEM(gathered[1:], BF16),
            pltpu.VMEM((2, q_width, depth), BF16),
            pltpu.VMEM((depth, width), BF16), pltpu.VMEM((depth, width), BF16),
            pltpu.VMEM(qkv.shape, BF16),
            pltpu.VMEM((length, HEAD_DIM), F32), pltpu.VMEM((length, HEAD_DIM), F32),
            pltpu.VMEM((HEAD_DIM, length), BF16), pltpu.VMEM(qkv.shape, BF16), pltpu.VMEM(qkv.shape, BF16),
            pltpu.VMEM((batches + 1,) + gathered[1:], BF16), pltpu.VMEM(boxes, BF16), pltpu.VMEM(boxes, BF16),
            pltpu.VMEM(mid.shape, F32),
            pltpu.VMEM((2, 2, tokens, share), BF16),
            pltpu.VMEM((max(2 * share, rows), depth), BF16), pltpu.VMEM((2, rows, q_width), BF16),
            pltpu.VMEM(sums[0], BF16), pltpu.VMEM(sums[1], BF16),
            pltpu.VMEM(sums[0], BF16), pltpu.VMEM(sums[1], BF16),
            [
                [pltpu.VMEM((2, item[0] // 2 ** (level + 2), item[1]), BF16) for level in range(len(bits))]
                for item in sums
            ],
            pltpu.VMEM((batches, tokens, 128), F32), pltpu.VMEM((batches, tokens, 128), F32),
            pltpu.VMEM((tokens, depth), BF16), pltpu.VMEM((2, 8, depth), F32),
            pltpu.VMEM((n - 1, 8, depth), F32), pltpu.VMEM((dp_count - 1, 8, depth), F32),
            dma((20,)), dma((2,)), dma((2, 2)),
            dma((batches + 1, 2, n - 1)), dma((batches + 1, 2, n - 1)),
            dma((2 * batches,)), dma((2 * batches,)), dma((2, batches)),
            dma((2, 2, len(bits))), dma((2, 2, len(bits))), dma((2, 2, len(bits))), dma((2, 2, len(bits))),
            dma((3, 2, len(bits))), dma((3, 2, len(bits))), dma((n, 3)), dma((n, 2)),
            dma((2, max(n, dp_count) - 1)), dma((2, max(n, dp_count) - 1)),
        ],
        compiler_params=communicate(3, 62),
        cost_estimate=cost(2e11, 100 * MIB),
    )(
        prefix, x, scales, gain, *tables, logs, ffn_gains, mid, dz_own, dz_oth, wo, wo_from, wq, wk, wv, qkv,
        a_own, a_oth, wdown, n1, o_own, o_oth, down, gate, up,
    )


def last_spread(values, meanwhile):
    count = lax.axis_size("dp")
    half = values.shape[0] // 2
    size, sides, halves = half // 2, [], []
    for way, bit in enumerate((0, count.bit_length() - 2)):
        sides.append((lax.axis_index("dp") >> bit) & 1)
        own = lax.dynamic_slice_in_dim(values, way * half + sides[-1] * size, size, 0)
        halves.append((own, lax.ppermute(own, "dp", [(i, i ^ (1 << bit)) for i in range(count)])))
    halves, meanwhile = lax.optimization_barrier((halves, meanwhile))
    pieces = []
    for side, (own, got) in zip(sides, halves):
        pieces += [jnp.where(side == 0, own, got), jnp.where(side == 0, got, own)]
    return jnp.concatenate([piece.astype(F32) for piece in pieces]), meanwhile


def body(
    hidden_in,
    attn_gain,
    ffn_gain,
    query_weight,
    key_weight,
    value_weight,
    output_weight,
    gate_weight,
    up_weight,
    down_weight,
    prefix_len,
    out_grad,
):
    col_count, row_count = lax.axis_size("col"), lax.axis_size("row")
    batches, tokens, _ = hidden_in.shape
    length = tokens * row_count
    heads = query_weight.shape[1] // HEAD_DIM // col_count
    row_kv = key_weight.shape[1] // HEAD_DIM
    shared_kv = row_kv < col_count
    q_width = heads * HEAD_DIM
    tables = rope_tables(length)
    (
        n1, n2, g_own, qkv, logs, o_own, o_oth, middle, scales, out_from,
        a_own, a_oth, dg_own, dg_oth, du_own, du_oth, first_result,
    ) = forward(
        prefix_len, hidden_in, attn_gain.reshape(1, -1), ffn_gain.reshape(1, -1), tables, out_grad,
        query_weight, key_weight, value_weight, output_weight, gate_weight, up_weight, down_weight,
        row_count, heads, shared_kv,
    )

    def flat(*items):
        return tuple(item.reshape(batches * length, item.shape[-1]) for item in items)

    dp_count = lax.axis_size("dp")
    a_own, a_oth, *grads = flat(a_own, a_oth, dg_own, dg_oth, du_own, du_oth)
    dz, dz_oth, middle_grad, down_sum, gate_sum, up_sum, ffn_gains = unit_grads(
        middle, scales, out_grad, ffn_gain.reshape(1, -1), *flat(g_own, n2), (a_own, a_oth, *grads),
        gate_weight, up_weight, row_count, dp_count,
    )
    in_grad, last_result, qkv_sum, output_sum, down_sum, gate_sum, up_sum, gains = backward(
        prefix_len, hidden_in, scales, attn_gain.reshape(1, -1), tables, logs, ffn_gains,
        middle, dz, dz_oth, output_weight, out_from, query_weight, key_weight, value_weight, qkv, a_own, a_oth, down_weight,
        *flat(n1, o_own, o_oth), down_sum, gate_sum, up_sum, heads, shared_kv, dp_count,
    )
    result = jnp.stack([first_result, last_result])
    width = q_width + 2 * HEAD_DIM

    def columns(first, size, shared):
        pieces = [
            qkv_sum[:, side * width + first : side * width + first + size].astype(F32)
            for side in range(col_count)
        ]
        return sum(pieces) if shared else jnp.concatenate(pieces, axis=1)

    gain_one, gain_two = gains[:batches].sum(axis=0), gains[batches : 2 * batches].sum(axis=0)
    meanwhile = (
        result,
        middle_grad + in_grad,
        gain_one,
        gain_two,
        columns(0, q_width, False),
        columns(q_width, HEAD_DIM, shared_kv),
        columns(q_width + HEAD_DIM, HEAD_DIM, shared_kv),
        output_sum.astype(F32),
        gate_sum.astype(F32),
        down_sum.astype(F32),
    )
    up_sum, (*first, down_sum) = last_spread(up_sum, meanwhile)
    return (*first, up_sum, down_sum)


def solution(mesh):
    return jax.shard_map(
        body,
        mesh=mesh,
        in_specs=(
            P(None, ("dp", "row"), "col"),
            P("col"),
            P("col"),
            P("col", "row"),
            P("col", "row"),
            P("col", "row"),
            P("row", "col"),
            P("col", "row"),
            P("col", "row"),
            P("row", "col"),
            P(None, "dp"),
            P(None, ("dp", "row"), "col"),
        ),
        out_specs=(
            P(None, ("dp", "row"), "col"),
            P(None, ("dp", "row"), "col"),
            P("col"),
            P("col"),
            P("col", "row"),
            P("col", "row"),
            P("col", "row"),
            P("row", "col"),
            P("col", "row"),
            P("col", "row"),
            P("row", "col"),
        ),
        check_vma=False,
    )
```

```python
import functools
import math

import jax
import jax.numpy as jnp
from jax import lax
from jax.experimental import pallas as pl
from jax.experimental.pallas import tpu as pltpu
from jax.sharding import PartitionSpec as P

WIDTH = 2048
HEADS = 16
KV_HEADS = 8
HEAD_DIM = 128
PREFIX_TOP = 512

epsilon = 1e-05
rope_base = 1000000.0
scale = 1.0 / math.sqrt(HEAD_DIM)
MIB = 1 << 20
F32 = jnp.float32
BF16 = jnp.bfloat16

NT = (((1,), (1,)), ((), ()))
NN = (((1,), (0,)), ((), ()))
TN = (((0,), (0,)), ((), ()))


def dot(left_side, right_side, dims):
    return lax.dot_general(left_side, right_side, dims, preferred_element_type=F32)


def params(mib, grid_rank):
    return pltpu.CompilerParams(
        dimension_semantics=("arbitrary",) * grid_rank, vmem_limit_bytes=mib * MIB
    )


def cost(flops, nbytes, exps=0):
    return pl.CostEstimate(flops=int(flops), bytes_accessed=int(nbytes), transcendentals=int(exps))


def whole(shape):
    return pl.BlockSpec(shape, lambda *_: (0,) * len(shape))


def rope_tables(first, rows):
    half_size = HEAD_DIM // 2
    lane = lax.broadcasted_iota(jnp.int32, (rows, HEAD_DIM), 1)
    inverse = jnp.exp((lane & (half_size - 1)).astype(F32) * (-math.log(rope_base) / half_size))
    angle = (lax.broadcasted_iota(jnp.int32, (rows, HEAD_DIM), 0) + first).astype(F32) * inverse
    sine = jnp.sin(angle)
    return jnp.cos(angle), jnp.where(lane < half_size, -sine, sine)


def rope(values, cosine, signed):
    return values * cosine + pltpu.roll(values, HEAD_DIM // 2, 1) * signed


def rope_back(values, cosine, signed):
    return values * cosine - pltpu.roll(values, HEAD_DIM // 2, 1) * signed


class Line:
    def __init__(self, n):
        self.n = n
        self.r = lax.axis_index("row")
        self.c = lax.axis_index("col")
        self.d = lax.axis_index("dp")

    def copy(self, src, dst, send, recv, **where):
        return pltpu.make_async_remote_copy(
            src_ref=src, dst_ref=dst, send_sem=send, recv_sem=recv, device_id=where,
            device_id_type=pl.DeviceIdType.MESH,
        )

    def up(self, src, dst, send, recv):
        return self.copy(src, dst, send, recv, row=self.r + 1)

    def down(self, src, dst, send, recv):
        return self.copy(src, dst, send, recv, row=self.r - 1)

    def across(self, src, dst, send, recv):
        return self.copy(src, dst, send, recv, col=1 - self.c)

    def barrier(self, core=True, bits=()):
        barrier = pltpu.get_barrier_semaphore()

        def signal(**where):
            pl.semaphore_signal(
                barrier, inc=1, device_id=where, device_id_type=pl.DeviceIdType.MESH
            )

        @pl.when(self.r > 0)
        def _():
            signal(row=self.r - 1)

        @pl.when(self.r < self.n - 1)
        def _():
            signal(row=self.r + 1)

        if core:
            signal(col=1 - self.c)
        for bit in bits:
            signal(dp=self.partner(bit))
        at_end = (self.r == 0) | (self.r == self.n - 1)
        others = int(core) + len(bits)

        @pl.when(at_end)
        def _():
            pl.semaphore_wait(barrier, 1 + others)

        @pl.when(jnp.logical_not(at_end))
        def _():
            pl.semaphore_wait(barrier, 2 + others)

    def wide_barrier(self, dp_count):
        barrier = pltpu.get_barrier_semaphore()
        peers = [dict(row=(self.r + at) % self.n) for at in range(1, self.n)]
        peers += [dict(dp=(self.d + at) % dp_count) for at in range(1, dp_count)]
        peers += [dict(col=1 - self.c)]
        for where in peers:
            pl.semaphore_signal(
                barrier, inc=1, device_id=where, device_id_type=pl.DeviceIdType.MESH
            )
        pl.semaphore_wait(barrier, len(peers))

    def side(self, bit):
        return (self.d // 2**bit) % 2

    def partner(self, bit):
        return self.d + (1 - 2 * self.side(bit)) * 2**bit

    def nearest(self, k):
        n = self.n
        code = 0
        for r in range(n):
            order = sorted(range(n), key=lambda q: (abs(q - r), q))
            code += order[k] * n**r
        place, result = self.r * 0 + code, 0
        for r in range(n):
            result = result + (place // n**r) % n * (1 - jnp.minimum(jnp.abs(self.r - r), 1))
        return result


class Gather:
    def __init__(self, line, own, oth, sends, recvs, first=None):
        self.line, self.own, self.oth, self.sends, self.recvs = line, own, oth, sends, recvs
        self.first = own.at[line.r] if first is None else first

    def hop(self, kind, q, src=None):
        way = (self.line.up, self.line.down)[kind]
        src = self.own.at[q] if src is None else src
        return way(src, self.own.at[q], self.sends.at[q, kind], self.recvs.at[q, 0])

    def cross(self, q, src=None):
        src = self.own.at[q] if src is None else src
        return self.line.across(src, self.oth.at[q], self.sends.at[q, 2], self.recvs.at[q, 1])

    def start(self):
        line = self.line

        @pl.when(line.r < line.n - 1)
        def _():
            self.hop(0, line.r, self.first).start()

        @pl.when(line.r > 0)
        def _():
            self.hop(1, line.r, self.first).start()

        self.cross(line.r, self.first).start()

    def step(self, s):
        line = self.line
        low, high = line.r - s, line.r + s

        @pl.when(low >= 0)
        def _():
            self.hop(0, low).wait_recv()

            @pl.when(line.r < line.n - 1)
            def _():
                self.hop(0, low).start()

            self.cross(low).start()

        @pl.when(high <= line.n - 1)
        def _():
            self.hop(1, high).wait_recv()

            @pl.when(line.r > 0)
            def _():
                self.hop(1, high).start()

            self.cross(high).start()

    def arrive(self, q):
        self.cross(q).wait_recv()

    def drain(self):
        line = self.line
        for q in range(line.n):

            @pl.when((line.r >= q) & (line.r < line.n - 1))
            def _(q=q):
                self.hop(0, q).wait_send()

            @pl.when((line.r <= q) & (line.r > 0))
            def _(q=q):
                self.hop(1, q).wait_send()

            self.cross(q).wait_send()


class Scatter:
    def __init__(self, line, part, ups, downs, sends, recvs):
        self.line, self.part, self.ups, self.downs = line, part, ups, downs
        self.sends, self.recvs = sends, recvs

    def hop(self, kind, s, target):
        way = (self.line.up, self.line.down)[kind]
        box = (self.ups, self.downs)[kind]
        return way(
            self.part.at[target], box.at[s - 1], self.sends.at[kind, s - 1], self.recvs.at[kind, s - 1]
        )

    def step(self, s):
        line = self.line
        for kind in range(2):
            behind = line.r if kind == 0 else line.n - 1 - line.r
            target = line.r + line.n - s if kind == 0 else line.r - (line.n - s)
            box = (self.ups, self.downs)[kind]

            @pl.when(behind <= s - 1)
            def _(kind=kind, behind=behind, target=target, box=box):
                if s > 1:

                    @pl.when(behind >= 1)
                    def _():
                        self.hop(kind, s - 1, target).wait_recv()
                        self.part[target] = (
                            self.part[target].astype(F32) + box[s - 2].astype(F32)
                        ).astype(BF16)

                self.hop(kind, s, target).start()

    def total(self, out):
        out[...] = self.part[self.line.r].astype(F32)
        self.add_received(out)

    def add_received(self, out):
        line = self.line
        last = line.n - 1

        @pl.when(line.r >= 1)
        def _():
            self.hop(0, last, line.r).wait_recv()
            out[...] += self.ups[last - 1].astype(F32)

        @pl.when(line.r <= last - 1)
        def _():
            self.hop(1, last, line.r).wait_recv()
            out[...] += self.downs[last - 1].astype(F32)

    def drain(self):
        line = self.line
        for s in range(1, line.n):

            @pl.when(line.r <= s - 1)
            def _(s=s):
                self.hop(0, s, line.r + line.n - s).wait_send()

            @pl.when(line.n - 1 - line.r <= s - 1)
            def _(s=s):
                self.hop(1, s, line.r - (line.n - s)).wait_send()


class Everywhere:
    def __init__(self, line, axis, place, count, ref, boxes, sends, recvs):
        self.line, self.axis, self.place, self.count = line, axis, place, count
        self.ref, self.boxes, self.sends, self.recvs = ref, boxes, sends, recvs

    def copy(self, at):
        return self.line.copy(
            self.ref, self.boxes.at[at - 1], self.sends.at[at - 1], self.recvs.at[at - 1],
            **{self.axis: (self.place + at) % self.count},
        )

    def start(self):
        for at in range(1, self.count):
            self.copy(at).start()

    def total(self):
        value = self.ref[...]
        for at in range(1, self.count):
            self.copy(at).wait_recv()
            value = value + self.boxes[at - 1]
        return value

    def drain(self):
        for at in range(1, self.count):
            self.copy(at).wait_send()


def levels_of(line, rows, bits):
    low, size, levels = 0, rows, []
    for bit in bits:
        size //= 2
        keep = low + line.side(bit) * size
        levels.append((size, keep, low + (1 - line.side(bit)) * size))
        low = keep
    return levels


def rows_of(at, size):
    return pl.ds(pl.multiple_of(at, 16), size)


class Reduce:
    def __init__(self, line, ref, boxes, bits, sends, recvs):
        self.line, self.ref, self.boxes, self.bits = line, ref, boxes, bits
        self.sends, self.recvs = sends, recvs
        self.levels = levels_of(line, ref.shape[0], bits)

    def copy(self, at):
        size, _, give = self.levels[at]
        return self.line.copy(
            self.ref.at[rows_of(give, size), :], self.boxes[at], self.sends.at[at], self.recvs.at[at],
            dp=self.line.partner(self.bits[at]),
        )

    def step(self, at, out=None):
        if at > 0:
            self.copy(at - 1).wait_recv()
            size, keep, _ = self.levels[at - 1]
            rows = rows_of(keep, size)
            kept = self.ref[rows, :].astype(F32) + self.boxes[at - 1][...].astype(F32)
            (self.ref if out is None else out)[rows, :] = kept.astype(BF16)
        if at < len(self.bits):
            self.copy(at).start()

    def kept(self):
        size, keep, _ = self.levels[-1]
        return rows_of(keep, size)

    def drain(self):
        for at in range(len(self.bits)):
            self.copy(at).wait_send()


class Spread:
    def __init__(self, line, ref, bits, sends, recvs, skip=0):
        self.line, self.ref, self.bits, self.sends, self.recvs = line, ref, bits, sends, recvs
        self.count = len(bits) - skip
        self.levels = levels_of(line, ref.shape[0], bits)

    def copy(self, at):
        level = len(self.bits) - 1 - at
        size, keep, _ = self.levels[level]
        part = self.ref.at[rows_of(keep, size), :]
        return self.line.copy(
            part, part, self.sends.at[at], self.recvs.at[at], dp=self.line.partner(self.bits[level])
        )

    def step(self, at):
        if 0 < at <= self.count:
            self.copy(at - 1).wait_recv()
        if at < self.count:
            self.copy(at).start()

    def drain(self):
        for at in range(self.count):
            self.copy(at).wait_send()


def two_ways(ref, bits):
    half = ref.shape[0] // 2
    return [(ref.at[pl.ds(at * half, half), :], bits if at == 0 else bits[::-1]) for at in range(2)]


def communicate(number, mib):
    return pltpu.CompilerParams(
        collective_id=number, has_side_effects=True, vmem_limit_bytes=mib * MIB
    )


def forward_kernel(
    n, heads, shared_kv,
    prefix_ref, x_ref, gain_one, gain_two,
    grad_in, wq, wk, wv, wo, wgate, wup, wdown,
    cos_out, sin_out, n1_out, n2_out, g_out, qkv_out, log_out, o_own_out, o_oth_out, mid_out, scale_out, wo_from,
    a_own_out, a_oth_out, dg_own_out, dg_oth_out, du_own_out, du_oth_out, result_out,
    n_own, n_oth, g_own, g_oth, w_own, w_from, wo_ref, wg_ref, wu_ref, wd_ref, wd_oth, a_ref,
    cos_ref, sin_ref, qkv_ref, vt_ref, o_own, o_oth, log_ref, part, ups, downs, total, scales, row_out, row_in, stage,
    gather_sends, gather_recvs, scatter_sends, scatter_recvs, cross_sends, cross_recvs, local_sems,
    unit_sends, unit_recvs, unit_stores, down_sends, down_recvs, a_sems,
):
    batches, tokens, depth = x_ref.shape
    length = n * tokens
    line = Line(n)
    r, c = line.r, line.c
    q_width = heads * HEAD_DIM
    k_col, v_col = q_width, q_width + HEAD_DIM
    share = wgate.shape[1] // 2
    kv_own = 0 if shared_kv else c * HEAD_DIM
    kv_oth = 0 if shared_kv else (1 - c) * HEAD_DIM

    def lanes(at, size):
        return pl.ds(pl.multiple_of(at, 128), size)

    def rows_at(at, size):
        return pl.ds(pl.multiple_of(at, size), size)

    local_count, cross_count = [0], [0]

    def local(src, dst):
        copy = pltpu.make_async_copy(src, dst, local_sems.at[local_count[0]])
        local_count[0] += 1
        copy.start()
        return copy

    def cross(src, dst):
        at = cross_count[0]
        cross_count[0] += 1
        return line.across(src, dst, cross_sends.at[at], cross_recvs.at[at])

    loads = [
        local(wq.at[:, lanes(c * q_width, q_width)], w_own.at[:, pl.ds(0, q_width)]),
        local(wk.at[:, lanes(kv_own, HEAD_DIM)], w_own.at[:, pl.ds(k_col, HEAD_DIM)]),
        local(wv.at[:, lanes(kv_own, HEAD_DIM)], w_own.at[:, pl.ds(v_col, HEAD_DIM)]),
    ]
    wo_load = local(wo, wo_ref)
    g_loads = [local(grad_in.at[m], g_own.at[m, r]) for m in range(batches)]
    unit_loads = [
        local(wgate.at[:, lanes(c * share, share)], wg_ref.at[0]),
        local(wup.at[:, lanes(c * share, share)], wu_ref.at[0]),
        local(wdown.at[rows_at(c * share, share), :], wd_ref.at[0]),
        local(wdown.at[rows_at((1 - c) * share, share), :], wd_oth),
    ]
    for m in range(batches):
        x = x_ref[m].astype(F32)
        squares = jnp.sum(x * x, axis=1, keepdims=True)
        row_out[0, m] = jnp.broadcast_to(squares, (tokens, 128))
    line.barrier()

    def row_cross(which, m):
        return cross(row_out.at[which, m], row_in.at[which, m])

    def norm_scale(which, m, copy):
        copy.wait_recv()
        squares = row_out[which, m] + row_in[which, m]
        value = lax.rsqrt(squares * (1.0 / WIDTH) + epsilon)
        scales[which, m] = value
        return value[:, :1]

    crosses = [row_cross(0, m) for m in range(batches)]
    for copy in crosses:
        copy.start()
    w_cross = [
        cross(wq.at[:, lanes((1 - c) * q_width, q_width)], w_from.at[:, pl.ds(0, q_width)]),
        cross(wk.at[:, lanes(kv_oth, HEAD_DIM)], w_from.at[:, pl.ds(k_col, HEAD_DIM)]),
        cross(wv.at[:, lanes(kv_oth, HEAD_DIM)], w_from.at[:, pl.ds(v_col, HEAD_DIM)]),
    ]
    gathers = [
        [
            Gather(line, own.at[m], oth.at[m], gather_sends.at[at, m], gather_recvs.at[at, m])
            for m in range(batches)
        ]
        for at, (own, oth) in enumerate(((n_own, n_oth), (g_own, g_oth), (n_own, n_oth)))
    ]
    n1, g, n2 = gathers
    rs = [
        Scatter(line, part.at[m], ups.at[m], downs.at[m], scatter_sends.at[m], scatter_recvs.at[m])
        for m in range(batches)
    ]
    for m in range(batches):
        scale_one = norm_scale(0, m, crosses[m])
        n_own[m, r] = (x_ref[m].astype(F32) * scale_one * gain_one[...]).astype(BF16)
        if m == 0:
            n1[0].start()
            for copy in w_cross:
                copy.start()

    @pl.loop(0, n)
    def _(p):
        rows = rows_at(p * tokens, tokens)
        cos_ref[rows, :], sin_ref[rows, :] = rope_tables(p * tokens, tokens)

    for copy in loads:
        copy.wait()
    for copy in w_cross:
        copy.wait_recv()

    def project(m, q):
        n1[m].arrive(q)
        rows = rows_at(q * tokens, tokens)
        pre = dot(n_own[m, q], w_own[...], NN) + dot(n_oth[m, q], w_from[...], NN)
        cosine, signed = cos_ref[rows, :], sin_ref[rows, :]
        for head in range(heads + 1):
            piece = pre[:, head * HEAD_DIM : (head + 1) * HEAD_DIM]
            qkv_ref[m, rows, pl.ds(head * HEAD_DIM, HEAD_DIM)] = rope(piece, cosine, signed).astype(BF16)
        values = pre[:, v_col : v_col + HEAD_DIM].astype(BF16)
        qkv_ref[m, rows, pl.ds(v_col, HEAD_DIM)] = values
        vt_ref[m, :, rows] = values.T

    block = min(256, length)
    count = length // block

    def attend_block(m, index):
        first = index * block
        extent = min(length, max(first + block, PREFIX_TOP))
        keys = qkv_ref[m, pl.ds(0, extent), pl.ds(k_col, HEAD_DIM)]
        key_at = lax.broadcasted_iota(jnp.int32, (extent, block), 0)
        query_at = lax.broadcasted_iota(jnp.int32, (extent, block), 1) + first
        allowed = (key_at <= query_at) | (key_at < prefix_ref[:, pl.ds(m, 1)])
        for head in range(heads):
            cols = pl.ds(head * HEAD_DIM, HEAD_DIM)
            query = qkv_ref[m, pl.ds(first, block), cols]
            scores = jnp.where(allowed, dot(keys, query, NT) * scale, -1e30)
            topmost = jnp.max(scores, axis=0, keepdims=True)
            exponent = jnp.exp(scores - topmost)
            summed = jnp.sum(exponent, axis=0, keepdims=True)
            weights = (exponent * (1.0 / summed)).astype(BF16)
            result = dot(vt_ref[m, :, pl.ds(0, extent)], weights, NN)
            o_own[m, pl.ds(first, block), cols] = result.T.astype(BF16)
            log_ref[m, pl.ds(head, 1), pl.ds(first, block)] = topmost + jnp.log(summed)

    def project_out(m):
        own_rows, oth_rows = rows_at(c * q_width, q_width), rows_at((1 - c) * q_width, q_width)

        @pl.loop(0, n)
        def _(p):
            rows = rows_at(p * tokens, tokens)
            value = dot(o_own[m, rows, :], wo_ref[own_rows, :], NN)
            value = value + dot(o_oth[m, rows, :], wo_ref[oth_rows, :], NN)
            part[m, p] = value.astype(BF16)

    def walk(m, first, last):
        for k in range(first, last):
            n1[m].step(k)
            project(m, line.nearest(k))

    def release(m, store):
        store.wait()
        n1[m].drain()

    def middle(m):
        rs[m].total(total.at[m])
        total[m] = total[m] + x_ref[m].astype(F32)
        mid = total[m]
        squares = jnp.sum(mid * mid, axis=1, keepdims=True)
        row_out[1, m] = jnp.broadcast_to(squares, (tokens, 128))
        copy = row_cross(1, m)
        copy.start()
        scale_two = norm_scale(1, m, copy)
        n_own[m, r] = (total[m] * scale_two * gain_two[...]).astype(BF16)
        crosses.append(copy)
        n2[m].start()

    outs = ((a_own_out, a_oth_out), (dg_own_out, dg_oth_out), (du_own_out, du_oth_out))
    order = [(m, k) for m in range(batches) for k in range(n)]

    def unit_away(at, kind):
        m, k = order[at]
        return line.across(
            stage.at[at % 2, kind], outs[kind][1].at[m, line.nearest(k)],
            unit_sends.at[at, kind], unit_recvs.at[at, kind],
        )

    def unit_kept(at, kind):
        m, k = order[at]
        return pltpu.make_async_copy(
            stage.at[at % 2, kind], outs[kind][0].at[m, line.nearest(k)], unit_stores.at[at, kind]
        )

    left = set()

    def unit_wait(at):
        if at in left:
            left.remove(at)
            for kind in range(3):
                unit_away(at, kind).wait_send()
                unit_kept(at, kind).wait()

    def units(at):
        m, k = order[at]
        q = line.nearest(k)
        n2[m].arrive(q)
        g[m].arrive(q)
        if at >= 2:
            unit_wait(at - 2)
        slot = at % 2
        size = min(256, share)

        @pl.loop(0, share // size)
        def _(b):
            cols = rows_at(b * size, size)
            gate = dot(n_own[m, q], wg_ref[0, :, cols], NN) + dot(n_oth[m, q], wg_ref[1, :, cols], NN)
            up = dot(n_own[m, q], wu_ref[0, :, cols], NN) + dot(n_oth[m, q], wu_ref[1, :, cols], NN)
            da = dot(g_own[m, q], wd_ref[0, cols, :], NT) + dot(g_oth[m, q], wd_ref[1, cols, :], NT)
            sigmoid = 1.0 / (1.0 + jnp.exp(-gate))
            silu = gate * sigmoid
            stage[slot, 0, :, cols] = (silu * up).astype(BF16)
            stage[slot, 1, :, cols] = (da * up * sigmoid * (1.0 + gate * (1.0 - sigmoid))).astype(BF16)
            stage[slot, 2, :, cols] = (da * silu).astype(BF16)

        left.add(at)
        for kind in range(3):
            unit_away(at, kind).start()
            unit_kept(at, kind).start()

    down_rs = Scatter(line, part.at[0], ups.at[0], downs.at[0], down_sends, down_recvs)

    def down_project():
        for k in range(n):
            unit_wait(k)
            unit_away(k, 0).wait_recv()
        rs[0].drain()

        for p in range(n):
            a_loads = [
                pltpu.make_async_copy(src.at[0, p], a_ref.at[side], a_sems.at[side])
                for side, src in enumerate((a_own_out, a_oth_out))
            ]
            for copy in a_loads:
                copy.start()
            for copy in a_loads:
                copy.wait()
            value = dot(a_ref[0], wd_ref[0], NN) + dot(a_ref[1], wd_oth[...], NN)
            part[0, p] = value.astype(BF16)

    half = (n + 1) // 2
    o_cross = [cross(o_own.at[m], o_oth.at[m]) for m in range(batches)]
    stores = []

    project(0, r)
    walk(0, 1, n - 1)
    n1[1].start()
    walk(0, n - 1, n)
    n1_stores = [local(n_own.at[0], n1_out.at[0])]
    project(1, r)
    for index in range(count // 2):
        attend_block(0, index)
    walk(1, 1, half)
    for index in range(count // 2, count):
        attend_block(0, index)
    o_cross[0].start()
    big_cross = [
        cross(wgate.at[:, lanes((1 - c) * share, share)], wg_ref.at[1]),
        cross(wup.at[:, lanes((1 - c) * share, share)], wu_ref.at[1]),
        cross(wdown.at[rows_at((1 - c) * share, share), :], wd_ref.at[1]),
        cross(wo.at[rows_at((1 - c) * q_width, q_width), :], wo_from),
    ]
    walk(1, half, n - 1)
    o_cross[0].wait_recv()
    wo_load.wait()
    project_out(0)
    rs[0].step(1)
    g_loads[0].wait()
    g[0].start()
    walk(1, n - 1, n)
    n1_stores.append(local(n_own.at[1], n1_out.at[1]))
    for copy in big_cross:
        copy.start()
    for index in range(count // 2):
        attend_block(1, index)
    for s in range(2, half + 1):
        rs[0].step(s)
    for index in range(count // 2, count):
        attend_block(1, index)
    o_cross[1].start()
    for k in range(1, half):
        g[0].step(k)
    release(0, n1_stores[0])
    for s in range(half + 1, n):
        rs[0].step(s)
    o_cross[1].wait_recv()
    project_out(1)
    rs[1].step(1)
    for k in range(half, n - 1):
        g[0].step(k)
    middle(0)
    release(1, n1_stores[1])
    for s in range(2, half + 1):
        rs[1].step(s)
    g[0].step(n - 1)
    for copy in unit_loads:
        copy.wait()
    for copy in big_cross:
        copy.wait_recv()
    g_loads[1].wait()
    stores += [local(g_own.at[0], g_out.at[0])]
    stores += [local(qkv_ref, qkv_out), local(log_ref, log_out)]
    stores += [local(cos_ref, cos_out), local(sin_ref, sin_out)]
    stores += [local(o_own, o_own_out), local(o_oth, o_oth_out)]
    mid_store = local(total.at[0], mid_out.at[0])
    units(0)
    for k in range(1, half):
        n2[0].step(k)
        units(k)
    for s in range(half + 1, n):
        rs[1].step(s)
    for k in range(half, n - 1):
        n2[0].step(k)
    g[1].start()
    for k in range(half, n - 1):
        units(k)
    middle(1)
    stores.append(local(total.at[1], mid_out.at[1]))
    stores.append(local(scales, scale_out))
    n2[0].step(n - 1)
    units(n - 1)
    units(n)
    down_project()
    down_rs.step(1)
    for k in range(1, n):
        g[1].step(k)
        n2[1].step(k)
        units(n + k)
        if k + 1 < n:
            down_rs.step(k + 1)
    stores += [local(g_own.at[1], g_out.at[1]), local(n_own, n2_out)]
    mid_store.wait()
    total[0] = total[0] + part[0, r].astype(F32)
    down_rs.add_received(total.at[0])
    part[0, r] = total[0].astype(BF16)
    stores.append(local(part.at[0, r], result_out))
    for at in range(2 * n):
        unit_wait(at)
        for kind in range(3):
            if at >= n or kind > 0:
                unit_away(at, kind).wait_recv()
    for copy in crosses + w_cross + o_cross + big_cross:
        copy.wait_send()
    for item in g + n2 + rs[1:] + [down_rs]:
        item.drain()
    for copy in stores:
        copy.wait()


def forward(
    prefix, x, gain_one, gain_two, grad_in, wq, wk, wv, wo, wgate, wup, wdown, n, heads, shared_kv
):
    batches, tokens, depth = x.shape
    length = n * tokens
    width = (heads + 2) * HEAD_DIM
    q_width = heads * HEAD_DIM
    share = wgate.shape[1] // 2
    vmem = pl.BlockSpec(memory_space=pltpu.VMEM)
    anywhere = pl.BlockSpec(memory_space=pl.ANY)
    gathered, units = (batches, n, tokens, depth), (batches, n, tokens, share)
    rows = (2, batches, tokens, 128)
    table = (length, HEAD_DIM)
    shapes = [
        (table, F32), (table, F32), (gathered, BF16), (gathered, BF16), (gathered, BF16),
        ((batches, length, width), BF16), ((batches, 8, length), F32),
        ((batches, length, q_width), BF16), ((batches, length, q_width), BF16),
        ((batches, tokens, depth), F32), (rows, F32), ((q_width, depth), BF16),
    ] + [(units, BF16)] * 6 + [((tokens, depth), BF16)]
    boxes = (batches, n - 1, tokens, depth)
    dma = pltpu.SemaphoreType.DMA
    return pl.pallas_call(
        functools.partial(forward_kernel, n, heads, shared_kv),
        in_specs=[vmem] * 4 + [anywhere] * 8,
        out_specs=[anywhere] * len(shapes),
        out_shape=[jax.ShapeDtypeStruct(*item) for item in shapes],
        scratch_shapes=[
            pltpu.VMEM(gathered, BF16), pltpu.VMEM(gathered, BF16),
            pltpu.VMEM(gathered, BF16), pltpu.VMEM(gathered, BF16),
            pltpu.VMEM((depth, width), BF16), pltpu.VMEM((depth, width), BF16),
            pltpu.VMEM(wo.shape, BF16),
            pltpu.VMEM((2, depth, share), BF16), pltpu.VMEM((2, depth, share), BF16),
            pltpu.VMEM((2, share, depth), BF16), pltpu.VMEM((share, depth), BF16),
            pltpu.VMEM((2, tokens, share), BF16), pltpu.VMEM(table, F32), pltpu.VMEM(table, F32),
            pltpu.VMEM((batches, length, width), BF16),
            pltpu.VMEM((batches, HEAD_DIM, length), BF16),
            pltpu.VMEM((batches, length, q_width), BF16), pltpu.VMEM((batches, length, q_width), BF16),
            pltpu.VMEM((batches, 8, length), F32),
            pltpu.VMEM(gathered, BF16), pltpu.VMEM(boxes, BF16), pltpu.VMEM(boxes, BF16),
            pltpu.VMEM((batches, tokens, depth), F32),
            pltpu.VMEM(rows, F32), pltpu.VMEM(rows, F32), pltpu.VMEM(rows, F32),
            pltpu.VMEM((2, 3, tokens, share), BF16),
            dma((3, batches, n, 3)), dma((3, batches, n, 2)),
            dma((batches, 2, n - 1)), dma((batches, 2, n - 1)), dma((13,)), dma((13,)), dma((26,)),
            dma((batches * n, 3)), dma((batches * n, 3)), dma((batches * n, 3)),
            dma((2, n - 1)), dma((2, n - 1)), dma((2,)),
        ],
        compiler_params=communicate(1, 63),
        cost_estimate=cost(2e11, 100 * MIB),
    )(prefix, x, gain_one, gain_two, grad_in, wq, wk, wv, wo, wgate, wup, wdown)


def unit_grads_kernel(
    n, bits,
    mid_ref, scales_ref, top_ref, gain_ref,
    g_in, n2_in, a_own, a_oth, dg_own, dg_oth, du_own, du_oth, wgate, wup,
    dz_out, dz_oth_out, mgrad_out, down_out, gate_out, up_out, gain_out,
    wg_ref, wu_ref, unit_ref, part, ups, downs, total, dz_ref, row_out, row_in,
    shared_ref, moving_ref, down_ref, gate_ref, up_ref, boxes,
    load_sems, unit_sems, moving_sems, scatter_sends, scatter_recvs, gather_sends, gather_recvs,
    cross_sends, cross_recvs, store_sems, reduce_sends, reduce_recvs, part_sems,
):
    batches, tokens, depth = mid_ref.shape
    share = a_own.shape[1]
    line = Line(n)
    r, c = line.r, line.c
    loads = [
        pltpu.make_async_copy(a, b, load_sems.at[i])
        for i, (a, b) in enumerate(((wgate, wg_ref), (wup, wu_ref), (g_in, shared_ref)))
    ]
    order = [(m, p) for m in range(batches) for p in range(n)]

    def unit_loads(at):
        return [
            pltpu.make_async_copy(
                src.at[pl.ds(at * tokens, tokens), :], unit_ref.at[at % 2, i], unit_sems.at[at % 2, i]
            )
            for i, src in enumerate((dg_own, dg_oth, du_own, du_oth))
        ]

    width = min(256, share)
    nb = share // width
    kinds = ((a_own, a_oth), (dg_own, dg_oth), (du_own, du_oth))

    def moving(kind, index, go):
        for side in range(2):

            @pl.when(index // nb == side)
            def _(side=side):
                cols = pl.ds(pl.multiple_of((index - side * nb) * width, width), width)
                copy = pltpu.make_async_copy(
                    kinds[kind][side].at[:, cols], moving_ref.at[index % 2], moving_sems.at[index % 2]
                )
                copy.start() if go else copy.wait()

    moving(0, 0, True)
    for copy in loads[::-1] + unit_loads(0):
        copy.start()
    line.barrier(bits=bits)
    scatters = [
        Scatter(line, part.at[m], ups.at[m], downs.at[m], scatter_sends.at[m], scatter_recvs.at[m])
        for m in range(batches)
    ]
    gathers = [
        Gather(
            line, dz_out.at[m], dz_oth_out.at[m], gather_sends.at[m], gather_recvs.at[m], dz_ref.at[m]
        )
        for m in range(batches - 1)
    ]
    reduces = []
    for kind, ref in enumerate((down_ref, gate_ref, up_ref)):
        pair = [
            Reduce(
                line, view, [box.at[way] for box in boxes[kind]], way_bits,
                reduce_sends.at[kind, way], reduce_recvs.at[kind, way],
            )
            for way, (view, way_bits) in enumerate(two_ways(ref, bits))
        ]
        reduces.append(pair)
    cols_own = pl.ds(pl.multiple_of(c * share, share), share)
    cols_oth = pl.ds(pl.multiple_of((1 - c) * share, share), share)

    def unit_part(at):
        m, p = order[at]
        for copy in unit_loads(at):
            copy.wait()
        if at + 1 < len(order):
            for copy in unit_loads(at + 1):
                copy.start()
        slot = at % 2
        block = min(512, depth)

        @pl.loop(0, depth // block)
        def _(b):
            rows = pl.ds(pl.multiple_of(b * block, block), block)
            value = dot(unit_ref[slot, 0], wg_ref[rows, cols_own], NT)
            value = value + dot(unit_ref[slot, 1], wg_ref[rows, cols_oth], NT)
            value = value + dot(unit_ref[slot, 2], wu_ref[rows, cols_own], NT)
            value = value + dot(unit_ref[slot, 3], wu_ref[rows, cols_oth], NT)
            part[m, p, :, rows] = value.astype(BF16)

    def weight_grad(kind, first=0, last=2 * nb):
        @pl.loop(first, last)
        def _(index):
            moving(kind, index, False)

            @pl.when(index + 1 < 2 * nb)
            def _():
                moving(kind, index + 1, True)

            side = index // nb
            place = (c + side * (1 - 2 * c)) * nb + index - side * nb
            cols = pl.ds(pl.multiple_of(place * width, width), width)
            if kind == 0:
                down_ref[cols, :] = dot(moving_ref[index % 2], shared_ref[...], TN).astype(BF16)
            else:
                ref = gate_ref if kind == 1 else up_ref
                ref[:, cols] = dot(shared_ref[...], moving_ref[index % 2], TN).astype(BF16)

        if last == 2 * nb and kind + 1 < len(kinds):
            moving(kind + 1, 0, True)

    def row_cross(m):
        return line.across(row_out.at[m], row_in.at[m], cross_sends.at[m], cross_recvs.at[m])

    def store(which, m, src, dst):
        return pltpu.make_async_copy(src, dst, store_sems.at[which, m])

    def middle(m):
        scatters[m].total(total.at[m])
        s = scales_ref[1, m][:, :1]
        gain_out[pl.ds(m, 1), :] = jnp.sum(total[m] * mid_ref[m] * s, axis=0, keepdims=True)
        total[m] = total[m] * gain_ref[...]
        inner = jnp.sum(total[m] * mid_ref[m], axis=1, keepdims=True)
        row_out[m] = jnp.broadcast_to(inner, (tokens, 128))
        row_cross(m).start()
        row_cross(m).wait_recv()
        inner = row_out[m, :, pl.ds(0, 1)] + row_in[m, :, pl.ds(0, 1)]
        result = (
            top_ref[m].astype(F32) + total[m] * s - mid_ref[m] * ((s * s * s) * inner * (1.0 / WIDTH))
        )
        total[m] = result
        dz_ref[m] = result.astype(BF16)
        if m < len(gathers):
            gathers[m].start()
        store(0, m, total.at[m], mgrad_out.at[m]).start()
        store(1, m, dz_ref.at[m], dz_out.at[m, r]).start()

    def steps(item, first, last):
        for s in range(first, last):
            item.step(s)

    def reduce_step(kind, at):
        for item in reduces[kind]:
            item.step(at)

    half = (n + 1) // 2
    loads[2].wait()
    weight_grad(0, 0, nb)
    for way, item in enumerate(reduces[0]):

        @pl.when(c == way)
        def _(item=item):
            item.step(0)

    weight_grad(0, nb, 2 * nb)
    for way, item in enumerate(reduces[0]):

        @pl.when(c != way)
        def _(item=item):
            item.step(0)

    n2_load = pltpu.make_async_copy(n2_in, shared_ref, load_sems.at[3])
    n2_load.start()
    for copy in loads[:2]:
        copy.wait()
    for at in range(n):
        unit_part(at)
    scatters[0].step(1)
    n2_load.wait()
    weight_grad(1)
    reduce_step(1, 0)
    steps(scatters[0], 2, half + 1)
    reduce_step(0, 1)
    for at in range(n, 2 * n):
        unit_part(at)
    steps(scatters[0], half + 1, n)
    scatters[1].step(1)
    weight_grad(2)
    reduce_step(2, 0)
    middle(0)
    steps(scatters[1], 2, half + 1)
    reduce_step(1, 1)
    steps(gathers[0], 1, half)
    steps(scatters[1], half + 1, n)
    steps(gathers[0], half, n - 1)
    reduce_step(2, 1)
    middle(1)
    steps(gathers[0], n - 1, n)
    for at in range(2, len(bits)):
        for kind in range(3):
            reduce_step(kind, at)
    outs = (down_out, gate_out, up_out)
    kept_stores = []
    for kind in range(3):
        reduce_step(kind, len(bits))
        for way, item in enumerate(reduces[kind]):
            out_view = two_ways(outs[kind], bits)[way][0]
            rows = item.kept()
            copy = pltpu.make_async_copy(
                item.ref.at[rows, :], out_view.at[rows, :], part_sems.at[kind, way]
            )
            copy.start()
            kept_stores.append(copy)
    for item in gathers:
        for q in range(n):
            item.arrive(q)
        item.drain()
    for m in range(batches):
        scatters[m].drain()
        row_cross(m).wait_send()
        store(0, m, total.at[m], mgrad_out.at[m]).wait()
        store(1, m, dz_ref.at[m], dz_out.at[m, r]).wait()
    for pair in reduces:
        for item in pair:
            item.drain()
    for copy in kept_stores:
        copy.wait()


def unit_grads(mid, scales, top, gain, g, n2, halves, wgate, wup, n, dp_count):
    batches, tokens, depth = mid.shape
    rows, share = halves[0].shape
    bits = list(range(dp_count.bit_length() - 1))
    vmem = pl.BlockSpec(memory_space=pltpu.VMEM)
    anywhere = pl.BlockSpec(memory_space=pl.ANY)
    gathered = (batches, n, tokens, depth)
    down_dims, gate_dims = (2 * share, depth), (depth, 2 * share)
    dims = (down_dims, gate_dims, gate_dims)
    shapes = [(gathered, BF16), ((batches - 1,) + gathered[1:], BF16), (mid.shape, F32)]
    shapes += [(item, BF16) for item in dims] + [((8, depth), F32)]
    boxes = (batches, n - 1, tokens, depth)
    width = min(256, share)
    dma = pltpu.SemaphoreType.DMA
    return pl.pallas_call(
        functools.partial(unit_grads_kernel, n, bits),
        in_specs=[vmem] * 4 + [anywhere] * 10,
        out_specs=[anywhere] * 6 + [vmem],
        out_shape=[jax.ShapeDtypeStruct(*item) for item in shapes],
        scratch_shapes=[
            pltpu.VMEM(wgate.shape, BF16), pltpu.VMEM(wup.shape, BF16),
            pltpu.VMEM((2, 4, tokens, share), BF16), pltpu.VMEM(gathered, BF16),
            pltpu.VMEM(boxes, BF16), pltpu.VMEM(boxes, BF16), pltpu.VMEM(mid.shape, F32),
            pltpu.VMEM(mid.shape, BF16),
            pltpu.VMEM((batches, tokens, 128), F32), pltpu.VMEM((batches, tokens, 128), F32),
            pltpu.VMEM((rows, depth), BF16), pltpu.VMEM((2, rows, width), BF16),
            pltpu.VMEM(down_dims, BF16), pltpu.VMEM(gate_dims, BF16), pltpu.VMEM(gate_dims, BF16),
            [
                [pltpu.VMEM((2, item[0] // 2 ** (level + 2), item[1]), BF16) for level in range(len(bits))]
                for item in dims
            ],
            dma((4,)), dma((2, 4)), dma((2,)), dma((batches, 2, n - 1)), dma((batches, 2, n - 1)),
            dma((batches, n, 3)), dma((batches, n, 2)), dma((batches,)), dma((batches,)),
            dma((2, batches)), dma((3, 2, len(bits))), dma((3, 2, len(bits))), dma((3, 2)),
        ],
        compiler_params=communicate(2, 62),
        cost_estimate=cost(2e11, 100 * MIB),
    )(mid, scales, top, gain, g, n2, *halves, wgate, wup)


def backward_kernel(
    n, heads, shared_kv, bits,
    prefix_ref, x_ref, scales_ref, gain_in, cos_ref, sin_ref, log_ref, ffn_gains,
    mid_in, dz_own_in, dz_oth_in, wo, wo_from, wq, wk, wv, qkv_in, a_own_in, a_oth_in, wdown, n1_in,
    o_own_in, o_oth_in, down_in, gate_in, up_in,
    grad_out, result_out, qkv_out, o_out, down_out, gate_out, up_out, gain_out,
    dz_ref, dz_oth, dz_last, wo_ref, w_own, w_oth, qkv_ref, dk_ref, dv_ref, kt_ref, dqkv_own, dqkv_oth,
    part, ups, downs, total, a_ref, wide_ref, o_ref, qkv_grad, o_grad, qkv_sum, o_sum, boxes,
    row_out, row_in, result_ref, gain_ref, row_boxes, dp_boxes,
    load_sems, dz_sems, a_sems, scatter_sends, scatter_recvs, cross_sends, cross_recvs, store_sems,
    reduce_sends, reduce_recvs, spread_sends, spread_recvs, unit_sends, unit_recvs,
    gather_sends, gather_recvs, gain_sends, gain_recvs,
):
    batches, tokens, depth = x_ref.shape
    length = n * tokens
    share = a_own_in.shape[1]
    line = Line(n)
    r, c = line.r, line.c
    q_width = heads * HEAD_DIM
    k_col, v_col = q_width, q_width + HEAD_DIM
    width = v_col + HEAD_DIM

    def lanes(at, size):
        return pl.ds(pl.multiple_of(at, 128), size)

    def rows_at(at, size):
        return pl.ds(pl.multiple_of(at, size), size)

    def qkv_columns(side, dst):
        kv = 0 if shared_kv else side * HEAD_DIM
        return [
            (wq.at[:, lanes(side * q_width, q_width)], dst.at[:, pl.ds(0, q_width)]),
            (wk.at[:, lanes(kv, HEAD_DIM)], dst.at[:, pl.ds(k_col, HEAD_DIM)]),
            (wv.at[:, lanes(kv, HEAD_DIM)], dst.at[:, pl.ds(v_col, HEAD_DIM)]),
        ]

    pairs = [(wdown, wide_ref.at[pl.ds(0, 2 * share), :]), (qkv_in, qkv_ref)]
    pairs += [(wo.at[rows_at(c * q_width, q_width), :], wo_ref.at[0]), (wo_from, wo_ref.at[1])]
    last = batches - 1
    pairs += [(dz_own_in.at[m], dz_ref.at[m]) for m in range(last)]
    first = len(pairs)
    pairs += qkv_columns(c, w_own) + qkv_columns(1 - c, w_oth)
    pairs += [(o_own_in, o_ref.at[0]), (o_oth_in, o_ref.at[1])]
    pairs += [(mid_in.at[last], total.at[last])]
    loads = [pltpu.make_async_copy(a, b, load_sems.at[i]) for i, (a, b) in enumerate(pairs)]
    n1_load = pltpu.make_async_copy(n1_in, wide_ref.at[pl.ds(0, batches * length), :], load_sems.at[len(pairs)])
    shard_load = pltpu.make_async_copy(
        dz_own_in.at[last, r], dz_ref.at[last, r], load_sems.at[len(pairs) + 1]
    )
    order = [(m, p) for m in range(batches) for p in range(n)]

    def a_loads(at):
        rows = pl.ds(at * tokens, tokens)
        return [
            pltpu.make_async_copy(src.at[rows, :], a_ref.at[at % 2, side], a_sems.at[at % 2, side])
            for side, src in enumerate((a_own_in, a_oth_in))
        ]

    def dz_load(at):
        m, p = order[at]
        return pltpu.make_async_copy(dz_oth_in.at[m, p], dz_oth.at[at % 2], dz_sems.at[at % 2])

    for copy in [shard_load] + loads[:1] + a_loads(last * n) + loads[1:first] + [dz_load(0)] + loads[first:]:
        copy.start()
    dp_count = 2 ** len(bits)
    line.wide_barrier(dp_count)
    gains = [
        Everywhere(line, "row", r, n, gain_ref.at[0], row_boxes, gain_sends.at[0], gain_recvs.at[0]),
        Everywhere(line, "dp", line.d, dp_count, gain_ref.at[1], dp_boxes, gain_sends.at[1], gain_recvs.at[1]),
    ]
    gather = Gather(line, dz_ref.at[last], dz_last, gather_sends, gather_recvs)
    spreads = [
        Spread(
            line, view, way_bits, unit_sends.at[kind, way], unit_recvs.at[kind, way], skip=int(kind == 2)
        )
        for kind, ref in enumerate((down_out, gate_out, up_out))
        for way, (view, way_bits) in enumerate(two_ways(ref, bits))
    ]
    *head_rs, out_rs = (
        Scatter(
            line, part.at[at], ups.at[at], downs.at[at], scatter_sends.at[at], scatter_recvs.at[at]
        )
        for at in range(batches + 1)
    )
    reduces, gatherers = [], []
    for kind, (ref, result) in enumerate(((qkv_grad, qkv_sum), (o_grad, o_sum))):
        results = two_ways(result, bits)
        for way, (view, way_bits) in enumerate(two_ways(ref, bits)):
            reduces.append(
                Reduce(
                    line, view, [box.at[way] for box in boxes[kind]], way_bits,
                    reduce_sends.at[kind, way], reduce_recvs.at[kind, way],
                )
            )
            gatherers.append(
                Spread(
                    line, results[way][0], way_bits, spread_sends.at[kind, way], spread_recvs.at[kind, way]
                )
            )
    count = len(bits)

    def total_step(items, at):
        for item in items:
            if at <= count:
                reduces[item].step(at, gatherers[item].ref if at == count else None)
            if at >= count:
                gatherers[item].step(at - count)

    def spread_step(which, at):
        for kind in which:
            for item in spreads[2 * kind : 2 * kind + 2]:
                item.step(at)

    own_rows, oth_rows = rows_at(c * share, share), rows_at((1 - c) * share, share)

    def down_part(at):
        m, p = order[at]
        for copy in a_loads(at):
            copy.wait()
        if at + 1 < len(order):
            for copy in a_loads(at + 1):
                copy.start()
        value = dot(a_ref[at % 2, 0], wide_ref[own_rows, :], NN)
        part[batches, p] = (value + dot(a_ref[at % 2, 1], wide_ref[oth_rows, :], NN)).astype(BF16)

    def grad_cross(m):
        return line.across(dqkv_own.at[m], dqkv_oth.at[m], cross_sends.at[m], cross_recvs.at[m])

    def row_cross(m):
        at = batches + m
        return line.across(row_out.at[m], row_in.at[m], cross_sends.at[at], cross_recvs.at[at])

    def store(which, m, src, dst):
        return pltpu.make_async_copy(src, dst, store_sems.at[which, m])

    def attend_start(m):
        dk_ref[...] = jnp.zeros_like(dk_ref)
        dv_ref[...] = jnp.zeros_like(dv_ref)
        kt_ref[...] = qkv_ref[m, :, pl.ds(k_col, HEAD_DIM)].T

    def attend_back(m, q):
        at = m * n + q
        if m < last:
            dz_load(at).wait()
            if at + 1 < last * n:
                dz_load(at + 1).start()
        else:
            gather.arrive(q)
        other = dz_oth[at % 2] if m < last else dz_last[q]
        rows = pl.ds(q * tokens, tokens)
        grads = dot(dz_ref[m, q], wo_ref[0], NT)
        grads = (grads + dot(other, wo_ref[1], NT)).astype(BF16)
        cosine, signed = cos_ref[rows, :], sin_ref[rows, :]
        extent = min(length, max((q + 1) * tokens, PREFIX_TOP))
        upto = pl.ds(0, extent)
        keys = qkv_ref[m, upto, pl.ds(k_col, HEAD_DIM)]
        values = qkv_ref[m, upto, pl.ds(v_col, HEAD_DIM)]
        key_at = lax.broadcasted_iota(jnp.int32, (extent, tokens), 0)
        query_at = lax.broadcasted_iota(jnp.int32, (extent, tokens), 1) + q * tokens
        allowed = (key_at <= query_at) | (key_at < prefix_ref[:, pl.ds(m, 1)])
        for head in range(heads):
            cols = pl.ds(head * HEAD_DIM, HEAD_DIM)
            query = qkv_ref[m, rows, cols]
            grad = grads[:, head * HEAD_DIM : (head + 1) * HEAD_DIM]
            raw = dot(keys, query, NT) * scale - log_ref[m, pl.ds(head, 1), rows]
            probs = jnp.exp(jnp.where(allowed, raw, -1e30))
            dv_ref[upto, :] += dot(probs.astype(BF16), grad, NN)
            prob_grad = dot(values, grad, NT)
            inner = jnp.sum(probs * prob_grad, axis=0, keepdims=True)
            rounded = (probs * (prob_grad - inner) * scale).astype(BF16)
            dk_ref[upto, :] += dot(rounded, query, NN)
            dq = dot(kt_ref[:, upto], rounded, NN).T
            dqkv_own[m, rows, cols] = rope_back(dq, cosine, signed).astype(BF16)

    def attend_end(m):
        dk = rope_back(dk_ref[...], cos_ref[...], sin_ref[...])
        dqkv_own[m, :, pl.ds(k_col, HEAD_DIM)] = dk.astype(BF16)
        dqkv_own[m, :, pl.ds(v_col, HEAD_DIM)] = dv_ref[...].astype(BF16)
        grad_cross(m).start()

    def head_part(m):
        grad_cross(m).wait_recv()

        @pl.loop(0, n)
        def _(p):
            rows = rows_at(p * tokens, tokens)
            value = dot(dqkv_own[m, rows, :], w_own[...], NT)
            part[m, p] = (value + dot(dqkv_oth[m, rows, :], w_oth[...], NT)).astype(BF16)

    def result():
        total[last] = total[last] + part[batches, r].astype(F32)
        out_rs.add_received(total.at[last])
        result_ref[...] = total[last].astype(BF16)
        store(0, 0, result_ref, result_out).start()

    def input_grad(m):
        head_rs[m].total(total.at[m])
        s = scales_ref[0, m][:, :1]
        x = x_ref[m].astype(F32)
        gain_ref[0, pl.ds(m, 1), :] = jnp.sum(total[m] * x * s, axis=0, keepdims=True)
        total[m] = total[m] * gain_in[...]
        inner = jnp.sum(total[m] * x, axis=1, keepdims=True)
        row_out[m] = jnp.broadcast_to(inner, (tokens, 128))
        row_cross(m).start()
        row_cross(m).wait_recv()
        inner = row_out[m, :, pl.ds(0, 1)] + row_in[m, :, pl.ds(0, 1)]
        total[m] = total[m] * s - x * ((s * s * s) * inner * (1.0 / WIDTH))
        store(1, m, total.at[m], grad_out.at[m]).start()

    def steps(item, first_step, last_step):
        for s in range(first_step, last_step):
            item.step(s)

    half = (n + 1) // 2
    spread_step((0, 1, 2), 0)
    shard_load.wait()
    gather.start()
    for copy in loads[1:first]:
        copy.wait()
    loads[0].wait()
    for at in range(last * n, len(order)):
        down_part(at)
    out_rs.step(1)
    n1_load.start()
    attend_start(0)
    for q in range(n // 2):
        attend_back(0, q)
    steps(gather, 1, half)
    for q in range(n // 2, n):
        attend_back(0, q)
    attend_end(0)
    steps(gather, half, n - 1)
    for copy in loads[first:]:
        copy.wait()
    head_part(0)
    head_rs[0].step(1)
    for at in range(1, count):
        spread_step((0,), at)
    steps(gather, n - 1, n)
    steps(out_rs, 2, half + 1)
    for side in range(2):
        place = c if side == 0 else 1 - c
        value = dot(o_ref[side], dz_ref[...].reshape(batches * length, depth), TN)
        o_grad[rows_at(place * q_width, q_width), :] = value.astype(BF16)
    total_step((2, 3), 0)
    attend_start(1)
    for q in range(n // 2):
        attend_back(1, q)
    steps(head_rs[0], 2, half + 1)
    for at in range(1, count):
        spread_step((1,), at)
    for q in range(n // 2, n):
        attend_back(1, q)
    attend_end(1)
    steps(out_rs, half + 1, n)
    total_step((2, 3), 1)
    head_part(1)
    head_rs[1].step(1)
    n1_load.wait()
    for side in range(2):
        place = c if side == 0 else 1 - c
        dqkv = (dqkv_own if side == 0 else dqkv_oth)[...].reshape(batches * length, width)
        value = dot(wide_ref[pl.ds(0, batches * length), :], dqkv, TN)
        qkv_grad[:, lanes(place * width, width)] = value.astype(BF16)
    total_step((0, 1), 0)
    steps(head_rs[0], half + 1, n)
    result()
    total_step((2, 3), 2)
    input_grad(0)
    total_step((0, 1), 1)
    turn, last_turn = 2, 2 * count
    for s in range(2, n):
        head_rs[1].step(s)
        if turn <= last_turn:
            total_step((0, 1), turn)
        if turn + 1 <= last_turn:
            total_step((2, 3), turn + 1)
        turn += 1
    input_grad(1)
    gain_ref[0, pl.ds(batches, batches), :] = ffn_gains[pl.ds(0, batches), :]
    gains[0].start()
    while turn <= last_turn:
        total_step((0, 1), turn)
        if turn + 1 <= last_turn:
            total_step((2, 3), turn + 1)
        turn += 1
    stores = [
        pltpu.make_async_copy(qkv_sum, qkv_out, load_sems.at[0]),
        pltpu.make_async_copy(o_sum, o_out, load_sems.at[1]),
    ]
    for copy in stores:
        copy.start()
    gain_ref[1] = gains[0].total()
    gains[1].start()
    for at in range(1, count):
        spread_step((2,), at)
    spread_step((0, 1, 2), count)
    for m in range(batches):
        grad_cross(m).wait_send()
        row_cross(m).wait_send()
        head_rs[m].drain()
        store(1, m, total.at[m], grad_out.at[m]).wait()
    out_rs.drain()
    store(0, 0, result_ref, result_out).wait()
    gather.drain()
    gain_out[...] = gains[1].total()
    for item in gains:
        item.drain()
    for item in spreads + reduces + gatherers:
        item.drain()
    for copy in stores:
        copy.wait()


def backward(
    prefix, x, scales, gain, tables, logs, ffn_gains, mid, dz_own, dz_oth, wo, wo_from, wq, wk, wv, qkv,
    a_own, a_oth, wdown, n1, o_own, o_oth, down, gate, up, heads, shared_kv, dp_count,
):
    batches, tokens, depth = x.shape
    n = dz_own.shape[1]
    length, width = qkv.shape[1:]
    rows, q_width = o_own.shape
    share = a_own.shape[1]
    bits = list(range(dp_count.bit_length() - 1))
    vmem = pl.BlockSpec(memory_space=pltpu.VMEM)
    anywhere = pl.BlockSpec(memory_space=pl.ANY)
    gathered = (batches, n, tokens, depth)
    boxes = (batches + 1, n - 1, tokens, depth)
    sums = [(depth, 2 * width), (2 * q_width, depth)]
    shapes = [(mid.shape, F32), ((tokens, depth), BF16)] + [(item, BF16) for item in sums]
    shapes += [(item.shape, BF16) for item in (down, gate, up)] + [((8, depth), F32)]
    dma = pltpu.SemaphoreType.DMA
    return pl.pallas_call(
        functools.partial(backward_kernel, n, heads, shared_kv, bits),
        in_specs=[vmem] * 8 + [anywhere] * 18,
        out_specs=[anywhere] * 7 + [vmem],
        out_shape=[jax.ShapeDtypeStruct(*item) for item in shapes],
        input_output_aliases={23: 4, 24: 5, 25: 6},
        scratch_shapes=[
            pltpu.VMEM(gathered, BF16), pltpu.VMEM((2, tokens, depth), BF16), pltpu.VMEM(gathered[1:], BF16),
            pltpu.VMEM((2, q_width, depth), BF16),
            pltpu.VMEM((depth, width), BF16), pltpu.VMEM((depth, width), BF16),
            pltpu.VMEM(qkv.shape, BF16),
            pltpu.VMEM((length, HEAD_DIM), F32), pltpu.VMEM((length, HEAD_DIM), F32),
            pltpu.VMEM((HEAD_DIM, length), BF16), pltpu.VMEM(qkv.shape, BF16), pltpu.VMEM(qkv.shape, BF16),
            pltpu.VMEM((batches + 1,) + gathered[1:], BF16), pltpu.VMEM(boxes, BF16), pltpu.VMEM(boxes, BF16),
            pltpu.VMEM(mid.shape, F32),
            pltpu.VMEM((2, 2, tokens, share), BF16),
            pltpu.VMEM((max(2 * share, rows), depth), BF16), pltpu.VMEM((2, rows, q_width), BF16),
            pltpu.VMEM(sums[0], BF16), pltpu.VMEM(sums[1], BF16),
            pltpu.VMEM(sums[0], BF16), pltpu.VMEM(sums[1], BF16),
            [
                [pltpu.VMEM((2, item[0] // 2 ** (level + 2), item[1]), BF16) for level in range(len(bits))]
                for item in sums
            ],
            pltpu.VMEM((batches, tokens, 128), F32), pltpu.VMEM((batches, tokens, 128), F32),
            pltpu.VMEM((tokens, depth), BF16), pltpu.VMEM((2, 8, depth), F32),
            pltpu.VMEM((n - 1, 8, depth), F32), pltpu.VMEM((dp_count - 1, 8, depth), F32),
            dma((20,)), dma((2,)), dma((2, 2)),
            dma((batches + 1, 2, n - 1)), dma((batches + 1, 2, n - 1)),
            dma((2 * batches,)), dma((2 * batches,)), dma((2, batches)),
            dma((2, 2, len(bits))), dma((2, 2, len(bits))), dma((2, 2, len(bits))), dma((2, 2, len(bits))),
            dma((3, 2, len(bits))), dma((3, 2, len(bits))), dma((n, 3)), dma((n, 2)),
            dma((2, max(n, dp_count) - 1)), dma((2, max(n, dp_count) - 1)),
        ],
        compiler_params=communicate(3, 62),
        cost_estimate=cost(2e11, 100 * MIB),
    )(
        prefix, x, scales, gain, *tables, logs, ffn_gains, mid, dz_own, dz_oth, wo, wo_from, wq, wk, wv, qkv,
        a_own, a_oth, wdown, n1, o_own, o_oth, down, gate, up,
    )


def last_spread(values, meanwhile):
    count = lax.axis_size("dp")
    half = values.shape[0] // 2
    size, sides, halves = half // 2, [], []
    for way, bit in enumerate((0, count.bit_length() - 2)):
        sides.append((lax.axis_index("dp") >> bit) & 1)
        own = lax.dynamic_slice_in_dim(values, way * half + sides[-1] * size, size, 0)
        halves.append((own, lax.ppermute(own, "dp", [(i, i ^ (1 << bit)) for i in range(count)])))
    halves, meanwhile = lax.optimization_barrier((halves, meanwhile))
    pieces = []
    for side, (own, got) in zip(sides, halves):
        pieces += [jnp.where(side == 0, own, got), jnp.where(side == 0, got, own)]
    return jnp.concatenate([piece.astype(F32) for piece in pieces]), meanwhile


def body(
    hidden_in,
    attn_gain,
    ffn_gain,
    query_weight,
    key_weight,
    value_weight,
    output_weight,
    gate_weight,
    up_weight,
    down_weight,
    prefix_len,
    out_grad,
):
    col_count, row_count = lax.axis_size("col"), lax.axis_size("row")
    batches, tokens, _ = hidden_in.shape
    length = tokens * row_count
    heads = query_weight.shape[1] // HEAD_DIM // col_count
    row_kv = key_weight.shape[1] // HEAD_DIM
    shared_kv = row_kv < col_count
    q_width = heads * HEAD_DIM
    prefix_row = prefix_len.reshape(1, batches)
    (
        cosine, signed, n1, n2, g_own, qkv, logs, o_own, o_oth, middle, scales, out_from,
        a_own, a_oth, dg_own, dg_oth, du_own, du_oth, first_result,
    ) = forward(
        prefix_row, hidden_in, attn_gain.reshape(1, -1), ffn_gain.reshape(1, -1), out_grad,
        query_weight, key_weight, value_weight, output_weight, gate_weight, up_weight, down_weight,
        row_count, heads, shared_kv,
    )

    def flat(*items):
        return tuple(item.reshape(batches * length, item.shape[-1]) for item in items)

    dp_count = lax.axis_size("dp")
    a_own, a_oth, *grads = flat(a_own, a_oth, dg_own, dg_oth, du_own, du_oth)
    dz, dz_oth, middle_grad, down_sum, gate_sum, up_sum, ffn_gains = unit_grads(
        middle, scales, out_grad, ffn_gain.reshape(1, -1), *flat(g_own, n2), (a_own, a_oth, *grads),
        gate_weight, up_weight, row_count, dp_count,
    )
    in_grad, last_result, qkv_sum, output_sum, down_sum, gate_sum, up_sum, gains = backward(
        prefix_row, hidden_in, scales, attn_gain.reshape(1, -1), (cosine, signed), logs, ffn_gains,
        middle, dz, dz_oth, output_weight, out_from, query_weight, key_weight, value_weight, qkv, a_own, a_oth, down_weight,
        *flat(n1, o_own, o_oth), down_sum, gate_sum, up_sum, heads, shared_kv, dp_count,
    )
    result = jnp.stack([first_result, last_result])
    width = q_width + 2 * HEAD_DIM

    def columns(first, size, shared):
        pieces = [
            qkv_sum[:, side * width + first : side * width + first + size].astype(F32)
            for side in range(col_count)
        ]
        return sum(pieces) if shared else jnp.concatenate(pieces, axis=1)

    gain_one, gain_two = gains[:batches].sum(axis=0), gains[batches : 2 * batches].sum(axis=0)
    meanwhile = (
        result,
        middle_grad + in_grad,
        gain_one,
        gain_two,
        columns(0, q_width, False),
        columns(q_width, HEAD_DIM, shared_kv),
        columns(q_width + HEAD_DIM, HEAD_DIM, shared_kv),
        output_sum.astype(F32),
        gate_sum.astype(F32),
        down_sum.astype(F32),
    )
    up_sum, (*first, down_sum) = last_spread(up_sum, meanwhile)
    return (*first, up_sum, down_sum)


def solution(mesh):
    return jax.shard_map(
        body,
        mesh=mesh,
        in_specs=(
            P(None, ("dp", "row"), "col"),
            P("col"),
            P("col"),
            P("col", "row"),
            P("col", "row"),
            P("col", "row"),
            P("row", "col"),
            P("col", "row"),
            P("col", "row"),
            P("row", "col"),
            P(None, "dp"),
            P(None, ("dp", "row"), "col"),
        ),
        out_specs=(
            P(None, ("dp", "row"), "col"),
            P(None, ("dp", "row"), "col"),
            P("col"),
            P("col"),
            P("col", "row"),
            P("col", "row"),
            P("col", "row"),
            P("row", "col"),
            P("col", "row"),
            P("col", "row"),
            P("row", "col"),
        ),
        check_vma=False,
    )
```

```python
import functools
import math

import jax
import jax.numpy as jnp
from jax import lax
from jax.experimental import pallas as pl
from jax.experimental.pallas import tpu as pltpu
from jax.sharding import PartitionSpec as P

WIDTH = 2048
HEADS = 16
KV_HEADS = 8
HEAD_DIM = 128
PREFIX_TOP = 512

epsilon = 1e-05
rope_base = 1000000.0
scale = 1.0 / math.sqrt(HEAD_DIM)
MIB = 1 << 20
F32 = jnp.float32
BF16 = jnp.bfloat16

NT = (((1,), (1,)), ((), ()))
NN = (((1,), (0,)), ((), ()))
TN = (((0,), (0,)), ((), ()))


def dot(left_side, right_side, dims):
    return lax.dot_general(left_side, right_side, dims, preferred_element_type=F32)


def params(mib, grid_rank):
    return pltpu.CompilerParams(
        dimension_semantics=("arbitrary",) * grid_rank, vmem_limit_bytes=mib * MIB
    )


def cost(flops, nbytes, exps=0):
    return pl.CostEstimate(flops=int(flops), bytes_accessed=int(nbytes), transcendentals=int(exps))


def whole(shape):
    return pl.BlockSpec(shape, lambda *_: (0,) * len(shape))


def rope_tables(first, rows):
    half_size = HEAD_DIM // 2
    lane = lax.broadcasted_iota(jnp.int32, (rows, HEAD_DIM), 1)
    inverse = jnp.exp((lane & (half_size - 1)).astype(F32) * (-math.log(rope_base) / half_size))
    angle = (lax.broadcasted_iota(jnp.int32, (rows, HEAD_DIM), 0) + first).astype(F32) * inverse
    sine = jnp.sin(angle)
    return jnp.cos(angle), jnp.where(lane < half_size, -sine, sine)


def rope(values, cosine, signed):
    return values * cosine + pltpu.roll(values, HEAD_DIM // 2, 1) * signed


def rope_back(values, cosine, signed):
    return values * cosine - pltpu.roll(values, HEAD_DIM // 2, 1) * signed


class Line:
    def __init__(self, n):
        self.n = n
        self.r = lax.axis_index("row")
        self.c = lax.axis_index("col")
        self.d = lax.axis_index("dp")

    def copy(self, src, dst, send, recv, **where):
        return pltpu.make_async_remote_copy(
            src_ref=src, dst_ref=dst, send_sem=send, recv_sem=recv, device_id=where,
            device_id_type=pl.DeviceIdType.MESH,
        )

    def up(self, src, dst, send, recv):
        return self.copy(src, dst, send, recv, row=self.r + 1)

    def down(self, src, dst, send, recv):
        return self.copy(src, dst, send, recv, row=self.r - 1)

    def across(self, src, dst, send, recv):
        return self.copy(src, dst, send, recv, col=1 - self.c)

    def barrier(self, core=True, bits=()):
        barrier = pltpu.get_barrier_semaphore()

        def signal(**where):
            pl.semaphore_signal(
                barrier, inc=1, device_id=where, device_id_type=pl.DeviceIdType.MESH
            )

        @pl.when(self.r > 0)
        def _():
            signal(row=self.r - 1)

        @pl.when(self.r < self.n - 1)
        def _():
            signal(row=self.r + 1)

        if core:
            signal(col=1 - self.c)
        for bit in bits:
            signal(dp=self.partner(bit))
        at_end = (self.r == 0) | (self.r == self.n - 1)
        others = int(core) + len(bits)

        @pl.when(at_end)
        def _():
            pl.semaphore_wait(barrier, 1 + others)

        @pl.when(jnp.logical_not(at_end))
        def _():
            pl.semaphore_wait(barrier, 2 + others)

    def wide_barrier(self, dp_count):
        barrier = pltpu.get_barrier_semaphore()
        peers = [dict(row=(self.r + at) % self.n) for at in range(1, self.n)]
        peers += [dict(dp=(self.d + at) % dp_count) for at in range(1, dp_count)]
        peers += [dict(col=1 - self.c)]
        for where in peers:
            pl.semaphore_signal(
                barrier, inc=1, device_id=where, device_id_type=pl.DeviceIdType.MESH
            )
        pl.semaphore_wait(barrier, len(peers))

    def side(self, bit):
        return (self.d // 2**bit) % 2

    def partner(self, bit):
        return self.d + (1 - 2 * self.side(bit)) * 2**bit

    def nearest(self, k):
        n = self.n
        code = 0
        for r in range(n):
            order = sorted(range(n), key=lambda q: (abs(q - r), q))
            code += order[k] * n**r
        place, result = self.r * 0 + code, 0
        for r in range(n):
            result = result + (place // n**r) % n * (1 - jnp.minimum(jnp.abs(self.r - r), 1))
        return result


class Gather:
    def __init__(self, line, own, oth, sends, recvs, first=None):
        self.line, self.own, self.oth, self.sends, self.recvs = line, own, oth, sends, recvs
        self.first = own.at[line.r] if first is None else first

    def hop(self, kind, q, src=None):
        way = (self.line.up, self.line.down)[kind]
        src = self.own.at[q] if src is None else src
        return way(src, self.own.at[q], self.sends.at[q, kind], self.recvs.at[q, 0])

    def cross(self, q, src=None):
        src = self.own.at[q] if src is None else src
        return self.line.across(src, self.oth.at[q], self.sends.at[q, 2], self.recvs.at[q, 1])

    def start(self):
        line = self.line

        @pl.when(line.r < line.n - 1)
        def _():
            self.hop(0, line.r, self.first).start()

        @pl.when(line.r > 0)
        def _():
            self.hop(1, line.r, self.first).start()

        self.cross(line.r, self.first).start()

    def step(self, s):
        line = self.line
        low, high = line.r - s, line.r + s

        @pl.when(low >= 0)
        def _():
            self.hop(0, low).wait_recv()

            @pl.when(line.r < line.n - 1)
            def _():
                self.hop(0, low).start()

            self.cross(low).start()

        @pl.when(high <= line.n - 1)
        def _():
            self.hop(1, high).wait_recv()

            @pl.when(line.r > 0)
            def _():
                self.hop(1, high).start()

            self.cross(high).start()

    def arrive(self, q):
        self.cross(q).wait_recv()

    def drain(self):
        line = self.line
        for q in range(line.n):

            @pl.when((line.r >= q) & (line.r < line.n - 1))
            def _(q=q):
                self.hop(0, q).wait_send()

            @pl.when((line.r <= q) & (line.r > 0))
            def _(q=q):
                self.hop(1, q).wait_send()

            self.cross(q).wait_send()


class Scatter:
    def __init__(self, line, part, ups, downs, sends, recvs):
        self.line, self.part, self.ups, self.downs = line, part, ups, downs
        self.sends, self.recvs = sends, recvs

    def hop(self, kind, s, target):
        way = (self.line.up, self.line.down)[kind]
        box = (self.ups, self.downs)[kind]
        return way(
            self.part.at[target], box.at[s - 1], self.sends.at[kind, s - 1], self.recvs.at[kind, s - 1]
        )

    def step(self, s):
        line = self.line
        for kind in range(2):
            behind = line.r if kind == 0 else line.n - 1 - line.r
            target = line.r + line.n - s if kind == 0 else line.r - (line.n - s)
            box = (self.ups, self.downs)[kind]

            @pl.when(behind <= s - 1)
            def _(kind=kind, behind=behind, target=target, box=box):
                if s > 1:

                    @pl.when(behind >= 1)
                    def _():
                        self.hop(kind, s - 1, target).wait_recv()
                        self.part[target] = (
                            self.part[target].astype(F32) + box[s - 2].astype(F32)
                        ).astype(BF16)

                self.hop(kind, s, target).start()

    def total(self, out):
        out[...] = self.part[self.line.r].astype(F32)
        self.add_received(out)

    def add_received(self, out):
        line = self.line
        last = line.n - 1

        @pl.when(line.r >= 1)
        def _():
            self.hop(0, last, line.r).wait_recv()
            out[...] += self.ups[last - 1].astype(F32)

        @pl.when(line.r <= last - 1)
        def _():
            self.hop(1, last, line.r).wait_recv()
            out[...] += self.downs[last - 1].astype(F32)

    def drain(self):
        line = self.line
        for s in range(1, line.n):

            @pl.when(line.r <= s - 1)
            def _(s=s):
                self.hop(0, s, line.r + line.n - s).wait_send()

            @pl.when(line.n - 1 - line.r <= s - 1)
            def _(s=s):
                self.hop(1, s, line.r - (line.n - s)).wait_send()


class Everywhere:
    def __init__(self, line, axis, place, count, ref, boxes, sends, recvs):
        self.line, self.axis, self.place, self.count = line, axis, place, count
        self.ref, self.boxes, self.sends, self.recvs = ref, boxes, sends, recvs

    def copy(self, at):
        return self.line.copy(
            self.ref, self.boxes.at[at - 1], self.sends.at[at - 1], self.recvs.at[at - 1],
            **{self.axis: (self.place + at) % self.count},
        )

    def start(self):
        for at in range(1, self.count):
            self.copy(at).start()

    def total(self):
        value = self.ref[...]
        for at in range(1, self.count):
            self.copy(at).wait_recv()
            value = value + self.boxes[at - 1]
        return value

    def drain(self):
        for at in range(1, self.count):
            self.copy(at).wait_send()


def levels_of(line, rows, bits):
    low, size, levels = 0, rows, []
    for bit in bits:
        size //= 2
        keep = low + line.side(bit) * size
        levels.append((size, keep, low + (1 - line.side(bit)) * size))
        low = keep
    return levels


def rows_of(at, size):
    return pl.ds(pl.multiple_of(at, 16), size)


class Reduce:
    def __init__(self, line, ref, boxes, bits, sends, recvs):
        self.line, self.ref, self.boxes, self.bits = line, ref, boxes, bits
        self.sends, self.recvs = sends, recvs
        self.levels = levels_of(line, ref.shape[0], bits)

    def copy(self, at):
        size, _, give = self.levels[at]
        return self.line.copy(
            self.ref.at[rows_of(give, size), :], self.boxes[at], self.sends.at[at], self.recvs.at[at],
            dp=self.line.partner(self.bits[at]),
        )

    def step(self, at, out=None):
        if at > 0:
            self.copy(at - 1).wait_recv()
            size, keep, _ = self.levels[at - 1]
            rows = rows_of(keep, size)
            kept = self.ref[rows, :].astype(F32) + self.boxes[at - 1][...].astype(F32)
            (self.ref if out is None else out)[rows, :] = kept.astype(BF16)
        if at < len(self.bits):
            self.copy(at).start()

    def kept(self):
        size, keep, _ = self.levels[-1]
        return rows_of(keep, size)

    def drain(self):
        for at in range(len(self.bits)):
            self.copy(at).wait_send()


class Spread:
    def __init__(self, line, ref, bits, sends, recvs, skip=0):
        self.line, self.ref, self.bits, self.sends, self.recvs = line, ref, bits, sends, recvs
        self.count = len(bits) - skip
        self.levels = levels_of(line, ref.shape[0], bits)

    def copy(self, at):
        level = len(self.bits) - 1 - at
        size, keep, _ = self.levels[level]
        part = self.ref.at[rows_of(keep, size), :]
        return self.line.copy(
            part, part, self.sends.at[at], self.recvs.at[at], dp=self.line.partner(self.bits[level])
        )

    def step(self, at):
        if 0 < at <= self.count:
            self.copy(at - 1).wait_recv()
        if at < self.count:
            self.copy(at).start()

    def drain(self):
        for at in range(self.count):
            self.copy(at).wait_send()


def two_ways(ref, bits):
    half = ref.shape[0] // 2
    return [(ref.at[pl.ds(at * half, half), :], bits if at == 0 else bits[::-1]) for at in range(2)]


def communicate(number, mib):
    return pltpu.CompilerParams(
        collective_id=number, has_side_effects=True, vmem_limit_bytes=mib * MIB
    )


def forward_kernel(
    n, heads, shared_kv,
    prefix_ref, x_ref, gain_one, gain_two,
    grad_in, wq, wk, wv, wo, wgate, wup, wdown,
    cos_out, sin_out, n1_out, n2_out, g_out, qkv_out, log_out, o_own_out, o_oth_out, mid_out, scale_out, wo_from,
    a_own_out, a_oth_out, dg_own_out, dg_oth_out, du_own_out, du_oth_out, result_out,
    n_own, n_oth, g_own, g_oth, w_own, w_from, wo_ref, wg_ref, wu_ref, wd_ref, wd_oth, a_ref,
    cos_ref, sin_ref, qkv_ref, vt_ref, o_own, o_oth, log_ref, part, ups, downs, total, scales, row_out, row_in, stage,
    gather_sends, gather_recvs, scatter_sends, scatter_recvs, cross_sends, cross_recvs, local_sems,
    unit_sends, unit_recvs, unit_stores, down_sends, down_recvs, a_sems,
):
    batches, tokens, depth = x_ref.shape
    length = n * tokens
    line = Line(n)
    r, c = line.r, line.c
    q_width = heads * HEAD_DIM
    k_col, v_col = q_width, q_width + HEAD_DIM
    share = wgate.shape[1] // 2
    kv_own = 0 if shared_kv else c * HEAD_DIM
    kv_oth = 0 if shared_kv else (1 - c) * HEAD_DIM

    def lanes(at, size):
        return pl.ds(pl.multiple_of(at, 128), size)

    def rows_at(at, size):
        return pl.ds(pl.multiple_of(at, size), size)

    local_count, cross_count = [0], [0]

    def local(src, dst):
        copy = pltpu.make_async_copy(src, dst, local_sems.at[local_count[0]])
        local_count[0] += 1
        copy.start()
        return copy

    def cross(src, dst):
        at = cross_count[0]
        cross_count[0] += 1
        return line.across(src, dst, cross_sends.at[at], cross_recvs.at[at])

    loads = [
        local(wq.at[:, lanes(c * q_width, q_width)], w_own.at[:, pl.ds(0, q_width)]),
        local(wk.at[:, lanes(kv_own, HEAD_DIM)], w_own.at[:, pl.ds(k_col, HEAD_DIM)]),
        local(wv.at[:, lanes(kv_own, HEAD_DIM)], w_own.at[:, pl.ds(v_col, HEAD_DIM)]),
    ]
    wo_load = local(wo, wo_ref)
    g_loads = [local(grad_in.at[m], g_own.at[m, r]) for m in range(batches)]
    unit_loads = [
        local(wgate.at[:, lanes(c * share, share)], wg_ref.at[0]),
        local(wup.at[:, lanes(c * share, share)], wu_ref.at[0]),
        local(wdown.at[rows_at(c * share, share), :], wd_ref.at[0]),
        local(wdown.at[rows_at((1 - c) * share, share), :], wd_oth),
    ]
    for m in range(batches):
        x = x_ref[m].astype(F32)
        squares = jnp.sum(x * x, axis=1, keepdims=True)
        row_out[0, m] = jnp.broadcast_to(squares, (tokens, 128))
    line.barrier()

    def row_cross(which, m):
        return cross(row_out.at[which, m], row_in.at[which, m])

    def norm_scale(which, m, copy):
        copy.wait_recv()
        squares = row_out[which, m] + row_in[which, m]
        value = lax.rsqrt(squares * (1.0 / WIDTH) + epsilon)
        scales[which, m] = value
        return value[:, :1]

    crosses = [row_cross(0, m) for m in range(batches)]
    for copy in crosses:
        copy.start()
    w_cross = [
        cross(wq.at[:, lanes((1 - c) * q_width, q_width)], w_from.at[:, pl.ds(0, q_width)]),
        cross(wk.at[:, lanes(kv_oth, HEAD_DIM)], w_from.at[:, pl.ds(k_col, HEAD_DIM)]),
        cross(wv.at[:, lanes(kv_oth, HEAD_DIM)], w_from.at[:, pl.ds(v_col, HEAD_DIM)]),
    ]
    gathers = [
        [
            Gather(line, own.at[m], oth.at[m], gather_sends.at[at, m], gather_recvs.at[at, m])
            for m in range(batches)
        ]
        for at, (own, oth) in enumerate(((n_own, n_oth), (g_own, g_oth), (n_own, n_oth)))
    ]
    n1, g, n2 = gathers
    rs = [
        Scatter(line, part.at[m], ups.at[m], downs.at[m], scatter_sends.at[m], scatter_recvs.at[m])
        for m in range(batches)
    ]
    for m in range(batches):
        scale_one = norm_scale(0, m, crosses[m])
        n_own[m, r] = (x_ref[m].astype(F32) * scale_one * gain_one[...]).astype(BF16)
        if m == 0:
            n1[0].start()
            for copy in w_cross:
                copy.start()

    @pl.loop(0, n)
    def _(p):
        rows = rows_at(p * tokens, tokens)
        cos_ref[rows, :], sin_ref[rows, :] = rope_tables(p * tokens, tokens)

    for copy in loads:
        copy.wait()
    for copy in w_cross:
        copy.wait_recv()

    def project(m, q):
        n1[m].arrive(q)
        rows = rows_at(q * tokens, tokens)
        pre = dot(n_own[m, q], w_own[...], NN) + dot(n_oth[m, q], w_from[...], NN)
        cosine, signed = cos_ref[rows, :], sin_ref[rows, :]
        for head in range(heads + 1):
            piece = pre[:, head * HEAD_DIM : (head + 1) * HEAD_DIM]
            qkv_ref[m, rows, pl.ds(head * HEAD_DIM, HEAD_DIM)] = rope(piece, cosine, signed).astype(BF16)
        values = pre[:, v_col : v_col + HEAD_DIM].astype(BF16)
        qkv_ref[m, rows, pl.ds(v_col, HEAD_DIM)] = values
        vt_ref[m, :, rows] = values.T

    block = min(256, length)
    count = length // block

    def attend_block(m, index):
        first = index * block
        extent = min(length, max(first + block, PREFIX_TOP))
        keys = qkv_ref[m, pl.ds(0, extent), pl.ds(k_col, HEAD_DIM)]
        key_at = lax.broadcasted_iota(jnp.int32, (extent, block), 0)
        query_at = lax.broadcasted_iota(jnp.int32, (extent, block), 1) + first
        allowed = (key_at <= query_at) | (key_at < prefix_ref[:, pl.ds(m, 1)])
        for head in range(heads):
            cols = pl.ds(head * HEAD_DIM, HEAD_DIM)
            query = qkv_ref[m, pl.ds(first, block), cols]
            scores = jnp.where(allowed, dot(keys, query, NT) * scale, -1e30)
            topmost = jnp.max(scores, axis=0, keepdims=True)
            exponent = jnp.exp(scores - topmost)
            summed = jnp.sum(exponent, axis=0, keepdims=True)
            weights = (exponent * (1.0 / summed)).astype(BF16)
            result = dot(vt_ref[m, :, pl.ds(0, extent)], weights, NN)
            o_own[m, pl.ds(first, block), cols] = result.T.astype(BF16)
            log_ref[m, pl.ds(head, 1), pl.ds(first, block)] = topmost + jnp.log(summed)

    def project_out(m):
        own_rows, oth_rows = rows_at(c * q_width, q_width), rows_at((1 - c) * q_width, q_width)

        @pl.loop(0, n)
        def _(p):
            rows = rows_at(p * tokens, tokens)
            value = dot(o_own[m, rows, :], wo_ref[own_rows, :], NN)
            value = value + dot(o_oth[m, rows, :], wo_ref[oth_rows, :], NN)
            part[m, p] = value.astype(BF16)

    def walk(m, first, last):
        for k in range(first, last):
            n1[m].step(k)
            project(m, line.nearest(k))

    def release(m, store):
        store.wait()
        n1[m].drain()

    def middle(m):
        rs[m].total(total.at[m])
        total[m] = total[m] + x_ref[m].astype(F32)
        mid = total[m]
        squares = jnp.sum(mid * mid, axis=1, keepdims=True)
        row_out[1, m] = jnp.broadcast_to(squares, (tokens, 128))
        copy = row_cross(1, m)
        copy.start()
        scale_two = norm_scale(1, m, copy)
        n_own[m, r] = (total[m] * scale_two * gain_two[...]).astype(BF16)
        crosses.append(copy)
        n2[m].start()

    outs = ((a_own_out, a_oth_out), (dg_own_out, dg_oth_out), (du_own_out, du_oth_out))
    order = [(m, k) for m in range(batches) for k in range(n)]

    def unit_away(at, kind):
        m, k = order[at]
        return line.across(
            stage.at[at % 2, kind], outs[kind][1].at[m, line.nearest(k)],
            unit_sends.at[at, kind], unit_recvs.at[at, kind],
        )

    def unit_kept(at, kind):
        m, k = order[at]
        return pltpu.make_async_copy(
            stage.at[at % 2, kind], outs[kind][0].at[m, line.nearest(k)], unit_stores.at[at, kind]
        )

    left = set()

    def unit_wait(at):
        if at in left:
            left.remove(at)
            for kind in range(3):
                unit_away(at, kind).wait_send()
                unit_kept(at, kind).wait()

    def units(at):
        m, k = order[at]
        q = line.nearest(k)
        n2[m].arrive(q)
        g[m].arrive(q)
        if at >= 2:
            unit_wait(at - 2)
        slot = at % 2
        size = min(256, share)

        @pl.loop(0, share // size)
        def _(b):
            cols = rows_at(b * size, size)
            gate = dot(n_own[m, q], wg_ref[0, :, cols], NN) + dot(n_oth[m, q], wg_ref[1, :, cols], NN)
            up = dot(n_own[m, q], wu_ref[0, :, cols], NN) + dot(n_oth[m, q], wu_ref[1, :, cols], NN)
            da = dot(g_own[m, q], wd_ref[0, cols, :], NT) + dot(g_oth[m, q], wd_ref[1, cols, :], NT)
            sigmoid = 1.0 / (1.0 + jnp.exp(-gate))
            silu = gate * sigmoid
            stage[slot, 0, :, cols] = (silu * up).astype(BF16)
            stage[slot, 1, :, cols] = (da * up * sigmoid * (1.0 + gate * (1.0 - sigmoid))).astype(BF16)
            stage[slot, 2, :, cols] = (da * silu).astype(BF16)

        left.add(at)
        for kind in range(3):
            unit_away(at, kind).start()
            unit_kept(at, kind).start()

    down_rs = Scatter(line, part.at[0], ups.at[0], downs.at[0], down_sends, down_recvs)

    def down_project():
        for k in range(n):
            unit_wait(k)
            unit_away(k, 0).wait_recv()
        rs[0].drain()

        for p in range(n):
            a_loads = [
                pltpu.make_async_copy(src.at[0, p], a_ref.at[side], a_sems.at[side])
                for side, src in enumerate((a_own_out, a_oth_out))
            ]
            for copy in a_loads:
                copy.start()
            for copy in a_loads:
                copy.wait()
            value = dot(a_ref[0], wd_ref[0], NN) + dot(a_ref[1], wd_oth[...], NN)
            part[0, p] = value.astype(BF16)

    half = (n + 1) // 2
    o_cross = [cross(o_own.at[m], o_oth.at[m]) for m in range(batches)]
    stores = []

    project(0, r)
    walk(0, 1, n - 1)
    n1[1].start()
    walk(0, n - 1, n)
    n1_stores = [local(n_own.at[0], n1_out.at[0])]
    project(1, r)
    for index in range(count // 2):
        attend_block(0, index)
    walk(1, 1, half)
    for index in range(count // 2, count):
        attend_block(0, index)
    o_cross[0].start()
    big_cross = [
        cross(wgate.at[:, lanes((1 - c) * share, share)], wg_ref.at[1]),
        cross(wup.at[:, lanes((1 - c) * share, share)], wu_ref.at[1]),
        cross(wdown.at[rows_at((1 - c) * share, share), :], wd_ref.at[1]),
        cross(wo.at[rows_at((1 - c) * q_width, q_width), :], wo_from),
    ]
    walk(1, half, n - 1)
    o_cross[0].wait_recv()
    wo_load.wait()
    project_out(0)
    rs[0].step(1)
    g_loads[0].wait()
    g[0].start()
    walk(1, n - 1, n)
    n1_stores.append(local(n_own.at[1], n1_out.at[1]))
    for copy in big_cross:
        copy.start()
    for index in range(count // 2):
        attend_block(1, index)
    for s in range(2, half + 1):
        rs[0].step(s)
    for index in range(count // 2, count):
        attend_block(1, index)
    o_cross[1].start()
    for k in range(1, half):
        g[0].step(k)
    release(0, n1_stores[0])
    for s in range(half + 1, n):
        rs[0].step(s)
    o_cross[1].wait_recv()
    project_out(1)
    rs[1].step(1)
    for k in range(half, n - 1):
        g[0].step(k)
    middle(0)
    release(1, n1_stores[1])
    for s in range(2, half + 1):
        rs[1].step(s)
    g[0].step(n - 1)
    for copy in unit_loads:
        copy.wait()
    for copy in big_cross:
        copy.wait_recv()
    g_loads[1].wait()
    stores += [local(g_own.at[0], g_out.at[0])]
    stores += [local(qkv_ref, qkv_out), local(log_ref, log_out)]
    stores += [local(cos_ref, cos_out), local(sin_ref, sin_out)]
    stores += [local(o_own, o_own_out), local(o_oth, o_oth_out)]
    mid_store = local(total.at[0], mid_out.at[0])
    units(0)
    for k in range(1, half):
        n2[0].step(k)
        units(k)
    for s in range(half + 1, n):
        rs[1].step(s)
    for k in range(half, n - 1):
        n2[0].step(k)
    g[1].start()
    for k in range(half, n - 1):
        units(k)
    middle(1)
    stores.append(local(total.at[1], mid_out.at[1]))
    stores.append(local(scales, scale_out))
    n2[0].step(n - 1)
    units(n - 1)
    down_project()
    down_rs.step(1)
    units(n)
    for k in range(1, n):
        g[1].step(k)
        n2[1].step(k)
        if k + 1 < n:
            down_rs.step(k + 1)
        units(n + k)
    stores += [local(g_own.at[1], g_out.at[1]), local(n_own, n2_out)]
    mid_store.wait()
    total[0] = total[0] + part[0, r].astype(F32)
    down_rs.add_received(total.at[0])
    part[0, r] = total[0].astype(BF16)
    stores.append(local(part.at[0, r], result_out))
    for at in range(2 * n):
        unit_wait(at)
        for kind in range(3):
            if at >= n or kind > 0:
                unit_away(at, kind).wait_recv()
    for copy in crosses + w_cross + o_cross + big_cross:
        copy.wait_send()
    for item in g + n2 + rs[1:] + [down_rs]:
        item.drain()
    for copy in stores:
        copy.wait()


def forward(
    prefix, x, gain_one, gain_two, grad_in, wq, wk, wv, wo, wgate, wup, wdown, n, heads, shared_kv
):
    batches, tokens, depth = x.shape
    length = n * tokens
    width = (heads + 2) * HEAD_DIM
    q_width = heads * HEAD_DIM
    share = wgate.shape[1] // 2
    vmem = pl.BlockSpec(memory_space=pltpu.VMEM)
    anywhere = pl.BlockSpec(memory_space=pl.ANY)
    gathered, units = (batches, n, tokens, depth), (batches, n, tokens, share)
    rows = (2, batches, tokens, 128)
    table = (length, HEAD_DIM)
    shapes = [
        (table, F32), (table, F32), (gathered, BF16), (gathered, BF16), (gathered, BF16),
        ((batches, length, width), BF16), ((batches, 8, length), F32),
        ((batches, length, q_width), BF16), ((batches, length, q_width), BF16),
        ((batches, tokens, depth), F32), (rows, F32), ((q_width, depth), BF16),
    ] + [(units, BF16)] * 6 + [((tokens, depth), BF16)]
    boxes = (batches, n - 1, tokens, depth)
    dma = pltpu.SemaphoreType.DMA
    return pl.pallas_call(
        functools.partial(forward_kernel, n, heads, shared_kv),
        in_specs=[vmem] * 4 + [anywhere] * 8,
        out_specs=[anywhere] * len(shapes),
        out_shape=[jax.ShapeDtypeStruct(*item) for item in shapes],
        scratch_shapes=[
            pltpu.VMEM(gathered, BF16), pltpu.VMEM(gathered, BF16),
            pltpu.VMEM(gathered, BF16), pltpu.VMEM(gathered, BF16),
            pltpu.VMEM((depth, width), BF16), pltpu.VMEM((depth, width), BF16),
            pltpu.VMEM(wo.shape, BF16),
            pltpu.VMEM((2, depth, share), BF16), pltpu.VMEM((2, depth, share), BF16),
            pltpu.VMEM((2, share, depth), BF16), pltpu.VMEM((share, depth), BF16),
            pltpu.VMEM((2, tokens, share), BF16), pltpu.VMEM(table, F32), pltpu.VMEM(table, F32),
            pltpu.VMEM((batches, length, width), BF16),
            pltpu.VMEM((batches, HEAD_DIM, length), BF16),
            pltpu.VMEM((batches, length, q_width), BF16), pltpu.VMEM((batches, length, q_width), BF16),
            pltpu.VMEM((batches, 8, length), F32),
            pltpu.VMEM(gathered, BF16), pltpu.VMEM(boxes, BF16), pltpu.VMEM(boxes, BF16),
            pltpu.VMEM((batches, tokens, depth), F32),
            pltpu.VMEM(rows, F32), pltpu.VMEM(rows, F32), pltpu.VMEM(rows, F32),
            pltpu.VMEM((2, 3, tokens, share), BF16),
            dma((3, batches, n, 3)), dma((3, batches, n, 2)),
            dma((batches, 2, n - 1)), dma((batches, 2, n - 1)), dma((13,)), dma((13,)), dma((26,)),
            dma((batches * n, 3)), dma((batches * n, 3)), dma((batches * n, 3)),
            dma((2, n - 1)), dma((2, n - 1)), dma((2,)),
        ],
        compiler_params=communicate(1, 63),
        cost_estimate=cost(2e11, 100 * MIB),
    )(prefix, x, gain_one, gain_two, grad_in, wq, wk, wv, wo, wgate, wup, wdown)


def unit_grads_kernel(
    n, bits,
    mid_ref, scales_ref, top_ref, gain_ref,
    g_in, n2_in, a_own, a_oth, dg_own, dg_oth, du_own, du_oth, wgate, wup,
    dz_out, dz_oth_out, mgrad_out, down_out, gate_out, up_out, gain_out,
    wg_ref, wu_ref, unit_ref, part, ups, downs, total, dz_ref, row_out, row_in,
    shared_ref, moving_ref, down_ref, gate_ref, up_ref, boxes,
    load_sems, unit_sems, moving_sems, scatter_sends, scatter_recvs, gather_sends, gather_recvs,
    cross_sends, cross_recvs, store_sems, reduce_sends, reduce_recvs, part_sems,
):
    batches, tokens, depth = mid_ref.shape
    share = a_own.shape[1]
    line = Line(n)
    r, c = line.r, line.c
    loads = [
        pltpu.make_async_copy(a, b, load_sems.at[i])
        for i, (a, b) in enumerate(((wgate, wg_ref), (wup, wu_ref), (g_in, shared_ref)))
    ]
    order = [(m, p) for m in range(batches) for p in range(n)]

    def unit_loads(at):
        return [
            pltpu.make_async_copy(
                src.at[pl.ds(at * tokens, tokens), :], unit_ref.at[at % 2, i], unit_sems.at[at % 2, i]
            )
            for i, src in enumerate((dg_own, dg_oth, du_own, du_oth))
        ]

    width = min(256, share)
    nb = share // width
    kinds = ((a_own, a_oth), (dg_own, dg_oth), (du_own, du_oth))

    def moving(kind, index, go):
        for side in range(2):

            @pl.when(index // nb == side)
            def _(side=side):
                cols = pl.ds(pl.multiple_of((index - side * nb) * width, width), width)
                copy = pltpu.make_async_copy(
                    kinds[kind][side].at[:, cols], moving_ref.at[index % 2], moving_sems.at[index % 2]
                )
                copy.start() if go else copy.wait()

    moving(0, 0, True)
    for copy in loads[::-1] + unit_loads(0):
        copy.start()
    line.barrier(bits=bits)
    scatters = [
        Scatter(line, part.at[m], ups.at[m], downs.at[m], scatter_sends.at[m], scatter_recvs.at[m])
        for m in range(batches)
    ]
    gathers = [
        Gather(
            line, dz_out.at[m], dz_oth_out.at[m], gather_sends.at[m], gather_recvs.at[m], dz_ref.at[m]
        )
        for m in range(batches - 1)
    ]
    reduces = []
    for kind, ref in enumerate((down_ref, gate_ref, up_ref)):
        pair = [
            Reduce(
                line, view, [box.at[way] for box in boxes[kind]], way_bits,
                reduce_sends.at[kind, way], reduce_recvs.at[kind, way],
            )
            for way, (view, way_bits) in enumerate(two_ways(ref, bits))
        ]
        reduces.append(pair)
    cols_own = pl.ds(pl.multiple_of(c * share, share), share)
    cols_oth = pl.ds(pl.multiple_of((1 - c) * share, share), share)

    def unit_part(at):
        m, p = order[at]
        for copy in unit_loads(at):
            copy.wait()
        if at + 1 < len(order):
            for copy in unit_loads(at + 1):
                copy.start()
        slot = at % 2
        block = min(512, depth)

        @pl.loop(0, depth // block)
        def _(b):
            rows = pl.ds(pl.multiple_of(b * block, block), block)
            value = dot(unit_ref[slot, 0], wg_ref[rows, cols_own], NT)
            value = value + dot(unit_ref[slot, 1], wg_ref[rows, cols_oth], NT)
            value = value + dot(unit_ref[slot, 2], wu_ref[rows, cols_own], NT)
            value = value + dot(unit_ref[slot, 3], wu_ref[rows, cols_oth], NT)
            part[m, p, :, rows] = value.astype(BF16)

    def weight_grad(kind, first=0, last=2 * nb):
        @pl.loop(first, last)
        def _(index):
            moving(kind, index, False)

            @pl.when(index + 1 < 2 * nb)
            def _():
                moving(kind, index + 1, True)

            side = index // nb
            place = (c + side * (1 - 2 * c)) * nb + index - side * nb
            cols = pl.ds(pl.multiple_of(place * width, width), width)
            if kind == 0:
                down_ref[cols, :] = dot(moving_ref[index % 2], shared_ref[...], TN).astype(BF16)
            else:
                ref = gate_ref if kind == 1 else up_ref
                ref[:, cols] = dot(shared_ref[...], moving_ref[index % 2], TN).astype(BF16)

        if last == 2 * nb and kind + 1 < len(kinds):
            moving(kind + 1, 0, True)

    def row_cross(m):
        return line.across(row_out.at[m], row_in.at[m], cross_sends.at[m], cross_recvs.at[m])

    def store(which, m, src, dst):
        return pltpu.make_async_copy(src, dst, store_sems.at[which, m])

    def middle(m):
        scatters[m].total(total.at[m])
        s = scales_ref[1, m][:, :1]
        gain_out[pl.ds(m, 1), :] = jnp.sum(total[m] * mid_ref[m] * s, axis=0, keepdims=True)
        total[m] = total[m] * gain_ref[...]
        inner = jnp.sum(total[m] * mid_ref[m], axis=1, keepdims=True)
        row_out[m] = jnp.broadcast_to(inner, (tokens, 128))
        row_cross(m).start()
        row_cross(m).wait_recv()
        inner = row_out[m, :, pl.ds(0, 1)] + row_in[m, :, pl.ds(0, 1)]
        result = (
            top_ref[m].astype(F32) + total[m] * s - mid_ref[m] * ((s * s * s) * inner * (1.0 / WIDTH))
        )
        total[m] = result
        dz_ref[m] = result.astype(BF16)
        if m < len(gathers):
            gathers[m].start()
        store(0, m, total.at[m], mgrad_out.at[m]).start()
        store(1, m, dz_ref.at[m], dz_out.at[m, r]).start()

    def steps(item, first, last):
        for s in range(first, last):
            item.step(s)

    def reduce_step(kind, at):
        for item in reduces[kind]:
            item.step(at)

    half = (n + 1) // 2
    loads[2].wait()
    weight_grad(0, 0, nb)
    for way, item in enumerate(reduces[0]):

        @pl.when(c == way)
        def _(item=item):
            item.step(0)

    weight_grad(0, nb, 2 * nb)
    for way, item in enumerate(reduces[0]):

        @pl.when(c != way)
        def _(item=item):
            item.step(0)

    n2_load = pltpu.make_async_copy(n2_in, shared_ref, load_sems.at[3])
    n2_load.start()
    for copy in loads[:2]:
        copy.wait()
    for at in range(n):
        unit_part(at)
    scatters[0].step(1)
    n2_load.wait()
    weight_grad(1)
    reduce_step(1, 0)
    steps(scatters[0], 2, half + 1)
    reduce_step(0, 1)
    for at in range(n, 2 * n):
        unit_part(at)
    steps(scatters[0], half + 1, n)
    scatters[1].step(1)
    weight_grad(2)
    reduce_step(2, 0)
    middle(0)
    steps(scatters[1], 2, half + 1)
    reduce_step(1, 1)
    steps(gathers[0], 1, half)
    steps(scatters[1], half + 1, n)
    steps(gathers[0], half, n - 1)
    reduce_step(2, 1)
    middle(1)
    steps(gathers[0], n - 1, n)
    for at in range(2, len(bits)):
        for kind in range(3):
            reduce_step(kind, at)
    outs = (down_out, gate_out, up_out)
    kept_stores = []
    for kind in range(3):
        reduce_step(kind, len(bits))
        for way, item in enumerate(reduces[kind]):
            out_view = two_ways(outs[kind], bits)[way][0]
            rows = item.kept()
            copy = pltpu.make_async_copy(
                item.ref.at[rows, :], out_view.at[rows, :], part_sems.at[kind, way]
            )
            copy.start()
            kept_stores.append(copy)
    for item in gathers:
        for q in range(n):
            item.arrive(q)
        item.drain()
    for m in range(batches):
        scatters[m].drain()
        row_cross(m).wait_send()
        store(0, m, total.at[m], mgrad_out.at[m]).wait()
        store(1, m, dz_ref.at[m], dz_out.at[m, r]).wait()
    for pair in reduces:
        for item in pair:
            item.drain()
    for copy in kept_stores:
        copy.wait()


def unit_grads(mid, scales, top, gain, g, n2, halves, wgate, wup, n, dp_count):
    batches, tokens, depth = mid.shape
    rows, share = halves[0].shape
    bits = list(range(dp_count.bit_length() - 1))
    vmem = pl.BlockSpec(memory_space=pltpu.VMEM)
    anywhere = pl.BlockSpec(memory_space=pl.ANY)
    gathered = (batches, n, tokens, depth)
    down_dims, gate_dims = (2 * share, depth), (depth, 2 * share)
    dims = (down_dims, gate_dims, gate_dims)
    shapes = [(gathered, BF16), ((batches - 1,) + gathered[1:], BF16), (mid.shape, F32)]
    shapes += [(item, BF16) for item in dims] + [((8, depth), F32)]
    boxes = (batches, n - 1, tokens, depth)
    width = min(256, share)
    dma = pltpu.SemaphoreType.DMA
    return pl.pallas_call(
        functools.partial(unit_grads_kernel, n, bits),
        in_specs=[vmem] * 4 + [anywhere] * 10,
        out_specs=[anywhere] * 6 + [vmem],
        out_shape=[jax.ShapeDtypeStruct(*item) for item in shapes],
        scratch_shapes=[
            pltpu.VMEM(wgate.shape, BF16), pltpu.VMEM(wup.shape, BF16),
            pltpu.VMEM((2, 4, tokens, share), BF16), pltpu.VMEM(gathered, BF16),
            pltpu.VMEM(boxes, BF16), pltpu.VMEM(boxes, BF16), pltpu.VMEM(mid.shape, F32),
            pltpu.VMEM(mid.shape, BF16),
            pltpu.VMEM((batches, tokens, 128), F32), pltpu.VMEM((batches, tokens, 128), F32),
            pltpu.VMEM((rows, depth), BF16), pltpu.VMEM((2, rows, width), BF16),
            pltpu.VMEM(down_dims, BF16), pltpu.VMEM(gate_dims, BF16), pltpu.VMEM(gate_dims, BF16),
            [
                [pltpu.VMEM((2, item[0] // 2 ** (level + 2), item[1]), BF16) for level in range(len(bits))]
                for item in dims
            ],
            dma((4,)), dma((2, 4)), dma((2,)), dma((batches, 2, n - 1)), dma((batches, 2, n - 1)),
            dma((batches, n, 3)), dma((batches, n, 2)), dma((batches,)), dma((batches,)),
            dma((2, batches)), dma((3, 2, len(bits))), dma((3, 2, len(bits))), dma((3, 2)),
        ],
        compiler_params=communicate(2, 62),
        cost_estimate=cost(2e11, 100 * MIB),
    )(mid, scales, top, gain, g, n2, *halves, wgate, wup)


def backward_kernel(
    n, heads, shared_kv, bits,
    prefix_ref, x_ref, scales_ref, gain_in, cos_ref, sin_ref, log_ref, ffn_gains,
    mid_in, dz_own_in, dz_oth_in, wo, wo_from, wq, wk, wv, qkv_in, a_own_in, a_oth_in, wdown, n1_in,
    o_own_in, o_oth_in, down_in, gate_in, up_in,
    grad_out, result_out, qkv_out, o_out, down_out, gate_out, up_out, gain_out,
    dz_ref, dz_oth, dz_last, wo_ref, w_own, w_oth, qkv_ref, dk_ref, dv_ref, kt_ref, dqkv_own, dqkv_oth,
    part, ups, downs, total, a_ref, wide_ref, o_ref, qkv_grad, o_grad, qkv_sum, o_sum, boxes,
    row_out, row_in, result_ref, gain_ref, row_boxes, dp_boxes,
    load_sems, dz_sems, a_sems, scatter_sends, scatter_recvs, cross_sends, cross_recvs, store_sems,
    reduce_sends, reduce_recvs, spread_sends, spread_recvs, unit_sends, unit_recvs,
    gather_sends, gather_recvs, gain_sends, gain_recvs,
):
    batches, tokens, depth = x_ref.shape
    length = n * tokens
    share = a_own_in.shape[1]
    line = Line(n)
    r, c = line.r, line.c
    q_width = heads * HEAD_DIM
    k_col, v_col = q_width, q_width + HEAD_DIM
    width = v_col + HEAD_DIM

    def lanes(at, size):
        return pl.ds(pl.multiple_of(at, 128), size)

    def rows_at(at, size):
        return pl.ds(pl.multiple_of(at, size), size)

    def qkv_columns(side, dst):
        kv = 0 if shared_kv else side * HEAD_DIM
        return [
            (wq.at[:, lanes(side * q_width, q_width)], dst.at[:, pl.ds(0, q_width)]),
            (wk.at[:, lanes(kv, HEAD_DIM)], dst.at[:, pl.ds(k_col, HEAD_DIM)]),
            (wv.at[:, lanes(kv, HEAD_DIM)], dst.at[:, pl.ds(v_col, HEAD_DIM)]),
        ]

    pairs = [(wdown, wide_ref.at[pl.ds(0, 2 * share), :]), (qkv_in, qkv_ref)]
    pairs += [(wo.at[rows_at(c * q_width, q_width), :], wo_ref.at[0]), (wo_from, wo_ref.at[1])]
    last = batches - 1
    pairs += [(dz_own_in.at[m], dz_ref.at[m]) for m in range(last)]
    first = len(pairs)
    pairs += qkv_columns(c, w_own) + qkv_columns(1 - c, w_oth)
    pairs += [(o_own_in, o_ref.at[0]), (o_oth_in, o_ref.at[1])]
    pairs += [(mid_in.at[last], total.at[last])]
    loads = [pltpu.make_async_copy(a, b, load_sems.at[i]) for i, (a, b) in enumerate(pairs)]
    n1_load = pltpu.make_async_copy(n1_in, wide_ref.at[pl.ds(0, batches * length), :], load_sems.at[len(pairs)])
    shard_load = pltpu.make_async_copy(
        dz_own_in.at[last, r], dz_ref.at[last, r], load_sems.at[len(pairs) + 1]
    )
    order = [(m, p) for m in range(batches) for p in range(n)]

    def a_loads(at):
        rows = pl.ds(at * tokens, tokens)
        return [
            pltpu.make_async_copy(src.at[rows, :], a_ref.at[at % 2, side], a_sems.at[at % 2, side])
            for side, src in enumerate((a_own_in, a_oth_in))
        ]

    def dz_load(at):
        m, p = order[at]
        return pltpu.make_async_copy(dz_oth_in.at[m, p], dz_oth.at[at % 2], dz_sems.at[at % 2])

    for copy in [shard_load] + loads[:1] + a_loads(last * n) + loads[1:first] + [dz_load(0)] + loads[first:]:
        copy.start()
    dp_count = 2 ** len(bits)
    line.wide_barrier(dp_count)
    gains = [
        Everywhere(line, "row", r, n, gain_ref.at[0], row_boxes, gain_sends.at[0], gain_recvs.at[0]),
        Everywhere(line, "dp", line.d, dp_count, gain_ref.at[1], dp_boxes, gain_sends.at[1], gain_recvs.at[1]),
    ]
    gather = Gather(line, dz_ref.at[last], dz_last, gather_sends, gather_recvs)
    spreads = [
        Spread(
            line, view, way_bits, unit_sends.at[kind, way], unit_recvs.at[kind, way], skip=int(kind == 2)
        )
        for kind, ref in enumerate((down_out, gate_out, up_out))
        for way, (view, way_bits) in enumerate(two_ways(ref, bits))
    ]
    *head_rs, out_rs = (
        Scatter(
            line, part.at[at], ups.at[at], downs.at[at], scatter_sends.at[at], scatter_recvs.at[at]
        )
        for at in range(batches + 1)
    )
    reduces, gatherers = [], []
    for kind, (ref, result) in enumerate(((qkv_grad, qkv_sum), (o_grad, o_sum))):
        results = two_ways(result, bits)
        for way, (view, way_bits) in enumerate(two_ways(ref, bits)):
            reduces.append(
                Reduce(
                    line, view, [box.at[way] for box in boxes[kind]], way_bits,
                    reduce_sends.at[kind, way], reduce_recvs.at[kind, way],
                )
            )
            gatherers.append(
                Spread(
                    line, results[way][0], way_bits, spread_sends.at[kind, way], spread_recvs.at[kind, way]
                )
            )
    count = len(bits)

    def total_step(items, at):
        for item in items:
            if at <= count:
                reduces[item].step(at, gatherers[item].ref if at == count else None)
            if at >= count:
                gatherers[item].step(at - count)

    def spread_step(which, at):
        for kind in which:
            for item in spreads[2 * kind : 2 * kind + 2]:
                item.step(at)

    own_rows, oth_rows = rows_at(c * share, share), rows_at((1 - c) * share, share)

    def down_part(at):
        m, p = order[at]
        for copy in a_loads(at):
            copy.wait()
        if at + 1 < len(order):
            for copy in a_loads(at + 1):
                copy.start()
        value = dot(a_ref[at % 2, 0], wide_ref[own_rows, :], NN)
        part[batches, p] = (value + dot(a_ref[at % 2, 1], wide_ref[oth_rows, :], NN)).astype(BF16)

    def grad_cross(m):
        return line.across(dqkv_own.at[m], dqkv_oth.at[m], cross_sends.at[m], cross_recvs.at[m])

    def row_cross(m):
        at = batches + m
        return line.across(row_out.at[m], row_in.at[m], cross_sends.at[at], cross_recvs.at[at])

    def store(which, m, src, dst):
        return pltpu.make_async_copy(src, dst, store_sems.at[which, m])

    def attend_start(m):
        dk_ref[...] = jnp.zeros_like(dk_ref)
        dv_ref[...] = jnp.zeros_like(dv_ref)
        kt_ref[...] = qkv_ref[m, :, pl.ds(k_col, HEAD_DIM)].T

    def attend_back(m, q):
        at = m * n + q
        if m < last:
            dz_load(at).wait()
            if at + 1 < last * n:
                dz_load(at + 1).start()
        else:
            gather.arrive(q)
        other = dz_oth[at % 2] if m < last else dz_last[q]
        rows = pl.ds(q * tokens, tokens)
        grads = dot(dz_ref[m, q], wo_ref[0], NT)
        grads = (grads + dot(other, wo_ref[1], NT)).astype(BF16)
        cosine, signed = cos_ref[rows, :], sin_ref[rows, :]
        extent = min(length, max((q + 1) * tokens, PREFIX_TOP))
        upto = pl.ds(0, extent)
        keys = qkv_ref[m, upto, pl.ds(k_col, HEAD_DIM)]
        values = qkv_ref[m, upto, pl.ds(v_col, HEAD_DIM)]
        key_at = lax.broadcasted_iota(jnp.int32, (extent, tokens), 0)
        query_at = lax.broadcasted_iota(jnp.int32, (extent, tokens), 1) + q * tokens
        allowed = (key_at <= query_at) | (key_at < prefix_ref[:, pl.ds(m, 1)])
        for head in range(heads):
            cols = pl.ds(head * HEAD_DIM, HEAD_DIM)
            query = qkv_ref[m, rows, cols]
            grad = grads[:, head * HEAD_DIM : (head + 1) * HEAD_DIM]
            raw = dot(keys, query, NT) * scale - log_ref[m, pl.ds(head, 1), rows]
            probs = jnp.exp(jnp.where(allowed, raw, -1e30))
            dv_ref[upto, :] += dot(probs.astype(BF16), grad, NN)
            prob_grad = dot(values, grad, NT)
            inner = jnp.sum(probs * prob_grad, axis=0, keepdims=True)
            rounded = (probs * (prob_grad - inner) * scale).astype(BF16)
            dk_ref[upto, :] += dot(rounded, query, NN)
            dq = dot(kt_ref[:, upto], rounded, NN).T
            dqkv_own[m, rows, cols] = rope_back(dq, cosine, signed).astype(BF16)

    def attend_end(m):
        dk = rope_back(dk_ref[...], cos_ref[...], sin_ref[...])
        dqkv_own[m, :, pl.ds(k_col, HEAD_DIM)] = dk.astype(BF16)
        dqkv_own[m, :, pl.ds(v_col, HEAD_DIM)] = dv_ref[...].astype(BF16)
        grad_cross(m).start()

    def head_part(m):
        grad_cross(m).wait_recv()

        @pl.loop(0, n)
        def _(p):
            rows = rows_at(p * tokens, tokens)
            value = dot(dqkv_own[m, rows, :], w_own[...], NT)
            part[m, p] = (value + dot(dqkv_oth[m, rows, :], w_oth[...], NT)).astype(BF16)

    def result():
        total[last] = total[last] + part[batches, r].astype(F32)
        out_rs.add_received(total.at[last])
        result_ref[...] = total[last].astype(BF16)
        store(0, 0, result_ref, result_out).start()

    def input_grad(m):
        head_rs[m].total(total.at[m])
        s = scales_ref[0, m][:, :1]
        x = x_ref[m].astype(F32)
        gain_ref[0, pl.ds(m, 1), :] = jnp.sum(total[m] * x * s, axis=0, keepdims=True)
        total[m] = total[m] * gain_in[...]
        inner = jnp.sum(total[m] * x, axis=1, keepdims=True)
        row_out[m] = jnp.broadcast_to(inner, (tokens, 128))
        row_cross(m).start()
        row_cross(m).wait_recv()
        inner = row_out[m, :, pl.ds(0, 1)] + row_in[m, :, pl.ds(0, 1)]
        total[m] = total[m] * s - x * ((s * s * s) * inner * (1.0 / WIDTH))
        store(1, m, total.at[m], grad_out.at[m]).start()

    def steps(item, first_step, last_step):
        for s in range(first_step, last_step):
            item.step(s)

    half = (n + 1) // 2
    spread_step((0, 1, 2), 0)
    shard_load.wait()
    gather.start()
    for copy in loads[1:first]:
        copy.wait()
    loads[0].wait()
    for at in range(last * n, len(order)):
        down_part(at)
    out_rs.step(1)
    n1_load.start()
    attend_start(0)
    for q in range(n // 2):
        attend_back(0, q)
    steps(gather, 1, half)
    for q in range(n // 2, n):
        attend_back(0, q)
    attend_end(0)
    steps(gather, half, n - 1)
    for copy in loads[first:]:
        copy.wait()
    head_part(0)
    head_rs[0].step(1)
    for at in range(1, count):
        spread_step((0,), at)
    steps(gather, n - 1, n)
    steps(out_rs, 2, half + 1)
    for side in range(2):
        place = c if side == 0 else 1 - c
        value = dot(o_ref[side], dz_ref[...].reshape(batches * length, depth), TN)
        o_grad[rows_at(place * q_width, q_width), :] = value.astype(BF16)
    total_step((2, 3), 0)
    attend_start(1)
    for q in range(n // 2):
        attend_back(1, q)
    steps(head_rs[0], 2, half + 1)
    for at in range(1, count):
        spread_step((1,), at)
    for q in range(n // 2, n):
        attend_back(1, q)
    attend_end(1)
    steps(out_rs, half + 1, n)
    total_step((2, 3), 1)
    head_part(1)
    head_rs[1].step(1)
    n1_load.wait()
    for side in range(2):
        place = c if side == 0 else 1 - c
        dqkv = (dqkv_own if side == 0 else dqkv_oth)[...].reshape(batches * length, width)
        value = dot(wide_ref[pl.ds(0, batches * length), :], dqkv, TN)
        qkv_grad[:, lanes(place * width, width)] = value.astype(BF16)
    total_step((0, 1), 0)
    steps(head_rs[0], half + 1, n)
    result()
    total_step((2, 3), 2)
    input_grad(0)
    total_step((0, 1), 1)
    turn, last_turn = 2, 2 * count
    for s in range(2, n):
        head_rs[1].step(s)
        if turn <= last_turn:
            total_step((0, 1), turn)
        if turn + 1 <= last_turn:
            total_step((2, 3), turn + 1)
        turn += 1
    input_grad(1)
    gain_ref[0, pl.ds(batches, batches), :] = ffn_gains[pl.ds(0, batches), :]
    gains[0].start()
    while turn <= last_turn:
        total_step((0, 1), turn)
        if turn + 1 <= last_turn:
            total_step((2, 3), turn + 1)
        turn += 1
    stores = [
        pltpu.make_async_copy(qkv_sum, qkv_out, load_sems.at[0]),
        pltpu.make_async_copy(o_sum, o_out, load_sems.at[1]),
    ]
    for copy in stores:
        copy.start()
    gain_ref[1] = gains[0].total()
    gains[1].start()
    for at in range(1, count):
        spread_step((2,), at)
    spread_step((0, 1, 2), count)
    for m in range(batches):
        grad_cross(m).wait_send()
        row_cross(m).wait_send()
        head_rs[m].drain()
        store(1, m, total.at[m], grad_out.at[m]).wait()
    out_rs.drain()
    store(0, 0, result_ref, result_out).wait()
    gather.drain()
    gain_out[...] = gains[1].total()
    for item in gains:
        item.drain()
    for item in spreads + reduces + gatherers:
        item.drain()
    for copy in stores:
        copy.wait()


def backward(
    prefix, x, scales, gain, tables, logs, ffn_gains, mid, dz_own, dz_oth, wo, wo_from, wq, wk, wv, qkv,
    a_own, a_oth, wdown, n1, o_own, o_oth, down, gate, up, heads, shared_kv, dp_count,
):
    batches, tokens, depth = x.shape
    n = dz_own.shape[1]
    length, width = qkv.shape[1:]
    rows, q_width = o_own.shape
    share = a_own.shape[1]
    bits = list(range(dp_count.bit_length() - 1))
    vmem = pl.BlockSpec(memory_space=pltpu.VMEM)
    anywhere = pl.BlockSpec(memory_space=pl.ANY)
    gathered = (batches, n, tokens, depth)
    boxes = (batches + 1, n - 1, tokens, depth)
    sums = [(depth, 2 * width), (2 * q_width, depth)]
    shapes = [(mid.shape, F32), ((tokens, depth), BF16)] + [(item, BF16) for item in sums]
    shapes += [(item.shape, BF16) for item in (down, gate, up)] + [((8, depth), F32)]
    dma = pltpu.SemaphoreType.DMA
    return pl.pallas_call(
        functools.partial(backward_kernel, n, heads, shared_kv, bits),
        in_specs=[vmem] * 8 + [anywhere] * 18,
        out_specs=[anywhere] * 7 + [vmem],
        out_shape=[jax.ShapeDtypeStruct(*item) for item in shapes],
        input_output_aliases={23: 4, 24: 5, 25: 6},
        scratch_shapes=[
            pltpu.VMEM(gathered, BF16), pltpu.VMEM((2, tokens, depth), BF16), pltpu.VMEM(gathered[1:], BF16),
            pltpu.VMEM((2, q_width, depth), BF16),
            pltpu.VMEM((depth, width), BF16), pltpu.VMEM((depth, width), BF16),
            pltpu.VMEM(qkv.shape, BF16),
            pltpu.VMEM((length, HEAD_DIM), F32), pltpu.VMEM((length, HEAD_DIM), F32),
            pltpu.VMEM((HEAD_DIM, length), BF16), pltpu.VMEM(qkv.shape, BF16), pltpu.VMEM(qkv.shape, BF16),
            pltpu.VMEM((batches + 1,) + gathered[1:], BF16), pltpu.VMEM(boxes, BF16), pltpu.VMEM(boxes, BF16),
            pltpu.VMEM(mid.shape, F32),
            pltpu.VMEM((2, 2, tokens, share), BF16),
            pltpu.VMEM((max(2 * share, rows), depth), BF16), pltpu.VMEM((2, rows, q_width), BF16),
            pltpu.VMEM(sums[0], BF16), pltpu.VMEM(sums[1], BF16),
            pltpu.VMEM(sums[0], BF16), pltpu.VMEM(sums[1], BF16),
            [
                [pltpu.VMEM((2, item[0] // 2 ** (level + 2), item[1]), BF16) for level in range(len(bits))]
                for item in sums
            ],
            pltpu.VMEM((batches, tokens, 128), F32), pltpu.VMEM((batches, tokens, 128), F32),
            pltpu.VMEM((tokens, depth), BF16), pltpu.VMEM((2, 8, depth), F32),
            pltpu.VMEM((n - 1, 8, depth), F32), pltpu.VMEM((dp_count - 1, 8, depth), F32),
            dma((20,)), dma((2,)), dma((2, 2)),
            dma((batches + 1, 2, n - 1)), dma((batches + 1, 2, n - 1)),
            dma((2 * batches,)), dma((2 * batches,)), dma((2, batches)),
            dma((2, 2, len(bits))), dma((2, 2, len(bits))), dma((2, 2, len(bits))), dma((2, 2, len(bits))),
            dma((3, 2, len(bits))), dma((3, 2, len(bits))), dma((n, 3)), dma((n, 2)),
            dma((2, max(n, dp_count) - 1)), dma((2, max(n, dp_count) - 1)),
        ],
        compiler_params=communicate(3, 62),
        cost_estimate=cost(2e11, 100 * MIB),
    )(
        prefix, x, scales, gain, *tables, logs, ffn_gains, mid, dz_own, dz_oth, wo, wo_from, wq, wk, wv, qkv,
        a_own, a_oth, wdown, n1, o_own, o_oth, down, gate, up,
    )


def last_spread(values, meanwhile):
    count = lax.axis_size("dp")
    half = values.shape[0] // 2
    size, sides, halves = half // 2, [], []
    for way, bit in enumerate((0, count.bit_length() - 2)):
        sides.append((lax.axis_index("dp") >> bit) & 1)
        own = lax.dynamic_slice_in_dim(values, way * half + sides[-1] * size, size, 0)
        halves.append((own, lax.ppermute(own, "dp", [(i, i ^ (1 << bit)) for i in range(count)])))
    halves, meanwhile = lax.optimization_barrier((halves, meanwhile))
    pieces = []
    for side, (own, got) in zip(sides, halves):
        pieces += [jnp.where(side == 0, own, got), jnp.where(side == 0, got, own)]
    return jnp.concatenate([piece.astype(F32) for piece in pieces]), meanwhile


def body(
    hidden_in,
    attn_gain,
    ffn_gain,
    query_weight,
    key_weight,
    value_weight,
    output_weight,
    gate_weight,
    up_weight,
    down_weight,
    prefix_len,
    out_grad,
):
    col_count, row_count = lax.axis_size("col"), lax.axis_size("row")
    batches, tokens, _ = hidden_in.shape
    length = tokens * row_count
    heads = query_weight.shape[1] // HEAD_DIM // col_count
    row_kv = key_weight.shape[1] // HEAD_DIM
    shared_kv = row_kv < col_count
    q_width = heads * HEAD_DIM
    prefix_row = prefix_len.reshape(1, batches)
    (
        cosine, signed, n1, n2, g_own, qkv, logs, o_own, o_oth, middle, scales, out_from,
        a_own, a_oth, dg_own, dg_oth, du_own, du_oth, first_result,
    ) = forward(
        prefix_row, hidden_in, attn_gain.reshape(1, -1), ffn_gain.reshape(1, -1), out_grad,
        query_weight, key_weight, value_weight, output_weight, gate_weight, up_weight, down_weight,
        row_count, heads, shared_kv,
    )

    def flat(*items):
        return tuple(item.reshape(batches * length, item.shape[-1]) for item in items)

    dp_count = lax.axis_size("dp")
    a_own, a_oth, *grads = flat(a_own, a_oth, dg_own, dg_oth, du_own, du_oth)
    dz, dz_oth, middle_grad, down_sum, gate_sum, up_sum, ffn_gains = unit_grads(
        middle, scales, out_grad, ffn_gain.reshape(1, -1), *flat(g_own, n2), (a_own, a_oth, *grads),
        gate_weight, up_weight, row_count, dp_count,
    )
    in_grad, last_result, qkv_sum, output_sum, down_sum, gate_sum, up_sum, gains = backward(
        prefix_row, hidden_in, scales, attn_gain.reshape(1, -1), (cosine, signed), logs, ffn_gains,
        middle, dz, dz_oth, output_weight, out_from, query_weight, key_weight, value_weight, qkv, a_own, a_oth, down_weight,
        *flat(n1, o_own, o_oth), down_sum, gate_sum, up_sum, heads, shared_kv, dp_count,
    )
    result = jnp.stack([first_result, last_result])
    width = q_width + 2 * HEAD_DIM

    def columns(first, size, shared):
        pieces = [
            qkv_sum[:, side * width + first : side * width + first + size].astype(F32)
            for side in range(col_count)
        ]
        return sum(pieces) if shared else jnp.concatenate(pieces, axis=1)

    gain_one, gain_two = gains[:batches].sum(axis=0), gains[batches : 2 * batches].sum(axis=0)
    meanwhile = (
        result,
        middle_grad + in_grad,
        gain_one,
        gain_two,
        columns(0, q_width, False),
        columns(q_width, HEAD_DIM, shared_kv),
        columns(q_width + HEAD_DIM, HEAD_DIM, shared_kv),
        output_sum.astype(F32),
        gate_sum.astype(F32),
        down_sum.astype(F32),
    )
    up_sum, (*first, down_sum) = last_spread(up_sum, meanwhile)
    return (*first, up_sum, down_sum)


def solution(mesh):
    return jax.shard_map(
        body,
        mesh=mesh,
        in_specs=(
            P(None, ("dp", "row"), "col"),
            P("col"),
            P("col"),
            P("col", "row"),
            P("col", "row"),
            P("col", "row"),
            P("row", "col"),
            P("col", "row"),
            P("col", "row"),
            P("row", "col"),
            P(None, "dp"),
            P(None, ("dp", "row"), "col"),
        ),
        out_specs=(
            P(None, ("dp", "row"), "col"),
            P(None, ("dp", "row"), "col"),
            P("col"),
            P("col"),
            P("col", "row"),
            P("col", "row"),
            P("col", "row"),
            P("row", "col"),
            P("col", "row"),
            P("col", "row"),
            P("row", "col"),
        ),
        check_vma=False,
    )
```
